32 devices in a mesh: groups: 2 (over x), tensor: 16 (over z, y, core).
Axes of the slice: x: 2, y: 2, z: 4, core: 2. Of those that a mesh axis runs over, the one named last changes fastest.
Arguments:
- queries: bfloat16 [2, 128, 8192], P(None, ('groups', 'tensor')), parts along dimension 1, may hold values from -8 to 8
- new_keys: bfloat16 [2, 128, 1024], P(None, ('groups', 'tensor')), parts along dimension 1, may hold values from -6 to 6
- new_values: bfloat16 [2, 128, 1024], P(None, ('groups', 'tensor')), parts along dimension 1, may hold values from -24 to 24
- cache_keys: bfloat16 [128, 512, 1024], P(('groups', 'tensor')), parts along dimension 0, may hold values from -8 to 8
- cache_values: bfloat16 [128, 512, 1024], P(('groups', 'tensor')), parts along dimension 0, may hold values from -24 to 24
- kv_len: int32 [128], P(('groups', 'tensor')), parts along dimension 0, may hold values from 2 to 512, as said below
- adapter_rows: int32 [24], P('groups'), parts along dimension 0, may hold values from 1 to 8, 64 in all
- adapter_rank: int32 [12], replicated, may hold values from 1 to 2, as said below
- adapter_owner: int32 [12], replicated, may hold values from 0 to 15, as said below
- out_weight: bfloat16 [8192, 8192], P(None, 'tensor'), may hold values from -0.0625 to 0.0625
- store_down: bfloat16 [16, 8192, 128], P('tensor'), may hold values from -0.0625 to 0.0625
- store_up: bfloat16 [16, 8192, 128], P('tensor'), may hold values from -0.5 to 0.5
Outputs:
- projected: bfloat16 [2, 128, 8192], P(None, 'groups', 'tensor'), parts along dimension 1
The draws below stay inside these ranges and needn't reach their ends.
There are 2 independent parts, one for each index of `groups`. The reference program is written for one: setup_inputs(seed, part) draws one part's arguments, and reference() takes and returns one part's arrays. A program takes and returns all parts, laid end to end along the dimension named above; an argument that names none is the same for every part. Nothing has to cross between parts.
Inputs may be any that keep to these rules, and one draw needn't show every extreme that they name: `kv_len`: 512 is reached by some request of every part. `adapter_rows`: sums to 64; some adapter has exactly 8 requests. `adapter_rank`: exactly 4 adapters have 2 blocks, the others 1. `adapter_owner`: the blocks of all adapters tile the store: every store index holds exactly one block.
All inputs are finite; a program needn't handle non-finite values.
Results may differ from the reference program's by a relative error of at most 0.0062.
Values may be sent and summed in bfloat16 or wider, within the bound.
No kernel may reach another device: no remote copies, remote signals or barrier semaphores. Data moves between devices by JAX's collectives and lax.ppermute only.
A program may use at most 128 MiB of HBM per device.

```python
import math
import jax
import jax.numpy as jnp
import numpy as np
from jax import lax

D = 8192
HQ = 64
KVH = 8
HD = 128
RB = 128
STEPS = 2
MOST = 8
CACHE = 512
ROWS = 64
NBLK = 16
NA = 12


def rank_layout(key):
    first, second = jax.random.split(key)
    picks = jax.random.permutation(first, NA)
    ranks = (1 + (picks < NBLK - NA).astype(jnp.int32)).astype(jnp.int32)
    order = jax.random.permutation(second, NA)
    laid = ranks[order]
    positions = (jnp.cumsum(laid) - laid).astype(jnp.int32)
    owners = jnp.zeros((NA,), jnp.int32).at[order].set(positions)
    return (ranks, owners)


def draw_adapter_rank(key, part):
    return rank_layout(key)[0]


def draw_adapter_owner(key, part):
    return rank_layout(key)[1]


def draw_kv_len(key, part):
    key = jax.random.fold_in(key, 7)
    first, second = jax.random.split(key)
    lengths = jax.random.randint(first, (ROWS,), 2, CACHE + 1)
    spot = jax.random.randint(second, (), 0, ROWS)
    return jnp.where(jnp.arange(ROWS) == spot, CACHE, lengths).astype(jnp.int32)


def draw_queries(key, part):
    key = jax.random.fold_in(key, 11)
    values = jnp.clip(jax.random.normal(key, (STEPS, ROWS, D), jnp.float32), -8.0, 8.0)
    return values.astype(jnp.bfloat16)


def draw_cache_keys(key, part):
    key = jax.random.fold_in(key, 13)
    values = jnp.clip(jax.random.normal(key, (ROWS, CACHE, KVH * HD), jnp.float32), -8.0, 8.0)
    return values.astype(jnp.bfloat16)


def block_scale(key, dims, cuts, low, high):
    level = 1.0
    for axis_at, shards_of in cuts:
        heights = jax.random.uniform(jax.random.fold_in(jax.random.fold_in(key, 6), axis_at), (shards_of,), jnp.float32, low / len(cuts), high / len(cuts))
        level = level * jnp.repeat(jnp.exp(heights), dims[axis_at] // shards_of).reshape((-1,) + (1,) * (len(dims) - 1 - axis_at))
    return level


def length_profile(count, total, reach, lean):
    loads = [(1 << 20) // math.isqrt(grade ** lean) + 1 for grade in range(2, count + 1)]
    surplus, given = total - reach - (count - 1), [1] * (count - 1)
    while surplus > 0:
        movable = [i for i in range(count - 1) if given[i] < reach]
        mass, remaining = sum([loads[i] for i in movable]), surplus
        for i in movable:
            extra = min(reach - given[i], max(1, remaining * loads[i] // mass), surplus)
            given[i] = given[i] + extra
            surplus = surplus - extra
    return np.array([reach] + given)


def uneven(own_key, amount, total, most, lean):
    if amount == 2:
        one = jax.random.randint(own_key, (), max(1, total - most), min(most, total - 1) + 1)
        return jnp.stack([one, total - one])
    tallies = jnp.asarray(length_profile(amount, total, most, lean), jnp.int32)
    couples = (amount - 1) // 2
    source_of, sink = tallies[1:1 + 2 * couples:2], tallies[2:2 + 2 * couples:2]
    slack = jnp.minimum(source_of - 1, most - sink)
    moved = jax.random.randint(jax.random.fold_in(own_key, 1), (couples,), 0, 1 << 20) % (slack + 1)
    tallies = tallies.at[1:1 + 2 * couples:2].set(source_of - moved).at[2:2 + 2 * couples:2].set(sink + moved)
    return tallies[jax.random.permutation(jax.random.fold_in(own_key, 2), amount)]


def scatter_about(rng, shape, width, reach, cuts=(), kind=jnp.bfloat16):
    values = width * jax.random.normal(rng, shape, jnp.float32)
    if cuts:
        values = values * block_scale(rng, shape, cuts, -0.22, 0.18)
    return jnp.clip(values, -reach, reach).astype(kind)


def setup_inputs(seed: int = 0, part: int = 0) -> dict:
    splits = jax.random.split(jax.random.key(seed), 13)
    own_keys = jax.random.split(jax.random.fold_in(splits[12], part), 13)
    queries = draw_queries(jax.random.fold_in(jax.random.fold_in(splits[12], part), 71), part)
    new_keys = scatter_about(own_keys[1], (STEPS, ROWS, KVH * HD), 1.0, 6.0, ((1, 16),))
    new_values = scatter_about(own_keys[2], (STEPS, ROWS, KVH * HD), 4.0, 24.0, ((1, 16),))
    cache_keys = draw_cache_keys(jax.random.fold_in(jax.random.fold_in(splits[12], part), 71), part)
    cache_values = scatter_about(own_keys[4], (ROWS, CACHE, KVH * HD), 4.0, 24.0, ((0, 16),))
    kv_len = draw_kv_len(jax.random.fold_in(jax.random.fold_in(splits[12], part), 71), part)
    adapter_rows = uneven(own_keys[6], NA, ROWS, MOST, 2).astype(jnp.int32)
    adapter_rank = draw_adapter_rank(jax.random.fold_in(splits[12], 71), part)
    adapter_owner = draw_adapter_owner(jax.random.fold_in(splits[12], 71), part)
    out_weight = scatter_about(splits[9], (D, D), D ** -0.5, 0.0625, ((1, 16),))
    store_down = scatter_about(splits[10], (NBLK, D, RB), D ** -0.5, 0.0625, ((0, 16),))
    store_up = scatter_about(splits[11], (NBLK, D, RB), RB ** -0.5, 0.5, ((0, 16),))
    return {"queries": queries, "new_keys": new_keys, "new_values": new_values, "cache_keys": cache_keys, "cache_values": cache_values, "kv_len": kv_len, "adapter_rows": adapter_rows, "adapter_rank": adapter_rank, "adapter_owner": adapter_owner, "out_weight": out_weight, "store_down": store_down, "store_up": store_up}


def attend(queries, new_keys, new_values, cache_keys, cache_values, kv_len):
    rows = queries.shape[1]
    group = HQ // KVH
    scale = HD ** -0.5
    query = queries.astype(jnp.float32).reshape(STEPS, rows, KVH, group, HD)
    ckeys = cache_keys.astype(jnp.float32).reshape(rows, CACHE, KVH, HD)
    cvals = cache_values.astype(jnp.float32).reshape(rows, CACHE, KVH, HD)
    nkeys = new_keys.astype(jnp.float32).reshape(STEPS, rows, KVH, HD)
    nvals = new_values.astype(jnp.float32).reshape(STEPS, rows, KVH, HD)
    older = jnp.einsum("trkgd,rlkd->trkgl", query, ckeys) * scale
    fresh = jnp.einsum("trkgd,srkd->trkgs", query, nkeys) * scale
    live = jnp.arange(CACHE)[None, :] < kv_len[:, None]
    older = jnp.where(live[None, :, None, None, :], older, -jnp.inf)
    causal = jnp.arange(STEPS)[:, None] >= jnp.arange(STEPS)[None, :]
    fresh = jnp.where(causal[:, None, None, None, :], fresh, -jnp.inf)
    top = jnp.maximum(jnp.max(older, axis=-1), jnp.max(fresh, axis=-1))[..., None]
    e_older = jnp.exp(older - top)
    e_fresh = jnp.exp(fresh - top)
    total = jnp.sum(e_older, axis=-1, keepdims=True) + jnp.sum(e_fresh, axis=-1, keepdims=True)
    p_older = (e_older / total).astype(jnp.bfloat16).astype(jnp.float32)
    p_fresh = (e_fresh / total).astype(jnp.bfloat16).astype(jnp.float32)
    mixed = jnp.einsum("trkgl,rlkd->trkgd", p_older, cvals) + jnp.einsum("trkgs,srkd->trkgd", p_fresh, nvals)
    return mixed.reshape(STEPS, rows, D).astype(jnp.bfloat16)


def reference(queries, new_keys, new_values, cache_keys, cache_values, kv_len, adapter_rows, adapter_rank, adapter_owner, out_weight, store_down, store_up):
    attended = attend(queries, new_keys, new_values, cache_keys, cache_values, kv_len)
    base = jnp.dot(attended.reshape(STEPS * ROWS, D), out_weight, preferred_element_type=jnp.float32).reshape(STEPS, ROWS, D)
    ends = jnp.cumsum(adapter_rows).astype(jnp.int32)
    starts = (ends - adapter_rows).astype(jnp.int32)
    row_ids = jnp.arange(ROWS, dtype=jnp.int32)
    row_adapter = jnp.sum((row_ids[:, None] >= ends[None, :]).astype(jnp.int32), axis=1)
    block_numbers = jnp.arange(NBLK, dtype=jnp.int32)
    owned = (block_numbers[None, :] >= adapter_owner[:, None]) & (block_numbers[None, :] < adapter_owner[:, None] + adapter_rank[:, None])
    block_adapter = jnp.sum(jnp.where(owned, jnp.arange(NA, dtype=jnp.int32)[:, None], 0), axis=0).astype(jnp.int32)
    firsts = jnp.minimum(starts, ROWS - MOST).astype(jnp.int32)

    def one_block(delta, block):
        adapter = block_adapter[block]
        first = firsts[adapter].astype(jnp.int32)
        rows = lax.dynamic_slice_in_dim(attended, first, MOST, 1)
        own = row_adapter[first + jnp.arange(MOST, dtype=jnp.int32)] == adapter
        low = jnp.dot(rows.reshape(STEPS * MOST, D), store_down[block], preferred_element_type=jnp.float32).reshape(STEPS, MOST, RB)
        low = jnp.where(own[None, :, None], low, 0.0).astype(jnp.bfloat16)
        part = jnp.dot(low.reshape(STEPS * MOST, RB), store_up[block].T, preferred_element_type=jnp.float32).reshape(STEPS, MOST, D)
        current = lax.dynamic_slice_in_dim(delta, first, MOST, 1)
        return lax.dynamic_update_slice_in_dim(delta, current + part, first, 1), None

    delta, unused = lax.scan(one_block, jnp.zeros((STEPS, ROWS, D), jnp.float32), block_numbers)
    return (base + delta).astype(jnp.bfloat16)
```

```python
import functools

import jax
import jax.numpy as jnp
from jax import lax
from jax.experimental import pallas as pl
from jax.experimental.pallas import tpu as pltpu
from jax.sharding import PartitionSpec as P

HQ = 64
KVH = 8
HD = 128
GROUP = HQ // KVH
MOST = 8
F32 = jnp.float32
BF16 = jnp.bfloat16
NT = (((1,), (1,)), ((), ()))


def dot(a, b):
    return jnp.dot(a, b, preferred_element_type=F32)


def dot_nt(a, b):
    return lax.dot_general(a, b, NT, preferred_element_type=F32)


def attend_kernel(
    len_ref, q_ref, nk_ref, nv_ref, k_ref, v_ref, out_ref, qs, nks, nvs, mixed
):
    steps, rows, width = q_ref.shape
    cache = k_ref.shape[1]
    both = steps * rows
    pack = steps * GROUP
    r = pl.program_id(0)

    @pl.when(r == 0)
    def _():
        flat = jnp.concatenate([q_ref[t].astype(F32) for t in range(steps)], axis=0)
        for k in range(KVH):
            heads = jnp.stack(
                [flat[:, (k * GROUP + g) * HD : (k * GROUP + g + 1) * HD] for g in range(GROUP)]
            )
            turned = jnp.swapaxes(heads, 0, 1)
            for i in range(rows):
                qs[i, k] = jnp.concatenate(
                    [turned[t * rows + i] for t in range(steps)], axis=0
                ).astype(BF16)
        for src, dst in ((nk_ref, nks), (nv_ref, nvs)):
            fresh = [src[t].astype(F32) for t in range(steps)]
            fresh.append(jnp.zeros((16 - both, src.shape[2]), F32))
            dst[...] = jnp.concatenate(fresh, axis=0).astype(BF16)

    scale = HD ** (-0.5)
    older = jnp.concatenate(
        [dot_nt(qs[r, k], k_ref[0, :, k * HD : (k + 1) * HD]) for k in range(KVH)], axis=0
    )
    fresh = jnp.concatenate(
        [dot_nt(qs[r, k], nks[:, k * HD : (k + 1) * HD]) for k in range(KVH)], axis=0
    )
    place = lax.broadcasted_iota(jnp.int32, older.shape, 1)
    older = jnp.where(place < len_ref[r], older * scale, -jnp.inf)
    slot = lax.broadcasted_iota(jnp.int32, fresh.shape, 1)
    step = (lax.broadcasted_iota(jnp.int32, fresh.shape, 0) // GROUP) % steps
    seen = (slot < both) & (slot % rows == r) & (slot // rows <= step)
    fresh = jnp.where(seen, fresh * scale, -jnp.inf)
    top = jnp.maximum(
        jnp.max(older, axis=1, keepdims=True), jnp.max(fresh, axis=1, keepdims=True)
    )
    e_older = jnp.exp(older - top)
    e_fresh = jnp.exp(fresh - top)
    total = jnp.sum(e_older, axis=1, keepdims=True) + jnp.sum(e_fresh, axis=1, keepdims=True)
    inverse = 1.0 / total
    p_older = (e_older * inverse).astype(BF16)
    p_fresh = (e_fresh * inverse).astype(BF16)
    for k in range(KVH):
        own = slice(k * pack, (k + 1) * pack)
        cols = slice(k * HD, (k + 1) * HD)
        mixed[r, k] = dot(p_older[own], v_ref[0, :, cols]) + dot(p_fresh[own], nvs[:, cols])

    @pl.when(r == rows - 1)
    def _():
        for k in range(KVH):
            turned = jnp.stack(
                [
                    mixed[i, k, t * GROUP : (t + 1) * GROUP, :]
                    for t in range(steps)
                    for i in range(rows)
                ]
            )
            heads = jnp.swapaxes(turned, 0, 1)
            for g in range(GROUP):
                at = (k * GROUP + g) * HD
                out_ref[:, at : at + HD] = heads[g].astype(BF16)


def attend(queries, new_keys, new_values, cache_keys, cache_values, kv_len):
    steps, rows, width = queries.shape
    cache, kv_width = cache_keys.shape[1:]
    pack = steps * GROUP
    whole = lambda r, lens: (0, 0, 0)
    mine = lambda r, lens: (r, 0, 0)
    flops = 4 * rows * steps * HQ * cache * HD
    return pl.pallas_call(
        attend_kernel,
        out_shape=jax.ShapeDtypeStruct((steps * rows, width), BF16),
        grid_spec=pltpu.PrefetchScalarGridSpec(
            num_scalar_prefetch=1,
            grid=(rows,),
            in_specs=[
                pl.BlockSpec((steps, rows, width), whole),
                pl.BlockSpec((steps, rows, kv_width), whole),
                pl.BlockSpec((steps, rows, kv_width), whole),
                pl.BlockSpec((1, cache, kv_width), mine),
                pl.BlockSpec((1, cache, kv_width), mine),
            ],
            out_specs=pl.BlockSpec((steps * rows, width), lambda r, lens: (0, 0)),
            scratch_shapes=[
                pltpu.VMEM((rows, KVH, pack, HD), BF16),
                pltpu.VMEM((16, kv_width), BF16),
                pltpu.VMEM((16, kv_width), BF16),
                pltpu.VMEM((rows, KVH, pack, HD), F32),
            ],
        ),
        compiler_params=pltpu.CompilerParams(vmem_limit_bytes=24 * 2**20),
        cost_estimate=pl.CostEstimate(
            flops=flops,
            bytes_accessed=4 * rows * cache * kv_width,
            transcendentals=rows * steps * HQ * cache,
        ),
        name="attend",
    )(kv_len, queries, new_keys, new_values, cache_keys, cache_values)


def row_place(index, steps, rows):
    both = steps * rows
    return (index // both) * rows + index % rows, (index % both) // rows


def delta_kernel(steps, rows, count_ref, rank_ref, owner_ref, a_ref, d_ref, u_ref, out_ref):
    block = lax.axis_index("tensor")
    total = a_ref.shape[0]
    parts, slots, cols = out_ref.shape
    start = jnp.int32(0)
    first = jnp.int32(0)
    amount = jnp.int32(0)
    for a in range(count_ref.shape[0]):
        owned = (owner_ref[a] <= block) & (block < owner_ref[a] + rank_ref[a])
        first = jnp.where(owned, start, first)
        amount = jnp.where(owned, count_ref[a], amount)
        start = start + count_ref[a]
    low = dot(a_ref[...], d_ref[0]).astype(BF16)
    slot = lax.broadcasted_iota(jnp.int32, (slots, total), 0)
    request, step = row_place(lax.broadcasted_iota(jnp.int32, (slots, total), 1), steps, rows)
    nth = slot % MOST
    pick = (step == slot // MOST) & (request == first + nth) & (nth < amount)
    chosen = dot(pick.astype(F32).astype(BF16), low).astype(BF16)
    for p in range(parts):
        out_ref[p] = dot_nt(chosen, u_ref[0, p * cols : (p + 1) * cols, :]).astype(BF16)


def delta_parts(gathered, store_down, store_up, tables, steps, rows, parts):
    total, width = gathered.shape
    slots = steps * MOST
    cols = width // parts
    rank_w = store_down.shape[2]
    vmem = pl.BlockSpec(memory_space=pltpu.VMEM)
    smem = pl.BlockSpec(memory_space=pltpu.SMEM)
    return pl.pallas_call(
        functools.partial(delta_kernel, steps, rows),
        out_shape=jax.ShapeDtypeStruct((parts, slots, cols), BF16),
        in_specs=[smem] * 3 + [vmem] * 3,
        out_specs=vmem,
        compiler_params=pltpu.CompilerParams(vmem_limit_bytes=40 * 2**20),
        cost_estimate=pl.CostEstimate(
            flops=2 * (total + slots) * width * rank_w,
            bytes_accessed=2 * width * (total + 2 * rank_w + slots),
            transcendentals=0,
        ),
        name="delta",
    )(*tables, gathered, store_down, store_up)


def base_kernel(a_ref, w_ref, out_ref):
    @pl.when(pl.program_id(0) == 0)
    def _():
        out_ref[...] = jnp.zeros_like(out_ref)

    out_ref[...] += dot(a_ref[...], w_ref[...])


def base_part(gathered, out_weight):
    total, width = gathered.shape
    cols = out_weight.shape[1]
    deep = 1024
    return pl.pallas_call(
        base_kernel,
        out_shape=jax.ShapeDtypeStruct((total, cols), F32),
        grid=(width // deep,),
        in_specs=[
            pl.BlockSpec((total, deep), lambda k: (0, k)),
            pl.BlockSpec((deep, cols), lambda k: (k, 0)),
        ],
        out_specs=pl.BlockSpec((total, cols), lambda k: (0, 0)),
        compiler_params=pltpu.CompilerParams(vmem_limit_bytes=24 * 2**20),
        cost_estimate=pl.CostEstimate(
            flops=2 * total * width * cols,
            bytes_accessed=2 * width * (total + cols) + 4 * total * cols,
            transcendentals=0,
        ),
        name="base",
    )(gathered, out_weight)


def join_kernel(rows, count_ref, rank_ref, owner_ref, base_ref, delta_ref, out_ref):
    steps, requests, cols = out_ref.shape
    parts, slots, _ = delta_ref.shape
    total = base_ref.shape[0]
    wide = parts * slots
    entry = lax.broadcasted_iota(jnp.int32, (1, wide), 1)
    block = entry // slots
    first = jnp.zeros((1, wide), jnp.int32)
    amount = jnp.zeros((1, wide), jnp.int32)
    start = jnp.int32(0)
    for a in range(count_ref.shape[0]):
        owned = (owner_ref[a] <= block) & (block < owner_ref[a] + rank_ref[a])
        first = jnp.where(owned, start, first)
        amount = jnp.where(owned, count_ref[a], amount)
        start = start + count_ref[a]
    nth = entry % MOST
    goal = jnp.where(nth < amount, first + nth, -1)
    goal_step = (entry % slots) // MOST
    request, step = row_place(lax.broadcasted_iota(jnp.int32, (total, 1), 0), steps, rows)
    place = (request == goal) & (step == goal_step)
    delta = dot(place.astype(F32).astype(BF16), delta_ref[...].reshape(wide, cols))
    result = (base_ref[...] + delta).astype(BF16)
    request, step = row_place(lax.broadcasted_iota(jnp.int32, (total, total), 1), steps, rows)
    goal = lax.broadcasted_iota(jnp.int32, (total, total), 0)
    order = (goal == step * requests + request).astype(F32).astype(BF16)
    turned = dot(order, result).astype(BF16)
    for t in range(steps):
        out_ref[t] = turned[t * requests : (t + 1) * requests]


def join(base, delta, tables, steps, rows):
    total, cols = base.shape
    vmem = pl.BlockSpec(memory_space=pltpu.VMEM)
    smem = pl.BlockSpec(memory_space=pltpu.SMEM)
    return pl.pallas_call(
        functools.partial(join_kernel, rows),
        out_shape=jax.ShapeDtypeStruct((steps, total // steps, cols), BF16),
        in_specs=[smem] * 3 + [vmem] * 2,
        out_specs=vmem,
        compiler_params=pltpu.CompilerParams(vmem_limit_bytes=24 * 2**20),
        name="join",
    )(*tables, base, delta)


def per_device(
    queries,
    new_keys,
    new_values,
    cache_keys,
    cache_values,
    kv_len,
    adapter_rows,
    adapter_rank,
    adapter_owner,
    out_weight,
    store_down,
    store_up,
):
    parts = lax.axis_size("tensor")
    steps, rows, width = queries.shape
    tables = (adapter_rows, adapter_rank, adapter_owner)
    attended = attend(queries, new_keys, new_values, cache_keys, cache_values, kv_len)
    gathered = lax.all_gather(attended, "tensor", axis=0, tiled=True)
    send = delta_parts(gathered, store_down, store_up, tables, steps, rows, parts)
    delta = lax.all_to_all(send, "tensor", split_axis=0, concat_axis=0, tiled=True)
    base = base_part(gathered, out_weight)
    return join(base, delta, tables, steps, rows)


def solution(mesh):
    in_specs = (
        P(None, ("groups", "tensor"), None),
        P(None, ("groups", "tensor"), None),
        P(None, ("groups", "tensor"), None),
        P(("groups", "tensor"), None, None),
        P(("groups", "tensor"), None, None),
        P(("groups", "tensor")),
        P("groups"),
        P(),
        P(),
        P(None, "tensor"),
        P("tensor", None, None),
        P("tensor", None, None),
    )
    out_specs = P(None, "groups", "tensor")
    return jax.shard_map(
        per_device, mesh=mesh, in_specs=in_specs, out_specs=out_specs, check_vma=False
    )
```

```python
import functools

import jax
import jax.numpy as jnp
from jax import lax
from jax.experimental import pallas as pl
from jax.experimental.pallas import tpu as pltpu
from jax.sharding import PartitionSpec as P

HQ = 64
KVH = 8
HD = 128
GROUP = HQ // KVH
MOST = 8
RING = 16
F32 = jnp.float32
BF16 = jnp.bfloat16
NT = (((1,), (1,)), ((), ()))


def dot(a, b):
    return jnp.dot(a, b, preferred_element_type=F32)


def dot_nt(a, b):
    return lax.dot_general(a, b, NT, preferred_element_type=F32)


def attend_kernel(
    len_ref, q_ref, nk_ref, nv_ref, k_ref, v_ref, out_ref, qs, nks, nvs, mixed
):
    steps, rows, width = q_ref.shape
    cache = k_ref.shape[1]
    both = steps * rows
    pack = steps * GROUP
    r = pl.program_id(0)

    @pl.when(r == 0)
    def _():
        flat = jnp.concatenate([q_ref[t].astype(F32) for t in range(steps)], axis=0)
        for k in range(KVH):
            heads = jnp.stack(
                [flat[:, (k * GROUP + g) * HD : (k * GROUP + g + 1) * HD] for g in range(GROUP)]
            )
            turned = jnp.swapaxes(heads, 0, 1)
            for i in range(rows):
                qs[i, k] = jnp.concatenate(
                    [turned[t * rows + i] for t in range(steps)], axis=0
                ).astype(BF16)
        for src, dst in ((nk_ref, nks), (nv_ref, nvs)):
            fresh = [src[t].astype(F32) for t in range(steps)]
            fresh.append(jnp.zeros((16 - both, src.shape[2]), F32))
            dst[...] = jnp.concatenate(fresh, axis=0).astype(BF16)

    scale = HD ** (-0.5)
    older = jnp.concatenate(
        [dot_nt(qs[r, k], k_ref[0, :, k * HD : (k + 1) * HD]) for k in range(KVH)], axis=0
    )
    fresh = jnp.concatenate(
        [dot_nt(qs[r, k], nks[:, k * HD : (k + 1) * HD]) for k in range(KVH)], axis=0
    )
    place = lax.broadcasted_iota(jnp.int32, older.shape, 1)
    older = jnp.where(place < len_ref[r], older * scale, -jnp.inf)
    slot = lax.broadcasted_iota(jnp.int32, fresh.shape, 1)
    step = (lax.broadcasted_iota(jnp.int32, fresh.shape, 0) // GROUP) % steps
    seen = (slot < both) & (slot % rows == r) & (slot // rows <= step)
    fresh = jnp.where(seen, fresh * scale, -jnp.inf)
    top = jnp.maximum(
        jnp.max(older, axis=1, keepdims=True), jnp.max(fresh, axis=1, keepdims=True)
    )
    e_older = jnp.exp(older - top)
    e_fresh = jnp.exp(fresh - top)
    total = jnp.sum(e_older, axis=1, keepdims=True) + jnp.sum(e_fresh, axis=1, keepdims=True)
    inverse = 1.0 / total
    p_older = (e_older * inverse).astype(BF16)
    p_fresh = (e_fresh * inverse).astype(BF16)
    for k in range(KVH):
        own = slice(k * pack, (k + 1) * pack)
        cols = slice(k * HD, (k + 1) * HD)
        mixed[r, k] = dot(p_older[own], v_ref[0, :, cols]) + dot(p_fresh[own], nvs[:, cols])

    @pl.when(r == rows - 1)
    def _():
        for k in range(KVH):
            turned = jnp.stack(
                [
                    mixed[i, k, t * GROUP : (t + 1) * GROUP, :]
                    for t in range(steps)
                    for i in range(rows)
                ]
            )
            heads = jnp.swapaxes(turned, 0, 1)
            for g in range(GROUP):
                at = (k * GROUP + g) * HD
                out_ref[:, at : at + HD] = heads[g].astype(BF16)


def attend(queries, new_keys, new_values, cache_keys, cache_values, kv_len):
    steps, rows, width = queries.shape
    cache, kv_width = cache_keys.shape[1:]
    pack = steps * GROUP
    whole = lambda r, lens: (0, 0, 0)
    mine = lambda r, lens: (r, 0, 0)
    flops = 4 * rows * steps * HQ * cache * HD
    return pl.pallas_call(
        attend_kernel,
        out_shape=jax.ShapeDtypeStruct((steps * rows, width), BF16),
        grid_spec=pltpu.PrefetchScalarGridSpec(
            num_scalar_prefetch=1,
            grid=(rows,),
            in_specs=[
                pl.BlockSpec((steps, rows, width), whole),
                pl.BlockSpec((steps, rows, kv_width), whole),
                pl.BlockSpec((steps, rows, kv_width), whole),
                pl.BlockSpec((1, cache, kv_width), mine),
                pl.BlockSpec((1, cache, kv_width), mine),
            ],
            out_specs=pl.BlockSpec((steps * rows, width), lambda r, lens: (0, 0)),
            scratch_shapes=[
                pltpu.VMEM((rows, KVH, pack, HD), BF16),
                pltpu.VMEM((16, kv_width), BF16),
                pltpu.VMEM((16, kv_width), BF16),
                pltpu.VMEM((rows, KVH, pack, HD), F32),
            ],
        ),
        compiler_params=pltpu.CompilerParams(vmem_limit_bytes=24 * 2**20),
        cost_estimate=pl.CostEstimate(
            flops=flops,
            bytes_accessed=4 * rows * cache * kv_width,
            transcendentals=rows * steps * HQ * cache,
        ),
        name="attend",
    )(
        kv_len,
        queries,
        new_keys,
        new_values,
        pltpu.with_memory_space_constraint(cache_keys, pltpu.HBM),
        pltpu.with_memory_space_constraint(cache_values, pltpu.HBM),
    )


def sender(slot, me, parts):
    if parts != RING:
        return slot
    ahead = (me // 4 + RING // 4 - slot // 4) % (RING // 4)
    return ahead * 4 + ((me % 4) ^ (slot % 4))


def row_place(index, me, parts, steps, rows):
    both = steps * rows
    return sender(index // both, me, parts) * rows + index % rows, (index % both) // rows


def gather(block, parts):
    if parts != RING:
        whole = lax.all_gather(block, "tensor", axis=0, tiled=False)
        return [whole[i] for i in range(parts)]
    devices = range(RING)

    def forward(x, back):
        pairs = [(i, (i + 4 * back) % RING) for i in devices]
        return lax.ppermute(x, "tensor", pairs)

    def flip(x, bit):
        return lax.ppermute(x, "tensor", [(i, i ^ bit) for i in devices])

    column = [block] + [forward(block, back) for back in range(1, RING // 4)]
    other = [flip(x, 2) for x in column]
    held = []
    for x, y in zip(column, other):
        held += [x, flip(x, 1), y, flip(y, 1)]
    return held


def delta_kernel(steps, rows, parts, count_ref, rank_ref, owner_ref, d_hbm, u_hbm, *rest):
    blocks, (out_ref, down, up, sems) = rest[:parts], rest[parts:]
    block = lax.axis_index("tensor")
    each, width = blocks[0].shape
    total = parts * each
    _, slots, cols = out_ref.shape
    cuts = 4
    deep = width // cuts
    copies = [
        pltpu.make_async_copy(
            src.at[0, pl.ds(i * deep, deep)], dst.at[pl.ds(i * deep, deep)], sems.at[j, i]
        )
        for j, (src, dst) in enumerate(((d_hbm, down), (u_hbm, up)))
        for i in range(cuts)
    ]
    for copy in copies:
        copy.start()
    start = jnp.int32(0)
    first = jnp.int32(0)
    amount = jnp.int32(0)
    for a in range(count_ref.shape[0]):
        owned = (owner_ref[a] <= block) & (block < owner_ref[a] + rank_ref[a])
        first = jnp.where(owned, start, first)
        amount = jnp.where(owned, count_ref[a], amount)
        start = start + count_ref[a]
    slot = lax.broadcasted_iota(jnp.int32, (slots, total), 0)
    place = lax.broadcasted_iota(jnp.int32, (slots, total), 1)
    request, step = row_place(place, block, parts, steps, rows)
    nth = slot % MOST
    pick = (step == slot // MOST) & (request == first + nth) & (nth < amount)
    low = jnp.zeros((total, down.shape[1]), F32)
    for i in range(cuts):
        at = slice(i * deep, (i + 1) * deep)
        copies[i].wait()
        low = low + dot(jnp.concatenate([b[:, at] for b in blocks], axis=0), down[at, :])
    chosen = dot(pick.astype(F32).astype(BF16), low.astype(BF16)).astype(BF16)
    for p in range(parts):
        if p % (parts // cuts) == 0:
            copies[cuts + p // (parts // cuts)].wait()
        out_ref[p] = dot_nt(chosen, up[p * cols : (p + 1) * cols, :]).astype(BF16)


def delta_parts(blocks, store_down, store_up, tables, steps, rows):
    parts = len(blocks)
    each, width = blocks[0].shape
    slots = steps * MOST
    cols = width // parts
    rank_w = store_down.shape[2]
    vmem = pl.BlockSpec(memory_space=pltpu.VMEM)
    smem = pl.BlockSpec(memory_space=pltpu.SMEM)
    hbm = pl.BlockSpec(memory_space=pl.ANY)
    return pl.pallas_call(
        functools.partial(delta_kernel, steps, rows, parts),
        out_shape=jax.ShapeDtypeStruct((parts, slots, cols), BF16),
        in_specs=[smem] * 3 + [hbm] * 2 + [vmem] * parts,
        out_specs=vmem,
        scratch_shapes=[
            pltpu.VMEM((width, rank_w), BF16),
            pltpu.VMEM((width, rank_w), BF16),
            pltpu.SemaphoreType.DMA((2, 4)),
        ],
        compiler_params=pltpu.CompilerParams(vmem_limit_bytes=40 * 2**20),
        cost_estimate=pl.CostEstimate(
            flops=2 * (parts * each + slots) * width * rank_w,
            bytes_accessed=2 * width * (parts * each + 2 * rank_w + slots),
            transcendentals=0,
        ),
        name="delta",
    )(
        *tables,
        pltpu.with_memory_space_constraint(store_down, pltpu.HBM),
        pltpu.with_memory_space_constraint(store_up, pltpu.HBM),
        *blocks,
    )


def base_kernel(*refs):
    blocks, (w_ref, out_ref) = refs[:-2], refs[-2:]

    @pl.when(pl.program_id(0) == 0)
    def _():
        out_ref[...] = jnp.zeros_like(out_ref)

    out_ref[...] += dot(jnp.concatenate([b[...] for b in blocks], axis=0), w_ref[...])


def base_part(blocks, out_weight):
    each, width = blocks[0].shape
    total = len(blocks) * each
    cols = out_weight.shape[1]
    deep = 1024
    return pl.pallas_call(
        base_kernel,
        out_shape=jax.ShapeDtypeStruct((total, cols), F32),
        grid=(width // deep,),
        in_specs=[pl.BlockSpec((each, deep), lambda k: (0, k))] * len(blocks)
        + [pl.BlockSpec((deep, cols), lambda k: (k, 0))],
        out_specs=pl.BlockSpec((total, cols), lambda k: (0, 0)),
        compiler_params=pltpu.CompilerParams(vmem_limit_bytes=24 * 2**20),
        cost_estimate=pl.CostEstimate(
            flops=2 * total * width * cols,
            bytes_accessed=2 * width * (total + cols) + 4 * total * cols,
            transcendentals=0,
        ),
        name="base",
    )(*blocks, out_weight)


def join_kernel(rows, count_ref, rank_ref, owner_ref, base_ref, delta_ref, out_ref):
    steps, requests, cols = out_ref.shape
    parts, slots, _ = delta_ref.shape
    total = base_ref.shape[0]
    me = lax.axis_index("tensor")
    wide = parts * slots
    entry = lax.broadcasted_iota(jnp.int32, (1, wide), 1)
    block = entry // slots
    first = jnp.zeros((1, wide), jnp.int32)
    amount = jnp.zeros((1, wide), jnp.int32)
    start = jnp.int32(0)
    for a in range(count_ref.shape[0]):
        owned = (owner_ref[a] <= block) & (block < owner_ref[a] + rank_ref[a])
        first = jnp.where(owned, start, first)
        amount = jnp.where(owned, count_ref[a], amount)
        start = start + count_ref[a]
    nth = entry % MOST
    goal = jnp.where(nth < amount, first + nth, -1)
    goal_step = (entry % slots) // MOST
    request, step = row_place(
        lax.broadcasted_iota(jnp.int32, (total, 1), 0), me, parts, steps, rows
    )
    place = (request == goal) & (step == goal_step)
    delta = dot(place.astype(F32).astype(BF16), delta_ref[...].reshape(wide, cols))
    result = (base_ref[...] + delta).astype(BF16)
    request, step = row_place(
        lax.broadcasted_iota(jnp.int32, (total, total), 1), me, parts, steps, rows
    )
    goal = lax.broadcasted_iota(jnp.int32, (total, total), 0)
    order = (goal == step * requests + request).astype(F32).astype(BF16)
    turned = dot(order, result).astype(BF16)
    for t in range(steps):
        out_ref[t] = turned[t * requests : (t + 1) * requests]


def join(base, delta, tables, steps, rows):
    total, cols = base.shape
    vmem = pl.BlockSpec(memory_space=pltpu.VMEM)
    smem = pl.BlockSpec(memory_space=pltpu.SMEM)
    return pl.pallas_call(
        functools.partial(join_kernel, rows),
        out_shape=jax.ShapeDtypeStruct((steps, total // steps, cols), BF16),
        in_specs=[smem] * 3 + [vmem] * 2,
        out_specs=vmem,
        compiler_params=pltpu.CompilerParams(vmem_limit_bytes=24 * 2**20),
        name="join",
    )(*tables, base, delta)


def per_device(
    queries,
    new_keys,
    new_values,
    cache_keys,
    cache_values,
    kv_len,
    adapter_rows,
    adapter_rank,
    adapter_owner,
    out_weight,
    store_down,
    store_up,
):
    parts = lax.axis_size("tensor")
    steps, rows, width = queries.shape
    tables = (adapter_rows, adapter_rank, adapter_owner)
    attended = attend(queries, new_keys, new_values, cache_keys, cache_values, kv_len)
    blocks = gather(attended, parts)
    send = delta_parts(blocks, store_down, store_up, tables, steps, rows)
    delta = lax.all_to_all(send, "tensor", split_axis=0, concat_axis=0, tiled=True)
    base = base_part(blocks, out_weight)
    return join(base, delta, tables, steps, rows)


def solution(mesh):
    in_specs = (
        P(None, ("groups", "tensor"), None),
        P(None, ("groups", "tensor"), None),
        P(None, ("groups", "tensor"), None),
        P(("groups", "tensor"), None, None),
        P(("groups", "tensor"), None, None),
        P(("groups", "tensor")),
        P("groups"),
        P(),
        P(),
        P(None, "tensor"),
        P("tensor", None, None),
        P("tensor", None, None),
    )
    out_specs = P(None, "groups", "tensor")
    return jax.shard_map(
        per_device, mesh=mesh, in_specs=in_specs, out_specs=out_specs, check_vma=False
    )
```

```python
import functools

import jax
import jax.numpy as jnp
from jax import lax
from jax.experimental import pallas as pl
from jax.experimental.pallas import tpu as pltpu
from jax.sharding import PartitionSpec as P

HQ = 64
KVH = 8
HD = 128
GROUP = HQ // KVH
MOST = 8
RING = 16
F32 = jnp.float32
BF16 = jnp.bfloat16
NT = (((1,), (1,)), ((), ()))


def in_hbm(*arrays):
    return [pltpu.with_memory_space_constraint(a, pltpu.HBM) for a in arrays]


def dot(a, b):
    return jnp.dot(a, b, preferred_element_type=F32)


def dot_nt(a, b):
    return lax.dot_general(a, b, NT, preferred_element_type=F32)


def attend_kernel(
    len_ref, q_ref, nk_ref, nv_ref, k_ref, v_ref, out_ref, turned_q, nks, nvs, mixed
):
    steps, rows, width = q_ref.shape
    cache = k_ref.shape[1]
    both = steps * rows
    pack = steps * GROUP
    r = pl.program_id(0)

    @pl.when(r == 0)
    def _():
        flat = jnp.concatenate([q_ref[t].astype(F32) for t in range(steps)], axis=0)
        heads = []
        for k in range(KVH):
            group = jnp.stack(
                [flat[:, (k * GROUP + g) * HD : (k * GROUP + g + 1) * HD] for g in range(GROUP)]
            )
            heads.append(jnp.swapaxes(group, 0, 1))
        column = lax.broadcasted_iota(jnp.int32, (HD, KVH * pack), 1)
        for i in range(rows):
            mine = jnp.concatenate(
                [heads[k][t * rows + i] for k in range(KVH) for t in range(steps)], axis=0
            )
            mine = jnp.transpose(mine)
            for k in range(KVH):
                turned_q[i, k * HD : (k + 1) * HD, :] = jnp.where(
                    column // pack == k, mine, 0.0
                ).astype(BF16)
        for src, dst in ((nk_ref, nks), (nv_ref, nvs)):
            fresh = [src[t].astype(F32) for t in range(steps)]
            fresh.append(jnp.zeros((16 - both, src.shape[2]), F32))
            dst[...] = jnp.concatenate(fresh, axis=0).astype(BF16)

    scale = HD ** (-0.5)
    older = dot(k_ref[0], turned_q[r]) * scale
    fresh = dot(nks[...], turned_q[r]) * scale
    place = lax.broadcasted_iota(jnp.int32, older.shape, 0)
    older = jnp.where(place < len_ref[r], older, -jnp.inf)
    slot = lax.broadcasted_iota(jnp.int32, fresh.shape, 0)
    step = (lax.broadcasted_iota(jnp.int32, fresh.shape, 1) // GROUP) % steps
    seen = (slot < both) & (slot % rows == r) & (slot // rows <= step)
    fresh = jnp.where(seen, fresh, -jnp.inf)
    top = jnp.maximum(
        jnp.max(older, axis=0, keepdims=True), jnp.max(fresh, axis=0, keepdims=True)
    )
    e_older = jnp.exp(older - top)
    e_fresh = jnp.exp(fresh - top)
    total = jnp.sum(e_older, axis=0, keepdims=True) + jnp.sum(e_fresh, axis=0, keepdims=True)
    inverse = 1.0 / total
    p_older = jnp.transpose(e_older * inverse).astype(BF16)
    p_fresh = jnp.transpose(e_fresh * inverse).astype(BF16)
    for k in range(0, KVH, 2):
        own = slice(k * pack, (k + 2) * pack)
        cols = slice(k * HD, (k + 2) * HD)
        pair = dot(p_older[own], v_ref[0, :, cols]) + dot(p_fresh[own], nvs[:, cols])
        mixed[r, k] = pair[:pack, :HD]
        mixed[r, k + 1] = pair[pack:, HD:]

    @pl.when(r == rows - 1)
    def _():
        for k in range(KVH):
            turned = jnp.stack(
                [
                    mixed[i, k, t * GROUP : (t + 1) * GROUP, :]
                    for t in range(steps)
                    for i in range(rows)
                ]
            )
            heads = jnp.swapaxes(turned, 0, 1)
            for g in range(GROUP):
                at = (k * GROUP + g) * HD
                out_ref[:, at : at + HD] = heads[g].astype(BF16)


def attend(queries, new_keys, new_values, cache_keys, cache_values, kv_len):
    steps, rows, width = queries.shape
    cache, kv_width = cache_keys.shape[1:]
    pack = steps * GROUP
    whole = lambda r, lens: (0, 0, 0)
    mine = lambda r, lens: (r, 0, 0)
    flops = 4 * rows * steps * HQ * cache * HD
    return pl.pallas_call(
        attend_kernel,
        out_shape=jax.ShapeDtypeStruct((steps * rows, width), BF16),
        grid_spec=pltpu.PrefetchScalarGridSpec(
            num_scalar_prefetch=1,
            grid=(rows,),
            in_specs=[
                pl.BlockSpec((steps, rows, width), whole),
                pl.BlockSpec((steps, rows, kv_width), whole),
                pl.BlockSpec((steps, rows, kv_width), whole),
                pl.BlockSpec((1, cache, kv_width), mine),
                pl.BlockSpec((1, cache, kv_width), mine),
            ],
            out_specs=pl.BlockSpec((steps * rows, width), lambda r, lens: (0, 0)),
            scratch_shapes=[
                pltpu.VMEM((rows, kv_width, KVH * pack), BF16),
                pltpu.VMEM((16, kv_width), BF16),
                pltpu.VMEM((16, kv_width), BF16),
                pltpu.VMEM((rows, KVH, pack, HD), F32),
            ],
        ),
        compiler_params=pltpu.CompilerParams(vmem_limit_bytes=24 * 2**20),
        cost_estimate=pl.CostEstimate(
            flops=flops,
            bytes_accessed=4 * rows * cache * kv_width,
            transcendentals=rows * steps * HQ * cache,
        ),
        name="attend",
    )(*in_hbm(kv_len, queries, new_keys, new_values, cache_keys, cache_values))


def sender(slot, me, parts):
    return me ^ slot if parts == RING else slot


def row_place(index, me, parts, steps, rows):
    both = steps * rows
    return sender(index // both, me, parts) * rows + index % rows, (index % both) // rows


def gather(block, parts):
    if parts != RING:
        whole = lax.all_gather(block, "tensor", axis=0, tiled=False)
        return [whole[i] for i in range(parts)]

    def flip(x, bits):
        return lax.ppermute(x, "tensor", [(i, i ^ bits) for i in range(RING)])

    core, y, z_near, z_far = 1, 2, 4, 8
    held = {0: block}
    held[z_far] = flip(block, z_far)
    held[z_near] = flip(block, z_near)
    held[y] = flip(block, y)
    held[y | z_near] = flip(held[z_near], y)
    held[y | z_far] = flip(held[z_far], y)
    held[y | z_far | z_near] = flip(held[z_far], y | z_near)
    held[z_far | z_near] = flip(held[z_far], z_near)
    for slot in list(held):
        held[slot | core] = flip(held[slot], core)
    return [held[slot] for slot in range(RING)]


def delta_kernel(steps, rows, parts, count_ref, rank_ref, owner_ref, d_hbm, u_hbm, *rest):
    blocks, (out_ref, down, up, sems) = rest[:parts], rest[parts:]
    block = lax.axis_index("tensor")
    each, width = blocks[0].shape
    total = parts * each
    _, slots, cols = out_ref.shape
    cuts = 4
    deep = width // cuts
    copies = [
        pltpu.make_async_copy(
            src.at[0, pl.ds(i * deep, deep)], dst.at[pl.ds(i * deep, deep)], sems.at[j, i]
        )
        for j, (src, dst) in enumerate(((d_hbm, down), (u_hbm, up)))
        for i in range(cuts)
    ]
    for copy in copies:
        copy.start()
    start = jnp.int32(0)
    first = jnp.int32(0)
    amount = jnp.int32(0)
    for a in range(count_ref.shape[0]):
        owned = (owner_ref[a] <= block) & (block < owner_ref[a] + rank_ref[a])
        first = jnp.where(owned, start, first)
        amount = jnp.where(owned, count_ref[a], amount)
        start = start + count_ref[a]
    slot = lax.broadcasted_iota(jnp.int32, (slots, total), 0)
    place = lax.broadcasted_iota(jnp.int32, (slots, total), 1)
    request, step = row_place(place, block, parts, steps, rows)
    nth = slot % MOST
    pick = (step == slot // MOST) & (request == first + nth) & (nth < amount)
    low = jnp.zeros((total, down.shape[1]), F32)
    for i in range(cuts):
        at = slice(i * deep, (i + 1) * deep)
        copies[i].wait()
        low = low + dot(jnp.concatenate([b[:, at] for b in blocks], axis=0), down[at, :])
    chosen = dot(pick.astype(F32).astype(BF16), low.astype(BF16)).astype(BF16)
    for p in range(parts):
        if p % (parts // cuts) == 0:
            copies[cuts + p // (parts // cuts)].wait()
        out_ref[p] = dot_nt(chosen, up[p * cols : (p + 1) * cols, :]).astype(BF16)


def delta_parts(blocks, store_down, store_up, tables, steps, rows):
    parts = len(blocks)
    each, width = blocks[0].shape
    slots = steps * MOST
    cols = width // parts
    rank_w = store_down.shape[2]
    vmem = pl.BlockSpec(memory_space=pltpu.VMEM)
    smem = pl.BlockSpec(memory_space=pltpu.SMEM)
    hbm = pl.BlockSpec(memory_space=pl.ANY)
    return pl.pallas_call(
        functools.partial(delta_kernel, steps, rows, parts),
        out_shape=jax.ShapeDtypeStruct((parts, slots, cols), BF16),
        in_specs=[smem] * 3 + [hbm] * 2 + [vmem] * parts,
        out_specs=vmem,
        scratch_shapes=[
            pltpu.VMEM((width, rank_w), BF16),
            pltpu.VMEM((width, rank_w), BF16),
            pltpu.SemaphoreType.DMA((2, 4)),
        ],
        compiler_params=pltpu.CompilerParams(vmem_limit_bytes=40 * 2**20),
        cost_estimate=pl.CostEstimate(
            flops=2 * (parts * each + slots) * width * rank_w,
            bytes_accessed=2 * width * (parts * each + 2 * rank_w + slots),
            transcendentals=0,
        ),
        name="delta",
    )(
        *in_hbm(*tables, store_down, store_up),
        *blocks,
    )


def base_kernel(*refs):
    blocks, (w_ref, out_ref) = refs[:-2], refs[-2:]

    @pl.when(pl.program_id(0) == 0)
    def _():
        out_ref[...] = jnp.zeros_like(out_ref)

    out_ref[...] += dot(jnp.concatenate([b[...] for b in blocks], axis=0), w_ref[...])


def base_part(blocks, out_weight):
    each, width = blocks[0].shape
    total = len(blocks) * each
    cols = out_weight.shape[1]
    deep = 1024
    return pl.pallas_call(
        base_kernel,
        out_shape=jax.ShapeDtypeStruct((total, cols), F32),
        grid=(width // deep,),
        in_specs=[pl.BlockSpec((each, deep), lambda k: (0, k))] * len(blocks)
        + [pl.BlockSpec((deep, cols), lambda k: (k, 0))],
        out_specs=pl.BlockSpec((total, cols), lambda k: (0, 0)),
        compiler_params=pltpu.CompilerParams(vmem_limit_bytes=24 * 2**20),
        cost_estimate=pl.CostEstimate(
            flops=2 * total * width * cols,
            bytes_accessed=2 * width * (total + cols) + 4 * total * cols,
            transcendentals=0,
        ),
        name="base",
    )(*blocks, *in_hbm(out_weight))


def join_kernel(rows, count_ref, rank_ref, owner_ref, base_ref, delta_ref, out_ref):
    steps, requests, cols = out_ref.shape
    parts, slots, _ = delta_ref.shape
    total = base_ref.shape[0]
    me = lax.axis_index("tensor")
    wide = parts * slots
    entry = lax.broadcasted_iota(jnp.int32, (1, wide), 1)
    block = entry // slots
    first = jnp.zeros((1, wide), jnp.int32)
    amount = jnp.zeros((1, wide), jnp.int32)
    start = jnp.int32(0)
    for a in range(count_ref.shape[0]):
        owned = (owner_ref[a] <= block) & (block < owner_ref[a] + rank_ref[a])
        first = jnp.where(owned, start, first)
        amount = jnp.where(owned, count_ref[a], amount)
        start = start + count_ref[a]
    nth = entry % MOST
    goal = jnp.where(nth < amount, first + nth, -1)
    goal_step = (entry % slots) // MOST
    request, step = row_place(
        lax.broadcasted_iota(jnp.int32, (total, 1), 0), me, parts, steps, rows
    )
    place = (request == goal) & (step == goal_step)
    delta = dot(place.astype(F32).astype(BF16), delta_ref[...].reshape(wide, cols))
    result = (base_ref[...] + delta).astype(BF16)
    request, step = row_place(
        lax.broadcasted_iota(jnp.int32, (total, total), 1), me, parts, steps, rows
    )
    goal = lax.broadcasted_iota(jnp.int32, (total, total), 0)
    order = (goal == step * requests + request).astype(F32).astype(BF16)
    turned = dot(order, result).astype(BF16)
    for t in range(steps):
        out_ref[t] = turned[t * requests : (t + 1) * requests]


def join(base, delta, tables, steps, rows):
    total, cols = base.shape
    vmem = pl.BlockSpec(memory_space=pltpu.VMEM)
    smem = pl.BlockSpec(memory_space=pltpu.SMEM)
    return pl.pallas_call(
        functools.partial(join_kernel, rows),
        out_shape=jax.ShapeDtypeStruct((steps, total // steps, cols), BF16),
        in_specs=[smem] * 3 + [vmem] * 2,
        out_specs=vmem,
        compiler_params=pltpu.CompilerParams(vmem_limit_bytes=24 * 2**20),
        name="join",
    )(*in_hbm(*tables), base, delta)


def per_device(
    queries,
    new_keys,
    new_values,
    cache_keys,
    cache_values,
    kv_len,
    adapter_rows,
    adapter_rank,
    adapter_owner,
    out_weight,
    store_down,
    store_up,
):
    parts = lax.axis_size("tensor")
    steps, rows, width = queries.shape
    tables = (adapter_rows, adapter_rank, adapter_owner)
    attended = attend(queries, new_keys, new_values, cache_keys, cache_values, kv_len)
    blocks = gather(attended, parts)
    send = delta_parts(blocks, store_down, store_up, tables, steps, rows)
    delta = lax.all_to_all(send, "tensor", split_axis=0, concat_axis=0, tiled=True)
    base = base_part(blocks, out_weight)
    return join(base, delta, tables, steps, rows)


def solution(mesh):
    in_specs = (
        P(None, ("groups", "tensor"), None),
        P(None, ("groups", "tensor"), None),
        P(None, ("groups", "tensor"), None),
        P(("groups", "tensor"), None, None),
        P(("groups", "tensor"), None, None),
        P(("groups", "tensor")),
        P("groups"),
        P(),
        P(),
        P(None, "tensor"),
        P("tensor", None, None),
        P("tensor", None, None),
    )
    out_specs = P(None, "groups", "tensor")
    return jax.shard_map(
        per_device, mesh=mesh, in_specs=in_specs, out_specs=out_specs, check_vma=False
    )
```

```python
import functools

import jax
import jax.numpy as jnp
from jax import lax
from jax.experimental import pallas as pl
from jax.experimental.pallas import tpu as pltpu
from jax.sharding import PartitionSpec as P

HQ = 64
KVH = 8
HD = 128
GROUP = HQ // KVH
MOST = 8
RING = 8
F32 = jnp.float32
BF16 = jnp.bfloat16
NT = (((1,), (1,)), ((), ()))


def in_hbm(*arrays):
    return [pltpu.with_memory_space_constraint(a, pltpu.HBM) for a in arrays]


def dot(a, b):
    return jnp.dot(a, b, preferred_element_type=F32)


def dot_nt(a, b):
    return lax.dot_general(a, b, NT, preferred_element_type=F32)


def attend_kernel(
    len_ref, q_hbm, nk_hbm, nv_hbm, k_hbm, v_hbm, d_hbm, u_hbm, out_ref, store_ref,
    q_ref, nk_ref, nv_ref, k_ref, v_ref, turned_q, nks, nvs, mixed, small_sems, sems, store_sems,
):
    steps, rows, width = q_ref.shape
    cache = k_ref.shape[1]
    both = steps * rows
    pack = steps * GROUP
    cuts = sems.shape[2]
    small = [
        pltpu.make_async_copy(src, dst, small_sems.at[i])
        for i, (src, dst) in enumerate(((q_hbm, q_ref), (nk_hbm, nk_ref), (nv_hbm, nv_ref)))
    ]
    large = []
    for r in range(rows):
        for j, (src, dst) in enumerate(((k_hbm, k_ref), (v_hbm, v_ref))):
            pieces = [pl.ds(i * (cache // cuts), cache // cuts) for i in range(cuts)]
            large.append(
                [
                    pltpu.make_async_copy(src.at[r, at], dst.at[r, at], sems.at[r, j, i])
                    for i, at in enumerate(pieces)
                ]
            )
    for copy in small:
        copy.start()
    for copies in large:
        for copy in copies:
            copy.start()
    deep = d_hbm.shape[1]
    stores = [
        pltpu.make_async_copy(src.at[0], store_ref.at[pl.ds(j * deep, deep)], store_sems.at[j])
        for j, src in enumerate((d_hbm, u_hbm))
    ]
    for copy in stores:
        copy.start()
    for copy in small:
        copy.wait()

    flat = jnp.concatenate([q_ref[t].astype(F32) for t in range(steps)], axis=0)
    heads = []
    for k in range(KVH):
        group = jnp.stack(
            [flat[:, (k * GROUP + g) * HD : (k * GROUP + g + 1) * HD] for g in range(GROUP)]
        )
        heads.append(jnp.swapaxes(group, 0, 1))
    column = lax.broadcasted_iota(jnp.int32, (HD, KVH * pack), 1)
    for r in range(rows):
        mine = jnp.concatenate(
            [heads[k][t * rows + r] for k in range(KVH) for t in range(steps)], axis=0
        )
        mine = jnp.transpose(mine)
        for k in range(KVH):
            turned_q[r, k * HD : (k + 1) * HD, :] = jnp.where(
                column // pack == k, mine, 0.0
            ).astype(BF16)
    for src, dst in ((nk_ref, nks), (nv_ref, nvs)):
        fresh = [src[t].astype(F32) for t in range(steps)]
        fresh.append(jnp.zeros((16 - both, src.shape[2]), F32))
        dst[...] = jnp.concatenate(fresh, axis=0).astype(BF16)

    scale = HD ** (-0.5)
    for r in range(rows):
        fresh = dot(nks[...], turned_q[r]) * scale
        slot = lax.broadcasted_iota(jnp.int32, fresh.shape, 0)
        step = (lax.broadcasted_iota(jnp.int32, fresh.shape, 1) // GROUP) % steps
        seen = (slot < both) & (slot % rows == r) & (slot // rows <= step)
        fresh = jnp.where(seen, fresh, -jnp.inf)
        for copy in large[2 * r]:
            copy.wait()
        older = dot(k_ref[r], turned_q[r]) * scale
        place = lax.broadcasted_iota(jnp.int32, older.shape, 0)
        older = jnp.where(place < len_ref[r], older, -jnp.inf)
        top = jnp.maximum(
            jnp.max(older, axis=0, keepdims=True), jnp.max(fresh, axis=0, keepdims=True)
        )
        e_older = jnp.exp(older - top)
        e_fresh = jnp.exp(fresh - top)
        total = jnp.sum(e_older, axis=0, keepdims=True) + jnp.sum(e_fresh, axis=0, keepdims=True)
        inverse = 1.0 / total
        p_older = jnp.transpose(e_older * inverse).astype(BF16)
        p_fresh = jnp.transpose(e_fresh * inverse).astype(BF16)
        for copy in large[2 * r + 1]:
            copy.wait()
        for k in range(0, KVH, 2):
            own = slice(k * pack, (k + 2) * pack)
            cols = slice(k * HD, (k + 2) * HD)
            pair = dot(p_older[own], v_ref[r, :, cols]) + dot(p_fresh[own], nvs[:, cols])
            mixed[r, k] = pair[:pack, :HD]
            mixed[r, k + 1] = pair[pack:, HD:]

    for k in range(KVH):
        turned = jnp.stack(
            [
                mixed[r, k, t * GROUP : (t + 1) * GROUP, :]
                for t in range(steps)
                for r in range(rows)
            ]
        )
        heads = jnp.swapaxes(turned, 0, 1)
        for g in range(GROUP):
            at = (k * GROUP + g) * HD
            out_ref[:, at : at + HD] = heads[g].astype(BF16)
    for copy in stores:
        copy.wait()


def attend(
    queries, new_keys, new_values, cache_keys, cache_values, kv_len, store_down, store_up
):
    steps, rows, width = queries.shape
    cache, kv_width = cache_keys.shape[1:]
    pack = steps * GROUP
    return pl.pallas_call(
        attend_kernel,
        out_shape=(
            jax.ShapeDtypeStruct((steps * rows, width), BF16),
            jax.ShapeDtypeStruct((2 * store_down.shape[1], store_down.shape[2]), BF16),
        ),
        in_specs=[pl.BlockSpec(memory_space=pltpu.SMEM)]
        + [pl.BlockSpec(memory_space=pl.ANY)] * 7,
        out_specs=(pl.BlockSpec(memory_space=pltpu.VMEM),) * 2,
        scratch_shapes=[
            pltpu.VMEM(queries.shape, BF16),
            pltpu.VMEM(new_keys.shape, BF16),
            pltpu.VMEM(new_values.shape, BF16),
            pltpu.VMEM(cache_keys.shape, BF16),
            pltpu.VMEM(cache_values.shape, BF16),
            pltpu.VMEM((rows, kv_width, KVH * pack), BF16),
            pltpu.VMEM((16, kv_width), BF16),
            pltpu.VMEM((16, kv_width), BF16),
            pltpu.VMEM((rows, KVH, pack, HD), F32),
            pltpu.SemaphoreType.DMA((3,)),
            pltpu.SemaphoreType.DMA((rows, 2, 2)),
            pltpu.SemaphoreType.DMA((2,)),
        ],
        compiler_params=pltpu.CompilerParams(vmem_limit_bytes=32 * 2**20),
        cost_estimate=pl.CostEstimate(
            flops=4 * rows * steps * HQ * cache * HD,
            bytes_accessed=4 * rows * cache * kv_width,
            transcendentals=rows * steps * HQ * cache,
        ),
        name="attend",
    )(
        *in_hbm(
            kv_len,
            queries,
            new_keys,
            new_values,
            cache_keys,
            cache_values,
            store_down,
            store_up,
        )
    )


def sender(slot, chip, chips):
    return chip ^ slot if chips == RING else slot


def swap(x, bits, parts):
    return lax.ppermute(x, "tensor", [(i, i ^ bits) for i in range(parts)])


def gather(block, parts):
    if parts // 2 != RING:
        groups = [list(range(core, parts, 2)) for core in range(2)]
        whole = lax.all_gather(block, "tensor", axis_index_groups=groups)
        return [whole[i] for i in range(parts // 2)]
    y, near, far = 1, 2, 4

    def flip(x, bits):
        return swap(x, 2 * bits, parts)

    held = {0: block}
    held[far] = flip(block, far)
    held[near] = flip(block, near)
    held[y] = flip(block, y)
    held[y | near] = flip(held[near], y)
    held[y | far] = flip(held[far], y)
    held[y | far | near] = flip(held[far], y | near)
    held[far | near] = flip(held[far], near)
    return [held[slot] for slot in range(RING)]


def turn_kernel(store_ref, out_ref):
    width = out_ref.shape[1]
    cuts = 4
    deep = width // cuts
    for i in range(cuts):
        at = slice(width + i * deep, width + (i + 1) * deep)
        out_ref[:, i * deep : (i + 1) * deep] = jnp.transpose(store_ref[at, :])


def turn(store):
    width, rank_w = store.shape[0] // 2, store.shape[1]
    vmem = pl.BlockSpec(memory_space=pltpu.VMEM)
    return pl.pallas_call(
        turn_kernel,
        out_shape=jax.ShapeDtypeStruct((rank_w, width), BF16),
        in_specs=[vmem],
        out_specs=vmem,
        compiler_params=pltpu.CompilerParams(vmem_limit_bytes=16 * 2**20),
        cost_estimate=pl.CostEstimate(
            flops=0, bytes_accessed=4 * width * rank_w, transcendentals=0
        ),
        name="turn",
    )(store)


def stage_weight_kernel(after, w_hbm, w_ref, sems):
    deep = w_hbm.shape[0] // sems.shape[0]
    copies = []
    for i in range(sems.shape[0]):
        at = pl.ds(i * deep, deep)
        copies.append(pltpu.make_async_copy(w_hbm.at[at], w_ref.at[at], sems.at[i]))
        copies[-1].start()
    for copy in copies:
        copy.wait()


def stage_weight(after, out_weight):
    return pl.pallas_call(
        stage_weight_kernel,
        out_shape=jax.ShapeDtypeStruct(out_weight.shape, BF16),
        in_specs=[pl.BlockSpec(memory_space=pl.ANY)] * 2,
        out_specs=pl.BlockSpec(memory_space=pltpu.VMEM),
        scratch_shapes=[pltpu.SemaphoreType.DMA((8,))],
        compiler_params=pltpu.CompilerParams(vmem_limit_bytes=16 * 2**20),
        cost_estimate=pl.CostEstimate(
            flops=4 * 10**10, bytes_accessed=4 * out_weight.size, transcendentals=0
        ),
        name="stage_weight",
    )(after, *in_hbm(out_weight))


def slot_request(first, amount, core, slot, rows):
    ahead = (core * rows + slot + 2 * MOST - first % MOST) % MOST
    return jnp.where(ahead < amount, first + ahead, -1)


def adapter_of(block, count_ref, rank_ref, owner_ref):
    start = jnp.int32(0)
    first = jnp.zeros_like(block)
    amount = jnp.zeros_like(block)
    for a in range(count_ref.shape[0]):
        owned = (owner_ref[a] <= block) & (block < owner_ref[a] + rank_ref[a])
        first = jnp.where(owned, start, first)
        amount = jnp.where(owned, count_ref[a], amount)
        start = start + count_ref[a]
    return first, amount


def iota(shape, dim):
    return lax.broadcasted_iota(jnp.int32, shape, dim)


def one_hot(mask):
    return mask.astype(F32).astype(BF16)


def delta_kernel(steps, rows, count_ref, rank_ref, owner_ref, *rest):
    (d0, d1, u0, u1), blocks, (_, out_ref, rows_ref) = rest[:4], rest[4:-3], rest[-3:]
    me = lax.axis_index("tensor")
    chip, core = me // 2, me % 2
    chips = len(blocks)
    each, width = blocks[0].shape
    total = chips * each
    parts, slots, cols = out_ref.shape
    rank_w = d0.shape[1]
    cuts = 8
    deep = width // cuts
    low = jnp.zeros((total, 2 * rank_w), F32)
    for i in range(cuts):
        at = slice(i * deep, (i + 1) * deep)
        piece = jnp.concatenate([b[:, at] for b in blocks], axis=0)
        rows_ref[:, at] = piece
        low = low + dot(piece, jnp.concatenate([d0[at, :], d1[at, :]], axis=1))
    low = low.astype(BF16)
    shape = (slots, total)
    slot, place = iota(shape, 0), iota(shape, 1)
    device = sender(place // each, chip, chips) * 2 + core
    request = device * rows + place % rows
    step = (place % each) // rows
    half = slots // 2
    first, amount = adapter_of(
        chip * 2 + (core + slot // half) % 2, count_ref, rank_ref, owner_ref
    )
    wanted = slot_request(first, amount, core, slot % rows, rows)
    chosen = dot(one_hot((request == wanted) & (step == (slot % half) // rows)), low)
    shape = chosen.shape
    own = iota(shape, 0) // half == iota(shape, 1) // rank_w
    chosen = jnp.where(own, chosen, 0.0).astype(BF16)
    for p in range(parts):
        at = slice(p * cols, (p + 1) * cols)
        turned = jnp.concatenate([u0[:, at], u1[:, at]], axis=0)
        out_ref[p] = dot(chosen, turned).astype(BF16)


def delta_parts(blocks, downs, ups, before, tables, steps, rows):
    each, width = blocks[0].shape
    parts = 2 * len(blocks)
    slots = 2 * steps * rows
    rank_w = downs[0].shape[1]
    vmem = pl.BlockSpec(memory_space=pltpu.VMEM)
    smem = pl.BlockSpec(memory_space=pltpu.SMEM)
    return pl.pallas_call(
        functools.partial(delta_kernel, steps, rows),
        out_shape=(
            jax.ShapeDtypeStruct((parts, slots, width // parts), BF16),
            jax.ShapeDtypeStruct((len(blocks) * each, width), BF16),
        ),
        in_specs=[smem] * 3
        + [vmem] * (4 + len(blocks))
        + [pl.BlockSpec(memory_space=pl.ANY)],
        out_specs=(vmem, vmem),
        compiler_params=pltpu.CompilerParams(vmem_limit_bytes=24 * 2**20),
        cost_estimate=pl.CostEstimate(
            flops=4 * (len(blocks) * each + slots) * width * rank_w,
            bytes_accessed=2 * width * (len(blocks) * each + 4 * rank_w + slots),
            transcendentals=0,
        ),
        name="delta",
    )(*in_hbm(*tables), *downs, *ups, *blocks, before)


def base_kernel(own_ref, other_ref, w_ref, out_ref):
    total, width = own_ref.shape
    cuts = 8
    deep = width // cuts
    for i in range(cuts):
        at = slice(i * deep, (i + 1) * deep)
        part = dot(jnp.concatenate([own_ref[:, at], other_ref[:, at]], axis=0), w_ref[at, :])
        out_ref[...] = part if i == 0 else out_ref[...] + part


def base_part(own, other, out_weight):
    total, width = own.shape
    cols = out_weight.shape[1]
    vmem = pl.BlockSpec(memory_space=pltpu.VMEM)
    return pl.pallas_call(
        base_kernel,
        out_shape=jax.ShapeDtypeStruct((2 * total, cols), F32),
        in_specs=[vmem] * 3,
        out_specs=vmem,
        compiler_params=pltpu.CompilerParams(vmem_limit_bytes=24 * 2**20),
        cost_estimate=pl.CostEstimate(
            flops=4 * total * width * cols,
            bytes_accessed=2 * width * (2 * total + cols) + 8 * total * cols,
            transcendentals=0,
        ),
        name="base",
    )(own, other, out_weight)


def join_kernel(rows, count_ref, rank_ref, owner_ref, base_ref, delta_ref, out_ref):
    me = lax.axis_index("tensor")
    chip, core = me // 2, me % 2
    steps, requests, cols = out_ref.shape
    parts, slots, _ = delta_ref.shape
    total = base_ref.shape[0]
    wide = parts * slots
    half = slots // 2
    each = steps * rows
    entry = iota((1, wide), 1)
    source, slot = entry // slots, entry % slots
    first, amount = adapter_of(
        source // 2 * 2 + (source + slot // half) % 2, count_ref, rank_ref, owner_ref
    )
    wanted = slot_request(first, amount, source % 2, slot % rows, rows)

    def row_place(index):
        turn = index // (total // 2)
        rest = index % (total // 2)
        device = sender(rest // each, chip, parts // 2) * 2 + (core + turn) % 2
        return device * rows + index % rows, (index % each) // rows

    request, step = row_place(iota((total, 1), 0))
    place = (request == wanted) & (step == (slot % half) // rows)
    delta = dot(one_hot(place), delta_ref[...].reshape(wide, cols))
    result = (base_ref[...] + delta).astype(BF16)
    request, step = row_place(iota((total, total), 1))
    order = one_hot(iota((total, total), 0) == step * requests + request)
    turned = dot(order, result).astype(BF16)
    for t in range(steps):
        out_ref[t] = turned[t * requests : (t + 1) * requests]


def join(base, delta, tables, steps, rows):
    total, cols = base.shape
    vmem = pl.BlockSpec(memory_space=pltpu.VMEM)
    smem = pl.BlockSpec(memory_space=pltpu.SMEM)
    return pl.pallas_call(
        functools.partial(join_kernel, rows),
        out_shape=jax.ShapeDtypeStruct((steps, total // steps, cols), BF16),
        in_specs=[smem] * 3 + [vmem] * 2,
        out_specs=vmem,
        compiler_params=pltpu.CompilerParams(vmem_limit_bytes=24 * 2**20),
        name="join",
    )(*in_hbm(*tables), base, delta)


def per_device(
    queries,
    new_keys,
    new_values,
    cache_keys,
    cache_values,
    kv_len,
    adapter_rows,
    adapter_rank,
    adapter_owner,
    out_weight,
    store_down,
    store_up,
):
    parts = lax.axis_size("tensor")
    steps, rows, width = queries.shape
    tables = (adapter_rows, adapter_rank, adapter_owner)
    attended, store = attend(
        queries, new_keys, new_values, cache_keys, cache_values, kv_len, store_down, store_up
    )
    blocks = gather(attended, parts)
    other = swap(store, 1, parts)
    weight = stage_weight(attended, out_weight)
    send, own_rows = delta_parts(
        blocks, (store, other), (turn(store), turn(other)), weight, tables, steps, rows
    )
    other_rows = swap(own_rows, 1, parts)
    delta = lax.all_to_all(send, "tensor", split_axis=0, concat_axis=0, tiled=True)
    base = base_part(own_rows, other_rows, weight)
    return join(base, delta, tables, steps, rows)


def solution(mesh):
    in_specs = (
        P(None, ("groups", "tensor"), None),
        P(None, ("groups", "tensor"), None),
        P(None, ("groups", "tensor"), None),
        P(("groups", "tensor"), None, None),
        P(("groups", "tensor"), None, None),
        P(("groups", "tensor")),
        P("groups"),
        P(),
        P(),
        P(None, "tensor"),
        P("tensor", None, None),
        P("tensor", None, None),
    )
    out_specs = P(None, "groups", "tensor")
    return jax.shard_map(
        per_device, mesh=mesh, in_specs=in_specs, out_specs=out_specs, check_vma=False
    )
```

```python
import functools

import jax
import jax.numpy as jnp
from jax import lax
from jax.experimental import pallas as pl
from jax.experimental.pallas import tpu as pltpu
from jax.sharding import PartitionSpec as P

HQ = 64
KVH = 8
HD = 128
GROUP = HQ // KVH
MOST = 8
RING = 16
F32 = jnp.float32
BF16 = jnp.bfloat16
NT = (((1,), (1,)), ((), ()))


def in_hbm(*arrays):
    return [pltpu.with_memory_space_constraint(a, pltpu.HBM) for a in arrays]


def iota(shape, dim):
    return lax.broadcasted_iota(jnp.int32, shape, dim)


def one_hot(mask):
    return mask.astype(F32).astype(BF16)


def dot(a, b):
    return jnp.dot(a, b, preferred_element_type=F32)


def dot_nt(a, b):
    return lax.dot_general(a, b, NT, preferred_element_type=F32)


def attend_kernel(
    len_ref, q_hbm, nk_hbm, nv_hbm, k_hbm, v_hbm, out_ref,
    q_ref, nk_ref, nv_ref, k_ref, v_ref, qs, nks, nvs, mixed, small_sems, sems,
):
    steps, rows, width = q_ref.shape
    cache = k_ref.shape[1]
    both = steps * rows
    pack = steps * GROUP
    cuts = sems.shape[2]
    small = [
        pltpu.make_async_copy(src, dst, small_sems.at[i])
        for i, (src, dst) in enumerate(((q_hbm, q_ref), (nk_hbm, nk_ref), (nv_hbm, nv_ref)))
    ]
    pieces = [pl.ds(i * (cache // cuts), cache // cuts) for i in range(cuts)]
    keys, values = [
        [
            [
                pltpu.make_async_copy(src.at[r, at], dst.at[r, at], sems.at[r, j, i])
                for i, at in enumerate(pieces)
            ]
            for r in range(rows)
        ]
        for j, (src, dst) in enumerate(((k_hbm, k_ref), (v_hbm, v_ref)))
    ]
    for copy in small + keys[0] + values[0] + keys[1] + values[1]:
        copy.start()
    for copy in small:
        copy.wait()

    flat = jnp.concatenate([q_ref[t].astype(F32) for t in range(steps)], axis=0)
    blank = jnp.zeros((pack, HD), F32)
    for k in range(KVH):
        group = jnp.stack(
            [flat[:, (k * GROUP + g) * HD : (k * GROUP + g + 1) * HD] for g in range(GROUP)]
        )
        turned = jnp.swapaxes(group, 0, 1)
        for r in range(rows):
            mine = jnp.concatenate([turned[t * rows + r] for t in range(steps)], axis=0)
            sides = [mine, blank] if k % 2 == 0 else [blank, mine]
            qs[r, k * pack : (k + 1) * pack, :] = jnp.concatenate(sides, axis=1).astype(BF16)
    for src, dst in ((nk_ref, nks), (nv_ref, nvs)):
        fresh = [src[t].astype(F32) for t in range(steps)]
        fresh.append(jnp.zeros((16 - both, src.shape[2]), F32))
        dst[...] = jnp.concatenate(fresh, axis=0).astype(BF16)

    scale = HD ** (-0.5)
    pairs = [
        (slice(k * pack, (k + 2) * pack), slice(k * HD, (k + 2) * HD)) for k in range(0, KVH, 2)
    ]
    for r in range(rows):
        if r + 2 < rows:
            for copy in keys[r + 2] + values[r + 2]:
                copy.start()
        fresh = jnp.concatenate(
            [dot_nt(qs[r, own, :], nks[:, cols]) for own, cols in pairs], axis=0
        )
        slot = iota(fresh.shape, 1)
        step = (iota(fresh.shape, 0) // GROUP) % steps
        seen = (slot < both) & (slot % rows == r) & (slot // rows <= step)
        fresh = jnp.where(seen, fresh * scale, -jnp.inf)
        for copy in keys[r]:
            copy.wait()
        older = jnp.concatenate(
            [dot_nt(qs[r, own, :], k_ref[r, :, cols]) for own, cols in pairs], axis=0
        )
        older = jnp.where(iota(older.shape, 1) < len_ref[r], older * scale, -jnp.inf)
        top = jnp.maximum(
            jnp.max(older, axis=1, keepdims=True), jnp.max(fresh, axis=1, keepdims=True)
        )
        e_older = jnp.exp(older - top)
        e_fresh = jnp.exp(fresh - top)
        total = jnp.sum(e_older, axis=1, keepdims=True) + jnp.sum(e_fresh, axis=1, keepdims=True)
        inverse = 1.0 / total
        p_older = (e_older * inverse).astype(BF16)
        p_fresh = (e_fresh * inverse).astype(BF16)
        for copy in values[r]:
            copy.wait()
        for k, (own, cols) in zip(range(0, KVH, 2), pairs):
            pair = dot(p_older[own], v_ref[r, :, cols]) + dot(p_fresh[own], nvs[:, cols])
            mixed[r, k] = pair[:pack, :HD]
            mixed[r, k + 1] = pair[pack:, HD:]

    for k in range(KVH):
        turned = jnp.stack(
            [
                mixed[r, k, t * GROUP : (t + 1) * GROUP, :]
                for t in range(steps)
                for r in range(rows)
            ]
        )
        heads = jnp.swapaxes(turned, 0, 1)
        for g in range(GROUP):
            at = (k * GROUP + g) * HD
            out_ref[:, at : at + HD] = heads[g].astype(BF16)


def attend(queries, new_keys, new_values, cache_keys, cache_values, kv_len):
    steps, rows, width = queries.shape
    cache, kv_width = cache_keys.shape[1:]
    pack = steps * GROUP
    return pl.pallas_call(
        attend_kernel,
        out_shape=jax.ShapeDtypeStruct((steps * rows, width), BF16),
        in_specs=[pl.BlockSpec(memory_space=pltpu.SMEM)]
        + [pl.BlockSpec(memory_space=pl.ANY)] * 5,
        out_specs=pl.BlockSpec(memory_space=pltpu.VMEM),
        scratch_shapes=[
            pltpu.VMEM(queries.shape, BF16),
            pltpu.VMEM(new_keys.shape, BF16),
            pltpu.VMEM(new_values.shape, BF16),
            pltpu.VMEM(cache_keys.shape, BF16),
            pltpu.VMEM(cache_values.shape, BF16),
            pltpu.VMEM((rows, KVH * pack, 2 * HD), BF16),
            pltpu.VMEM((16, kv_width), BF16),
            pltpu.VMEM((16, kv_width), BF16),
            pltpu.VMEM((rows, KVH, pack, HD), F32),
            pltpu.SemaphoreType.DMA((3,)),
            pltpu.SemaphoreType.DMA((rows, 2, 2)),
        ],
        compiler_params=pltpu.CompilerParams(vmem_limit_bytes=32 * 2**20),
        cost_estimate=pl.CostEstimate(
            flops=4 * rows * steps * HQ * cache * HD,
            bytes_accessed=4 * rows * cache * kv_width,
            transcendentals=rows * steps * HQ * cache,
        ),
        name="attend",
    )(*in_hbm(kv_len, queries, new_keys, new_values, cache_keys, cache_values))


def sender(slot, me, parts):
    return me ^ slot if parts == RING else slot


def row_place(index, me, parts, steps, rows):
    both = steps * rows
    return sender(index // both, me, parts) * rows + index % rows, (index % both) // rows


def gather(block, parts):
    if parts != RING:
        whole = lax.all_gather(block, "tensor", axis=0, tiled=False)
        return [whole[i] for i in range(parts)]

    def flip(x, bits):
        return lax.ppermute(x, "tensor", [(i, i ^ bits) for i in range(RING)])

    core, y, z_near, z_far = 1, 2, 4, 8
    held = {0: block}
    held[z_far] = flip(block, z_far)
    held[z_near] = flip(block, z_near)
    held[y] = flip(block, y)
    held[y | z_near] = flip(block, y | z_near)
    held[y | z_far] = flip(held[z_far], y)
    held[y | z_far | z_near] = flip(held[z_far], y | z_near)
    held[z_far | z_near] = flip(held[z_far], z_near)
    for slot in list(held):
        held[slot | core] = flip(held[slot], core)
    return [held[slot] for slot in range(RING)]


def stage_kernel(after, d_hbm, u_hbm, d_ref, ut_ref, up, sems):
    width = u_hbm.shape[1]
    cuts = sems.shape[1]
    deep = width // cuts
    copies = []
    for j, (src, dst) in enumerate(((u_hbm, up), (d_hbm, d_ref))):
        for i in range(cuts):
            at = pl.ds(i * deep, deep)
            copies.append(pltpu.make_async_copy(src.at[0, at], dst.at[at], sems.at[j, i]))
            copies[-1].start()
    for i in range(cuts):
        copies[i].wait()
        at = slice(i * deep, (i + 1) * deep)
        ut_ref[:, at] = jnp.transpose(up[at, :])
    for copy in copies[cuts:]:
        copy.wait()


def stage(after, store_down, store_up):
    width, rank_w = store_down.shape[1:]
    vmem = pl.BlockSpec(memory_space=pltpu.VMEM)
    return pl.pallas_call(
        stage_kernel,
        out_shape=(
            jax.ShapeDtypeStruct((width, rank_w), BF16),
            jax.ShapeDtypeStruct((rank_w, width), BF16),
        ),
        in_specs=[pl.BlockSpec(memory_space=pl.ANY)] * 3,
        out_specs=(vmem, vmem),
        scratch_shapes=[
            pltpu.VMEM((width, rank_w), BF16),
            pltpu.SemaphoreType.DMA((2, 4)),
        ],
        compiler_params=pltpu.CompilerParams(vmem_limit_bytes=16 * 2**20),
        cost_estimate=pl.CostEstimate(
            flops=4 * 10**10, bytes_accessed=8 * width * rank_w, transcendentals=0
        ),
        name="stage",
    )(after, *in_hbm(store_down, store_up))


def delta_kernel(steps, rows, count_ref, rank_ref, owner_ref, d_ref, ut_ref, *rest):
    blocks, (out_ref, rows_ref) = rest[:-2], rest[-2:]
    block = lax.axis_index("tensor")
    parts, slots, cols = out_ref.shape
    each, width = blocks[0].shape
    total = parts * each
    cuts = 8
    deep = width // cuts
    low = jnp.zeros((total, d_ref.shape[1]), F32)
    for i in range(cuts):
        at = slice(i * deep, (i + 1) * deep)
        piece = jnp.concatenate([b[:, at] for b in blocks], axis=0)
        rows_ref[:, at] = piece
        low = low + dot(piece, d_ref[at, :])
    start = jnp.int32(0)
    first = jnp.int32(0)
    amount = jnp.int32(0)
    for a in range(count_ref.shape[0]):
        owned = (owner_ref[a] <= block) & (block < owner_ref[a] + rank_ref[a])
        first = jnp.where(owned, start, first)
        amount = jnp.where(owned, count_ref[a], amount)
        start = start + count_ref[a]
    slot = iota((slots, total), 0)
    request, step = row_place(iota((slots, total), 1), block, parts, steps, rows)
    nth = slot % MOST
    pick = (step == slot // MOST) & (request == first + nth) & (nth < amount)
    chosen = dot(one_hot(pick), low.astype(BF16)).astype(BF16)
    for p in range(parts):
        out_ref[p] = dot(chosen, ut_ref[:, p * cols : (p + 1) * cols]).astype(BF16)


def delta_parts(blocks, down, up, tables, steps, rows):
    parts = len(blocks)
    each, width = blocks[0].shape
    slots = steps * MOST
    rank_w = down.shape[1]
    vmem = pl.BlockSpec(memory_space=pltpu.VMEM)
    smem = pl.BlockSpec(memory_space=pltpu.SMEM)
    return pl.pallas_call(
        functools.partial(delta_kernel, steps, rows),
        out_shape=(
            jax.ShapeDtypeStruct((parts, slots, width // parts), BF16),
            jax.ShapeDtypeStruct((parts * each, width), BF16),
        ),
        in_specs=[smem] * 3 + [vmem] * (2 + parts),
        out_specs=(vmem, vmem),
        compiler_params=pltpu.CompilerParams(vmem_limit_bytes=24 * 2**20),
        cost_estimate=pl.CostEstimate(
            flops=2 * (parts * each + slots) * width * rank_w,
            bytes_accessed=2 * width * (2 * parts * each + 2 * rank_w + slots),
            transcendentals=0,
        ),
        name="delta",
    )(*in_hbm(*tables), down, up, *blocks)


def base_kernel(a_ref, w_ref, out_ref):
    width = a_ref.shape[1]
    cuts = 8
    deep = width // cuts
    for i in range(cuts):
        at = slice(i * deep, (i + 1) * deep)
        part = dot(a_ref[:, at], w_ref[at, :])
        out_ref[...] = part if i == 0 else out_ref[...] + part


def base_part(gathered, out_weight):
    total, width = gathered.shape
    cols = out_weight.shape[1]
    vmem = pl.BlockSpec(memory_space=pltpu.VMEM)
    return pl.pallas_call(
        base_kernel,
        out_shape=jax.ShapeDtypeStruct((total, cols), F32),
        in_specs=[vmem] * 2,
        out_specs=vmem,
        compiler_params=pltpu.CompilerParams(vmem_limit_bytes=24 * 2**20),
        cost_estimate=pl.CostEstimate(
            flops=2 * total * width * cols,
            bytes_accessed=2 * width * (total + cols) + 4 * total * cols,
            transcendentals=0,
        ),
        name="base",
    )(gathered, out_weight)


def join_kernel(rows, count_ref, rank_ref, owner_ref, base_ref, delta_ref, out_ref):
    steps, requests, cols = out_ref.shape
    parts, slots, _ = delta_ref.shape
    total = base_ref.shape[0]
    me = lax.axis_index("tensor")
    wide = parts * slots
    entry = lax.broadcasted_iota(jnp.int32, (1, wide), 1)
    block = entry // slots
    first = jnp.zeros((1, wide), jnp.int32)
    amount = jnp.zeros((1, wide), jnp.int32)
    start = jnp.int32(0)
    for a in range(count_ref.shape[0]):
        owned = (owner_ref[a] <= block) & (block < owner_ref[a] + rank_ref[a])
        first = jnp.where(owned, start, first)
        amount = jnp.where(owned, count_ref[a], amount)
        start = start + count_ref[a]
    nth = entry % MOST
    goal = jnp.where(nth < amount, first + nth, -1)
    goal_step = (entry % slots) // MOST
    request, step = row_place(
        lax.broadcasted_iota(jnp.int32, (total, 1), 0), me, parts, steps, rows
    )
    place = (request == goal) & (step == goal_step)
    delta = dot(place.astype(F32).astype(BF16), delta_ref[...].reshape(wide, cols))
    result = (base_ref[...] + delta).astype(BF16)
    request, step = row_place(
        lax.broadcasted_iota(jnp.int32, (total, total), 1), me, parts, steps, rows
    )
    goal = lax.broadcasted_iota(jnp.int32, (total, total), 0)
    order = (goal == step * requests + request).astype(F32).astype(BF16)
    turned = dot(order, result).astype(BF16)
    for t in range(steps):
        out_ref[t] = turned[t * requests : (t + 1) * requests]


def join(base, delta, tables, steps, rows):
    total, cols = base.shape
    vmem = pl.BlockSpec(memory_space=pltpu.VMEM)
    smem = pl.BlockSpec(memory_space=pltpu.SMEM)
    return pl.pallas_call(
        functools.partial(join_kernel, rows),
        out_shape=jax.ShapeDtypeStruct((steps, total // steps, cols), BF16),
        in_specs=[smem] * 3 + [vmem] * 2,
        out_specs=vmem,
        compiler_params=pltpu.CompilerParams(vmem_limit_bytes=24 * 2**20),
        name="join",
    )(*in_hbm(*tables), base, delta)


def per_device(
    queries,
    new_keys,
    new_values,
    cache_keys,
    cache_values,
    kv_len,
    adapter_rows,
    adapter_rank,
    adapter_owner,
    out_weight,
    store_down,
    store_up,
):
    parts = lax.axis_size("tensor")
    steps, rows, width = queries.shape
    tables = (adapter_rows, adapter_rank, adapter_owner)
    attended = attend(queries, new_keys, new_values, cache_keys, cache_values, kv_len)
    blocks = gather(attended, parts)
    down, up = stage(blocks[2], store_down, store_up)
    send, gathered = delta_parts(blocks, down, up, tables, steps, rows)
    delta = lax.all_to_all(send, "tensor", split_axis=0, concat_axis=0, tiled=True)
    base = base_part(gathered, out_weight)
    return join(base, delta, tables, steps, rows)


def solution(mesh):
    in_specs = (
        P(None, ("groups", "tensor"), None),
        P(None, ("groups", "tensor"), None),
        P(None, ("groups", "tensor"), None),
        P(("groups", "tensor"), None, None),
        P(("groups", "tensor"), None, None),
        P(("groups", "tensor")),
        P("groups"),
        P(),
        P(),
        P(None, "tensor"),
        P("tensor", None, None),
        P("tensor", None, None),
    )
    out_specs = P(None, "groups", "tensor")
    return jax.shard_map(
        per_device, mesh=mesh, in_specs=in_specs, out_specs=out_specs, check_vma=False
    )
```

```python
import functools

import jax
import jax.numpy as jnp
from jax import lax
from jax.experimental import pallas as pl
from jax.experimental.pallas import tpu as pltpu
from jax.sharding import PartitionSpec as P

HQ = 64
KVH = 8
HD = 128
GROUP = HQ // KVH
MOST = 8
RING = 8
F32 = jnp.float32
BF16 = jnp.bfloat16
NT = (((1,), (1,)), ((), ()))


def in_hbm(*arrays):
    return [pltpu.with_memory_space_constraint(a, pltpu.HBM) for a in arrays]


def iota(shape, dim):
    return lax.broadcasted_iota(jnp.int32, shape, dim)


def one_hot(mask):
    return mask.astype(F32).astype(BF16)


def dot(a, b):
    return jnp.dot(a, b, preferred_element_type=F32)


def dot_nt(a, b):
    return lax.dot_general(a, b, NT, preferred_element_type=F32)


def attend_kernel(
    len_hbm, q_hbm, nk_hbm, nv_hbm, k_hbm, v_hbm, d_hbm, u_hbm,
    out_ref, d_ref, keep_ref, give_ref,
    len_ref, q_ref, nk_ref, nv_ref, k_ref, v_ref, qs, nks, nvs, raw, mixed,
    small_sems, sems, store_sems,
):
    steps, rows, width = q_ref.shape
    cache = k_ref.shape[1]
    both = steps * rows
    pack = steps * GROUP
    cuts = sems.shape[2]
    core = lax.axis_index("tensor") % 2
    chips = store_sems.shape[1]
    cols = keep_ref.shape[0] // chips

    small = [
        pltpu.make_async_copy(src, dst, small_sems.at[i])
        for i, (src, dst) in enumerate(
            ((q_hbm, q_ref), (len_hbm, len_ref), (nk_hbm, nk_ref), (nv_hbm, nv_ref))
        )
    ]
    pieces = [pl.ds(i * (cache // cuts), cache // cuts) for i in range(cuts)]
    keys, values = [
        [
            [
                pltpu.make_async_copy(src.at[r, at], dst.at[r, at], sems.at[r, j, i])
                for i, at in enumerate(pieces)
            ]
            for r in range(rows)
        ]
        for j, (src, dst) in enumerate(((k_hbm, k_ref), (v_hbm, v_ref)))
    ]
    deep = d_ref.shape[0] // chips
    store = [
        pltpu.make_async_copy(
            d_hbm.at[0, pl.ds(i * deep, deep)], d_ref.at[pl.ds(i * deep, deep)], store_sems.at[0, i]
        )
        for i in range(chips)
    ]
    for j, (side, dst) in enumerate(((core, keep_ref), (1 - core, give_ref))):
        for i in range(chips):
            at = pl.multiple_of((2 * i + side) * cols, cols)
            store.append(
                pltpu.make_async_copy(
                    u_hbm.at[0, pl.ds(at, cols)],
                    dst.at[pl.ds(i * cols, cols)],
                    store_sems.at[1 + j, i],
                )
            )
    queue = [keys[0], values[0], keys[1]]
    for r in range(rows):
        queue += [values[r + 1]] if r + 1 < rows else [store]
        queue += [keys[r + 2]] if r + 2 < rows else []
    for copy in small + queue[0] + queue[1] + queue[2]:
        copy.start()
    queue = queue[3:]
    for copy in small:
        copy.wait()

    flat = jnp.concatenate([q_ref[t].astype(F32) for t in range(steps)], axis=0)
    blank = jnp.zeros((pack, HD), F32)
    for k in range(KVH):
        group = jnp.stack(
            [flat[:, (k * GROUP + g) * HD : (k * GROUP + g + 1) * HD] for g in range(GROUP)]
        )
        turned = jnp.swapaxes(group, 0, 1)
        for r in range(rows):
            mine = jnp.concatenate([turned[t * rows + r] for t in range(steps)], axis=0)
            sides = [mine, blank] if k % 2 == 0 else [blank, mine]
            qs[r, k * pack : (k + 1) * pack, :] = jnp.concatenate(sides, axis=1).astype(BF16)
    for src, dst in ((nk_ref, nks), (nv_ref, nvs)):
        fresh = [src[t].astype(F32) for t in range(steps)]
        fresh.append(jnp.zeros((16 - both, src.shape[2]), F32))
        dst[...] = jnp.concatenate(fresh, axis=0).astype(BF16)

    scale = HD ** (-0.5)
    pairs = [
        (slice(k * pack, (k + 2) * pack), slice(k * HD, (k + 2) * HD)) for k in range(0, KVH, 2)
    ]
    for turn in range(rows + 1):
        if turn < rows:
            for copy in keys[turn]:
                copy.wait()
        if turn > 0:
            for copy in values[turn - 1]:
                copy.wait()
        for copies in queue[2 * turn : 2 * turn + 2]:
            for copy in copies:
                copy.start()
        if turn < rows:
            for own, cols_k in pairs:
                raw[turn % 2, own, :cache] = dot_nt(qs[turn, own, :], k_ref[turn, :, cols_k])
        if turn == 0:
            continue
        r = turn - 1
        fresh = jnp.concatenate(
            [dot_nt(qs[r, own, :], nks[:, cols_k]) for own, cols_k in pairs], axis=0
        )
        slot = iota(fresh.shape, 1)
        step = (iota(fresh.shape, 0) // GROUP) % steps
        seen = (slot < both) & (slot % rows == r) & (slot // rows <= step)
        fresh = jnp.where(seen, fresh * scale, -jnp.inf)
        older = raw[r % 2]
        older = jnp.where(iota(older.shape, 1) < len_ref[r], older * scale, -jnp.inf)
        top = jnp.maximum(
            jnp.max(older, axis=1, keepdims=True), jnp.max(fresh, axis=1, keepdims=True)
        )
        e_older = jnp.exp(older - top)
        e_fresh = jnp.exp(fresh - top)
        total = jnp.sum(e_older, axis=1, keepdims=True) + jnp.sum(e_fresh, axis=1, keepdims=True)
        inverse = 1.0 / total
        p_older = (e_older * inverse).astype(BF16)
        p_fresh = (e_fresh * inverse).astype(BF16)
        for k, (own, cols_k) in zip(range(0, KVH, 2), pairs):
            pair = dot(p_older[own], v_ref[r, :, cols_k]) + dot(p_fresh[own], nvs[:, cols_k])
            mixed[r, k] = pair[:pack, :HD]
            mixed[r, k + 1] = pair[pack:, HD:]

    for k in range(KVH):
        turned = jnp.stack(
            [
                mixed[r, k, t * GROUP : (t + 1) * GROUP, :]
                for t in range(steps)
                for r in range(rows)
            ]
        )
        heads = jnp.swapaxes(turned, 0, 1)
        for g in range(GROUP):
            at = (k * GROUP + g) * HD
            out_ref[:, at : at + HD] = heads[g].astype(BF16)
    for copy in store:
        copy.wait()


def attend(
    queries, new_keys, new_values, cache_keys, cache_values, kv_len, store_down, store_up, parts
):
    steps, rows, width = queries.shape
    cache, kv_width = cache_keys.shape[1:]
    pack = steps * GROUP
    rank_w = store_down.shape[2]
    vmem = pl.BlockSpec(memory_space=pltpu.VMEM)
    return pl.pallas_call(
        attend_kernel,
        out_shape=(
            jax.ShapeDtypeStruct((steps * rows, width), BF16),
            jax.ShapeDtypeStruct((width, rank_w), BF16),
            jax.ShapeDtypeStruct((width // 2, rank_w), BF16),
            jax.ShapeDtypeStruct((width // 2, rank_w), BF16),
        ),
        in_specs=[pl.BlockSpec(memory_space=pl.ANY)] * 8,
        out_specs=(vmem,) * 4,
        scratch_shapes=[
            pltpu.SMEM(kv_len.shape, jnp.int32),
            pltpu.VMEM(queries.shape, BF16),
            pltpu.VMEM(new_keys.shape, BF16),
            pltpu.VMEM(new_values.shape, BF16),
            pltpu.VMEM(cache_keys.shape, BF16),
            pltpu.VMEM(cache_values.shape, BF16),
            pltpu.VMEM((rows, KVH * pack, 2 * HD), BF16),
            pltpu.VMEM((16, kv_width), BF16),
            pltpu.VMEM((16, kv_width), BF16),
            pltpu.VMEM((2, KVH * pack, cache), F32),
            pltpu.VMEM((rows, KVH, pack, HD), F32),
            pltpu.SemaphoreType.DMA((4,)),
            pltpu.SemaphoreType.DMA((rows, 2, 2)),
            pltpu.SemaphoreType.DMA((3, parts // 2)),
        ],
        compiler_params=pltpu.CompilerParams(vmem_limit_bytes=32 * 2**20),
        cost_estimate=pl.CostEstimate(
            flops=4 * rows * steps * HQ * cache * HD,
            bytes_accessed=4 * rows * cache * kv_width,
            transcendentals=rows * steps * HQ * cache,
        ),
        name="attend",
    )(
        *in_hbm(
            kv_len,
            queries,
            new_keys,
            new_values,
            cache_keys,
            cache_values,
            store_down,
            store_up,
        )
    )


def sender(slot, chip, chips):
    return chip ^ slot if chips == RING else slot


def row_place(index, me, chips, steps, rows):
    both = steps * rows
    block = index // both
    device = sender(block // 2, me // 2, chips) * 2 + (me + block) % 2
    return device * rows + index % rows, (index % both) // rows


def swap(x, bits, parts):
    return lax.ppermute(x, "tensor", [(i, i ^ bits) for i in range(parts)])


def stage_kernel(half, after, w_hbm, w_ref, sems):
    deep = w_ref.shape[0] // sems.shape[0]
    copies = []
    for i in range(sems.shape[0]):
        at = pl.ds(half * w_ref.shape[0] + i * deep, deep)
        copies.append(pltpu.make_async_copy(w_hbm.at[at], w_ref.at[pl.ds(i * deep, deep)], sems.at[i]))
        copies[-1].start()
    for copy in copies:
        copy.wait()


def stage(after, out_weight, half):
    width, cols = out_weight.shape
    return pl.pallas_call(
        functools.partial(stage_kernel, half),
        out_shape=jax.ShapeDtypeStruct((width // 2, cols), BF16),
        in_specs=[pl.BlockSpec(memory_space=pl.ANY)] * 2,
        out_specs=pl.BlockSpec(memory_space=pltpu.VMEM),
        scratch_shapes=[pltpu.SemaphoreType.DMA((8,))],
        compiler_params=pltpu.CompilerParams(vmem_limit_bytes=8 * 2**20),
        cost_estimate=pl.CostEstimate(
            flops=2 * 10**10, bytes_accessed=2 * out_weight.size, transcendentals=0
        ),
        name="stage",
    )(after, *in_hbm(out_weight))


def gather(block, give, out_weight, parts):
    if parts // 2 != RING:
        whole = lax.all_gather(block, "tensor")
        core = lax.axis_index("tensor") % 2
        pairs = whole.reshape(parts // 2, 2, *block.shape)
        pairs = jnp.where(core == 0, pairs, pairs[:, ::-1])
        held = [pairs[i // 2, i % 2] for i in range(parts)]
        weights = [stage(block, out_weight, half) for half in range(2)]
        return held, weights, swap(give, 1, parts)
    core, y, near, far = 1, 2, 4, 8
    held = {0: block}
    held[far] = swap(block, far, parts)
    held[near] = swap(block, near, parts)
    held[y] = swap(block, y, parts)
    first = stage(block, out_weight, 0)
    held[near], held[y], first, give = lax.optimization_barrier(
        (held[near], held[y], first, give)
    )
    held[near | y] = swap(held[near], y, parts)
    other = swap(give, core, parts)
    second = stage(held[near], out_weight, 1)
    held[far], second = lax.optimization_barrier((held[far], second))
    held[far | y] = swap(held[far], y, parts)
    held[far | near | y] = swap(held[far], near | y, parts)
    held[far | near] = swap(held[far], near, parts)
    for slot in list(held):
        held[slot | core] = swap(held[slot], core, parts)
    return [held[slot] for slot in range(parts)], [first, second], other


def low_kernel(order, steps, rows, count_ref, rank_ref, owner_ref, d_ref, *rest):
    (*blocks, out_ref, rows_ref) = rest
    blocks = [blocks[order.index(i)] for i in range(len(blocks))]
    block = lax.axis_index("tensor")
    slots = out_ref.shape[0]
    parts = len(blocks)
    each, width = blocks[0].shape
    total = parts * each
    cuts = 8
    deep = width // cuts
    low = jnp.zeros((total, d_ref.shape[1]), F32)
    for i in range(cuts):
        at = slice(i * deep, (i + 1) * deep)
        piece = jnp.concatenate([b[:, at] for b in blocks], axis=0)
        rows_ref[:, at] = piece
        low = low + dot(piece, d_ref[at, :])
    start = jnp.int32(0)
    first = jnp.int32(0)
    amount = jnp.int32(0)
    for a in range(count_ref.shape[0]):
        owned = (owner_ref[a] <= block) & (block < owner_ref[a] + rank_ref[a])
        first = jnp.where(owned, start, first)
        amount = jnp.where(owned, count_ref[a], amount)
        start = start + count_ref[a]
    slot = iota((slots, total), 0)
    request, step = row_place(iota((slots, total), 1), block, parts // 2, steps, rows)
    nth = slot % MOST
    pick = (step == slot // MOST) & (request == first + nth) & (nth < amount)
    out_ref[...] = dot(one_hot(pick), low.astype(BF16)).astype(BF16)


def low_rows(blocks, down, tables, steps, rows):
    parts = len(blocks)
    each, width = blocks[0].shape
    slots = steps * MOST
    rank_w = down.shape[1]
    order = [i for i in range(parts) if i // 2 != 5] + [i for i in range(parts) if i // 2 == 5]
    vmem = pl.BlockSpec(memory_space=pltpu.VMEM)
    smem = pl.BlockSpec(memory_space=pltpu.SMEM)
    return pl.pallas_call(
        functools.partial(low_kernel, order, steps, rows),
        out_shape=(
            jax.ShapeDtypeStruct((slots, rank_w), BF16),
            jax.ShapeDtypeStruct((parts * each, width), BF16),
        ),
        in_specs=[smem] * 3 + [vmem] * (1 + parts),
        out_specs=(vmem, vmem),
        compiler_params=pltpu.CompilerParams(vmem_limit_bytes=24 * 2**20),
        cost_estimate=pl.CostEstimate(
            flops=2 * parts * each * width * rank_w,
            bytes_accessed=2 * width * (2 * parts * each + rank_w),
            transcendentals=0,
        ),
        name="low",
    )(*in_hbm(*tables), down, *[blocks[i] for i in order])


def delta_kernel(own_ref, other_ref, keep_ref, taken_ref, *outs):
    chips = len(outs)
    chip = lax.axis_index("tensor") // 2
    slots = own_ref.shape[0]
    cols = outs[0].shape[1]
    for k in range(chips):
        at = pl.ds(pl.multiple_of(sender(k, chip, chips) * cols, cols), cols)
        outs[k][:slots, :] = dot_nt(own_ref[...], keep_ref[at, :]).astype(BF16)
        outs[k][slots:, :] = dot_nt(other_ref[...], taken_ref[at, :]).astype(BF16)


def deltas(own, other, keep, taken, chips):
    slots, rank_w = own.shape
    cols = keep.shape[0] // chips
    vmem = pl.BlockSpec(memory_space=pltpu.VMEM)
    return pl.pallas_call(
        delta_kernel,
        out_shape=[jax.ShapeDtypeStruct((2 * slots, cols), BF16)] * chips,
        in_specs=[vmem] * 4,
        out_specs=[vmem] * chips,
        compiler_params=pltpu.CompilerParams(vmem_limit_bytes=16 * 2**20),
        cost_estimate=pl.CostEstimate(
            flops=4 * slots * rank_w * keep.shape[0],
            bytes_accessed=4 * keep.shape[0] * (rank_w + slots),
            transcendentals=0,
        ),
        name="delta",
    )(own, other, keep, taken)


def send(pieces, parts):
    chips = len(pieces)
    if chips != RING:
        groups = [list(range(core, parts, 2)) for core in range(2)]
        all_pieces = lax.all_to_all(
            jnp.stack(pieces), "tensor", 0, 0, axis_index_groups=groups, tiled=True
        )
        return [all_pieces[i] for i in range(chips)]
    got = {0: pieces[0]}
    for k in range(1, chips):
        got[k] = swap(pieces[k], 2 * k, parts)
    return [got[k] for k in range(chips)]


def base_kernel(a_ref, first_ref, second_ref, out_ref):
    half = first_ref.shape[0]
    cuts = 4
    deep = half // cuts
    for j, w_ref in enumerate((first_ref, second_ref)):
        for i in range(cuts):
            part = dot(
                a_ref[:, j * half + i * deep : j * half + (i + 1) * deep],
                w_ref[i * deep : (i + 1) * deep, :],
            )
            out_ref[...] = part if i + j == 0 else out_ref[...] + part


def base_part(gathered, weights):
    total, width = gathered.shape
    cols = weights[0].shape[1]
    vmem = pl.BlockSpec(memory_space=pltpu.VMEM)
    return pl.pallas_call(
        base_kernel,
        out_shape=jax.ShapeDtypeStruct((total, cols), F32),
        in_specs=[vmem] * 3,
        out_specs=vmem,
        compiler_params=pltpu.CompilerParams(vmem_limit_bytes=24 * 2**20),
        cost_estimate=pl.CostEstimate(
            flops=2 * total * width * cols,
            bytes_accessed=2 * width * (total + cols) + 4 * total * cols,
            transcendentals=0,
        ),
        name="base",
    )(gathered, *weights)


def join_kernel(order, rows, count_ref, rank_ref, owner_ref, base_ref, *rest):
    (*pieces, out_ref) = rest
    pieces = [pieces[order.index(i)] for i in range(len(pieces))]
    me = lax.axis_index("tensor")
    steps, requests, cols = out_ref.shape
    chips = len(pieces)
    slots = pieces[0].shape[0] // 2
    total = base_ref.shape[0]
    wide = chips * 2 * slots
    entry = iota((1, wide), 1)
    source = entry // slots
    block = sender(source // 2, me // 2, chips) * 2 + (me + source) % 2
    first = jnp.zeros((1, wide), jnp.int32)
    amount = jnp.zeros((1, wide), jnp.int32)
    start = jnp.int32(0)
    for a in range(count_ref.shape[0]):
        owned = (owner_ref[a] <= block) & (block < owner_ref[a] + rank_ref[a])
        first = jnp.where(owned, start, first)
        amount = jnp.where(owned, count_ref[a], amount)
        start = start + count_ref[a]
    nth = entry % MOST
    goal = jnp.where(nth < amount, first + nth, -1)
    goal_step = (entry % slots) // MOST
    request, step = row_place(iota((total, 1), 0), me, chips, steps, rows)
    place = one_hot((request == goal) & (step == goal_step))
    delta = dot(place, jnp.concatenate([piece[...] for piece in pieces], axis=0))
    result = (base_ref[...] + delta).astype(BF16)
    request, step = row_place(iota((total, total), 1), me, chips, steps, rows)
    order = one_hot(iota((total, total), 0) == step * requests + request)
    turned = dot(order, result).astype(BF16)
    for t in range(steps):
        out_ref[t] = turned[t * requests : (t + 1) * requests]


def join(base, pieces, tables, steps, rows):
    total, cols = base.shape
    chips = len(pieces)
    order = [0] + [*range(chips // 2, chips)] + [*range(1, chips // 2)]
    vmem = pl.BlockSpec(memory_space=pltpu.VMEM)
    smem = pl.BlockSpec(memory_space=pltpu.SMEM)
    return pl.pallas_call(
        functools.partial(join_kernel, order, rows),
        out_shape=jax.ShapeDtypeStruct((steps, total // steps, cols), BF16),
        in_specs=[smem] * 3 + [vmem] * (1 + len(pieces)),
        out_specs=vmem,
        compiler_params=pltpu.CompilerParams(vmem_limit_bytes=24 * 2**20),
        name="join",
    )(*in_hbm(*tables), base, *[pieces[i] for i in order])


def per_device(
    queries,
    new_keys,
    new_values,
    cache_keys,
    cache_values,
    kv_len,
    adapter_rows,
    adapter_rank,
    adapter_owner,
    out_weight,
    store_down,
    store_up,
):
    parts = lax.axis_size("tensor")
    steps, rows, width = queries.shape
    tables = (adapter_rows, adapter_rank, adapter_owner)
    attended, down, keep, give = attend(
        queries,
        new_keys,
        new_values,
        cache_keys,
        cache_values,
        kv_len,
        store_down,
        store_up,
        parts,
    )
    blocks, weights, taken = gather(attended, give, out_weight, parts)
    own, gathered = low_rows(blocks, down, tables, steps, rows)
    other = swap(own, 1, parts)
    base = base_part(gathered, weights)
    other, base = lax.optimization_barrier((other, base))
    pieces = send(deltas(own, other, keep, taken, parts // 2), parts)
    return join(base, pieces, tables, steps, rows)


def solution(mesh):
    in_specs = (
        P(None, ("groups", "tensor"), None),
        P(None, ("groups", "tensor"), None),
        P(None, ("groups", "tensor"), None),
        P(("groups", "tensor"), None, None),
        P(("groups", "tensor"), None, None),
        P(("groups", "tensor")),
        P("groups"),
        P(),
        P(),
        P(None, "tensor"),
        P("tensor", None, None),
        P("tensor", None, None),
    )
    out_specs = P(None, "groups", "tensor")
    return jax.shard_map(
        per_device, mesh=mesh, in_specs=in_specs, out_specs=out_specs, check_vma=False
    )
```

```python
import functools

import jax
import jax.numpy as jnp
from jax import lax
from jax.experimental import pallas as pl
from jax.experimental.pallas import tpu as pltpu
from jax.sharding import PartitionSpec as P

HQ = 64
KVH = 8
HD = 128
GROUP = HQ // KVH
MOST = 8
RING = 16
ORDER = [0,1,6,7,2,3,4,5,8,9,12,13,14,15,10,11]
F32 = jnp.float32
BF16 = jnp.bfloat16
NT = (((1,), (1,)), ((), ()))


def in_hbm(*arrays):
    return [pltpu.with_memory_space_constraint(a, pltpu.HBM) for a in arrays]


def iota(shape, dim):
    return lax.broadcasted_iota(jnp.int32, shape, dim)


def one_hot(mask):
    return mask.astype(F32).astype(BF16)


def dot(a, b):
    return jnp.dot(a, b, preferred_element_type=F32)


def dot_nt(a, b):
    return lax.dot_general(a, b, NT, preferred_element_type=F32)


def attend_kernel(
    len_hbm, q_hbm, nk_hbm, nv_hbm, k_hbm, v_hbm, out_ref,
    len_ref, q_ref, nk_ref, nv_ref, k_ref, v_ref, turned_q, nks, nvs, raw, mixed,
    small_sems, sems,
):
    steps, rows, width = q_ref.shape
    cache = k_ref.shape[1]
    both = steps * rows
    pack = steps * GROUP
    cuts = sems.shape[2]

    small = [
        pltpu.make_async_copy(src, dst, small_sems.at[i])
        for i, (src, dst) in enumerate(
            ((q_hbm, q_ref), (len_hbm, len_ref), (nk_hbm, nk_ref), (nv_hbm, nv_ref))
        )
    ]
    pieces = [pl.ds(i * (cache // cuts), cache // cuts) for i in range(cuts)]
    keys, values = [
        [
            [
                pltpu.make_async_copy(src.at[r, at], dst.at[r, at], sems.at[r, j, i])
                for i, at in enumerate(pieces)
            ]
            for r in range(rows)
        ]
        for j, (src, dst) in enumerate(((k_hbm, k_ref), (v_hbm, v_ref)))
    ]
    queue = [keys[0], values[0], keys[1]]
    for r in range(rows):
        queue += [values[r + 1]] if r + 1 < rows else [[]]
        queue += [keys[r + 2]] if r + 2 < rows else []
    for copy in small + queue[0] + queue[1] + queue[2]:
        copy.start()
    queue = queue[3:]
    for copy in small:
        copy.wait()

    flat = jnp.concatenate([q_ref[t].astype(F32) for t in range(steps)], axis=0)
    heads = []
    for k in range(KVH):
        group = jnp.stack(
            [flat[:, (k * GROUP + g) * HD : (k * GROUP + g + 1) * HD] for g in range(GROUP)]
        )
        heads.append(jnp.swapaxes(group, 0, 1))
    column = iota((HD, KVH * pack), 1)
    for r in range(rows):
        mine = jnp.concatenate(
            [heads[k][t * rows + r] for k in range(KVH) for t in range(steps)], axis=0
        )
        mine = jnp.transpose(mine)
        for k in range(KVH):
            turned_q[r, k * HD : (k + 1) * HD, :] = jnp.where(
                column // pack == k, mine, 0.0
            ).astype(BF16)
    for src, dst in ((nk_ref, nks), (nv_ref, nvs)):
        fresh = [src[t].astype(F32) for t in range(steps)]
        fresh.append(jnp.zeros((16 - both, src.shape[2]), F32))
        dst[...] = jnp.concatenate(fresh, axis=0).astype(BF16)

    scale = HD ** (-0.5)
    pairs = [
        (slice(k * pack, (k + 2) * pack), slice(k * HD, (k + 2) * HD)) for k in range(0, KVH, 2)
    ]
    for turn in range(rows + 1):
        if turn < rows:
            for copy in keys[turn]:
                copy.wait()
        if turn > 0:
            for copy in values[turn - 1]:
                copy.wait()
        for copies in queue[2 * turn : 2 * turn + 2]:
            for copy in copies:
                copy.start()
        if turn < rows:
            raw[turn % 2] = dot(k_ref[turn], turned_q[turn])
        if turn == 0:
            continue
        r = turn - 1
        fresh = dot(nks[...], turned_q[r])
        slot = iota(fresh.shape, 0)
        step = (iota(fresh.shape, 1) // GROUP) % steps
        seen = (slot < both) & (slot % rows == r) & (slot // rows <= step)
        fresh = jnp.where(seen, fresh * scale, -jnp.inf)
        older = raw[r % 2]
        older = jnp.where(iota(older.shape, 0) < len_ref[r], older * scale, -jnp.inf)
        top = jnp.maximum(
            jnp.max(older, axis=0, keepdims=True), jnp.max(fresh, axis=0, keepdims=True)
        )
        e_older = jnp.exp(older - top)
        e_fresh = jnp.exp(fresh - top)
        total = jnp.sum(e_older, axis=0, keepdims=True) + jnp.sum(e_fresh, axis=0, keepdims=True)
        inverse = 1.0 / total
        p_older = jnp.transpose((e_older * inverse).astype(BF16))
        p_fresh = jnp.transpose((e_fresh * inverse).astype(BF16))
        for k, (own, cols_k) in zip(range(0, KVH, 2), pairs):
            pair = dot(p_older[own], v_ref[r, :, cols_k]) + dot(p_fresh[own], nvs[:, cols_k])
            mixed[r, k] = pair[:pack, :HD]
            mixed[r, k + 1] = pair[pack:, HD:]

    for k in range(KVH):
        turned = jnp.stack(
            [
                mixed[r, k, t * GROUP : (t + 1) * GROUP, :]
                for t in range(steps)
                for r in range(rows)
            ]
        )
        heads = jnp.swapaxes(turned, 0, 1)
        for g in range(GROUP):
            at = (k * GROUP + g) * HD
            out_ref[:, at : at + HD] = heads[g].astype(BF16)


def attend(queries, new_keys, new_values, cache_keys, cache_values, kv_len):
    steps, rows, width = queries.shape
    cache, kv_width = cache_keys.shape[1:]
    pack = steps * GROUP
    return pl.pallas_call(
        attend_kernel,
        out_shape=jax.ShapeDtypeStruct((steps * rows, width), BF16),
        in_specs=[pl.BlockSpec(memory_space=pl.ANY)] * 6,
        out_specs=pl.BlockSpec(memory_space=pltpu.VMEM),
        scratch_shapes=[
            pltpu.SMEM(kv_len.shape, jnp.int32),
            pltpu.VMEM(queries.shape, BF16),
            pltpu.VMEM(new_keys.shape, BF16),
            pltpu.VMEM(new_values.shape, BF16),
            pltpu.VMEM(cache_keys.shape, BF16),
            pltpu.VMEM(cache_values.shape, BF16),
            pltpu.VMEM((rows, kv_width, KVH * pack), BF16),
            pltpu.VMEM((16, kv_width), BF16),
            pltpu.VMEM((16, kv_width), BF16),
            pltpu.VMEM((2, cache, KVH * pack), F32),
            pltpu.VMEM((rows, KVH, pack, HD), F32),
            pltpu.SemaphoreType.DMA((4,)),
            pltpu.SemaphoreType.DMA((rows, 2, 2)),
        ],
        compiler_params=pltpu.CompilerParams(vmem_limit_bytes=32 * 2**20),
        cost_estimate=pl.CostEstimate(
            flops=4 * rows * steps * HQ * cache * HD,
            bytes_accessed=4 * rows * cache * kv_width,
            transcendentals=rows * steps * HQ * cache,
        ),
        name="attend",
    )(*in_hbm(kv_len, queries, new_keys, new_values, cache_keys, cache_values))


def sender(slot, me, parts):
    return me ^ slot if parts == RING else slot


def swap(x, bits, parts):
    return lax.ppermute(x, "tensor", [(i, i ^ bits) for i in range(parts)])


def prepare_kernel(
    rows, count_ref, rank_ref, owner_ref, after, d_hbm, u_hbm,
    d_ref, u_ref, pick_ref, place_ref, order_ref, sems,
):
    me = lax.axis_index("tensor")
    cuts = sems.shape[1]
    deep = d_ref.shape[0] // cuts
    copies = []
    for j, (src, dst) in enumerate(((d_hbm, d_ref), (u_hbm, u_ref))):
        for i in range(cuts):
            at = pl.ds(i * deep, deep)
            copies.append(pltpu.make_async_copy(src.at[0, at], dst.at[at], sems.at[j, i]))
            copies[-1].start()
    slots, total = pick_ref.shape
    steps = slots // MOST
    each = steps * rows
    parts = total // each
    requests = parts * rows

    def adapter_of(block):
        first = jnp.zeros(block.shape, jnp.int32)
        amount = jnp.zeros(block.shape, jnp.int32)
        start = jnp.int32(0)
        for a in range(count_ref.shape[0]):
            owned = (owner_ref[a] <= block) & (block < owner_ref[a] + rank_ref[a])
            first = jnp.where(owned, start, first)
            amount = jnp.where(owned, count_ref[a], amount)
            start = start + count_ref[a]
        return first, amount

    def row_place(index):
        device = sender(index // each, me, parts)
        return device * rows + index % rows, (index % each) // rows

    row = iota((slots, 1), 0)
    nth = row % MOST
    first, amount = adapter_of(jnp.zeros_like(row) + me)
    request, step = row_place(iota((1, total), 1))
    pick = (request == first + nth) & (nth < amount) & (step == row // MOST)
    pick_ref[...] = one_hot(pick)

    request, step = row_place(iota((total, total), 1))
    order_ref[...] = one_hot(iota((total, total), 0) == step * requests + request)

    entry = iota((1, parts * slots), 1)
    nth = entry % MOST
    first, amount = adapter_of(entry // slots)
    goal = jnp.where(nth < amount, (entry % slots) // MOST * requests + first + nth, -1)
    place_ref[...] = one_hot(iota((total, parts * slots), 0) == goal)
    for copy in copies:
        copy.wait()


def prepare(after, store_down, store_up, tables, steps, rows, parts):
    width, rank_w = store_down.shape[1:]
    total = parts * steps * rows
    slots = steps * MOST
    vmem = pl.BlockSpec(memory_space=pltpu.VMEM)
    shapes = [(width, rank_w)] * 2 + [(slots, total), (total, parts * slots), (total, total)]
    return pl.pallas_call(
        functools.partial(prepare_kernel, rows),
        out_shape=[jax.ShapeDtypeStruct(shape, BF16) for shape in shapes],
        in_specs=[pl.BlockSpec(memory_space=pltpu.SMEM)] * 3
        + [pl.BlockSpec(memory_space=pl.ANY)] * 3,
        out_specs=[vmem] * len(shapes),
        scratch_shapes=[pltpu.SemaphoreType.DMA((2, 4))],
        compiler_params=pltpu.CompilerParams(vmem_limit_bytes=16 * 2**20),
        cost_estimate=pl.CostEstimate(
            flops=2 * 10**10, bytes_accessed=8 * width * rank_w, transcendentals=0
        ),
        name="prepare",
    )(*in_hbm(*tables), after, *in_hbm(store_down, store_up))


def gather(block, prepared, parts):
    if parts != RING:
        whole = lax.all_gather(block, "tensor")
        return [whole[i] for i in range(parts)], prepared
    core, y, near, far = 1, 2, 4, 8
    held = {0: block}
    held[far] = swap(block, far, parts)
    held[near] = swap(block, near, parts)
    held[y] = swap(block, y, parts)
    held[near | y] = swap(block, near | y, parts)
    held[far], *prepared = lax.optimization_barrier((held[far], *prepared))
    held[far | y] = swap(held[far], y, parts)
    held[far | near | y] = swap(held[far], near | y, parts)
    held[far | near] = swap(held[far], near, parts)
    names = (near, y, near | y, far | near)
    held.update(zip(names, lax.optimization_barrier(tuple(held[n] for n in names))))
    for slot in list(held):
        held[slot | core] = swap(held[slot], core, parts)
    return [held[slot] for slot in range(parts)], prepared


def delta_kernel(at_slot, *refs):
    (*blocks, pick_ref, d_ref, u_ref, out_ref, rows_ref) = refs
    blocks = [blocks[at_slot.index(i)] for i in range(len(blocks))]
    parts, slots, cols = out_ref.shape
    each, width = blocks[0].shape
    cuts = 8
    deep = width // cuts
    low = jnp.zeros((parts * each, d_ref.shape[1]), F32)
    for i in range(cuts):
        at = slice(i * deep, (i + 1) * deep)
        piece = jnp.concatenate([b[:, at] for b in blocks], axis=0)
        rows_ref[:, at] = piece
        low = low + dot(piece, d_ref[at, :])
    chosen = dot(pick_ref[...], low.astype(BF16)).astype(BF16)
    for p in range(parts):
        out_ref[p] = dot_nt(chosen, u_ref[p * cols : (p + 1) * cols, :]).astype(BF16)


def deltas(blocks, pick, down, up):
    parts = len(blocks)
    each, width = blocks[0].shape
    slots = pick.shape[0]
    rank_w = down.shape[1]
    vmem = pl.BlockSpec(memory_space=pltpu.VMEM)
    at_slot = ORDER if parts == RING else [*range(parts)]
    return pl.pallas_call(
        functools.partial(delta_kernel, at_slot),
        out_shape=(
            jax.ShapeDtypeStruct((parts, slots, width // parts), BF16),
            jax.ShapeDtypeStruct((parts * each, width), BF16),
        ),
        in_specs=[vmem] * (3 + parts),
        out_specs=(vmem, vmem),
        compiler_params=pltpu.CompilerParams(vmem_limit_bytes=24 * 2**20),
        cost_estimate=pl.CostEstimate(
            flops=2 * (parts * each + slots) * width * rank_w,
            bytes_accessed=2 * width * (2 * parts * each + 2 * rank_w + slots),
            transcendentals=0,
        ),
        name="delta",
    )(*[blocks[i] for i in at_slot], pick, down, up)


def base_kernel(a_ref, w_ref, order_ref, out_ref):
    width = a_ref.shape[1]
    cuts = 8
    deep = width // cuts
    for i in range(cuts):
        at = slice(i * deep, (i + 1) * deep)
        part = dot(dot(order_ref[...], a_ref[:, at]).astype(BF16), w_ref[at, :])
        out_ref[...] = part if i == 0 else out_ref[...] + part


def base_part(gathered, out_weight, order):
    total, width = gathered.shape
    cols = out_weight.shape[1]
    vmem = pl.BlockSpec(memory_space=pltpu.VMEM)
    return pl.pallas_call(
        base_kernel,
        out_shape=jax.ShapeDtypeStruct((total, cols), F32),
        in_specs=[vmem] * 3,
        out_specs=vmem,
        compiler_params=pltpu.CompilerParams(vmem_limit_bytes=24 * 2**20),
        cost_estimate=pl.CostEstimate(
            flops=2 * total * width * (cols + total),
            bytes_accessed=2 * width * (total + cols) + 4 * total * cols,
            transcendentals=0,
        ),
        name="base",
    )(gathered, out_weight, order)


def join_kernel(base_ref, place_ref, delta_ref, out_ref):
    steps, requests, cols = out_ref.shape
    parts, slots, _ = delta_ref.shape
    delta = dot(place_ref[...], delta_ref[...].reshape(parts * slots, cols))
    result = (base_ref[...] + delta).astype(BF16)
    for t in range(steps):
        out_ref[t] = result[t * requests : (t + 1) * requests]


def join(base, place, delta, steps):
    total, cols = base.shape
    vmem = pl.BlockSpec(memory_space=pltpu.VMEM)
    return pl.pallas_call(
        join_kernel,
        out_shape=jax.ShapeDtypeStruct((steps, total // steps, cols), BF16),
        in_specs=[vmem] * 3,
        out_specs=vmem,
        compiler_params=pltpu.CompilerParams(vmem_limit_bytes=24 * 2**20),
        name="join",
    )(base, place, delta)


def per_device(
    queries,
    new_keys,
    new_values,
    cache_keys,
    cache_values,
    kv_len,
    adapter_rows,
    adapter_rank,
    adapter_owner,
    out_weight,
    store_down,
    store_up,
):
    parts = lax.axis_size("tensor")
    steps, rows, width = queries.shape
    tables = (adapter_rows, adapter_rank, adapter_owner)
    attended = attend(queries, new_keys, new_values, cache_keys, cache_values, kv_len)
    prepared = prepare(attended, store_down, store_up, tables, steps, rows, parts)
    blocks, (down, up, pick, place, order) = gather(attended, prepared, parts)
    send, gathered = deltas(blocks, pick, down, up)
    delta = lax.all_to_all(send, "tensor", split_axis=0, concat_axis=0, tiled=True)
    base = base_part(gathered, out_weight, order)
    return join(base, place, delta, steps)


def solution(mesh):
    in_specs = (
        P(None, ("groups", "tensor"), None),
        P(None, ("groups", "tensor"), None),
        P(None, ("groups", "tensor"), None),
        P(("groups", "tensor"), None, None),
        P(("groups", "tensor"), None, None),
        P(("groups", "tensor")),
        P("groups"),
        P(),
        P(),
        P(None, "tensor"),
        P("tensor", None, None),
        P("tensor", None, None),
    )
    out_specs = P(None, "groups", "tensor")
    return jax.shard_map(
        per_device, mesh=mesh, in_specs=in_specs, out_specs=out_specs, check_vma=False
    )
```

```python
import functools

import jax
import jax.numpy as jnp
from jax import lax
from jax.experimental import pallas as pl
from jax.experimental.pallas import tpu as pltpu
from jax.sharding import PartitionSpec as P

HQ = 64
KVH = 8
HD = 128
GROUP = HQ // KVH
MOST = 8
RING = 16
ORDER = [0, 1, 8, 9, 12, 13, 14, 15, 10, 11, 4, 5, 2, 3, 6, 7]
F32 = jnp.float32
BF16 = jnp.bfloat16
NT = (((1,), (1,)), ((), ()))


def in_hbm(*arrays):
    return [pltpu.with_memory_space_constraint(a, pltpu.HBM) for a in arrays]


def iota(shape, dim):
    return lax.broadcasted_iota(jnp.int32, shape, dim)


def one_hot(mask):
    return mask.astype(F32).astype(BF16)


def dot(a, b):
    return jnp.dot(a, b, preferred_element_type=F32)


def dot_nt(a, b):
    return lax.dot_general(a, b, NT, preferred_element_type=F32)


def sender(slot, me, parts):
    return me ^ slot if parts == RING else slot


def write_plan(rows, count_ref, rank_ref, owner_ref, pick_ref, place_ref, order_ref):
    me = lax.axis_index("tensor")
    slots, total = pick_ref.shape
    steps = slots // MOST
    each = steps * rows
    parts = total // each
    requests = parts * rows

    def adapter_of(block):
        first = jnp.zeros(block.shape, jnp.int32)
        amount = jnp.zeros(block.shape, jnp.int32)
        start = jnp.int32(0)
        for a in range(count_ref.shape[0]):
            owned = (owner_ref[a] <= block) & (block < owner_ref[a] + rank_ref[a])
            first = jnp.where(owned, start, first)
            amount = jnp.where(owned, count_ref[a], amount)
            start = start + count_ref[a]
        return first, amount

    def row_place(index):
        device = sender(index // each, me, parts)
        return device * rows + index % rows, (index % each) // rows

    row = iota((slots, 1), 0)
    nth = row % MOST
    first, amount = adapter_of(jnp.zeros_like(row) + me)
    request, step = row_place(iota((1, total), 1))
    pick = (request == first + nth) & (nth < amount) & (step == row // MOST)
    pick_ref[...] = one_hot(pick)

    request, step = row_place(iota((1, total), 1))
    order_ref[...] = one_hot(iota((total, total), 0) == step * requests + request)

    entry = iota((1, parts * slots), 1)
    nth = entry % MOST
    first, amount = adapter_of(entry // slots)
    goal = jnp.where(nth < amount, (entry % slots) // MOST * requests + first + nth, -1)
    place_ref[...] = one_hot(iota((total, parts * slots), 0) == goal)


def attend_kernel(
    len_hbm, q_hbm, nk_hbm, nv_hbm, k_hbm, v_hbm, d_hbm, u_hbm, count_hbm, rank_hbm, owner_hbm,
    out_ref, d_ref, u_ref, pick_ref, place_ref, order_ref,
    len_ref, count_ref, rank_ref, owner_ref, q_ref, nk_ref, nv_ref, k_ref, v_ref, turned_q, nks, nvs, raw, mixed,
    small_sems, sems, store_sems,
):
    steps, rows, width = q_ref.shape
    cache = k_ref.shape[1]
    both = steps * rows
    pack = steps * GROUP
    cuts = sems.shape[2]

    small = [
        pltpu.make_async_copy(src, dst, small_sems.at[i])
        for i, (src, dst) in enumerate(
            (
                (q_hbm, q_ref),
                (nk_hbm, nk_ref),
                (nv_hbm, nv_ref),
                (len_hbm, len_ref),
                (count_hbm, count_ref),
                (rank_hbm, rank_ref),
                (owner_hbm, owner_ref),
            )
        )
    ]
    pieces = [pl.ds(i * (cache // cuts), cache // cuts) for i in range(cuts)]
    keys, values = [
        [
            [
                pltpu.make_async_copy(src.at[r, at], dst.at[r, at], sems.at[r, j, i])
                for i, at in enumerate(pieces)
            ]
            for r in range(rows)
        ]
        for j, (src, dst) in enumerate(((k_hbm, k_ref), (v_hbm, v_ref)))
    ]
    deep = d_ref.shape[0] // store_sems.shape[1]
    store = [
        pltpu.make_async_copy(
            src.at[0, pl.ds(i * deep, deep)], dst.at[pl.ds(i * deep, deep)], store_sems.at[j, i]
        )
        for j, (src, dst) in enumerate(((d_hbm, d_ref), (u_hbm, u_ref)))
        for i in range(store_sems.shape[1])
    ]
    queue = [keys[0], values[0], keys[1]]
    for r in range(rows):
        queue += [values[r + 1]] if r + 1 < rows else [store]
        queue += [keys[r + 2]] if r + 2 < rows else []
    for copy in small + queue[0] + queue[1] + queue[2]:
        copy.start()
    queue = queue[3:]
    for copy in small:
        copy.wait()

    flat = jnp.concatenate([q_ref[t].astype(F32) for t in range(steps)], axis=0)
    heads = []
    for k in range(KVH):
        group = jnp.stack(
            [flat[:, (k * GROUP + g) * HD : (k * GROUP + g + 1) * HD] for g in range(GROUP)]
        )
        heads.append(jnp.swapaxes(group, 0, 1))
    column = iota((HD, KVH * pack), 1)
    for r in range(rows):
        mine = jnp.concatenate(
            [heads[k][t * rows + r] for k in range(KVH) for t in range(steps)], axis=0
        )
        mine = jnp.transpose(mine)
        for k in range(KVH):
            turned_q[r, k * HD : (k + 1) * HD, :] = jnp.where(
                column // pack == k, mine, 0.0
            ).astype(BF16)
    for src, dst in ((nk_ref, nks), (nv_ref, nvs)):
        fresh = [src[t].astype(F32) for t in range(steps)]
        fresh.append(jnp.zeros((16 - both, src.shape[2]), F32))
        dst[...] = jnp.concatenate(fresh, axis=0).astype(BF16)

    write_plan(rows, count_ref, rank_ref, owner_ref, pick_ref, place_ref, order_ref)

    scale = HD ** (-0.5)
    pairs = [
        (slice(k * pack, (k + 2) * pack), slice(k * HD, (k + 2) * HD)) for k in range(0, KVH, 2)
    ]
    for turn in range(rows + 1):
        if turn < rows:
            for copy in keys[turn]:
                copy.wait()
        if turn > 0:
            for copy in values[turn - 1]:
                copy.wait()
        for copies in queue[2 * turn : 2 * turn + 2]:
            for copy in copies:
                copy.start()
        if turn < rows:
            raw[turn % 2] = dot(k_ref[turn], turned_q[turn])
        if turn == 0:
            continue
        r = turn - 1
        fresh = dot(nks[...], turned_q[r])
        slot = iota(fresh.shape, 0)
        step = (iota(fresh.shape, 1) // GROUP) % steps
        seen = (slot < both) & (slot % rows == r) & (slot // rows <= step)
        fresh = jnp.where(seen, fresh * scale, -jnp.inf)
        older = raw[r % 2]
        older = jnp.where(iota(older.shape, 0) < len_ref[r], older * scale, -jnp.inf)
        top = jnp.maximum(
            jnp.max(older, axis=0, keepdims=True), jnp.max(fresh, axis=0, keepdims=True)
        )
        e_older = jnp.exp(older - top)
        e_fresh = jnp.exp(fresh - top)
        total = jnp.sum(e_older, axis=0, keepdims=True) + jnp.sum(e_fresh, axis=0, keepdims=True)
        inverse = 1.0 / total
        p_older = jnp.transpose((e_older * inverse).astype(BF16))
        p_fresh = jnp.transpose((e_fresh * inverse).astype(BF16))
        for k, (own, cols_k) in zip(range(0, KVH, 2), pairs):
            pair = dot(p_older[own], v_ref[r, :, cols_k]) + dot(p_fresh[own], nvs[:, cols_k])
            mixed[r, k] = pair[:pack, :HD]
            mixed[r, k + 1] = pair[pack:, HD:]

    for k in range(KVH):
        turned = jnp.stack(
            [
                mixed[r, k, t * GROUP : (t + 1) * GROUP, :]
                for t in range(steps)
                for r in range(rows)
            ]
        )
        heads = jnp.swapaxes(turned, 0, 1)
        for g in range(GROUP):
            at = (k * GROUP + g) * HD
            out_ref[:, at : at + HD] = heads[g].astype(BF16)
    for copy in store:
        copy.wait()


def attend(
    queries,
    new_keys,
    new_values,
    cache_keys,
    cache_values,
    kv_len,
    store_down,
    store_up,
    tables,
    parts,
):
    steps, rows, width = queries.shape
    cache, kv_width = cache_keys.shape[1:]
    pack = steps * GROUP
    rank_w = store_down.shape[2]
    total = parts * steps * rows
    slots = steps * MOST
    shapes = [(steps * rows, width), (width, rank_w), (width, rank_w)]
    shapes += [(slots, total), (total, parts * slots), (total, total)]
    return pl.pallas_call(
        attend_kernel,
        out_shape=[jax.ShapeDtypeStruct(shape, BF16) for shape in shapes],
        in_specs=[pl.BlockSpec(memory_space=pl.ANY)] * 11,
        out_specs=[pl.BlockSpec(memory_space=pltpu.VMEM)] * len(shapes),
        scratch_shapes=[
            pltpu.SMEM(kv_len.shape, jnp.int32),
            *[pltpu.SMEM(table.shape, jnp.int32) for table in tables],
            pltpu.VMEM(queries.shape, BF16),
            pltpu.VMEM(new_keys.shape, BF16),
            pltpu.VMEM(new_values.shape, BF16),
            pltpu.VMEM(cache_keys.shape, BF16),
            pltpu.VMEM(cache_values.shape, BF16),
            pltpu.VMEM((rows, kv_width, KVH * pack), BF16),
            pltpu.VMEM((16, kv_width), BF16),
            pltpu.VMEM((16, kv_width), BF16),
            pltpu.VMEM((2, cache, KVH * pack), F32),
            pltpu.VMEM((rows, KVH, pack, HD), F32),
            pltpu.SemaphoreType.DMA((7,)),
            pltpu.SemaphoreType.DMA((rows, 2, 2)),
            pltpu.SemaphoreType.DMA((2, 4)),
        ],
        compiler_params=pltpu.CompilerParams(vmem_limit_bytes=32 * 2**20),
        cost_estimate=pl.CostEstimate(
            flops=4 * rows * steps * HQ * cache * HD,
            bytes_accessed=4 * rows * cache * kv_width,
            transcendentals=rows * steps * HQ * cache,
        ),
        name="attend",
    )(
        *in_hbm(
            kv_len,
            queries,
            new_keys,
            new_values,
            cache_keys,
            cache_values,
            store_down,
            store_up,
            *tables,
        )
    )


def swap(x, bits, parts):
    return lax.ppermute(x, "tensor", [(i, i ^ bits) for i in range(parts)])


def gather(block, parts):
    if parts != RING:
        whole = lax.all_gather(block, "tensor")
        return [whole[i] for i in range(parts)]
    core, y, near, far = 1, 2, 4, 8
    held = {0: block}
    held[far] = swap(block, far, parts)
    held[near] = swap(block, near, parts)
    held[y] = swap(block, y, parts)
    held[near | y] = swap(held[y], near, parts)
    held[far | y] = swap(held[far], y, parts)
    held[far | near | y] = swap(held[far], near | y, parts)
    held[far | near] = swap(held[far], near, parts)
    for slot in list(held):
        held[slot | core] = swap(held[slot], core, parts)
    return [held[slot] for slot in range(parts)]


def delta_kernel(at_slot, *refs):
    (*blocks, pick_ref, d_ref, u_ref, out_ref, rows_ref) = refs
    blocks = [blocks[at_slot.index(i)] for i in range(len(blocks))]
    parts, slots, cols = out_ref.shape
    each, width = blocks[0].shape
    cuts = 8
    deep = width // cuts
    low = jnp.zeros((parts * each, d_ref.shape[1]), F32)
    for i in range(cuts):
        at = slice(i * deep, (i + 1) * deep)
        piece = jnp.concatenate([b[:, at] for b in blocks], axis=0)
        rows_ref[:, at] = piece
        low = low + dot(piece, d_ref[at, :])
    chosen = dot(pick_ref[...], low.astype(BF16)).astype(BF16)
    for p in range(parts):
        out_ref[p] = dot_nt(chosen, u_ref[p * cols : (p + 1) * cols, :]).astype(BF16)


def deltas(blocks, pick, down, up):
    parts = len(blocks)
    each, width = blocks[0].shape
    slots = pick.shape[0]
    rank_w = down.shape[1]
    vmem = pl.BlockSpec(memory_space=pltpu.VMEM)
    at_slot = ORDER if parts == RING else [*range(parts)]
    return pl.pallas_call(
        functools.partial(delta_kernel, at_slot),
        out_shape=(
            jax.ShapeDtypeStruct((parts, slots, width // parts), BF16),
            jax.ShapeDtypeStruct((parts * each, width), BF16),
        ),
        in_specs=[vmem] * (3 + parts),
        out_specs=(vmem, vmem),
        compiler_params=pltpu.CompilerParams(vmem_limit_bytes=24 * 2**20),
        cost_estimate=pl.CostEstimate(
            flops=2 * (parts * each + slots) * width * rank_w,
            bytes_accessed=2 * width * (2 * parts * each + 2 * rank_w + slots),
            transcendentals=0,
        ),
        name="delta",
    )(*[blocks[i] for i in at_slot], pick, down, up)


def base_kernel(a_ref, w_ref, order_ref, out_ref):
    width = a_ref.shape[1]
    cuts = 8
    deep = width // cuts
    for i in range(cuts):
        at = slice(i * deep, (i + 1) * deep)
        part = dot(dot(order_ref[...], a_ref[:, at]).astype(BF16), w_ref[at, :])
        out_ref[...] = part if i == 0 else out_ref[...] + part


def base_part(gathered, out_weight, order):
    total, width = gathered.shape
    cols = out_weight.shape[1]
    vmem = pl.BlockSpec(memory_space=pltpu.VMEM)
    return pl.pallas_call(
        base_kernel,
        out_shape=jax.ShapeDtypeStruct((total, cols), F32),
        in_specs=[vmem] * 3,
        out_specs=vmem,
        compiler_params=pltpu.CompilerParams(vmem_limit_bytes=24 * 2**20),
        cost_estimate=pl.CostEstimate(
            flops=2 * total * width * (cols + total),
            bytes_accessed=2 * width * (total + cols) + 4 * total * cols,
            transcendentals=0,
        ),
        name="base",
    )(gathered, out_weight, order)


def join_kernel(base_ref, place_ref, delta_ref, out_ref):
    steps, requests, cols = out_ref.shape
    parts, slots, _ = delta_ref.shape
    delta = dot(place_ref[...], delta_ref[...].reshape(parts * slots, cols))
    result = (base_ref[...] + delta).astype(BF16)
    for t in range(steps):
        out_ref[t] = result[t * requests : (t + 1) * requests]


def join(base, place, delta, steps):
    total, cols = base.shape
    vmem = pl.BlockSpec(memory_space=pltpu.VMEM)
    return pl.pallas_call(
        join_kernel,
        out_shape=jax.ShapeDtypeStruct((steps, total // steps, cols), BF16),
        in_specs=[vmem] * 3,
        out_specs=vmem,
        compiler_params=pltpu.CompilerParams(vmem_limit_bytes=24 * 2**20),
        name="join",
    )(base, place, delta)


def per_device(
    queries,
    new_keys,
    new_values,
    cache_keys,
    cache_values,
    kv_len,
    adapter_rows,
    adapter_rank,
    adapter_owner,
    out_weight,
    store_down,
    store_up,
):
    parts = lax.axis_size("tensor")
    steps, rows, width = queries.shape
    tables = (adapter_rows, adapter_rank, adapter_owner)
    attended, down, up, pick, place, order = attend(
        queries,
        new_keys,
        new_values,
        cache_keys,
        cache_values,
        kv_len,
        store_down,
        store_up,
        tables,
        parts,
    )
    blocks = gather(attended, parts)
    send, gathered = deltas(blocks, pick, down, up)
    delta = lax.all_to_all(send, "tensor", split_axis=0, concat_axis=0, tiled=True)
    base = base_part(gathered, out_weight, order)
    return join(base, place, delta, steps)


def solution(mesh):
    in_specs = (
        P(None, ("groups", "tensor"), None),
        P(None, ("groups", "tensor"), None),
        P(None, ("groups", "tensor"), None),
        P(("groups", "tensor"), None, None),
        P(("groups", "tensor"), None, None),
        P(("groups", "tensor")),
        P("groups"),
        P(),
        P(),
        P(None, "tensor"),
        P("tensor", None, None),
        P("tensor", None, None),
    )
    out_specs = P(None, "groups", "tensor")
    return jax.shard_map(
        per_device, mesh=mesh, in_specs=in_specs, out_specs=out_specs, check_vma=False
    )
```

```python
import functools

import jax
import jax.numpy as jnp
from jax import lax
from jax.experimental import pallas as pl
from jax.experimental.pallas import tpu as pltpu
from jax.sharding import PartitionSpec as P

HQ = 64
KVH = 8
HD = 128
GROUP = HQ // KVH
MOST = 8
RING = 16
ORDER = [0, 1, 2, 3, 4, 5, 6, 7, 8, 9, 12, 13, 14, 15, 10, 11]
F32 = jnp.float32
BF16 = jnp.bfloat16
NT = (((1,), (1,)), ((), ()))


def in_hbm(*arrays):
    return [pltpu.with_memory_space_constraint(a, pltpu.HBM) for a in arrays]


def iota(shape, dim):
    return lax.broadcasted_iota(jnp.int32, shape, dim)


def one_hot(mask):
    return mask.astype(F32).astype(BF16)


def dot(a, b):
    return jnp.dot(a, b, preferred_element_type=F32)


def dot_nt(a, b):
    return lax.dot_general(a, b, NT, preferred_element_type=F32)


def sender(slot, me, parts):
    return me ^ slot if parts == RING else slot


def write_plan(rows, count_ref, rank_ref, owner_ref, pick_ref, place_ref, order_ref):
    me = lax.axis_index("tensor")
    slots, total = pick_ref.shape
    steps = slots // MOST
    each = steps * rows
    parts = total // each
    requests = parts * rows

    def adapter_of(block):
        first = jnp.zeros(block.shape, jnp.int32)
        amount = jnp.zeros(block.shape, jnp.int32)
        start = jnp.int32(0)
        for a in range(count_ref.shape[0]):
            owned = (owner_ref[a] <= block) & (block < owner_ref[a] + rank_ref[a])
            first = jnp.where(owned, start, first)
            amount = jnp.where(owned, count_ref[a], amount)
            start = start + count_ref[a]
        return first, amount

    def row_place(index):
        device = sender(index // each, me, parts)
        return device * rows + index % rows, (index % each) // rows

    row = iota((slots, 1), 0)
    nth = row % MOST
    first, amount = adapter_of(jnp.zeros_like(row) + me)
    request, step = row_place(iota((1, total), 1))
    pick = (request == first + nth) & (nth < amount) & (step == row // MOST)
    pick_ref[...] = one_hot(pick)

    request, step = row_place(iota((1, total), 1))
    order_ref[...] = one_hot(iota((total, total), 0) == step * requests + request)

    entry = iota((1, parts * slots), 1)
    nth = entry % MOST
    first, amount = adapter_of(entry // slots)
    goal = jnp.where(nth < amount, (entry % slots) // MOST * requests + first + nth, -1)
    place_ref[...] = one_hot(iota((total, parts * slots), 0) == goal)


def attend_kernel(
    len_hbm, q_hbm, nk_hbm, nv_hbm, k_hbm, v_hbm, d_hbm, u_hbm, count_hbm, rank_hbm, owner_hbm,
    out_ref, d_ref, u_ref, pick_ref, place_ref, order_ref,
    len_ref, count_ref, rank_ref, owner_ref, q_ref, nk_ref, nv_ref, k_ref, v_ref, turned_q, nks, nvs, raw, mixed,
    small_sems, sems, store_sems,
):
    steps, rows, width = q_ref.shape
    cache = k_ref.shape[1]
    both = steps * rows
    pack = steps * GROUP
    cuts = sems.shape[2]

    small = [
        pltpu.make_async_copy(src, dst, small_sems.at[i])
        for i, (src, dst) in enumerate(
            (
                (q_hbm, q_ref),
                (nk_hbm, nk_ref),
                (nv_hbm, nv_ref),
                (len_hbm, len_ref),
                (count_hbm, count_ref),
                (rank_hbm, rank_ref),
                (owner_hbm, owner_ref),
            )
        )
    ]
    pieces = [pl.ds(i * (cache // cuts), cache // cuts) for i in range(cuts)]
    keys, values = [
        [
            [
                pltpu.make_async_copy(src.at[r, at], dst.at[r, at], sems.at[r, j, i])
                for i, at in enumerate(pieces)
            ]
            for r in range(rows)
        ]
        for j, (src, dst) in enumerate(((k_hbm, k_ref), (v_hbm, v_ref)))
    ]
    deep = d_ref.shape[0] // store_sems.shape[1]
    store = [
        pltpu.make_async_copy(
            src.at[0, pl.ds(i * deep, deep)], dst.at[pl.ds(i * deep, deep)], store_sems.at[j, i]
        )
        for j, (src, dst) in enumerate(((d_hbm, d_ref), (u_hbm, u_ref)))
        for i in range(store_sems.shape[1])
    ]
    queue = [keys[0], values[0], keys[1]]
    for r in range(rows):
        queue += [values[r + 1]] if r + 1 < rows else [store]
        queue += [keys[r + 2]] if r + 2 < rows else []
    for copy in small + queue[0] + queue[1] + queue[2]:
        copy.start()
    queue = queue[3:]
    for copy in small:
        copy.wait()

    flat = jnp.concatenate([q_ref[t].astype(F32) for t in range(steps)], axis=0)
    heads = []
    for k in range(KVH):
        group = jnp.stack(
            [flat[:, (k * GROUP + g) * HD : (k * GROUP + g + 1) * HD] for g in range(GROUP)]
        )
        heads.append(jnp.swapaxes(group, 0, 1))
    column = iota((HD, KVH * pack), 1)
    for r in range(rows):
        mine = jnp.concatenate(
            [heads[k][t * rows + r] for k in range(KVH) for t in range(steps)], axis=0
        )
        mine = jnp.transpose(mine)
        for k in range(KVH):
            turned_q[r, k * HD : (k + 1) * HD, :] = jnp.where(
                column // pack == k, mine, 0.0
            ).astype(BF16)
    for src, dst in ((nk_ref, nks), (nv_ref, nvs)):
        fresh = [src[t].astype(F32) for t in range(steps)]
        fresh.append(jnp.zeros((16 - both, src.shape[2]), F32))
        dst[...] = jnp.concatenate(fresh, axis=0).astype(BF16)

    write_plan(rows, count_ref, rank_ref, owner_ref, pick_ref, place_ref, order_ref)

    scale = HD ** (-0.5)
    pairs = [
        (slice(k * pack, (k + 2) * pack), slice(k * HD, (k + 2) * HD)) for k in range(0, KVH, 2)
    ]
    for turn in range(rows + 1):
        if turn < rows:
            for copy in keys[turn]:
                copy.wait()
        if turn > 0:
            for copy in values[turn - 1]:
                copy.wait()
        for copies in queue[2 * turn : 2 * turn + 2]:
            for copy in copies:
                copy.start()
        if turn < rows:
            raw[turn % 2] = dot(k_ref[turn], turned_q[turn])
        if turn == 0:
            continue
        r = turn - 1
        fresh = dot(nks[...], turned_q[r])
        slot = iota(fresh.shape, 0)
        step = (iota(fresh.shape, 1) // GROUP) % steps
        seen = (slot < both) & (slot % rows == r) & (slot // rows <= step)
        fresh = jnp.where(seen, fresh * scale, -jnp.inf)
        older = raw[r % 2]
        older = jnp.where(iota(older.shape, 0) < len_ref[r], older * scale, -jnp.inf)
        top = jnp.maximum(
            jnp.max(older, axis=0, keepdims=True), jnp.max(fresh, axis=0, keepdims=True)
        )
        e_older = jnp.exp(older - top)
        e_fresh = jnp.exp(fresh - top)
        total = jnp.sum(e_older, axis=0, keepdims=True) + jnp.sum(e_fresh, axis=0, keepdims=True)
        inverse = 1.0 / total
        p_older = jnp.transpose((e_older * inverse).astype(BF16))
        p_fresh = jnp.transpose((e_fresh * inverse).astype(BF16))
        for k, (own, cols_k) in zip(range(0, KVH, 2), pairs):
            pair = dot(p_older[own], v_ref[r, :, cols_k]) + dot(p_fresh[own], nvs[:, cols_k])
            mixed[r, k] = pair[:pack, :HD]
            mixed[r, k + 1] = pair[pack:, HD:]

    for k in range(KVH):
        turned = jnp.stack(
            [
                mixed[r, k, t * GROUP : (t + 1) * GROUP, :]
                for t in range(steps)
                for r in range(rows)
            ]
        )
        heads = jnp.swapaxes(turned, 0, 1)
        for g in range(GROUP):
            at = (k * GROUP + g) * HD
            out_ref[:, at : at + HD] = heads[g].astype(BF16)
    for copy in store:
        copy.wait()


def attend(
    queries,
    new_keys,
    new_values,
    cache_keys,
    cache_values,
    kv_len,
    store_down,
    store_up,
    tables,
    parts,
):
    steps, rows, width = queries.shape
    cache, kv_width = cache_keys.shape[1:]
    pack = steps * GROUP
    rank_w = store_down.shape[2]
    total = parts * steps * rows
    slots = steps * MOST
    shapes = [(steps * rows, width), (width, rank_w), (width, rank_w)]
    shapes += [(slots, total), (total, parts * slots), (total, total)]
    return pl.pallas_call(
        attend_kernel,
        out_shape=[jax.ShapeDtypeStruct(shape, BF16) for shape in shapes],
        in_specs=[pl.BlockSpec(memory_space=pl.ANY)] * 11,
        out_specs=[pl.BlockSpec(memory_space=pltpu.VMEM)] * len(shapes),
        scratch_shapes=[
            pltpu.SMEM(kv_len.shape, jnp.int32),
            *[pltpu.SMEM(table.shape, jnp.int32) for table in tables],
            pltpu.VMEM(queries.shape, BF16),
            pltpu.VMEM(new_keys.shape, BF16),
            pltpu.VMEM(new_values.shape, BF16),
            pltpu.VMEM(cache_keys.shape, BF16),
            pltpu.VMEM(cache_values.shape, BF16),
            pltpu.VMEM((rows, kv_width, KVH * pack), BF16),
            pltpu.VMEM((16, kv_width), BF16),
            pltpu.VMEM((16, kv_width), BF16),
            pltpu.VMEM((2, cache, KVH * pack), F32),
            pltpu.VMEM((rows, KVH, pack, HD), F32),
            pltpu.SemaphoreType.DMA((7,)),
            pltpu.SemaphoreType.DMA((rows, 2, 2)),
            pltpu.SemaphoreType.DMA((2, 4)),
        ],
        compiler_params=pltpu.CompilerParams(vmem_limit_bytes=32 * 2**20),
        cost_estimate=pl.CostEstimate(
            flops=4 * rows * steps * HQ * cache * HD,
            bytes_accessed=4 * rows * cache * kv_width,
            transcendentals=rows * steps * HQ * cache,
        ),
        name="attend",
    )(
        *in_hbm(
            kv_len,
            queries,
            new_keys,
            new_values,
            cache_keys,
            cache_values,
            store_down,
            store_up,
            *tables,
        )
    )


def swap(x, bits, parts):
    return lax.ppermute(x, "tensor", [(i, i ^ bits) for i in range(parts)])


def gather(block, parts):
    if parts != RING:
        whole = lax.all_gather(block, "tensor")
        return [whole[i] for i in range(parts)]
    core, y, near, far = 1, 2, 4, 8
    held = {0: block}
    held[far] = swap(block, far, parts)
    held[near] = swap(block, near, parts)
    held[y] = swap(block, y, parts)
    held[far | y] = swap(held[far], y, parts)
    held[far | near | y] = swap(held[far], near | y, parts)
    held[far | near] = swap(held[far], near, parts)
    mixed = jnp.where(lax.axis_index("tensor") % 2 == 0, held[near], held[y])
    pairs = [(i, i ^ (y if i % 2 == 0 else near)) for i in range(parts)]
    held[near | y] = lax.ppermute(mixed, "tensor", pairs)
    for slot in list(held):
        held[slot | core] = swap(held[slot], core, parts)
    return [held[slot] for slot in range(parts)]


def delta_kernel(at_slot, *refs):
    (*blocks, pick_ref, d_ref, u_ref, out_ref, rows_ref) = refs
    blocks = [blocks[at_slot.index(i)] for i in range(len(blocks))]
    parts, slots, cols = out_ref.shape
    each, width = blocks[0].shape
    cuts = 8
    deep = width // cuts
    low = jnp.zeros((parts * each, d_ref.shape[1]), F32)
    for i in range(cuts):
        at = slice(i * deep, (i + 1) * deep)
        piece = jnp.concatenate([b[:, at] for b in blocks], axis=0)
        rows_ref[:, at] = piece
        low = low + dot(piece, d_ref[at, :])
    chosen = dot(pick_ref[...], low.astype(BF16)).astype(BF16)
    for p in range(parts):
        out_ref[p] = dot_nt(chosen, u_ref[p * cols : (p + 1) * cols, :]).astype(BF16)


def deltas(blocks, pick, down, up):
    parts = len(blocks)
    each, width = blocks[0].shape
    slots = pick.shape[0]
    rank_w = down.shape[1]
    vmem = pl.BlockSpec(memory_space=pltpu.VMEM)
    at_slot = ORDER if parts == RING else [*range(parts)]
    return pl.pallas_call(
        functools.partial(delta_kernel, at_slot),
        out_shape=(
            jax.ShapeDtypeStruct((parts, slots, width // parts), BF16),
            jax.ShapeDtypeStruct((parts * each, width), BF16),
        ),
        in_specs=[vmem] * (3 + parts),
        out_specs=(vmem, vmem),
        compiler_params=pltpu.CompilerParams(vmem_limit_bytes=24 * 2**20),
        cost_estimate=pl.CostEstimate(
            flops=2 * (parts * each + slots) * width * rank_w,
            bytes_accessed=2 * width * (2 * parts * each + 2 * rank_w + slots),
            transcendentals=0,
        ),
        name="delta",
    )(*[blocks[i] for i in at_slot], pick, down, up)


def base_kernel(a_ref, w_ref, order_ref, out_ref):
    width = a_ref.shape[1]
    cuts = 8
    deep = width // cuts
    for i in range(cuts):
        at = slice(i * deep, (i + 1) * deep)
        part = dot(dot(order_ref[...], a_ref[:, at]).astype(BF16), w_ref[at, :])
        out_ref[...] = part if i == 0 else out_ref[...] + part


def base_part(gathered, out_weight, order):
    total, width = gathered.shape
    cols = out_weight.shape[1]
    vmem = pl.BlockSpec(memory_space=pltpu.VMEM)
    return pl.pallas_call(
        base_kernel,
        out_shape=jax.ShapeDtypeStruct((total, cols), F32),
        in_specs=[vmem] * 3,
        out_specs=vmem,
        compiler_params=pltpu.CompilerParams(vmem_limit_bytes=24 * 2**20),
        cost_estimate=pl.CostEstimate(
            flops=2 * total * width * (cols + total),
            bytes_accessed=2 * width * (total + cols) + 4 * total * cols,
            transcendentals=0,
        ),
        name="base",
    )(gathered, out_weight, order)


def join_kernel(base_ref, place_ref, delta_ref, out_ref):
    steps, requests, cols = out_ref.shape
    parts, slots, _ = delta_ref.shape
    delta = dot(place_ref[...], delta_ref[...].reshape(parts * slots, cols))
    result = (base_ref[...] + delta).astype(BF16)
    for t in range(steps):
        out_ref[t] = result[t * requests : (t + 1) * requests]


def join(base, place, delta, steps):
    total, cols = base.shape
    vmem = pl.BlockSpec(memory_space=pltpu.VMEM)
    return pl.pallas_call(
        join_kernel,
        out_shape=jax.ShapeDtypeStruct((steps, total // steps, cols), BF16),
        in_specs=[vmem] * 3,
        out_specs=vmem,
        compiler_params=pltpu.CompilerParams(vmem_limit_bytes=24 * 2**20),
        name="join",
    )(base, place, delta)


def per_device(
    queries,
    new_keys,
    new_values,
    cache_keys,
    cache_values,
    kv_len,
    adapter_rows,
    adapter_rank,
    adapter_owner,
    out_weight,
    store_down,
    store_up,
):
    parts = lax.axis_size("tensor")
    steps, rows, width = queries.shape
    tables = (adapter_rows, adapter_rank, adapter_owner)
    attended, down, up, pick, place, order = attend(
        queries,
        new_keys,
        new_values,
        cache_keys,
        cache_values,
        kv_len,
        store_down,
        store_up,
        tables,
        parts,
    )
    blocks = gather(attended, parts)
    send, gathered = deltas(blocks, pick, down, up)
    delta = lax.all_to_all(send, "tensor", split_axis=0, concat_axis=0, tiled=True)
    base = base_part(gathered, out_weight, order)
    return join(base, place, delta, steps)


def solution(mesh):
    in_specs = (
        P(None, ("groups", "tensor"), None),
        P(None, ("groups", "tensor"), None),
        P(None, ("groups", "tensor"), None),
        P(("groups", "tensor"), None, None),
        P(("groups", "tensor"), None, None),
        P(("groups", "tensor")),
        P("groups"),
        P(),
        P(),
        P(None, "tensor"),
        P("tensor", None, None),
        P("tensor", None, None),
    )
    out_specs = P(None, "groups", "tensor")
    return jax.shard_map(
        per_device, mesh=mesh, in_specs=in_specs, out_specs=out_specs, check_vma=False
    )
```

```python
import functools

import jax
import jax.numpy as jnp
from jax import lax
from jax.experimental import pallas as pl
from jax.experimental.pallas import tpu as pltpu
from jax.sharding import PartitionSpec as P

HQ = 64
KVH = 8
HD = 128
GROUP = HQ // KVH
MOST = 8
RING = 16
QUAD = 4
F32 = jnp.float32
BF16 = jnp.bfloat16
NT = (((1,), (1,)), ((), ()))


def in_hbm(*arrays):
    return [pltpu.with_memory_space_constraint(a, pltpu.HBM) for a in arrays]


def iota(shape, dim):
    return lax.broadcasted_iota(jnp.int32, shape, dim)


def one_hot(mask):
    return mask.astype(F32).astype(BF16)


def dot(a, b):
    return jnp.dot(a, b, preferred_element_type=F32)


def dot_nt(a, b):
    return lax.dot_general(a, b, NT, preferred_element_type=F32)


def sender(slot, me, parts):
    if parts != RING:
        return slot
    four, member = slot // QUAD, slot % QUAD
    half = (me // 8 + four // 2) % 2
    return half * 8 + member * 2 + (me + four) % 2


def write_plan(rows, count_ref, rank_ref, owner_ref, pick_ref, place_ref, order_ref):
    me = lax.axis_index("tensor")
    slots, total = pick_ref.shape
    steps = slots // MOST
    each = steps * rows
    parts = total // each
    requests = parts * rows

    def adapter_of(block):
        first = jnp.zeros(block.shape, jnp.int32)
        amount = jnp.zeros(block.shape, jnp.int32)
        start = jnp.int32(0)
        for a in range(count_ref.shape[0]):
            owned = (owner_ref[a] <= block) & (block < owner_ref[a] + rank_ref[a])
            first = jnp.where(owned, start, first)
            amount = jnp.where(owned, count_ref[a], amount)
            start = start + count_ref[a]
        return first, amount

    def row_place(index):
        device = sender(index // each, me, parts)
        return device * rows + index % rows, (index % each) // rows

    row = iota((slots, 1), 0)
    nth = row % MOST
    first, amount = adapter_of(jnp.zeros_like(row) + me)
    request, step = row_place(iota((1, total), 1))
    pick = (request == first + nth) & (nth < amount) & (step == row // MOST)
    pick_ref[...] = one_hot(pick)

    request, step = row_place(iota((1, total), 1))
    order_ref[...] = one_hot(iota((total, total), 0) == step * requests + request)

    entry = iota((1, parts * slots), 1)
    nth = entry % MOST
    first, amount = adapter_of(entry // slots)
    goal = jnp.where(nth < amount, (entry % slots) // MOST * requests + first + nth, -1)
    place_ref[...] = one_hot(iota((total, parts * slots), 0) == goal)


def attend_kernel(
    len_hbm, q_hbm, nk_hbm, nv_hbm, k_hbm, v_hbm, d_hbm, u_hbm, count_hbm, rank_hbm, owner_hbm,
    out_ref, spread_ref, d_ref, u_ref, pick_ref, place_ref, order_ref,
    len_ref, count_ref, rank_ref, owner_ref, q_ref, nk_ref, nv_ref, k_ref, v_ref, turned_q, nks, nvs, raw, mixed,
    small_sems, sems, store_sems,
):
    steps, rows, width = q_ref.shape
    cache = k_ref.shape[1]
    both = steps * rows
    pack = steps * GROUP
    cuts = sems.shape[2]

    small = [
        pltpu.make_async_copy(src, dst, small_sems.at[i])
        for i, (src, dst) in enumerate(
            (
                (q_hbm, q_ref),
                (nk_hbm, nk_ref),
                (nv_hbm, nv_ref),
                (len_hbm, len_ref),
                (count_hbm, count_ref),
                (rank_hbm, rank_ref),
                (owner_hbm, owner_ref),
            )
        )
    ]
    pieces = [pl.ds(i * (cache // cuts), cache // cuts) for i in range(cuts)]
    keys, values = [
        [
            [
                pltpu.make_async_copy(src.at[r, at], dst.at[r, at], sems.at[r, j, i])
                for i, at in enumerate(pieces)
            ]
            for r in range(rows)
        ]
        for j, (src, dst) in enumerate(((k_hbm, k_ref), (v_hbm, v_ref)))
    ]
    deep = d_ref.shape[0] // store_sems.shape[1]
    store = [
        pltpu.make_async_copy(
            src.at[0, pl.ds(i * deep, deep)], dst.at[pl.ds(i * deep, deep)], store_sems.at[j, i]
        )
        for j, (src, dst) in enumerate(((d_hbm, d_ref), (u_hbm, u_ref)))
        for i in range(store_sems.shape[1])
    ]
    queue = [keys[0], values[0], keys[1]]
    for r in range(rows):
        queue += [values[r + 1]] if r + 1 < rows else [store]
        queue += [keys[r + 2]] if r + 2 < rows else []
    for copy in small + queue[0] + queue[1] + queue[2]:
        copy.start()
    queue = queue[3:]
    for copy in small:
        copy.wait()

    flat = jnp.concatenate([q_ref[t].astype(F32) for t in range(steps)], axis=0)
    heads = []
    for k in range(KVH):
        group = jnp.stack(
            [flat[:, (k * GROUP + g) * HD : (k * GROUP + g + 1) * HD] for g in range(GROUP)]
        )
        heads.append(jnp.swapaxes(group, 0, 1))
    column = iota((HD, KVH * pack), 1)
    for r in range(rows):
        mine = jnp.concatenate(
            [heads[k][t * rows + r] for k in range(KVH) for t in range(steps)], axis=0
        )
        mine = jnp.transpose(mine)
        for k in range(KVH):
            turned_q[r, k * HD : (k + 1) * HD, :] = jnp.where(
                column // pack == k, mine, 0.0
            ).astype(BF16)
    for src, dst in ((nk_ref, nks), (nv_ref, nvs)):
        fresh = [src[t].astype(F32) for t in range(steps)]
        fresh.append(jnp.zeros((16 - both, src.shape[2]), F32))
        dst[...] = jnp.concatenate(fresh, axis=0).astype(BF16)

    write_plan(rows, count_ref, rank_ref, owner_ref, pick_ref, place_ref, order_ref)

    scale = HD ** (-0.5)
    pairs = [
        (slice(k * pack, (k + 2) * pack), slice(k * HD, (k + 2) * HD)) for k in range(0, KVH, 2)
    ]
    for turn in range(rows + 1):
        if turn < rows:
            for copy in keys[turn]:
                copy.wait()
        if turn > 0:
            for copy in values[turn - 1]:
                copy.wait()
        for copies in queue[2 * turn : 2 * turn + 2]:
            for copy in copies:
                copy.start()
        if turn < rows:
            raw[turn % 2] = dot(k_ref[turn], turned_q[turn])
        if turn == 0:
            continue
        r = turn - 1
        fresh = dot(nks[...], turned_q[r])
        slot = iota(fresh.shape, 0)
        step = (iota(fresh.shape, 1) // GROUP) % steps
        seen = (slot < both) & (slot % rows == r) & (slot // rows <= step)
        fresh = jnp.where(seen, fresh * scale, -jnp.inf)
        older = raw[r % 2]
        older = jnp.where(iota(older.shape, 0) < len_ref[r], older * scale, -jnp.inf)
        top = jnp.maximum(
            jnp.max(older, axis=0, keepdims=True), jnp.max(fresh, axis=0, keepdims=True)
        )
        e_older = jnp.exp(older - top)
        e_fresh = jnp.exp(fresh - top)
        total = jnp.sum(e_older, axis=0, keepdims=True) + jnp.sum(e_fresh, axis=0, keepdims=True)
        inverse = 1.0 / total
        p_older = jnp.transpose((e_older * inverse).astype(BF16))
        p_fresh = jnp.transpose((e_fresh * inverse).astype(BF16))
        for k, (own, cols_k) in zip(range(0, KVH, 2), pairs):
            pair = dot(p_older[own], v_ref[r, :, cols_k]) + dot(p_fresh[own], nvs[:, cols_k])
            mixed[r, k] = pair[:pack, :HD]
            mixed[r, k + 1] = pair[pack:, HD:]

    for k in range(KVH):
        turned = jnp.stack(
            [
                mixed[r, k, t * GROUP : (t + 1) * GROUP, :]
                for t in range(steps)
                for r in range(rows)
            ]
        )
        heads = jnp.swapaxes(turned, 0, 1)
        for g in range(GROUP):
            at = (k * GROUP + g) * HD
            out_ref[:, at : at + HD] = heads[g].astype(BF16)
            for i in range(spread_ref.shape[0]):
                spread_ref[i, :, at : at + HD] = heads[g].astype(BF16)
    for copy in store:
        copy.wait()


def attend(
    queries,
    new_keys,
    new_values,
    cache_keys,
    cache_values,
    kv_len,
    store_down,
    store_up,
    tables,
    parts,
):
    steps, rows, width = queries.shape
    cache, kv_width = cache_keys.shape[1:]
    pack = steps * GROUP
    rank_w = store_down.shape[2]
    total = parts * steps * rows
    slots = steps * MOST
    shapes = [(steps * rows, width), (QUAD, steps * rows, width), (width, rank_w), (width, rank_w)]
    shapes += [(slots, total), (total, parts * slots), (total, total)]
    return pl.pallas_call(
        attend_kernel,
        out_shape=[jax.ShapeDtypeStruct(shape, BF16) for shape in shapes],
        in_specs=[pl.BlockSpec(memory_space=pl.ANY)] * 11,
        out_specs=[pl.BlockSpec(memory_space=pltpu.VMEM)] * len(shapes),
        scratch_shapes=[
            pltpu.SMEM(kv_len.shape, jnp.int32),
            *[pltpu.SMEM(table.shape, jnp.int32) for table in tables],
            pltpu.VMEM(queries.shape, BF16),
            pltpu.VMEM(new_keys.shape, BF16),
            pltpu.VMEM(new_values.shape, BF16),
            pltpu.VMEM(cache_keys.shape, BF16),
            pltpu.VMEM(cache_values.shape, BF16),
            pltpu.VMEM((rows, kv_width, KVH * pack), BF16),
            pltpu.VMEM((16, kv_width), BF16),
            pltpu.VMEM((16, kv_width), BF16),
            pltpu.VMEM((2, cache, KVH * pack), F32),
            pltpu.VMEM((rows, KVH, pack, HD), F32),
            pltpu.SemaphoreType.DMA((7,)),
            pltpu.SemaphoreType.DMA((rows, 2, 2)),
            pltpu.SemaphoreType.DMA((2, 4)),
        ],
        compiler_params=pltpu.CompilerParams(vmem_limit_bytes=32 * 2**20),
        cost_estimate=pl.CostEstimate(
            flops=4 * rows * steps * HQ * cache * HD,
            bytes_accessed=4 * rows * cache * kv_width,
            transcendentals=rows * steps * HQ * cache,
        ),
        name="attend",
    )(
        *in_hbm(
            kv_len,
            queries,
            new_keys,
            new_values,
            cache_keys,
            cache_values,
            store_down,
            store_up,
            *tables,
        )
    )


def swap(x, bits, parts):
    return lax.ppermute(x, "tensor", [(i, i ^ bits) for i in range(parts)])


def spread_kernel(block_ref, out_ref):
    for i in range(out_ref.shape[0]):
        out_ref[i] = block_ref[...]


def spread_out(block):
    vmem = pl.BlockSpec(memory_space=pltpu.VMEM)
    return pl.pallas_call(
        spread_kernel,
        out_shape=jax.ShapeDtypeStruct((QUAD, *block.shape), block.dtype),
        in_specs=[vmem],
        out_specs=vmem,
        compiler_params=pltpu.CompilerParams(vmem_limit_bytes=8 * 2**20),
        cost_estimate=pl.CostEstimate(
            flops=0, bytes_accessed=2 * (QUAD + 1) * block.size, transcendentals=0
        ),
        name="spread",
    )(block)


def gather(block, spread, parts):
    if parts != RING:
        return [lax.all_gather(block, "tensor")]
    quads = [[8 * half + 2 * i + core for i in range(QUAD)] for half in range(2) for core in range(2)]

    def exchange(x):
        return lax.all_to_all(x, "tensor", 0, 0, axis_index_groups=quads, tiled=True)

    far = swap(block, 8, parts)
    near_half = exchange(spread)
    far_half = exchange(spread_out(far))
    return [near_half, swap(near_half, 1, parts), far_half, swap(far_half, 1, parts)]


def delta_kernel(*refs):
    (*blocks, pick_ref, d_ref, u_ref, out_ref, rows_ref) = refs
    parts, slots, cols = out_ref.shape
    count, each, width = blocks[0].shape
    cuts = 8
    deep = width // cuts
    low = jnp.zeros((parts * each, d_ref.shape[1]), F32)
    for i in range(cuts):
        at = slice(i * deep, (i + 1) * deep)
        piece = jnp.concatenate([b[j, :, at] for b in blocks for j in range(count)], axis=0)
        rows_ref[:, at] = piece
        low = low + dot(piece, d_ref[at, :])
    chosen = dot(pick_ref[...], low.astype(BF16)).astype(BF16)
    for p in range(parts):
        out_ref[p] = dot_nt(chosen, u_ref[p * cols : (p + 1) * cols, :]).astype(BF16)


def deltas(blocks, pick, down, up, parts):
    _, each, width = blocks[0].shape
    slots = pick.shape[0]
    rank_w = down.shape[1]
    vmem = pl.BlockSpec(memory_space=pltpu.VMEM)
    return pl.pallas_call(
        delta_kernel,
        out_shape=(
            jax.ShapeDtypeStruct((parts, slots, width // parts), BF16),
            jax.ShapeDtypeStruct((parts * each, width), BF16),
        ),
        in_specs=[vmem] * (3 + len(blocks)),
        out_specs=(vmem, vmem),
        compiler_params=pltpu.CompilerParams(vmem_limit_bytes=24 * 2**20),
        cost_estimate=pl.CostEstimate(
            flops=2 * (parts * each + slots) * width * rank_w,
            bytes_accessed=2 * width * (2 * parts * each + 2 * rank_w + slots),
            transcendentals=0,
        ),
        name="delta",
    )(*blocks, pick, down, up)


def base_kernel(a_ref, w_ref, order_ref, out_ref):
    width = a_ref.shape[1]
    cuts = 8
    deep = width // cuts
    for i in range(cuts):
        at = slice(i * deep, (i + 1) * deep)
        part = dot(dot(order_ref[...], a_ref[:, at]).astype(BF16), w_ref[at, :])
        out_ref[...] = part if i == 0 else out_ref[...] + part


def base_part(gathered, out_weight, order):
    total, width = gathered.shape
    cols = out_weight.shape[1]
    vmem = pl.BlockSpec(memory_space=pltpu.VMEM)
    return pl.pallas_call(
        base_kernel,
        out_shape=jax.ShapeDtypeStruct((total, cols), F32),
        in_specs=[vmem] * 3,
        out_specs=vmem,
        compiler_params=pltpu.CompilerParams(vmem_limit_bytes=24 * 2**20),
        cost_estimate=pl.CostEstimate(
            flops=2 * total * width * (cols + total),
            bytes_accessed=2 * width * (total + cols) + 4 * total * cols,
            transcendentals=0,
        ),
        name="base",
    )(gathered, out_weight, order)


def join_kernel(base_ref, place_ref, delta_ref, out_ref):
    steps, requests, cols = out_ref.shape
    parts, slots, _ = delta_ref.shape
    delta = dot(place_ref[...], delta_ref[...].reshape(parts * slots, cols))
    result = (base_ref[...] + delta).astype(BF16)
    for t in range(steps):
        out_ref[t] = result[t * requests : (t + 1) * requests]


def join(base, place, delta, steps):
    total, cols = base.shape
    vmem = pl.BlockSpec(memory_space=pltpu.VMEM)
    return pl.pallas_call(
        join_kernel,
        out_shape=jax.ShapeDtypeStruct((steps, total // steps, cols), BF16),
        in_specs=[vmem] * 3,
        out_specs=vmem,
        compiler_params=pltpu.CompilerParams(vmem_limit_bytes=24 * 2**20),
        name="join",
    )(base, place, delta)


def per_device(
    queries,
    new_keys,
    new_values,
    cache_keys,
    cache_values,
    kv_len,
    adapter_rows,
    adapter_rank,
    adapter_owner,
    out_weight,
    store_down,
    store_up,
):
    parts = lax.axis_size("tensor")
    steps, rows, width = queries.shape
    tables = (adapter_rows, adapter_rank, adapter_owner)
    attended, spread, down, up, pick, place, order = attend(
        queries,
        new_keys,
        new_values,
        cache_keys,
        cache_values,
        kv_len,
        store_down,
        store_up,
        tables,
        parts,
    )
    blocks = gather(attended, spread, parts)
    send, gathered = deltas(blocks, pick, down, up, parts)
    delta = lax.all_to_all(send, "tensor", split_axis=0, concat_axis=0, tiled=True)
    base = base_part(gathered, out_weight, order)
    return join(base, place, delta, steps)


def solution(mesh):
    in_specs = (
        P(None, ("groups", "tensor"), None),
        P(None, ("groups", "tensor"), None),
        P(None, ("groups", "tensor"), None),
        P(("groups", "tensor"), None, None),
        P(("groups", "tensor"), None, None),
        P(("groups", "tensor")),
        P("groups"),
        P(),
        P(),
        P(None, "tensor"),
        P("tensor", None, None),
        P("tensor", None, None),
    )
    out_specs = P(None, "groups", "tensor")
    return jax.shard_map(
        per_device, mesh=mesh, in_specs=in_specs, out_specs=out_specs, check_vma=False
    )
```

```python
import functools
import math

import jax
import jax.numpy as jnp
from jax import lax
from jax.experimental import pallas as pl
from jax.experimental.pallas import tpu as pltpu
from jax.sharding import PartitionSpec as P

HQ = 64
KVH = 8
HD = 128
GROUP = HQ // KVH
MOST = 8
RING = 16
ORDER = [0, 1, 6, 7, 4, 5, 2, 3, 8, 9, 12, 13, 14, 15, 10, 11]
F32 = jnp.float32
BF16 = jnp.bfloat16
NT = (((1,), (1,)), ((), ()))


def in_hbm(*arrays):
    return [pltpu.with_memory_space_constraint(a, pltpu.HBM) for a in arrays]


def iota(shape, dim):
    return lax.broadcasted_iota(jnp.int32, shape, dim)


def one_hot(mask):
    return mask.astype(F32).astype(BF16)


def dot(a, b):
    return jnp.dot(a, b, preferred_element_type=F32)


def dot_nt(a, b):
    return lax.dot_general(a, b, NT, preferred_element_type=F32)


def sender(slot, me, parts):
    return me ^ slot if parts == RING else slot


def write_plan(rows, count_ref, rank_ref, owner_ref, pick_ref, place_ref, order_ref):
    me = lax.axis_index("tensor")
    slots, total = pick_ref.shape
    steps = slots // MOST
    each = steps * rows
    parts = total // each
    requests = parts * rows

    def adapter_of(block):
        first = jnp.zeros(block.shape, jnp.int32)
        amount = jnp.zeros(block.shape, jnp.int32)
        start = jnp.int32(0)
        for a in range(count_ref.shape[0]):
            owned = (owner_ref[a] <= block) & (block < owner_ref[a] + rank_ref[a])
            first = jnp.where(owned, start, first)
            amount = jnp.where(owned, count_ref[a], amount)
            start = start + count_ref[a]
        return first, amount

    def row_place(index):
        device = sender(index // each, me, parts)
        return device * rows + index % rows, (index % each) // rows

    row = iota((slots, 1), 0)
    nth = row % MOST
    first, amount = adapter_of(jnp.zeros_like(row) + me)
    request, step = row_place(iota((1, total), 1))
    pick = (request == first + nth) & (nth < amount) & (step == row // MOST)
    pick_ref[...] = one_hot(pick)

    request, step = row_place(iota((1, total), 1))
    order_ref[...] = one_hot(iota((total, total), 0) == step * requests + request)

    entry = iota((1, parts * slots), 1)
    nth = entry % MOST
    first, amount = adapter_of(entry // slots)
    goal = jnp.where(nth < amount, (entry % slots) // MOST * requests + first + nth, -1)
    place_ref[...] = one_hot(iota((total, parts * slots), 0) == goal)


def attend_kernel(
    len_hbm, q_hbm, nk_hbm, nv_hbm, k_hbm, v_hbm, d_hbm, u_hbm, count_hbm, rank_hbm, owner_hbm,
    out_ref, d_ref, u_ref, pick_ref, place_ref, order_ref,
    len_ref, count_ref, rank_ref, owner_ref, q_ref, nk_ref, nv_ref, k_ref, v_ref, turned_q, nks, nvs, raw, mixed,
    small_sems, sems, store_sems,
):
    steps, rows, width = q_ref.shape
    cache = k_ref.shape[1]
    both = steps * rows
    pack = steps * GROUP
    cuts = sems.shape[2]

    small = [
        pltpu.make_async_copy(src, dst, small_sems.at[i])
        for i, (src, dst) in enumerate(
            (
                (q_hbm, q_ref),
                (nk_hbm, nk_ref),
                (nv_hbm, nv_ref),
                (len_hbm, len_ref),
                (count_hbm, count_ref),
                (rank_hbm, rank_ref),
                (owner_hbm, owner_ref),
            )
        )
    ]
    pieces = [pl.ds(i * (cache // cuts), cache // cuts) for i in range(cuts)]
    keys, values = [
        [
            [
                pltpu.make_async_copy(src.at[r, at], dst.at[r, at], sems.at[r, j, i])
                for i, at in enumerate(pieces)
            ]
            for r in range(rows)
        ]
        for j, (src, dst) in enumerate(((k_hbm, k_ref), (v_hbm, v_ref)))
    ]
    deep = d_ref.shape[0] // store_sems.shape[1]
    store = [
        pltpu.make_async_copy(
            src.at[0, pl.ds(i * deep, deep)], dst.at[pl.ds(i * deep, deep)], store_sems.at[j, i]
        )
        for j, (src, dst) in enumerate(((d_hbm, d_ref), (u_hbm, u_ref)))
        for i in range(store_sems.shape[1])
    ]
    queue = [keys[0], values[0], keys[1]]
    for r in range(rows):
        queue += [values[r + 1]] if r + 1 < rows else [store]
        queue += [keys[r + 2]] if r + 2 < rows else []
    for copy in small + queue[0]:
        copy.start()
    for copy in small:
        copy.wait()
    for copy in queue[1] + queue[2]:
        copy.start()
    queue = queue[3:]

    flat = jnp.concatenate([q_ref[t].astype(F32) for t in range(steps)], axis=0)
    heads = []
    for k in range(KVH):
        group = jnp.stack(
            [flat[:, (k * GROUP + g) * HD : (k * GROUP + g + 1) * HD] for g in range(GROUP)]
        )
        heads.append(jnp.swapaxes(group, 0, 1))
    column = iota((HD, KVH * pack), 1)
    for r in range(rows):
        mine = jnp.concatenate(
            [heads[k][t * rows + r] for k in range(KVH) for t in range(steps)], axis=0
        )
        mine = jnp.transpose(mine)
        for k in range(KVH):
            turned_q[r, k * HD : (k + 1) * HD, :] = jnp.where(
                column // pack == k, mine, 0.0
            ).astype(BF16)
    for src, dst in ((nk_ref, nks), (nv_ref, nvs)):
        fresh = [src[t].astype(F32) for t in range(steps)]
        fresh.append(jnp.zeros((16 - both, src.shape[2]), F32))
        dst[...] = jnp.concatenate(fresh, axis=0).astype(BF16)

    write_plan(rows, count_ref, rank_ref, owner_ref, pick_ref, place_ref, order_ref)

    rate = HD ** (-0.5) * math.log2(math.e)
    pairs = [
        (slice(k * pack, (k + 2) * pack), slice(k * HD, (k + 2) * HD)) for k in range(0, KVH, 2)
    ]
    for turn in range(rows + 1):
        if turn < rows:
            for copy in keys[turn]:
                copy.wait()
        if turn > 0:
            for copy in values[turn - 1]:
                copy.wait()
        for copies in queue[2 * turn : 2 * turn + 2]:
            for copy in copies:
                copy.start()
        if turn < rows:
            raw[turn % 2] = dot(k_ref[turn], turned_q[turn])
        if turn == 0:
            continue
        r = turn - 1
        fresh = dot(nks[...], turned_q[r])
        slot = iota(fresh.shape, 0)
        step = (iota(fresh.shape, 1) // GROUP) % steps
        seen = (slot < both) & (slot % rows == r) & (slot // rows <= step)
        fresh = jnp.where(seen, fresh, -jnp.inf)
        older = raw[r % 2]
        older = jnp.where(iota(older.shape, 0) < len_ref[r], older, -jnp.inf)
        top = jnp.maximum(
            jnp.max(older, axis=0, keepdims=True), jnp.max(fresh, axis=0, keepdims=True)
        )
        e_older = jnp.exp2((older - top) * rate)
        e_fresh = jnp.exp2((fresh - top) * rate)
        total = jnp.sum(e_older, axis=0, keepdims=True) + jnp.sum(e_fresh, axis=0, keepdims=True)
        inverse = 1.0 / total
        p_older = jnp.transpose((e_older * inverse).astype(BF16))
        p_fresh = jnp.transpose((e_fresh * inverse).astype(BF16))
        for k, (own, cols_k) in zip(range(0, KVH, 2), pairs):
            pair = dot(p_older[own], v_ref[r, :, cols_k]) + dot(p_fresh[own], nvs[:, cols_k])
            mixed[r, k] = pair[:pack, :HD]
            mixed[r, k + 1] = pair[pack:, HD:]

    for k in range(KVH):
        turned = jnp.stack(
            [
                mixed[r, k, t * GROUP : (t + 1) * GROUP, :]
                for t in range(steps)
                for r in range(rows)
            ]
        )
        heads = jnp.swapaxes(turned, 0, 1)
        for g in range(GROUP):
            at = (k * GROUP + g) * HD
            out_ref[:, at : at + HD] = heads[g].astype(BF16)
    for copy in store:
        copy.wait()


def attend(
    queries,
    new_keys,
    new_values,
    cache_keys,
    cache_values,
    kv_len,
    store_down,
    store_up,
    tables,
    parts,
):
    steps, rows, width = queries.shape
    cache, kv_width = cache_keys.shape[1:]
    pack = steps * GROUP
    rank_w = store_down.shape[2]
    total = parts * steps * rows
    slots = steps * MOST
    shapes = [(steps * rows, width), (width, rank_w), (width, rank_w)]
    shapes += [(slots, total), (total, parts * slots), (total, total)]
    return pl.pallas_call(
        attend_kernel,
        out_shape=[jax.ShapeDtypeStruct(shape, BF16) for shape in shapes],
        in_specs=[pl.BlockSpec(memory_space=pl.ANY)] * 11,
        out_specs=[pl.BlockSpec(memory_space=pltpu.VMEM)] * len(shapes),
        scratch_shapes=[
            pltpu.SMEM(kv_len.shape, jnp.int32),
            *[pltpu.SMEM(table.shape, jnp.int32) for table in tables],
            pltpu.VMEM(queries.shape, BF16),
            pltpu.VMEM(new_keys.shape, BF16),
            pltpu.VMEM(new_values.shape, BF16),
            pltpu.VMEM(cache_keys.shape, BF16),
            pltpu.VMEM(cache_values.shape, BF16),
            pltpu.VMEM((rows, kv_width, KVH * pack), BF16),
            pltpu.VMEM((16, kv_width), BF16),
            pltpu.VMEM((16, kv_width), BF16),
            pltpu.VMEM((2, cache, KVH * pack), F32),
            pltpu.VMEM((rows, KVH, pack, HD), F32),
            pltpu.SemaphoreType.DMA((7,)),
            pltpu.SemaphoreType.DMA((rows, 2, 2)),
            pltpu.SemaphoreType.DMA((2, 4)),
        ],
        compiler_params=pltpu.CompilerParams(vmem_limit_bytes=32 * 2**20),
        cost_estimate=pl.CostEstimate(
            flops=4 * rows * steps * HQ * cache * HD,
            bytes_accessed=4 * rows * cache * kv_width,
            transcendentals=rows * steps * HQ * cache,
        ),
        name="attend",
    )(
        *in_hbm(
            kv_len,
            queries,
            new_keys,
            new_values,
            cache_keys,
            cache_values,
            store_down,
            store_up,
            *tables,
        )
    )


def swap(x, bits, parts):
    return lax.ppermute(x, "tensor", [(i, i ^ bits) for i in range(parts)])


def gather(block, parts):
    if parts != RING:
        whole = lax.all_gather(block, "tensor")
        return [whole[i] for i in range(parts)]
    core, y, near, far = 1, 2, 4, 8
    held = {0: block}
    held[far] = swap(block, far, parts)
    held[near] = swap(block, near, parts)
    held[y] = swap(block, y, parts)
    held[near | y] = swap(block, near | y, parts)
    held[far | y] = swap(held[far], y, parts)
    held[far | near | y] = swap(held[far], near | y, parts)
    held[far | near] = swap(held[far], near, parts)
    for slot in list(held):
        held[slot | core] = swap(held[slot], core, parts)
    return [held[slot] for slot in range(parts)]


def delta_kernel(at_slot, *refs):
    (*blocks, pick_ref, d_ref, u_ref, out_ref, rows_ref) = refs
    blocks = [blocks[at_slot.index(i)] for i in range(len(blocks))]
    parts, slots, cols = out_ref.shape
    each, width = blocks[0].shape
    cuts = 8
    deep = width // cuts
    low = jnp.zeros((parts * each, d_ref.shape[1]), F32)
    for i in range(cuts):
        at = slice(i * deep, (i + 1) * deep)
        piece = jnp.concatenate([b[:, at] for b in blocks], axis=0)
        rows_ref[:, at] = piece
        low = low + dot(piece, d_ref[at, :])
    chosen = dot(pick_ref[...], low.astype(BF16)).astype(BF16)
    for p in range(parts):
        out_ref[p] = dot_nt(chosen, u_ref[p * cols : (p + 1) * cols, :]).astype(BF16)


def deltas(blocks, pick, down, up):
    parts = len(blocks)
    each, width = blocks[0].shape
    slots = pick.shape[0]
    rank_w = down.shape[1]
    vmem = pl.BlockSpec(memory_space=pltpu.VMEM)
    at_slot = ORDER if parts == RING else [*range(parts)]
    return pl.pallas_call(
        functools.partial(delta_kernel, at_slot),
        out_shape=(
            jax.ShapeDtypeStruct((parts, slots, width // parts), BF16),
            jax.ShapeDtypeStruct((parts * each, width), BF16),
        ),
        in_specs=[vmem] * (3 + parts),
        out_specs=(vmem, vmem),
        compiler_params=pltpu.CompilerParams(vmem_limit_bytes=24 * 2**20),
        cost_estimate=pl.CostEstimate(
            flops=2 * (parts * each + slots) * width * rank_w,
            bytes_accessed=2 * width * (2 * parts * each + 2 * rank_w + slots),
            transcendentals=0,
        ),
        name="delta",
    )(*[blocks[i] for i in at_slot], pick, down, up)


def base_kernel(a_ref, w_ref, order_ref, out_ref):
    width = a_ref.shape[1]
    cuts = 8
    deep = width // cuts
    for i in range(cuts):
        at = slice(i * deep, (i + 1) * deep)
        part = dot(dot(order_ref[...], a_ref[:, at]).astype(BF16), w_ref[at, :])
        out_ref[...] = part if i == 0 else out_ref[...] + part


def base_part(gathered, out_weight, order):
    total, width = gathered.shape
    cols = out_weight.shape[1]
    vmem = pl.BlockSpec(memory_space=pltpu.VMEM)
    return pl.pallas_call(
        base_kernel,
        out_shape=jax.ShapeDtypeStruct((total, cols), F32),
        in_specs=[vmem] * 3,
        out_specs=vmem,
        compiler_params=pltpu.CompilerParams(vmem_limit_bytes=24 * 2**20),
        cost_estimate=pl.CostEstimate(
            flops=2 * total * width * (cols + total),
            bytes_accessed=2 * width * (total + cols) + 4 * total * cols,
            transcendentals=0,
        ),
        name="base",
    )(gathered, out_weight, order)


def join_kernel(base_ref, place_ref, delta_ref, out_ref):
    steps, requests, cols = out_ref.shape
    parts, slots, _ = delta_ref.shape
    delta = dot(place_ref[...], delta_ref[...].reshape(parts * slots, cols))
    result = (base_ref[...] + delta).astype(BF16)
    for t in range(steps):
        out_ref[t] = result[t * requests : (t + 1) * requests]


def join(base, place, delta, steps):
    total, cols = base.shape
    vmem = pl.BlockSpec(memory_space=pltpu.VMEM)
    return pl.pallas_call(
        join_kernel,
        out_shape=jax.ShapeDtypeStruct((steps, total // steps, cols), BF16),
        in_specs=[vmem] * 3,
        out_specs=vmem,
        compiler_params=pltpu.CompilerParams(vmem_limit_bytes=24 * 2**20),
        name="join",
    )(base, place, delta)


def per_device(
    queries,
    new_keys,
    new_values,
    cache_keys,
    cache_values,
    kv_len,
    adapter_rows,
    adapter_rank,
    adapter_owner,
    out_weight,
    store_down,
    store_up,
):
    parts = lax.axis_size("tensor")
    steps, rows, width = queries.shape
    tables = (adapter_rows, adapter_rank, adapter_owner)
    attended, down, up, pick, place, order = attend(
        queries,
        new_keys,
        new_values,
        cache_keys,
        cache_values,
        kv_len,
        store_down,
        store_up,
        tables,
        parts,
    )
    blocks = gather(attended, parts)
    send, gathered = deltas(blocks, pick, down, up)
    delta = lax.all_to_all(send, "tensor", split_axis=0, concat_axis=0, tiled=True)
    base = base_part(gathered, out_weight, order)
    return join(base, place, delta, steps)


def solution(mesh):
    in_specs = (
        P(None, ("groups", "tensor"), None),
        P(None, ("groups", "tensor"), None),
        P(None, ("groups", "tensor"), None),
        P(("groups", "tensor"), None, None),
        P(("groups", "tensor"), None, None),
        P(("groups", "tensor")),
        P("groups"),
        P(),
        P(),
        P(None, "tensor"),
        P("tensor", None, None),
        P("tensor", None, None),
    )
    out_specs = P(None, "groups", "tensor")
    return jax.shard_map(
        per_device, mesh=mesh, in_specs=in_specs, out_specs=out_specs, check_vma=False
    )
```

```python
import functools
import math

import jax
import jax.numpy as jnp
from jax import lax
from jax.experimental import pallas as pl
from jax.experimental.pallas import tpu as pltpu
from jax.sharding import PartitionSpec as P

HQ = 64
KVH = 8
HD = 128
GROUP = HQ // KVH
MOST = 8
RING = 16
CORE, Y, NEAR, FAR = 1, 2, 4, 8
FLIPS = [0, Y, NEAR, FAR, FAR | Y, FAR | NEAR | Y, FAR | NEAR, NEAR | Y]
FLIPS += [CORE | flip for flip in FLIPS]
HAND = [0, 6, 5, 11, 1, 7, 4, 10, 3, 9, 2, 8]
F32 = jnp.float32
BF16 = jnp.bfloat16
NT = (((1,), (1,)), ((), ()))


def in_hbm(*arrays):
    return [pltpu.with_memory_space_constraint(a, pltpu.HBM) for a in arrays]


def iota(shape, dim):
    return lax.broadcasted_iota(jnp.int32, shape, dim)


def one_hot(mask):
    return mask.astype(F32).astype(BF16)


def dot(a, b):
    return jnp.dot(a, b, preferred_element_type=F32)


def dot_nt(a, b):
    return lax.dot_general(a, b, NT, preferred_element_type=F32)


def sender(slot, me, parts):
    if parts != RING:
        return slot
    flips = jnp.zeros_like(slot)
    for i, flip in enumerate(FLIPS):
        flips = jnp.where(slot == i, flip, flips)
    return me ^ flips


def write_plan(rows, count_ref, rank_ref, owner_ref, pick_ref, place_ref, order_ref):
    me = lax.axis_index("tensor")
    slots, total = pick_ref.shape
    steps = slots // MOST
    each = steps * rows
    parts = total // each
    requests = parts * rows

    def adapter_of(block):
        first = jnp.zeros(block.shape, jnp.int32)
        amount = jnp.zeros(block.shape, jnp.int32)
        start = jnp.int32(0)
        for a in range(count_ref.shape[0]):
            owned = (owner_ref[a] <= block) & (block < owner_ref[a] + rank_ref[a])
            first = jnp.where(owned, start, first)
            amount = jnp.where(owned, count_ref[a], amount)
            start = start + count_ref[a]
        return first, amount

    def row_place(index):
        device = sender(index // each, me, parts)
        return device * rows + index % rows, (index % each) // rows

    row = iota((slots, 1), 0)
    nth = row % MOST
    first, amount = adapter_of(jnp.zeros_like(row) + me)
    request, step = row_place(iota((1, total), 1))
    pick = (request == first + nth) & (nth < amount) & (step == row // MOST)
    pick_ref[...] = one_hot(pick)

    request, step = row_place(iota((1, total), 1))
    order_ref[...] = one_hot(iota((total, total), 0) == step * requests + request)

    entry = iota((1, parts * slots), 1)
    nth = entry % MOST
    first, amount = adapter_of(entry // slots)
    goal = jnp.where(nth < amount, (entry % slots) // MOST * requests + first + nth, -1)
    place_ref[...] = one_hot(iota((total, parts * slots), 0) == goal)


def attend_kernel(
    len_hbm, q_hbm, nk_hbm, nv_hbm, k_hbm, v_hbm, d_hbm, u_hbm, count_hbm, rank_hbm, owner_hbm,
    out_ref, d_ref, u_ref, pick_ref, place_ref, order_ref,
    len_ref, count_ref, rank_ref, owner_ref, q_ref, nk_ref, nv_ref, k_ref, v_ref, turned_q, nks, nvs, raw, mixed,
    small_sems, sems, store_sems,
):
    steps, rows, width = q_ref.shape
    cache = k_ref.shape[1]
    both = steps * rows
    pack = steps * GROUP
    cuts = sems.shape[2]

    small = [
        pltpu.make_async_copy(src, dst, small_sems.at[i])
        for i, (src, dst) in enumerate(
            (
                (q_hbm, q_ref),
                (nk_hbm, nk_ref),
                (nv_hbm, nv_ref),
                (len_hbm, len_ref),
                (count_hbm, count_ref),
                (rank_hbm, rank_ref),
                (owner_hbm, owner_ref),
            )
        )
    ]
    pieces = [pl.ds(i * (cache // cuts), cache // cuts) for i in range(cuts)]
    keys, values = [
        [
            [
                pltpu.make_async_copy(src.at[r, at], dst.at[r, at], sems.at[r, j, i])
                for i, at in enumerate(pieces)
            ]
            for r in range(rows)
        ]
        for j, (src, dst) in enumerate(((k_hbm, k_ref), (v_hbm, v_ref)))
    ]
    deep = d_ref.shape[0] // store_sems.shape[1]
    store = [
        pltpu.make_async_copy(
            src.at[0, pl.ds(i * deep, deep)], dst.at[pl.ds(i * deep, deep)], store_sems.at[j, i]
        )
        for j, (src, dst) in enumerate(((d_hbm, d_ref), (u_hbm, u_ref)))
        for i in range(store_sems.shape[1])
    ]
    queue = [keys[0], values[0], keys[1]]
    for r in range(rows):
        queue += [values[r + 1]] if r + 1 < rows else [store]
        queue += [keys[r + 2]] if r + 2 < rows else []
    for copy in small + queue[0] + queue[1] + queue[2]:
        copy.start()
    for copy in small:
        copy.wait()
    for copy in queue[3] + queue[4]:
        copy.start()
    queue = queue[5:]

    flat = jnp.concatenate([q_ref[t].astype(F32) for t in range(steps)], axis=0)
    heads = []
    for k in range(KVH):
        group = jnp.stack(
            [flat[:, (k * GROUP + g) * HD : (k * GROUP + g + 1) * HD] for g in range(GROUP)]
        )
        heads.append(jnp.swapaxes(group, 0, 1))
    column = iota((HD, KVH * pack), 1)
    for r in range(rows):
        mine = jnp.concatenate(
            [heads[k][t * rows + r] for k in range(KVH) for t in range(steps)], axis=0
        )
        mine = jnp.transpose(mine)
        for k in range(KVH):
            turned_q[r, k * HD : (k + 1) * HD, :] = jnp.where(
                column // pack == k, mine, 0.0
            ).astype(BF16)
    for src, dst in ((nk_ref, nks), (nv_ref, nvs)):
        fresh = [src[t].astype(F32) for t in range(steps)]
        fresh.append(jnp.zeros((16 - both, src.shape[2]), F32))
        dst[...] = jnp.concatenate(fresh, axis=0).astype(BF16)

    write_plan(rows, count_ref, rank_ref, owner_ref, pick_ref, place_ref, order_ref)

    rate = HD ** (-0.5) * math.log2(math.e)
    pairs = [
        (slice(k * pack, (k + 2) * pack), slice(k * HD, (k + 2) * HD)) for k in range(0, KVH, 2)
    ]
    for turn in range(rows + 1):
        if turn < rows:
            for copy in keys[turn]:
                copy.wait()
        if turn > 0:
            for copy in values[turn - 1]:
                copy.wait()
        for copies in queue[2 * turn : 2 * turn + 2]:
            for copy in copies:
                copy.start()
        if turn < rows:
            raw[turn % 2] = dot(k_ref[turn], turned_q[turn])
        if turn == 0:
            continue
        r = turn - 1
        fresh = dot(nks[...], turned_q[r])
        slot = iota(fresh.shape, 0)
        step = (iota(fresh.shape, 1) // GROUP) % steps
        seen = (slot < both) & (slot % rows == r) & (slot // rows <= step)
        fresh = jnp.where(seen, fresh, -jnp.inf)
        older = raw[r % 2]
        older = jnp.where(iota(older.shape, 0) < len_ref[r], older, -jnp.inf)
        top = jnp.maximum(
            jnp.max(older, axis=0, keepdims=True), jnp.max(fresh, axis=0, keepdims=True)
        )
        e_older = jnp.exp2((older - top) * rate)
        e_fresh = jnp.exp2((fresh - top) * rate)
        total = jnp.sum(e_older, axis=0, keepdims=True) + jnp.sum(e_fresh, axis=0, keepdims=True)
        inverse = 1.0 / total
        p_older = jnp.transpose((e_older * inverse).astype(BF16))
        p_fresh = jnp.transpose((e_fresh * inverse).astype(BF16))
        for k, (own, cols_k) in zip(range(0, KVH, 2), pairs):
            pair = dot(p_older[own], v_ref[r, :, cols_k]) + dot(p_fresh[own], nvs[:, cols_k])
            mixed[r, k] = pair[:pack, :HD]
            mixed[r, k + 1] = pair[pack:, HD:]

    for k in range(KVH):
        turned = jnp.stack(
            [
                mixed[r, k, t * GROUP : (t + 1) * GROUP, :]
                for t in range(steps)
                for r in range(rows)
            ]
        )
        heads = jnp.swapaxes(turned, 0, 1)
        for g in range(GROUP):
            at = (k * GROUP + g) * HD
            out_ref[:, at : at + HD] = heads[g].astype(BF16)
    for copy in store:
        copy.wait()


def attend(
    queries,
    new_keys,
    new_values,
    cache_keys,
    cache_values,
    kv_len,
    store_down,
    store_up,
    tables,
    parts,
):
    steps, rows, width = queries.shape
    cache, kv_width = cache_keys.shape[1:]
    pack = steps * GROUP
    rank_w = store_down.shape[2]
    total = parts * steps * rows
    slots = steps * MOST
    shapes = [(steps * rows, width), (width, rank_w), (width, rank_w)]
    shapes += [(slots, total), (total, parts * slots), (total, total)]
    return pl.pallas_call(
        attend_kernel,
        out_shape=[jax.ShapeDtypeStruct(shape, BF16) for shape in shapes],
        in_specs=[pl.BlockSpec(memory_space=pl.ANY)] * 11,
        out_specs=[pl.BlockSpec(memory_space=pltpu.VMEM)] * len(shapes),
        scratch_shapes=[
            pltpu.SMEM(kv_len.shape, jnp.int32),
            *[pltpu.SMEM(table.shape, jnp.int32) for table in tables],
            pltpu.VMEM(queries.shape, BF16),
            pltpu.VMEM(new_keys.shape, BF16),
            pltpu.VMEM(new_values.shape, BF16),
            pltpu.VMEM(cache_keys.shape, BF16),
            pltpu.VMEM(cache_values.shape, BF16),
            pltpu.VMEM((rows, kv_width, KVH * pack), BF16),
            pltpu.VMEM((16, kv_width), BF16),
            pltpu.VMEM((16, kv_width), BF16),
            pltpu.VMEM((2, cache, KVH * pack), F32),
            pltpu.VMEM((rows, KVH, pack, HD), F32),
            pltpu.SemaphoreType.DMA((7,)),
            pltpu.SemaphoreType.DMA((rows, 2, 2)),
            pltpu.SemaphoreType.DMA((2, 4)),
        ],
        compiler_params=pltpu.CompilerParams(vmem_limit_bytes=32 * 2**20),
        cost_estimate=pl.CostEstimate(
            flops=4 * rows * steps * HQ * cache * HD,
            bytes_accessed=4 * rows * cache * kv_width,
            transcendentals=rows * steps * HQ * cache,
        ),
        name="attend",
    )(
        *in_hbm(
            kv_len,
            queries,
            new_keys,
            new_values,
            cache_keys,
            cache_values,
            store_down,
            store_up,
            *tables,
        )
    )


def swap(x, bits, parts):
    return lax.ppermute(x, "tensor", [(i, i ^ bits) for i in range(parts)])


def pack_kernel(own_ref, y_ref, near_ref, out_ref, mixed_ref):
    for i, src in enumerate((own_ref, y_ref, near_ref)):
        out_ref[i] = src[...]
    core = lax.axis_index("tensor") % 2

    @pl.when(core == 0)
    def _():
        mixed_ref[...] = near_ref[...]

    @pl.when(core == 1)
    def _():
        mixed_ref[...] = y_ref[...]


def pack(own, y, near):
    vmem = pl.BlockSpec(memory_space=pltpu.VMEM)
    return pl.pallas_call(
        pack_kernel,
        out_shape=(
            jax.ShapeDtypeStruct((3, *own.shape), own.dtype),
            jax.ShapeDtypeStruct(own.shape, own.dtype),
        ),
        in_specs=[vmem] * 3,
        out_specs=(vmem, vmem),
        compiler_params=pltpu.CompilerParams(vmem_limit_bytes=4 * 2**20),
        cost_estimate=pl.CostEstimate(flops=0, bytes_accessed=14 * own.size, transcendentals=0),
        name="pack",
    )(own, y, near)


def gather(block, parts):
    if parts != RING:
        return [lax.all_gather(block, "tensor")]
    far = swap(block, FAR, parts)
    near = swap(block, NEAR, parts)
    y = swap(block, Y, parts)
    packed, mixed = pack(block, y, near)
    far, packed = lax.optimization_barrier((far, packed))
    across = swap(far, CORE, parts)
    mixed, across = lax.optimization_barrier((mixed, across))
    pairs = [(i, i ^ (Y if i % 2 == 0 else NEAR)) for i in range(parts)]
    blocks = [
        packed,
        far,
        swap(far, Y, parts),
        swap(far, NEAR | Y, parts),
        swap(far, NEAR, parts),
        lax.ppermute(mixed, "tensor", pairs),
    ]
    swapped = [across if x is far else swap(x, CORE, parts) for x in blocks]
    return blocks + swapped


def delta_kernel(hand, *refs):
    (*blocks, pick_ref, d_ref, u_ref, out_ref, rows_ref) = refs
    blocks = [blocks[hand.index(i)] for i in range(len(blocks))]
    parts, slots, cols = out_ref.shape
    each, width = blocks[0].shape[-2:]
    views = []
    for b in blocks:
        views += [b.at[i] for i in range(b.shape[0])] if len(b.shape) == 3 else [b]
    cuts = 8
    deep = width // cuts
    low = jnp.zeros((parts * each, d_ref.shape[1]), F32)
    for i in range(cuts):
        at = slice(i * deep, (i + 1) * deep)
        piece = jnp.concatenate([view[:, at] for view in views], axis=0)
        rows_ref[:, at] = piece
        low = low + dot(piece, d_ref[at, :])
    chosen = dot(pick_ref[...], low.astype(BF16)).astype(BF16)
    for p in range(parts):
        out_ref[p] = dot_nt(chosen, u_ref[p * cols : (p + 1) * cols, :]).astype(BF16)


def deltas(blocks, pick, down, up, parts):
    each, width = blocks[0].shape[-2:]
    slots = pick.shape[0]
    rank_w = down.shape[1]
    vmem = pl.BlockSpec(memory_space=pltpu.VMEM)
    hand = HAND if len(blocks) > 1 else [0]
    return pl.pallas_call(
        functools.partial(delta_kernel, hand),
        out_shape=(
            jax.ShapeDtypeStruct((parts, slots, width // parts), BF16),
            jax.ShapeDtypeStruct((parts * each, width), BF16),
        ),
        in_specs=[vmem] * (3 + len(blocks)),
        out_specs=(vmem, vmem),
        compiler_params=pltpu.CompilerParams(vmem_limit_bytes=24 * 2**20),
        cost_estimate=pl.CostEstimate(
            flops=2 * (parts * each + slots) * width * rank_w,
            bytes_accessed=2 * width * (2 * parts * each + 2 * rank_w + slots),
            transcendentals=0,
        ),
        name="delta",
    )(*[blocks[i] for i in hand], pick, down, up)


def base_kernel(a_ref, w_ref, order_ref, out_ref):
    width = a_ref.shape[1]
    cuts = 8
    deep = width // cuts
    for i in range(cuts):
        at = slice(i * deep, (i + 1) * deep)
        part = dot(dot(order_ref[...], a_ref[:, at]).astype(BF16), w_ref[at, :])
        out_ref[...] = part if i == 0 else out_ref[...] + part


def base_part(gathered, out_weight, order):
    total, width = gathered.shape
    cols = out_weight.shape[1]
    vmem = pl.BlockSpec(memory_space=pltpu.VMEM)
    return pl.pallas_call(
        base_kernel,
        out_shape=jax.ShapeDtypeStruct((total, cols), F32),
        in_specs=[vmem] * 3,
        out_specs=vmem,
        compiler_params=pltpu.CompilerParams(vmem_limit_bytes=24 * 2**20),
        cost_estimate=pl.CostEstimate(
            flops=2 * total * width * (cols + total),
            bytes_accessed=2 * width * (total + cols) + 4 * total * cols,
            transcendentals=0,
        ),
        name="base",
    )(gathered, out_weight, order)


def join_kernel(base_ref, place_ref, delta_ref, out_ref):
    steps, requests, cols = out_ref.shape
    parts, slots, _ = delta_ref.shape
    delta = dot(place_ref[...], delta_ref[...].reshape(parts * slots, cols))
    result = (base_ref[...] + delta).astype(BF16)
    for t in range(steps):
        out_ref[t] = result[t * requests : (t + 1) * requests]


def join(base, place, delta, steps):
    total, cols = base.shape
    vmem = pl.BlockSpec(memory_space=pltpu.VMEM)
    return pl.pallas_call(
        join_kernel,
        out_shape=jax.ShapeDtypeStruct((steps, total // steps, cols), BF16),
        in_specs=[vmem] * 3,
        out_specs=vmem,
        compiler_params=pltpu.CompilerParams(vmem_limit_bytes=24 * 2**20),
        name="join",
    )(base, place, delta)


def per_device(
    queries,
    new_keys,
    new_values,
    cache_keys,
    cache_values,
    kv_len,
    adapter_rows,
    adapter_rank,
    adapter_owner,
    out_weight,
    store_down,
    store_up,
):
    parts = lax.axis_size("tensor")
    steps, rows, width = queries.shape
    tables = (adapter_rows, adapter_rank, adapter_owner)
    attended, down, up, pick, place, order = attend(
        queries,
        new_keys,
        new_values,
        cache_keys,
        cache_values,
        kv_len,
        store_down,
        store_up,
        tables,
        parts,
    )
    blocks = gather(attended, parts)
    send, gathered = deltas(blocks, pick, down, up, parts)
    delta = lax.all_to_all(send, "tensor", split_axis=0, concat_axis=0, tiled=True)
    base = base_part(gathered, out_weight, order)
    return join(base, place, delta, steps)


def solution(mesh):
    in_specs = (
        P(None, ("groups", "tensor"), None),
        P(None, ("groups", "tensor"), None),
        P(None, ("groups", "tensor"), None),
        P(("groups", "tensor"), None, None),
        P(("groups", "tensor"), None, None),
        P(("groups", "tensor")),
        P("groups"),
        P(),
        P(),
        P(None, "tensor"),
        P("tensor", None, None),
        P("tensor", None, None),
    )
    out_specs = P(None, "groups", "tensor")
    return jax.shard_map(
        per_device, mesh=mesh, in_specs=in_specs, out_specs=out_specs, check_vma=False
    )
```

```python
import functools
import math

import jax
import jax.numpy as jnp
from jax import lax
from jax.experimental import pallas as pl
from jax.experimental.pallas import tpu as pltpu
from jax.sharding import PartitionSpec as P

HQ = 64
KVH = 8
HD = 128
GROUP = HQ // KVH
MOST = 8
RING = 16
ORDER = [0, 1, 2, 3, 4, 5, 6, 7, 8, 9, 10, 11, 12, 13, 14, 15]
F32 = jnp.float32
BF16 = jnp.bfloat16
NT = (((1,), (1,)), ((), ()))


def in_hbm(*arrays):
    return [pltpu.with_memory_space_constraint(a, pltpu.HBM) for a in arrays]


def iota(shape, dim):
    return lax.broadcasted_iota(jnp.int32, shape, dim)


def one_hot(mask):
    return mask.astype(F32).astype(BF16)


def dot(a, b):
    return jnp.dot(a, b, preferred_element_type=F32)


def dot_nt(a, b):
    return lax.dot_general(a, b, NT, preferred_element_type=F32)


def sender(slot, me, parts):
    return me ^ slot if parts == RING else slot


def write_plan(rows, count_ref, rank_ref, owner_ref, pick_ref, place_ref, order_ref):
    me = lax.axis_index("tensor")
    slots, total = pick_ref.shape
    steps = slots // MOST
    each = steps * rows
    parts = total // each
    requests = parts * rows

    def adapter_of(block):
        first = jnp.zeros(block.shape, jnp.int32)
        amount = jnp.zeros(block.shape, jnp.int32)
        start = jnp.int32(0)
        for a in range(count_ref.shape[0]):
            owned = (owner_ref[a] <= block) & (block < owner_ref[a] + rank_ref[a])
            first = jnp.where(owned, start, first)
            amount = jnp.where(owned, count_ref[a], amount)
            start = start + count_ref[a]
        return first, amount

    def row_place(index):
        device = sender(index // each, me, parts)
        return device * rows + index % rows, (index % each) // rows

    row = iota((slots, 1), 0)
    nth = row % MOST
    first, amount = adapter_of(jnp.zeros_like(row) + me)
    request, step = row_place(iota((1, total), 1))
    pick = (request == first + nth) & (nth < amount) & (step == row // MOST)
    pick_ref[...] = one_hot(pick)

    request, step = row_place(iota((1, total), 1))
    order_ref[...] = one_hot(iota((total, total), 0) == step * requests + request)

    entry = iota((1, parts * slots), 1)
    nth = entry % MOST
    first, amount = adapter_of(entry // slots)
    goal = jnp.where(nth < amount, (entry % slots) // MOST * requests + first + nth, -1)
    place_ref[...] = one_hot(iota((total, parts * slots), 0) == goal)


def attend_kernel(
    len_hbm, q_hbm, nk_hbm, nv_hbm, k_hbm, v_hbm, d_hbm, u_hbm, count_hbm, rank_hbm, owner_hbm,
    out_ref, d_ref, u_ref, pick_ref, place_ref, order_ref,
    len_ref, count_ref, rank_ref, owner_ref, q_ref, nk_ref, nv_ref, k_ref, v_ref, turned_q, nks, nvs, raw, mixed,
    small_sems, sems, store_sems,
):
    steps, rows, width = q_ref.shape
    cache = k_ref.shape[1]
    both = steps * rows
    pack = steps * GROUP
    cuts = sems.shape[2]

    small = [
        pltpu.make_async_copy(src, dst, small_sems.at[i])
        for i, (src, dst) in enumerate(
            (
                (q_hbm, q_ref),
                (nk_hbm, nk_ref),
                (nv_hbm, nv_ref),
                (len_hbm, len_ref),
                (count_hbm, count_ref),
                (rank_hbm, rank_ref),
                (owner_hbm, owner_ref),
            )
        )
    ]
    pieces = [pl.ds(i * (cache // cuts), cache // cuts) for i in range(cuts)]
    keys, values = [
        [
            [
                pltpu.make_async_copy(src.at[r, at], dst.at[r, at], sems.at[r, j, i])
                for i, at in enumerate(pieces)
            ]
            for r in range(rows)
        ]
        for j, (src, dst) in enumerate(((k_hbm, k_ref), (v_hbm, v_ref)))
    ]
    deep = d_ref.shape[0] // store_sems.shape[1]
    store = [
        pltpu.make_async_copy(
            src.at[0, pl.ds(i * deep, deep)], dst.at[pl.ds(i * deep, deep)], store_sems.at[j, i]
        )
        for j, (src, dst) in enumerate(((d_hbm, d_ref), (u_hbm, u_ref)))
        for i in range(store_sems.shape[1])
    ]
    queue = [keys[0], values[0], keys[1]]
    for r in range(rows):
        queue += [values[r + 1]] if r + 1 < rows else [store]
        queue += [keys[r + 2]] if r + 2 < rows else []
    for copy in small + queue[0] + queue[1] + queue[2]:
        copy.start()
    for copy in small:
        copy.wait()
    for copy in queue[3] + queue[4]:
        copy.start()
    queue = queue[5:]

    flat = jnp.concatenate([q_ref[t].astype(F32) for t in range(steps)], axis=0)
    heads = []
    for k in range(KVH):
        group = jnp.stack(
            [flat[:, (k * GROUP + g) * HD : (k * GROUP + g + 1) * HD] for g in range(GROUP)]
        )
        heads.append(jnp.swapaxes(group, 0, 1))
    column = iota((HD, KVH * pack), 1)
    for r in range(rows):
        mine = jnp.concatenate(
            [heads[k][t * rows + r] for k in range(KVH) for t in range(steps)], axis=0
        )
        mine = jnp.transpose(mine)
        for k in range(KVH):
            turned_q[r, k * HD : (k + 1) * HD, :] = jnp.where(
                column // pack == k, mine, 0.0
            ).astype(BF16)
    for src, dst in ((nk_ref, nks), (nv_ref, nvs)):
        fresh = [src[t].astype(F32) for t in range(steps)]
        fresh.append(jnp.zeros((16 - both, src.shape[2]), F32))
        dst[...] = jnp.concatenate(fresh, axis=0).astype(BF16)

    write_plan(rows, count_ref, rank_ref, owner_ref, pick_ref, place_ref, order_ref)

    rate = HD ** (-0.5) * math.log2(math.e)
    pairs = [
        (slice(k * pack, (k + 2) * pack), slice(k * HD, (k + 2) * HD)) for k in range(0, KVH, 2)
    ]
    for turn in range(rows + 1):
        if turn < rows:
            for copy in keys[turn]:
                copy.wait()
        if turn > 0:
            for copy in values[turn - 1]:
                copy.wait()
        for copies in queue[2 * turn : 2 * turn + 2]:
            for copy in copies:
                copy.start()
        if turn < rows:
            raw[turn % 2] = dot(k_ref[turn], turned_q[turn])
        if turn == 0:
            continue
        r = turn - 1
        fresh = dot(nks[...], turned_q[r])
        slot = iota(fresh.shape, 0)
        step = (iota(fresh.shape, 1) // GROUP) % steps
        seen = (slot < both) & (slot % rows == r) & (slot // rows <= step)
        fresh = jnp.where(seen, fresh, -jnp.inf)
        older = raw[r % 2]
        older = jnp.where(iota(older.shape, 0) < len_ref[r], older, -jnp.inf)
        top = jnp.maximum(
            jnp.max(older, axis=0, keepdims=True), jnp.max(fresh, axis=0, keepdims=True)
        )
        e_older = jnp.exp2((older - top) * rate)
        e_fresh = jnp.exp2((fresh - top) * rate)
        total = jnp.sum(e_older, axis=0, keepdims=True) + jnp.sum(e_fresh, axis=0, keepdims=True)
        inverse = 1.0 / total
        p_older = jnp.transpose((e_older * inverse).astype(BF16))
        p_fresh = jnp.transpose((e_fresh * inverse).astype(BF16))
        for k, (own, cols_k) in zip(range(0, KVH, 2), pairs):
            pair = dot(p_older[own], v_ref[r, :, cols_k]) + dot(p_fresh[own], nvs[:, cols_k])
            mixed[r, k] = pair[:pack, :HD]
            mixed[r, k + 1] = pair[pack:, HD:]

    for k in range(KVH):
        turned = jnp.stack(
            [
                mixed[r, k, t * GROUP : (t + 1) * GROUP, :]
                for t in range(steps)
                for r in range(rows)
            ]
        )
        heads = jnp.swapaxes(turned, 0, 1)
        for g in range(GROUP):
            at = (k * GROUP + g) * HD
            out_ref[:, at : at + HD] = heads[g].astype(BF16)
    for copy in store:
        copy.wait()


def attend(
    queries,
    new_keys,
    new_values,
    cache_keys,
    cache_values,
    kv_len,
    store_down,
    store_up,
    tables,
    parts,
):
    steps, rows, width = queries.shape
    cache, kv_width = cache_keys.shape[1:]
    pack = steps * GROUP
    rank_w = store_down.shape[2]
    total = parts * steps * rows
    slots = steps * MOST
    shapes = [(steps * rows, width), (width, rank_w), (width, rank_w)]
    shapes += [(slots, total), (total, parts * slots), (total, total)]
    return pl.pallas_call(
        attend_kernel,
        out_shape=[jax.ShapeDtypeStruct(shape, BF16) for shape in shapes],
        in_specs=[pl.BlockSpec(memory_space=pl.ANY)] * 11,
        out_specs=[pl.BlockSpec(memory_space=pltpu.VMEM)] * len(shapes),
        scratch_shapes=[
            pltpu.SMEM(kv_len.shape, jnp.int32),
            *[pltpu.SMEM(table.shape, jnp.int32) for table in tables],
            pltpu.VMEM(queries.shape, BF16),
            pltpu.VMEM(new_keys.shape, BF16),
            pltpu.VMEM(new_values.shape, BF16),
            pltpu.VMEM(cache_keys.shape, BF16),
            pltpu.VMEM(cache_values.shape, BF16),
            pltpu.VMEM((rows, kv_width, KVH * pack), BF16),
            pltpu.VMEM((16, kv_width), BF16),
            pltpu.VMEM((16, kv_width), BF16),
            pltpu.VMEM((2, cache, KVH * pack), F32),
            pltpu.VMEM((rows, KVH, pack, HD), F32),
            pltpu.SemaphoreType.DMA((7,)),
            pltpu.SemaphoreType.DMA((rows, 2, 2)),
            pltpu.SemaphoreType.DMA((2, 4)),
        ],
        compiler_params=pltpu.CompilerParams(vmem_limit_bytes=32 * 2**20),
        cost_estimate=pl.CostEstimate(
            flops=4 * rows * steps * HQ * cache * HD,
            bytes_accessed=4 * rows * cache * kv_width,
            transcendentals=rows * steps * HQ * cache,
        ),
        name="attend",
    )(
        *in_hbm(
            kv_len,
            queries,
            new_keys,
            new_values,
            cache_keys,
            cache_values,
            store_down,
            store_up,
            *tables,
        )
    )


def swap(x, bits, parts):
    return lax.ppermute(x, "tensor", [(i, i ^ bits) for i in range(parts)])


def gather(block, parts):
    if parts != RING:
        whole = lax.all_gather(block, "tensor")
        return [whole[i] for i in range(parts)]
    core, y, near, far = 1, 2, 4, 8
    held = {0: block}
    held[far] = swap(block, far, parts)
    held[near] = swap(block, near, parts)
    held[y] = swap(block, y, parts)
    held[near | y] = swap(block, near | y, parts)
    held[far | y] = swap(held[far], y, parts)
    held[far | near | y] = swap(held[far], near | y, parts)
    held[far | near] = swap(held[far], near, parts)
    for slot in list(held):
        held[slot | core] = swap(held[slot], core, parts)
    return [held[slot] for slot in range(parts)]


def delta_kernel(at_slot, *refs):
    (*blocks, pick_ref, d_ref, u_ref, out_ref, rows_ref) = refs
    blocks = [blocks[at_slot.index(i)] for i in range(len(blocks))]
    parts, slots, cols = out_ref.shape
    each, width = blocks[0].shape
    cuts = 8
    deep = width // cuts
    low = jnp.zeros((parts * each, d_ref.shape[1]), F32)
    for i in range(cuts):
        at = slice(i * deep, (i + 1) * deep)
        piece = jnp.concatenate([b[:, at] for b in blocks], axis=0)
        rows_ref[:, at] = piece
        low = low + dot(piece, d_ref[at, :])
    chosen = dot(pick_ref[...], low.astype(BF16)).astype(BF16)
    for p in range(parts):
        out_ref[p] = dot_nt(chosen, u_ref[p * cols : (p + 1) * cols, :]).astype(BF16)


def deltas(blocks, pick, down, up):
    parts = len(blocks)
    each, width = blocks[0].shape
    slots = pick.shape[0]
    rank_w = down.shape[1]
    vmem = pl.BlockSpec(memory_space=pltpu.VMEM)
    at_slot = ORDER if parts == RING else [*range(parts)]
    return pl.pallas_call(
        functools.partial(delta_kernel, at_slot),
        out_shape=(
            jax.ShapeDtypeStruct((parts, slots, width // parts), BF16),
            jax.ShapeDtypeStruct((parts * each, width), BF16),
        ),
        in_specs=[vmem] * (3 + parts),
        out_specs=(vmem, vmem),
        compiler_params=pltpu.CompilerParams(vmem_limit_bytes=24 * 2**20),
        cost_estimate=pl.CostEstimate(
            flops=2 * (parts * each + slots) * width * rank_w,
            bytes_accessed=2 * width * (2 * parts * each + 2 * rank_w + slots),
            transcendentals=0,
        ),
        name="delta",
    )(*[blocks[i] for i in at_slot], pick, down, up)


def base_kernel(a_ref, w_ref, order_ref, out_ref):
    width = a_ref.shape[1]
    cuts = 8
    deep = width // cuts
    for i in range(cuts):
        at = slice(i * deep, (i + 1) * deep)
        part = dot(dot(order_ref[...], a_ref[:, at]).astype(BF16), w_ref[at, :])
        out_ref[...] = part if i == 0 else out_ref[...] + part


def base_part(gathered, out_weight, order):
    total, width = gathered.shape
    cols = out_weight.shape[1]
    vmem = pl.BlockSpec(memory_space=pltpu.VMEM)
    return pl.pallas_call(
        base_kernel,
        out_shape=jax.ShapeDtypeStruct((total, cols), F32),
        in_specs=[vmem] * 3,
        out_specs=vmem,
        compiler_params=pltpu.CompilerParams(vmem_limit_bytes=24 * 2**20),
        cost_estimate=pl.CostEstimate(
            flops=2 * total * width * (cols + total),
            bytes_accessed=2 * width * (total + cols) + 4 * total * cols,
            transcendentals=0,
        ),
        name="base",
    )(gathered, out_weight, order)


def join_kernel(base_ref, place_ref, delta_ref, out_ref):
    steps, requests, cols = out_ref.shape
    parts, slots, _ = delta_ref.shape
    delta = dot(place_ref[...], delta_ref[...].reshape(parts * slots, cols))
    result = (base_ref[...] + delta).astype(BF16)
    for t in range(steps):
        out_ref[t] = result[t * requests : (t + 1) * requests]


def join(base, place, delta, steps):
    total, cols = base.shape
    vmem = pl.BlockSpec(memory_space=pltpu.VMEM)
    return pl.pallas_call(
        join_kernel,
        out_shape=jax.ShapeDtypeStruct((steps, total // steps, cols), BF16),
        in_specs=[vmem] * 3,
        out_specs=vmem,
        compiler_params=pltpu.CompilerParams(vmem_limit_bytes=24 * 2**20),
        name="join",
    )(base, place, delta)


def per_device(
    queries,
    new_keys,
    new_values,
    cache_keys,
    cache_values,
    kv_len,
    adapter_rows,
    adapter_rank,
    adapter_owner,
    out_weight,
    store_down,
    store_up,
):
    parts = lax.axis_size("tensor")
    steps, rows, width = queries.shape
    tables = (adapter_rows, adapter_rank, adapter_owner)
    attended, down, up, pick, place, order = attend(
        queries,
        new_keys,
        new_values,
        cache_keys,
        cache_values,
        kv_len,
        store_down,
        store_up,
        tables,
        parts,
    )
    blocks = gather(attended, parts)
    send, gathered = deltas(blocks, pick, down, up)
    delta = lax.all_to_all(send, "tensor", split_axis=0, concat_axis=0, tiled=True)
    base = base_part(gathered, out_weight, order)
    return join(base, place, delta, steps)


def solution(mesh):
    in_specs = (
        P(None, ("groups", "tensor"), None),
        P(None, ("groups", "tensor"), None),
        P(None, ("groups", "tensor"), None),
        P(("groups", "tensor"), None, None),
        P(("groups", "tensor"), None, None),
        P(("groups", "tensor")),
        P("groups"),
        P(),
        P(),
        P(None, "tensor"),
        P("tensor", None, None),
        P("tensor", None, None),
    )
    out_specs = P(None, "groups", "tensor")
    return jax.shard_map(
        per_device, mesh=mesh, in_specs=in_specs, out_specs=out_specs, check_vma=False
    )
```

```python
import functools
import math

import jax
import jax.numpy as jnp
from jax import lax
from jax.experimental import pallas as pl
from jax.experimental.pallas import tpu as pltpu
from jax.sharding import PartitionSpec as P

HQ = 64
KVH = 8
HD = 128
GROUP = HQ // KVH
MOST = 8
RING = 16
ORDER = [0, 1, 2, 3, 4, 5, 6, 7, 8, 9, 10, 11, 12, 13, 14, 15]
F32 = jnp.float32
BF16 = jnp.bfloat16
NT = (((1,), (1,)), ((), ()))


def in_hbm(*arrays):
    return [pltpu.with_memory_space_constraint(a, pltpu.HBM) for a in arrays]


def iota(shape, dim):
    return lax.broadcasted_iota(jnp.int32, shape, dim)


def one_hot(mask):
    return mask.astype(F32).astype(BF16)


def dot(a, b):
    return jnp.dot(a, b, preferred_element_type=F32)


def dot_nt(a, b):
    return lax.dot_general(a, b, NT, preferred_element_type=F32)


def sender(slot, me, parts):
    return me ^ slot if parts == RING else slot


def write_plan(rows, count_ref, rank_ref, owner_ref, pick_ref, place_ref, order_ref):
    me = lax.axis_index("tensor")
    slots, total = pick_ref.shape
    steps = slots // MOST
    each = steps * rows
    parts = total // each
    requests = parts * rows

    def adapter_of(block):
        first = jnp.zeros(block.shape, jnp.int32)
        amount = jnp.zeros(block.shape, jnp.int32)
        start = jnp.int32(0)
        for a in range(count_ref.shape[0]):
            owned = (owner_ref[a] <= block) & (block < owner_ref[a] + rank_ref[a])
            first = jnp.where(owned, start, first)
            amount = jnp.where(owned, count_ref[a], amount)
            start = start + count_ref[a]
        return first, amount

    def row_place(index):
        device = sender(index // each, me, parts)
        return device * rows + index % rows, (index % each) // rows

    row = iota((slots, 1), 0)
    nth = row % MOST
    first, amount = adapter_of(jnp.zeros_like(row) + me)
    request, step = row_place(iota((1, total), 1))
    pick = (request == first + nth) & (nth < amount) & (step == row // MOST)
    pick_ref[...] = one_hot(pick)

    request, step = row_place(iota((1, total), 1))
    order_ref[...] = one_hot(iota((total, total), 0) == step * requests + request)

    entry = iota((1, parts * slots), 1)
    nth = entry % MOST
    first, amount = adapter_of(entry // slots)
    goal = jnp.where(nth < amount, (entry % slots) // MOST * requests + first + nth, -1)
    place_ref[...] = one_hot(iota((total, parts * slots), 0) == goal)


def attend_kernel(
    len_hbm, q_hbm, nk_hbm, nv_hbm, k_hbm, v_hbm, d_hbm, u_hbm, count_hbm, rank_hbm, owner_hbm,
    out_ref, d_ref, u_ref, pick_ref, place_ref, order_ref,
    len_ref, count_ref, rank_ref, owner_ref, q_ref, nk_ref, nv_ref, k_ref, v_ref, turned_q, nks, nvs, raw, mixed,
    small_sems, sems, store_sems,
):
    steps, rows, width = q_ref.shape
    cache = k_ref.shape[1]
    both = steps * rows
    pack = steps * GROUP
    cuts = sems.shape[2]

    small = [
        pltpu.make_async_copy(src, dst, small_sems.at[i])
        for i, (src, dst) in enumerate(
            (
                (q_hbm, q_ref),
                (nk_hbm, nk_ref),
                (nv_hbm, nv_ref),
                (len_hbm, len_ref),
                (count_hbm, count_ref),
                (rank_hbm, rank_ref),
                (owner_hbm, owner_ref),
            )
        )
    ]
    pieces = [pl.ds(i * (cache // cuts), cache // cuts) for i in range(cuts)]
    keys, values = [
        [
            [
                pltpu.make_async_copy(src.at[r, at], dst.at[r, at], sems.at[r, j, i])
                for i, at in enumerate(pieces)
            ]
            for r in range(rows)
        ]
        for j, (src, dst) in enumerate(((k_hbm, k_ref), (v_hbm, v_ref)))
    ]
    deep = d_ref.shape[0] // store_sems.shape[1]
    store = [
        pltpu.make_async_copy(
            src.at[0, pl.ds(i * deep, deep)], dst.at[pl.ds(i * deep, deep)], store_sems.at[j, i]
        )
        for j, (src, dst) in enumerate(((d_hbm, d_ref), (u_hbm, u_ref)))
        for i in range(store_sems.shape[1])
    ]
    queue = [keys[0], values[0], keys[1]]
    for r in range(rows):
        queue += [values[r + 1]] if r + 1 < rows else [store]
        queue += [keys[r + 2]] if r + 2 < rows else []
    for copy in small + queue[0] + queue[1] + queue[2]:
        copy.start()
    for copy in small:
        copy.wait()
    for copy in queue[3] + queue[4]:
        copy.start()
    queue = queue[5:]

    flat = jnp.concatenate([q_ref[t].astype(F32) for t in range(steps)], axis=0)
    heads = []
    for k in range(KVH):
        group = jnp.stack(
            [flat[:, (k * GROUP + g) * HD : (k * GROUP + g + 1) * HD] for g in range(GROUP)]
        )
        heads.append(jnp.swapaxes(group, 0, 1))
    column = iota((HD, KVH * pack), 1)
    for r in range(rows):
        mine = jnp.concatenate(
            [heads[k][t * rows + r] for k in range(KVH) for t in range(steps)], axis=0
        )
        mine = jnp.transpose(mine)
        for k in range(KVH):
            turned_q[r, k * HD : (k + 1) * HD, :] = jnp.where(
                column // pack == k, mine, 0.0
            ).astype(BF16)
    for src, dst in ((nk_ref, nks), (nv_ref, nvs)):
        fresh = [src[t].astype(F32) for t in range(steps)]
        fresh.append(jnp.zeros((16 - both, src.shape[2]), F32))
        dst[...] = jnp.concatenate(fresh, axis=0).astype(BF16)

    write_plan(rows, count_ref, rank_ref, owner_ref, pick_ref, place_ref, order_ref)

    rate = HD ** (-0.5) * math.log2(math.e)
    pairs = [
        (slice(k * pack, (k + 2) * pack), slice(k * HD, (k + 2) * HD)) for k in range(0, KVH, 2)
    ]
    for turn in range(rows + 1):
        if turn < rows:
            for copy in keys[turn]:
                copy.wait()
        if turn > 0:
            for copy in values[turn - 1]:
                copy.wait()
        for copies in queue[2 * turn : 2 * turn + 2]:
            for copy in copies:
                copy.start()
        if turn < rows:
            raw[turn % 2] = dot(k_ref[turn], turned_q[turn])
        if turn == 0:
            continue
        r = turn - 1
        fresh = dot(nks[...], turned_q[r])
        slot = iota(fresh.shape, 0)
        step = (iota(fresh.shape, 1) // GROUP) % steps
        seen = (slot < both) & (slot % rows == r) & (slot // rows <= step)
        fresh = jnp.where(seen, fresh, -jnp.inf)
        older = raw[r % 2]
        older = jnp.where(iota(older.shape, 0) < len_ref[r], older, -jnp.inf)
        top = jnp.maximum(
            jnp.max(older, axis=0, keepdims=True), jnp.max(fresh, axis=0, keepdims=True)
        )
        e_older = jnp.exp2((older - top) * rate)
        e_fresh = jnp.exp2((fresh - top) * rate)
        total = jnp.sum(e_older, axis=0, keepdims=True) + jnp.sum(e_fresh, axis=0, keepdims=True)
        inverse = 1.0 / total
        p_older = jnp.transpose((e_older * inverse).astype(BF16))
        p_fresh = jnp.transpose((e_fresh * inverse).astype(BF16))
        for k, (own, cols_k) in zip(range(0, KVH, 2), pairs):
            pair = dot(p_older[own], v_ref[r, :, cols_k]) + dot(p_fresh[own], nvs[:, cols_k])
            mixed[r, k] = pair[:pack, :HD]
            mixed[r, k + 1] = pair[pack:, HD:]

    for k in range(KVH):
        turned = jnp.stack(
            [
                mixed[r, k, t * GROUP : (t + 1) * GROUP, :]
                for t in range(steps)
                for r in range(rows)
            ]
        )
        heads = jnp.swapaxes(turned, 0, 1)
        for g in range(GROUP):
            at = (k * GROUP + g) * HD
            out_ref[:, at : at + HD] = heads[g].astype(BF16)
    for copy in store:
        copy.wait()


def attend(
    queries,
    new_keys,
    new_values,
    cache_keys,
    cache_values,
    kv_len,
    store_down,
    store_up,
    tables,
    parts,
):
    steps, rows, width = queries.shape
    cache, kv_width = cache_keys.shape[1:]
    pack = steps * GROUP
    rank_w = store_down.shape[2]
    total = parts * steps * rows
    slots = steps * MOST
    shapes = [(steps * rows, width), (width, rank_w), (width, rank_w)]
    shapes += [(slots, total), (total, parts * slots), (total, total)]
    return pl.pallas_call(
        attend_kernel,
        out_shape=[jax.ShapeDtypeStruct(shape, BF16) for shape in shapes],
        in_specs=[pl.BlockSpec(memory_space=pl.ANY)] * 11,
        out_specs=[pl.BlockSpec(memory_space=pltpu.VMEM)] * len(shapes),
        scratch_shapes=[
            pltpu.SMEM(kv_len.shape, jnp.int32),
            *[pltpu.SMEM(table.shape, jnp.int32) for table in tables],
            pltpu.VMEM(queries.shape, BF16),
            pltpu.VMEM(new_keys.shape, BF16),
            pltpu.VMEM(new_values.shape, BF16),
            pltpu.VMEM(cache_keys.shape, BF16),
            pltpu.VMEM(cache_values.shape, BF16),
            pltpu.VMEM((rows, kv_width, KVH * pack), BF16),
            pltpu.VMEM((16, kv_width), BF16),
            pltpu.VMEM((16, kv_width), BF16),
            pltpu.VMEM((2, cache, KVH * pack), F32),
            pltpu.VMEM((rows, KVH, pack, HD), F32),
            pltpu.SemaphoreType.DMA((7,)),
            pltpu.SemaphoreType.DMA((rows, 2, 2)),
            pltpu.SemaphoreType.DMA((2, 4)),
        ],
        compiler_params=pltpu.CompilerParams(vmem_limit_bytes=32 * 2**20),
        cost_estimate=pl.CostEstimate(
            flops=4 * rows * steps * HQ * cache * HD,
            bytes_accessed=4 * rows * cache * kv_width,
            transcendentals=rows * steps * HQ * cache,
        ),
        name="attend",
    )(
        *in_hbm(
            kv_len,
            queries,
            new_keys,
            new_values,
            cache_keys,
            cache_values,
            store_down,
            store_up,
            *tables,
        )
    )


def swap(x, bits, parts):
    return lax.ppermute(x, "tensor", [(i, i ^ bits) for i in range(parts)])


def gather(block, parts):
    if parts != RING:
        whole = lax.all_gather(block, "tensor")
        return [whole[i] for i in range(parts)]
    core, y, near, far = 1, 2, 4, 8
    held = {0: block}
    held[far] = swap(block, far, parts)
    held[near] = swap(block, near, parts)
    held[y] = swap(block, y, parts)
    held[near | y] = swap(block, near | y, parts)
    held[far | y] = swap(held[far], y, parts)
    held[far | near | y] = swap(held[far], near | y, parts)
    held[far | near] = swap(held[far], near, parts)
    for slot in list(held):
        held[slot | core] = swap(held[slot], core, parts)
    return [held[slot] for slot in range(parts)]


def delta_kernel(at_slot, *refs):
    (*blocks, pick_ref, d_ref, u_ref, out_ref, rows_ref) = refs
    blocks = [blocks[at_slot.index(i)] for i in range(len(blocks))]
    parts, slots, cols = out_ref.shape
    each, width = blocks[0].shape
    cuts = 8
    deep = width // cuts
    low = jnp.zeros((parts * each, d_ref.shape[1]), F32)
    for i in range(cuts):
        at = slice(i * deep, (i + 1) * deep)
        piece = jnp.concatenate([b[:, at] for b in blocks], axis=0)
        rows_ref[:, at] = piece
        low = low + dot(piece, d_ref[at, :])
    chosen = dot(pick_ref[...], low.astype(BF16)).astype(BF16)
    for p in range(parts):
        out_ref[p] = dot_nt(chosen, u_ref[p * cols : (p + 1) * cols, :]).astype(BF16)


def deltas(blocks, pick, down, up):
    parts = len(blocks)
    each, width = blocks[0].shape
    slots = pick.shape[0]
    rank_w = down.shape[1]
    vmem = pl.BlockSpec(memory_space=pltpu.VMEM)
    at_slot = ORDER if parts == RING else [*range(parts)]
    return pl.pallas_call(
        functools.partial(delta_kernel, at_slot),
        out_shape=(
            pltpu.VMEM((parts, slots, width // parts), BF16),
            jax.ShapeDtypeStruct((parts * each, width), BF16),
        ),
        in_specs=[vmem] * (3 + parts),
        out_specs=(vmem, vmem),
        compiler_params=pltpu.CompilerParams(vmem_limit_bytes=24 * 2**20),
        cost_estimate=pl.CostEstimate(
            flops=2 * (parts * each + slots) * width * rank_w,
            bytes_accessed=2 * width * (2 * parts * each + 2 * rank_w + slots),
            transcendentals=0,
        ),
        name="delta",
    )(*[blocks[i] for i in at_slot], pick, down, up)


def base_kernel(a_ref, w_ref, order_ref, out_ref):
    width = a_ref.shape[1]
    cuts = 8
    deep = width // cuts
    for i in range(cuts):
        at = slice(i * deep, (i + 1) * deep)
        part = dot(dot(order_ref[...], a_ref[:, at]).astype(BF16), w_ref[at, :])
        out_ref[...] = part if i == 0 else out_ref[...] + part


def base_part(gathered, out_weight, order):
    total, width = gathered.shape
    cols = out_weight.shape[1]
    vmem = pl.BlockSpec(memory_space=pltpu.VMEM)
    return pl.pallas_call(
        base_kernel,
        out_shape=jax.ShapeDtypeStruct((total, cols), F32),
        in_specs=[vmem] * 3,
        out_specs=vmem,
        compiler_params=pltpu.CompilerParams(vmem_limit_bytes=24 * 2**20),
        cost_estimate=pl.CostEstimate(
            flops=2 * total * width * (cols + total),
            bytes_accessed=2 * width * (total + cols) + 4 * total * cols,
            transcendentals=0,
        ),
        name="base",
    )(gathered, out_weight, order)


def join_kernel(base_ref, place_ref, delta_ref, out_ref):
    steps, requests, cols = out_ref.shape
    parts, slots, _ = delta_ref.shape
    delta = dot(place_ref[...], delta_ref[...].reshape(parts * slots, cols))
    result = (base_ref[...] + delta).astype(BF16)
    for t in range(steps):
        out_ref[t] = result[t * requests : (t + 1) * requests]


def join(base, place, delta, steps):
    total, cols = base.shape
    vmem = pl.BlockSpec(memory_space=pltpu.VMEM)
    return pl.pallas_call(
        join_kernel,
        out_shape=jax.ShapeDtypeStruct((steps, total // steps, cols), BF16),
        in_specs=[vmem] * 3,
        out_specs=vmem,
        compiler_params=pltpu.CompilerParams(vmem_limit_bytes=24 * 2**20),
        name="join",
    )(base, place, delta)


def per_device(
    queries,
    new_keys,
    new_values,
    cache_keys,
    cache_values,
    kv_len,
    adapter_rows,
    adapter_rank,
    adapter_owner,
    out_weight,
    store_down,
    store_up,
):
    parts = lax.axis_size("tensor")
    steps, rows, width = queries.shape
    tables = (adapter_rows, adapter_rank, adapter_owner)
    attended, down, up, pick, place, order = attend(
        queries,
        new_keys,
        new_values,
        cache_keys,
        cache_values,
        kv_len,
        store_down,
        store_up,
        tables,
        parts,
    )
    blocks = gather(attended, parts)
    send, gathered = deltas(blocks, pick, down, up)
    delta = lax.all_to_all(send, "tensor", split_axis=0, concat_axis=0, tiled=True)
    base = base_part(gathered, out_weight, order)
    return join(base, place, delta, steps)


def solution(mesh):
    in_specs = (
        P(None, ("groups", "tensor"), None),
        P(None, ("groups", "tensor"), None),
        P(None, ("groups", "tensor"), None),
        P(("groups", "tensor"), None, None),
        P(("groups", "tensor"), None, None),
        P(("groups", "tensor")),
        P("groups"),
        P(),
        P(),
        P(None, "tensor"),
        P("tensor", None, None),
        P("tensor", None, None),
    )
    out_specs = P(None, "groups", "tensor")
    return jax.shard_map(
        per_device, mesh=mesh, in_specs=in_specs, out_specs=out_specs, check_vma=False
    )
```

```python
import functools
import math

import jax
import jax.numpy as jnp
from jax import lax
from jax.experimental import pallas as pl
from jax.experimental.pallas import tpu as pltpu
from jax.sharding import PartitionSpec as P

HQ = 64
KVH = 8
HD = 128
GROUP = HQ // KVH
MOST = 8
RING = 16
ORDER = [0, 1, 2, 3, 4, 5, 6, 7, 8, 9, 10, 11, 12, 13, 14, 15]
F32 = jnp.float32
BF16 = jnp.bfloat16
NT = (((1,), (1,)), ((), ()))


def in_hbm(*arrays):
    return [pltpu.with_memory_space_constraint(a, pltpu.HBM) for a in arrays]


def iota(shape, dim):
    return lax.broadcasted_iota(jnp.int32, shape, dim)


def one_hot(mask):
    return mask.astype(F32).astype(BF16)


def dot(a, b):
    return jnp.dot(a, b, preferred_element_type=F32)


def dot_nt(a, b):
    return lax.dot_general(a, b, NT, preferred_element_type=F32)


def sender(slot, me, parts):
    return me ^ slot if parts == RING else slot


def write_plan(rows, count_ref, rank_ref, owner_ref, pick_ref, place_ref, order_ref):
    me = lax.axis_index("tensor")
    slots, total = pick_ref.shape
    steps = slots // MOST
    each = steps * rows
    parts = total // each
    requests = parts * rows

    def adapter_of(block):
        first = jnp.zeros(block.shape, jnp.int32)
        amount = jnp.zeros(block.shape, jnp.int32)
        start = jnp.int32(0)
        for a in range(count_ref.shape[0]):
            owned = (owner_ref[a] <= block) & (block < owner_ref[a] + rank_ref[a])
            first = jnp.where(owned, start, first)
            amount = jnp.where(owned, count_ref[a], amount)
            start = start + count_ref[a]
        return first, amount

    def row_place(index):
        device = sender(index // each, me, parts)
        return device * rows + index % rows, (index % each) // rows

    row = iota((slots, 1), 0)
    nth = row % MOST
    first, amount = adapter_of(jnp.zeros_like(row) + me)
    request, step = row_place(iota((1, total), 1))
    pick = (request == first + nth) & (nth < amount) & (step == row // MOST)
    pick_ref[...] = one_hot(pick)

    request, step = row_place(iota((1, total), 1))
    order_ref[...] = one_hot(iota((total, total), 0) == step * requests + request)

    entry = iota((1, parts * slots), 1)
    nth = entry % MOST
    first, amount = adapter_of(entry // slots)
    goal = jnp.where(nth < amount, (entry % slots) // MOST * requests + first + nth, -1)
    place_ref[...] = one_hot(iota((total, parts * slots), 0) == goal)


def attend_kernel(
    len_hbm, q_hbm, nk_hbm, nv_hbm, k_hbm, v_hbm, d_hbm, u_hbm, count_hbm, rank_hbm, owner_hbm,
    out_ref, d_ref, u_ref, pick_ref, place_ref, order_ref,
    len_ref, count_ref, rank_ref, owner_ref, q_ref, nk_ref, nv_ref, k_ref, v_ref, turned_q, nks, nvs, raw, mixed,
    small_sems, sems, store_sems,
):
    steps, rows, width = q_ref.shape
    cache = k_ref.shape[1]
    both = steps * rows
    pack = steps * GROUP
    cuts = sems.shape[2]

    small = [
        pltpu.make_async_copy(src, dst, small_sems.at[i])
        for i, (src, dst) in enumerate(
            (
                (q_hbm, q_ref),
                (nk_hbm, nk_ref),
                (nv_hbm, nv_ref),
                (len_hbm, len_ref),
                (count_hbm, count_ref),
                (rank_hbm, rank_ref),
                (owner_hbm, owner_ref),
            )
        )
    ]
    pieces = [pl.ds(i * (cache // cuts), cache // cuts) for i in range(cuts)]
    keys, values = [
        [
            [
                pltpu.make_async_copy(src.at[r, at], dst.at[r, at], sems.at[r, j, i])
                for i, at in enumerate(pieces)
            ]
            for r in range(rows)
        ]
        for j, (src, dst) in enumerate(((k_hbm, k_ref), (v_hbm, v_ref)))
    ]
    deep = d_ref.shape[0] // store_sems.shape[1]
    store = [
        pltpu.make_async_copy(
            src.at[0, pl.ds(i * deep, deep)], dst.at[pl.ds(i * deep, deep)], store_sems.at[j, i]
        )
        for j, (src, dst) in enumerate(((d_hbm, d_ref), (u_hbm, u_ref)))
        for i in range(store_sems.shape[1])
    ]
    queue = [keys[0], values[0], keys[1]]
    for r in range(rows):
        queue += [values[r + 1]] if r + 1 < rows else [store]
        queue += [keys[r + 2]] if r + 2 < rows else []
    for copy in small + queue[0] + queue[1] + queue[2]:
        copy.start()
    for copy in small:
        copy.wait()
    for copy in queue[3] + queue[4]:
        copy.start()
    queue = queue[5:]

    flat = jnp.concatenate([q_ref[t].astype(F32) for t in range(steps)], axis=0)
    heads = []
    for k in range(KVH):
        group = jnp.stack(
            [flat[:, (k * GROUP + g) * HD : (k * GROUP + g + 1) * HD] for g in range(GROUP)]
        )
        heads.append(jnp.swapaxes(group, 0, 1))
    column = iota((HD, KVH * pack), 1)
    for r in range(rows):
        mine = jnp.concatenate(
            [heads[k][t * rows + r] for k in range(KVH) for t in range(steps)], axis=0
        )
        mine = jnp.transpose(mine)
        for k in range(KVH):
            turned_q[r, k * HD : (k + 1) * HD, :] = jnp.where(
                column // pack == k, mine, 0.0
            ).astype(BF16)
    for src, dst in ((nk_ref, nks), (nv_ref, nvs)):
        fresh = [src[t].astype(F32) for t in range(steps)]
        fresh.append(jnp.zeros((16 - both, src.shape[2]), F32))
        dst[...] = jnp.concatenate(fresh, axis=0).astype(BF16)

    write_plan(rows, count_ref, rank_ref, owner_ref, pick_ref, place_ref, order_ref)

    rate = HD ** (-0.5) * math.log2(math.e)
    for turn in range(rows + 1):
        if turn < rows:
            for copy in keys[turn]:
                copy.wait()
        if turn > 0:
            for copy in values[turn - 1]:
                copy.wait()
        for copies in queue[2 * turn : 2 * turn + 2]:
            for copy in copies:
                copy.start()
        if turn < rows:
            raw[turn % 2] = dot(k_ref[turn], turned_q[turn])
        if turn == 0:
            continue
        r = turn - 1
        fresh = dot(nks[...], turned_q[r])
        slot = iota(fresh.shape, 0)
        step = (iota(fresh.shape, 1) // GROUP) % steps
        seen = (slot < both) & (slot % rows == r) & (slot // rows <= step)
        fresh = jnp.where(seen, fresh, -jnp.inf)
        older = raw[r % 2]
        older = jnp.where(iota(older.shape, 0) < len_ref[r], older, -jnp.inf)
        top = jnp.maximum(
            jnp.max(older, axis=0, keepdims=True), jnp.max(fresh, axis=0, keepdims=True)
        )
        e_older = jnp.exp2((older - top) * rate)
        e_fresh = jnp.exp2((fresh - top) * rate)
        total = jnp.sum(e_older, axis=0, keepdims=True) + jnp.sum(e_fresh, axis=0, keepdims=True)
        inverse = 1.0 / total
        p_older = jnp.transpose((e_older * inverse).astype(BF16))
        p_fresh = jnp.transpose((e_fresh * inverse).astype(BF16))
        older_mix = dot(p_older, v_ref[r])
        fresh_mix = dot(p_fresh, nvs[...])
        for k in range(KVH):
            own, cols_k = slice(k * pack, (k + 1) * pack), slice(k * HD, (k + 1) * HD)
            mixed[r, k] = older_mix[own, cols_k] + fresh_mix[own, cols_k]

    for k in range(KVH):
        turned = jnp.stack(
            [
                mixed[r, k, t * GROUP : (t + 1) * GROUP, :]
                for t in range(steps)
                for r in range(rows)
            ]
        )
        heads = jnp.swapaxes(turned, 0, 1)
        for g in range(GROUP):
            at = (k * GROUP + g) * HD
            out_ref[:, at : at + HD] = heads[g].astype(BF16)
    for copy in store:
        copy.wait()


def attend(
    queries,
    new_keys,
    new_values,
    cache_keys,
    cache_values,
    kv_len,
    store_down,
    store_up,
    tables,
    parts,
):
    steps, rows, width = queries.shape
    cache, kv_width = cache_keys.shape[1:]
    pack = steps * GROUP
    rank_w = store_down.shape[2]
    total = parts * steps * rows
    slots = steps * MOST
    shapes = [(steps * rows, width), (width, rank_w), (width, rank_w)]
    shapes += [(slots, total), (total, parts * slots), (total, total)]
    return pl.pallas_call(
        attend_kernel,
        out_shape=[jax.ShapeDtypeStruct(shape, BF16) for shape in shapes],
        in_specs=[pl.BlockSpec(memory_space=pl.ANY)] * 11,
        out_specs=[pl.BlockSpec(memory_space=pltpu.VMEM)] * len(shapes),
        scratch_shapes=[
            pltpu.SMEM(kv_len.shape, jnp.int32),
            *[pltpu.SMEM(table.shape, jnp.int32) for table in tables],
            pltpu.VMEM(queries.shape, BF16),
            pltpu.VMEM(new_keys.shape, BF16),
            pltpu.VMEM(new_values.shape, BF16),
            pltpu.VMEM(cache_keys.shape, BF16),
            pltpu.VMEM(cache_values.shape, BF16),
            pltpu.VMEM((rows, kv_width, KVH * pack), BF16),
            pltpu.VMEM((16, kv_width), BF16),
            pltpu.VMEM((16, kv_width), BF16),
            pltpu.VMEM((2, cache, KVH * pack), F32),
            pltpu.VMEM((rows, KVH, pack, HD), F32),
            pltpu.SemaphoreType.DMA((7,)),
            pltpu.SemaphoreType.DMA((rows, 2, 2)),
            pltpu.SemaphoreType.DMA((2, 4)),
        ],
        compiler_params=pltpu.CompilerParams(vmem_limit_bytes=32 * 2**20),
        cost_estimate=pl.CostEstimate(
            flops=4 * rows * steps * HQ * cache * HD,
            bytes_accessed=4 * rows * cache * kv_width,
            transcendentals=rows * steps * HQ * cache,
        ),
        name="attend",
    )(
        *in_hbm(
            kv_len,
            queries,
            new_keys,
            new_values,
            cache_keys,
            cache_values,
            store_down,
            store_up,
            *tables,
        )
    )


def swap(x, bits, parts):
    return lax.ppermute(x, "tensor", [(i, i ^ bits) for i in range(parts)])


def gather(block, parts):
    if parts != RING:
        whole = lax.all_gather(block, "tensor")
        return [whole[i] for i in range(parts)]
    core, y, near, far = 1, 2, 4, 8
    held = {0: block}
    held[far] = swap(block, far, parts)
    held[near] = swap(block, near, parts)
    held[y] = swap(block, y, parts)
    held[near | y] = swap(block, near | y, parts)
    held[far | y] = swap(held[far], y, parts)
    held[far | near | y] = swap(held[far], near | y, parts)
    held[far | near] = swap(held[far], near, parts)
    for slot in list(held):
        held[slot | core] = swap(held[slot], core, parts)
    return [held[slot] for slot in range(parts)]


def delta_kernel(at_slot, *refs):
    (*blocks, pick_ref, d_ref, u_ref, out_ref, rows_ref) = refs
    blocks = [blocks[at_slot.index(i)] for i in range(len(blocks))]
    parts, slots, cols = out_ref.shape
    each, width = blocks[0].shape
    for i in range(0, len(blocks), 2):
        pair = jnp.concatenate([blocks[i][...], blocks[i + 1][...]], axis=0)
        rows_ref[i * each : (i + 2) * each, :] = pair
    low = dot(rows_ref[...], d_ref[...]).astype(BF16)
    chosen = dot(pick_ref[...], low).astype(BF16)
    raised = dot_nt(chosen, u_ref[...]).astype(BF16)
    for p in range(parts):
        out_ref[p] = raised[:, p * cols : (p + 1) * cols]


def deltas(blocks, pick, down, up):
    parts = len(blocks)
    each, width = blocks[0].shape
    slots = pick.shape[0]
    rank_w = down.shape[1]
    vmem = pl.BlockSpec(memory_space=pltpu.VMEM)
    at_slot = ORDER if parts == RING else [*range(parts)]
    return pl.pallas_call(
        functools.partial(delta_kernel, at_slot),
        out_shape=(
            jax.ShapeDtypeStruct((parts, slots, width // parts), BF16),
            jax.ShapeDtypeStruct((parts * each, width), BF16),
        ),
        in_specs=[vmem] * (3 + parts),
        out_specs=(vmem, vmem),
        compiler_params=pltpu.CompilerParams(vmem_limit_bytes=24 * 2**20),
        cost_estimate=pl.CostEstimate(
            flops=2 * (parts * each + slots) * width * rank_w,
            bytes_accessed=2 * width * (2 * parts * each + 2 * rank_w + slots),
            transcendentals=0,
        ),
        name="delta",
    )(*[blocks[i] for i in at_slot], pick, down, up)


def base_kernel(a_ref, w_ref, order_ref, out_ref):
    width = a_ref.shape[1]
    cuts = 8
    deep = width // cuts
    for i in range(cuts):
        at = slice(i * deep, (i + 1) * deep)
        part = dot(dot(order_ref[...], a_ref[:, at]).astype(BF16), w_ref[at, :])
        out_ref[...] = part if i == 0 else out_ref[...] + part


def base_part(gathered, out_weight, order):
    total, width = gathered.shape
    cols = out_weight.shape[1]
    vmem = pl.BlockSpec(memory_space=pltpu.VMEM)
    return pl.pallas_call(
        base_kernel,
        out_shape=jax.ShapeDtypeStruct((total, cols), F32),
        in_specs=[vmem] * 3,
        out_specs=vmem,
        compiler_params=pltpu.CompilerParams(vmem_limit_bytes=24 * 2**20),
        cost_estimate=pl.CostEstimate(
            flops=2 * total * width * (cols + total),
            bytes_accessed=2 * width * (total + cols) + 4 * total * cols,
            transcendentals=0,
        ),
        name="base",
    )(gathered, out_weight, order)


def join_kernel(base_ref, place_ref, delta_ref, out_ref):
    steps, requests, cols = out_ref.shape
    parts, slots, _ = delta_ref.shape
    delta = dot(place_ref[...], delta_ref[...].reshape(parts * slots, cols))
    result = (base_ref[...] + delta).astype(BF16)
    for t in range(steps):
        out_ref[t] = result[t * requests : (t + 1) * requests]


def join(base, place, delta, steps):
    total, cols = base.shape
    vmem = pl.BlockSpec(memory_space=pltpu.VMEM)
    return pl.pallas_call(
        join_kernel,
        out_shape=jax.ShapeDtypeStruct((steps, total // steps, cols), BF16),
        in_specs=[vmem] * 3,
        out_specs=vmem,
        compiler_params=pltpu.CompilerParams(vmem_limit_bytes=24 * 2**20),
        name="join",
    )(base, place, delta)


def per_device(
    queries,
    new_keys,
    new_values,
    cache_keys,
    cache_values,
    kv_len,
    adapter_rows,
    adapter_rank,
    adapter_owner,
    out_weight,
    store_down,
    store_up,
):
    parts = lax.axis_size("tensor")
    steps, rows, width = queries.shape
    tables = (adapter_rows, adapter_rank, adapter_owner)
    attended, down, up, pick, place, order = attend(
        queries,
        new_keys,
        new_values,
        cache_keys,
        cache_values,
        kv_len,
        store_down,
        store_up,
        tables,
        parts,
    )
    blocks = gather(attended, parts)
    send, gathered = deltas(blocks, pick, down, up)
    delta = lax.all_to_all(send, "tensor", split_axis=0, concat_axis=0, tiled=True)
    base = base_part(gathered, out_weight, order)
    return join(base, place, delta, steps)


def solution(mesh):
    in_specs = (
        P(None, ("groups", "tensor"), None),
        P(None, ("groups", "tensor"), None),
        P(None, ("groups", "tensor"), None),
        P(("groups", "tensor"), None, None),
        P(("groups", "tensor"), None, None),
        P(("groups", "tensor")),
        P("groups"),
        P(),
        P(),
        P(None, "tensor"),
        P("tensor", None, None),
        P("tensor", None, None),
    )
    out_specs = P(None, "groups", "tensor")
    return jax.shard_map(
        per_device, mesh=mesh, in_specs=in_specs, out_specs=out_specs, check_vma=False
    )
```

```python
import functools
import math

import jax
import jax.numpy as jnp
from jax import lax
from jax.experimental import pallas as pl
from jax.experimental.pallas import tpu as pltpu
from jax.sharding import PartitionSpec as P

HQ = 64
KVH = 8
HD = 128
GROUP = HQ // KVH
MOST = 8
RING = 16
ORDER = [0, 1, 2, 3, 4, 5, 6, 7, 8, 9, 10, 11, 12, 13, 14, 15]
F32 = jnp.float32
BF16 = jnp.bfloat16
NT = (((1,), (1,)), ((), ()))


def in_hbm(*arrays):
    return [pltpu.with_memory_space_constraint(a, pltpu.HBM) for a in arrays]


def iota(shape, dim):
    return lax.broadcasted_iota(jnp.int32, shape, dim)


def one_hot(mask):
    return mask.astype(F32).astype(BF16)


def dot(a, b):
    return jnp.dot(a, b, preferred_element_type=F32)


def dot_nt(a, b):
    return lax.dot_general(a, b, NT, preferred_element_type=F32)


def sender(slot, me, parts):
    return me ^ slot if parts == RING else slot


def write_plan(rows, count_ref, rank_ref, owner_ref, pick_ref, place_ref, order_ref):
    me = lax.axis_index("tensor")
    slots, total = pick_ref.shape
    steps = slots // MOST
    each = steps * rows
    parts = total // each
    requests = parts * rows

    def adapter_of(block):
        first = jnp.zeros(block.shape, jnp.int32)
        amount = jnp.zeros(block.shape, jnp.int32)
        start = jnp.int32(0)
        for a in range(count_ref.shape[0]):
            owned = (owner_ref[a] <= block) & (block < owner_ref[a] + rank_ref[a])
            first = jnp.where(owned, start, first)
            amount = jnp.where(owned, count_ref[a], amount)
            start = start + count_ref[a]
        return first, amount

    def row_place(index):
        device = sender(index // each, me, parts)
        return device * rows + index % rows, (index % each) // rows

    row = iota((slots, 1), 0)
    nth = row % MOST
    first, amount = adapter_of(jnp.zeros_like(row) + me)
    request, step = row_place(iota((1, total), 1))
    pick = (request == first + nth) & (nth < amount) & (step == row // MOST)
    pick_ref[...] = one_hot(pick)

    request, step = row_place(iota((1, total), 1))
    order_ref[...] = one_hot(iota((total, total), 0) == step * requests + request)

    entry = iota((1, parts * slots), 1)
    nth = entry % MOST
    first, amount = adapter_of(entry // slots)
    goal = jnp.where(nth < amount, (entry % slots) // MOST * requests + first + nth, -1)
    place_ref[...] = one_hot(iota((total, parts * slots), 0) == goal)


def attend_kernel(
    len_hbm, q_hbm, nk_hbm, nv_hbm, k_hbm, v_hbm, d_hbm, u_hbm, count_hbm, rank_hbm, owner_hbm,
    out_ref, d_ref, u_ref, pick_ref, place_ref, order_ref,
    len_ref, count_ref, rank_ref, owner_ref, q_ref, nk_ref, nv_ref, k_ref, v_ref, turned_q, nks, nvs, raw, mixed,
    small_sems, sems, store_sems,
):
    steps, rows, width = q_ref.shape
    cache = k_ref.shape[1]
    both = steps * rows
    pack = steps * GROUP
    cuts = sems.shape[2]

    small = [
        pltpu.make_async_copy(src, dst, small_sems.at[i])
        for i, (src, dst) in enumerate(
            (
                (q_hbm, q_ref),
                (nk_hbm, nk_ref),
                (nv_hbm, nv_ref),
                (len_hbm, len_ref),
                (count_hbm, count_ref),
                (rank_hbm, rank_ref),
                (owner_hbm, owner_ref),
            )
        )
    ]
    pieces = [pl.ds(i * (cache // cuts), cache // cuts) for i in range(cuts)]
    keys, values = [
        [
            [
                pltpu.make_async_copy(src.at[r, at], dst.at[r, at], sems.at[r, j, i])
                for i, at in enumerate(pieces)
            ]
            for r in range(rows)
        ]
        for j, (src, dst) in enumerate(((k_hbm, k_ref), (v_hbm, v_ref)))
    ]
    deep = d_ref.shape[0] // store_sems.shape[1]
    store = [
        pltpu.make_async_copy(
            src.at[0, pl.ds(i * deep, deep)], dst.at[pl.ds(i * deep, deep)], store_sems.at[j, i]
        )
        for j, (src, dst) in enumerate(((d_hbm, d_ref), (u_hbm, u_ref)))
        for i in range(store_sems.shape[1])
    ]
    queue = [keys[0], values[0], keys[1]]
    for r in range(rows):
        queue += [values[r + 1]] if r + 1 < rows else [store]
        queue += [keys[r + 2]] if r + 2 < rows else []
    for copy in small + queue[0] + queue[1] + queue[2]:
        copy.start()
    for copy in small:
        copy.wait()
    for copy in queue[3] + queue[4]:
        copy.start()
    queue = queue[5:]

    flat = jnp.concatenate([q_ref[t].astype(F32) for t in range(steps)], axis=0)
    heads = []
    for k in range(KVH):
        group = jnp.stack(
            [flat[:, (k * GROUP + g) * HD : (k * GROUP + g + 1) * HD] for g in range(GROUP)]
        )
        heads.append(jnp.swapaxes(group, 0, 1))
    column = iota((HD, KVH * pack), 1)
    for r in range(rows):
        mine = jnp.concatenate(
            [heads[k][t * rows + r] for k in range(KVH) for t in range(steps)], axis=0
        )
        mine = jnp.transpose(mine)
        for k in range(KVH):
            turned_q[r, k * HD : (k + 1) * HD, :] = jnp.where(
                column // pack == k, mine, 0.0
            ).astype(BF16)
    for src, dst in ((nk_ref, nks), (nv_ref, nvs)):
        fresh = [src[t].astype(F32) for t in range(steps)]
        fresh.append(jnp.zeros((16 - both, src.shape[2]), F32))
        dst[...] = jnp.concatenate(fresh, axis=0).astype(BF16)

    write_plan(rows, count_ref, rank_ref, owner_ref, pick_ref, place_ref, order_ref)

    rate = HD ** (-0.5) * math.log2(math.e)
    pairs = [
        (slice(k * pack, (k + 2) * pack), slice(k * HD, (k + 2) * HD)) for k in range(0, KVH, 2)
    ]
    for turn in range(rows + 1):
        if turn < rows:
            for copy in keys[turn]:
                copy.wait()
        if turn > 0:
            for copy in values[turn - 1]:
                copy.wait()
        for copies in queue[2 * turn : 2 * turn + 2]:
            for copy in copies:
                copy.start()
        if turn < rows:
            raw[turn % 2] = dot(k_ref[turn], turned_q[turn])
        if turn == 0:
            continue
        r = turn - 1
        fresh = dot(nks[...], turned_q[r])
        slot = iota(fresh.shape, 0)
        step = (iota(fresh.shape, 1) // GROUP) % steps
        seen = (slot < both) & (slot % rows == r) & (slot // rows <= step)
        fresh = jnp.where(seen, fresh, -jnp.inf)
        older = raw[r % 2]
        older = jnp.where(iota(older.shape, 0) < len_ref[r], older, -jnp.inf)
        top = jnp.maximum(
            jnp.max(older, axis=0, keepdims=True), jnp.max(fresh, axis=0, keepdims=True)
        )
        e_older = jnp.exp2((older - top) * rate)
        e_fresh = jnp.exp2((fresh - top) * rate)
        total = jnp.sum(e_older, axis=0, keepdims=True) + jnp.sum(e_fresh, axis=0, keepdims=True)
        inverse = 1.0 / total
        p_older = jnp.transpose((e_older * inverse).astype(BF16))
        p_fresh = jnp.transpose((e_fresh * inverse).astype(BF16))
        for k, (own, cols_k) in zip(range(0, KVH, 2), pairs):
            pair = dot(p_older[own], v_ref[r, :, cols_k]) + dot(p_fresh[own], nvs[:, cols_k])
            mixed[r, k] = pair[:pack, :HD]
            mixed[r, k + 1] = pair[pack:, HD:]

    for k in range(KVH):
        turned = jnp.stack(
            [
                mixed[r, k, t * GROUP : (t + 1) * GROUP, :]
                for t in range(steps)
                for r in range(rows)
            ]
        )
        heads = jnp.swapaxes(turned, 0, 1)
        for g in range(GROUP):
            at = (k * GROUP + g) * HD
            out_ref[:, at : at + HD] = heads[g].astype(BF16)
    for copy in store:
        copy.wait()


def attend(
    queries,
    new_keys,
    new_values,
    cache_keys,
    cache_values,
    kv_len,
    store_down,
    store_up,
    tables,
    parts,
):
    steps, rows, width = queries.shape
    cache, kv_width = cache_keys.shape[1:]
    pack = steps * GROUP
    rank_w = store_down.shape[2]
    total = parts * steps * rows
    slots = steps * MOST
    shapes = [(steps * rows, width), (width, rank_w), (width, rank_w)]
    shapes += [(slots, total), (total, parts * slots), (total, total)]
    return pl.pallas_call(
        attend_kernel,
        out_shape=[jax.ShapeDtypeStruct(shape, BF16) for shape in shapes],
        in_specs=[pl.BlockSpec(memory_space=pl.ANY)] * 11,
        out_specs=[pl.BlockSpec(memory_space=pltpu.VMEM)] * len(shapes),
        scratch_shapes=[
            pltpu.SMEM(kv_len.shape, jnp.int32),
            *[pltpu.SMEM(table.shape, jnp.int32) for table in tables],
            pltpu.VMEM(queries.shape, BF16),
            pltpu.VMEM(new_keys.shape, BF16),
            pltpu.VMEM(new_values.shape, BF16),
            pltpu.VMEM(cache_keys.shape, BF16),
            pltpu.VMEM(cache_values.shape, BF16),
            pltpu.VMEM((rows, kv_width, KVH * pack), BF16),
            pltpu.VMEM((16, kv_width), BF16),
            pltpu.VMEM((16, kv_width), BF16),
            pltpu.VMEM((2, cache, KVH * pack), F32),
            pltpu.VMEM((rows, KVH, pack, HD), F32),
            pltpu.SemaphoreType.DMA((7,)),
            pltpu.SemaphoreType.DMA((rows, 2, 2)),
            pltpu.SemaphoreType.DMA((2, 4)),
        ],
        compiler_params=pltpu.CompilerParams(vmem_limit_bytes=32 * 2**20),
        cost_estimate=pl.CostEstimate(
            flops=4 * rows * steps * HQ * cache * HD,
            bytes_accessed=4 * rows * cache * kv_width,
            transcendentals=rows * steps * HQ * cache,
        ),
        name="attend",
    )(
        *in_hbm(
            kv_len,
            queries,
            new_keys,
            new_values,
            cache_keys,
            cache_values,
            store_down,
            store_up,
            *tables,
        )
    )


def swap(x, bits, parts):
    return lax.ppermute(x, "tensor", [(i, i ^ bits) for i in range(parts)])


def gather(block, parts):
    if parts != RING:
        whole = lax.all_gather(block, "tensor")
        return [whole[i] for i in range(parts)]
    core, y, near, far = 1, 2, 4, 8
    held = {0: block}
    held[far] = swap(block, far, parts)
    held[near] = swap(block, near, parts)
    held[y] = swap(block, y, parts)
    held[far | near] = swap(held[far], near, parts)
    held[far | y] = swap(held[far], y, parts)
    held[near | y] = swap(held[y], near, parts)
    held[far | near | y] = swap(held[far | near], y, parts)
    for slot in list(held):
        held[slot | core] = swap(held[slot], core, parts)
    return [held[slot] for slot in range(parts)]


def delta_kernel(at_slot, *refs):
    (*blocks, pick_ref, d_ref, u_ref, out_ref, rows_ref) = refs
    blocks = [blocks[at_slot.index(i)] for i in range(len(blocks))]
    parts, slots, cols = out_ref.shape
    each, width = blocks[0].shape
    cuts = 8
    deep = width // cuts
    low = jnp.zeros((parts * each, d_ref.shape[1]), F32)
    for i in range(cuts):
        at = slice(i * deep, (i + 1) * deep)
        piece = jnp.concatenate([b[:, at] for b in blocks], axis=0)
        rows_ref[:, at] = piece
        low = low + dot(piece, d_ref[at, :])
    chosen = dot(pick_ref[...], low.astype(BF16)).astype(BF16)
    for p in range(parts):
        out_ref[p] = dot_nt(chosen, u_ref[p * cols : (p + 1) * cols, :]).astype(BF16)


def deltas(blocks, pick, down, up):
    parts = len(blocks)
    each, width = blocks[0].shape
    slots = pick.shape[0]
    rank_w = down.shape[1]
    vmem = pl.BlockSpec(memory_space=pltpu.VMEM)
    at_slot = ORDER if parts == RING else [*range(parts)]
    return pl.pallas_call(
        functools.partial(delta_kernel, at_slot),
        out_shape=(
            jax.ShapeDtypeStruct((parts, slots, width // parts), BF16),
            jax.ShapeDtypeStruct((parts * each, width), BF16),
        ),
        in_specs=[vmem] * (3 + parts),
        out_specs=(vmem, vmem),
        compiler_params=pltpu.CompilerParams(vmem_limit_bytes=24 * 2**20),
        cost_estimate=pl.CostEstimate(
            flops=2 * (parts * each + slots) * width * rank_w,
            bytes_accessed=2 * width * (2 * parts * each + 2 * rank_w + slots),
            transcendentals=0,
        ),
        name="delta",
    )(*[blocks[i] for i in at_slot], pick, down, up)


def base_kernel(a_ref, w_ref, order_ref, out_ref):
    width = a_ref.shape[1]
    cuts = 8
    deep = width // cuts
    for i in range(cuts):
        at = slice(i * deep, (i + 1) * deep)
        part = dot(dot(order_ref[...], a_ref[:, at]).astype(BF16), w_ref[at, :])
        out_ref[...] = part if i == 0 else out_ref[...] + part


def base_part(gathered, out_weight, order):
    total, width = gathered.shape
    cols = out_weight.shape[1]
    vmem = pl.BlockSpec(memory_space=pltpu.VMEM)
    return pl.pallas_call(
        base_kernel,
        out_shape=jax.ShapeDtypeStruct((total, cols), F32),
        in_specs=[vmem] * 3,
        out_specs=vmem,
        compiler_params=pltpu.CompilerParams(vmem_limit_bytes=24 * 2**20),
        cost_estimate=pl.CostEstimate(
            flops=2 * total * width * (cols + total),
            bytes_accessed=2 * width * (total + cols) + 4 * total * cols,
            transcendentals=0,
        ),
        name="base",
    )(gathered, out_weight, order)


def join_kernel(base_ref, place_ref, delta_ref, out_ref):
    steps, requests, cols = out_ref.shape
    parts, slots, _ = delta_ref.shape
    delta = dot(place_ref[...], delta_ref[...].reshape(parts * slots, cols))
    result = (base_ref[...] + delta).astype(BF16)
    for t in range(steps):
        out_ref[t] = result[t * requests : (t + 1) * requests]


def join(base, place, delta, steps):
    total, cols = base.shape
    vmem = pl.BlockSpec(memory_space=pltpu.VMEM)
    return pl.pallas_call(
        join_kernel,
        out_shape=jax.ShapeDtypeStruct((steps, total // steps, cols), BF16),
        in_specs=[vmem] * 3,
        out_specs=vmem,
        compiler_params=pltpu.CompilerParams(vmem_limit_bytes=24 * 2**20),
        name="join",
    )(base, place, delta)


def per_device(
    queries,
    new_keys,
    new_values,
    cache_keys,
    cache_values,
    kv_len,
    adapter_rows,
    adapter_rank,
    adapter_owner,
    out_weight,
    store_down,
    store_up,
):
    parts = lax.axis_size("tensor")
    steps, rows, width = queries.shape
    tables = (adapter_rows, adapter_rank, adapter_owner)
    attended, down, up, pick, place, order = attend(
        queries,
        new_keys,
        new_values,
        cache_keys,
        cache_values,
        kv_len,
        store_down,
        store_up,
        tables,
        parts,
    )
    blocks = gather(attended, parts)
    send, gathered = deltas(blocks, pick, down, up)
    delta = lax.all_to_all(send, "tensor", split_axis=0, concat_axis=0, tiled=True)
    base = base_part(gathered, out_weight, order)
    return join(base, place, delta, steps)


def solution(mesh):
    in_specs = (
        P(None, ("groups", "tensor"), None),
        P(None, ("groups", "tensor"), None),
        P(None, ("groups", "tensor"), None),
        P(("groups", "tensor"), None, None),
        P(("groups", "tensor"), None, None),
        P(("groups", "tensor")),
        P("groups"),
        P(),
        P(),
        P(None, "tensor"),
        P("tensor", None, None),
        P("tensor", None, None),
    )
    out_specs = P(None, "groups", "tensor")
    return jax.shard_map(
        per_device, mesh=mesh, in_specs=in_specs, out_specs=out_specs, check_vma=False
    )
```

```python
import functools
import math

import jax
import jax.numpy as jnp
from jax import lax
from jax.experimental import pallas as pl
from jax.experimental.pallas import tpu as pltpu
from jax.sharding import PartitionSpec as P

HQ = 64
KVH = 8
HD = 128
GROUP = HQ // KVH
MOST = 8
RING = 16
ORDER = [0, 1, 2, 3, 4, 5, 6, 7, 8, 9, 10, 11, 12, 13, 14, 15]
F32 = jnp.float32
BF16 = jnp.bfloat16
NT = (((1,), (1,)), ((), ()))


def in_hbm(*arrays):
    return [pltpu.with_memory_space_constraint(a, pltpu.HBM) for a in arrays]


def iota(shape, dim):
    return lax.broadcasted_iota(jnp.int32, shape, dim)


def one_hot(mask):
    return mask.astype(F32).astype(BF16)


def dot(a, b):
    return jnp.dot(a, b, preferred_element_type=F32)


def dot_nt(a, b):
    return lax.dot_general(a, b, NT, preferred_element_type=F32)


def sender(slot, me, parts):
    return me ^ slot if parts == RING else slot


def write_plan(rows, count_ref, rank_ref, owner_ref, pick_ref, place_ref, order_ref):
    me = lax.axis_index("tensor")
    slots, total = pick_ref.shape
    steps = slots // MOST
    each = steps * rows
    parts = total // each
    requests = parts * rows

    def adapter_of(block):
        first = jnp.zeros(block.shape, jnp.int32)
        amount = jnp.zeros(block.shape, jnp.int32)
        start = jnp.int32(0)
        for a in range(count_ref.shape[0]):
            owned = (owner_ref[a] <= block) & (block < owner_ref[a] + rank_ref[a])
            first = jnp.where(owned, start, first)
            amount = jnp.where(owned, count_ref[a], amount)
            start = start + count_ref[a]
        return first, amount

    def row_place(index):
        device = sender(index // each, me, parts)
        return device * rows + index % rows, (index % each) // rows

    row = iota((slots, 1), 0)
    nth = row % MOST
    first, amount = adapter_of(jnp.zeros_like(row) + me)
    request, step = row_place(iota((1, total), 1))
    pick = (request == first + nth) & (nth < amount) & (step == row // MOST)
    pick_ref[...] = one_hot(pick)

    request, step = row_place(iota((1, total), 1))
    order_ref[...] = one_hot(iota((total, total), 0) == step * requests + request)

    entry = iota((1, parts * slots), 1)
    nth = entry % MOST
    first, amount = adapter_of(parts - 1 - entry // slots)
    goal = jnp.where(nth < amount, (entry % slots) // MOST * requests + first + nth, -1)
    place_ref[...] = one_hot(iota((total, parts * slots), 0) == goal)


def attend_kernel(
    len_hbm, q_hbm, nk_hbm, nv_hbm, k_hbm, v_hbm, d_hbm, u_hbm, count_hbm, rank_hbm, owner_hbm,
    out_ref, d_ref, u_ref, pick_ref, place_ref, order_ref,
    len_ref, count_ref, rank_ref, owner_ref, q_ref, nk_ref, nv_ref, k_ref, v_ref, turned_q, nks, nvs, raw, mixed,
    small_sems, sems, store_sems,
):
    steps, rows, width = q_ref.shape
    cache = k_ref.shape[1]
    both = steps * rows
    pack = steps * GROUP
    cuts = sems.shape[2]

    small = [
        pltpu.make_async_copy(src, dst, small_sems.at[i])
        for i, (src, dst) in enumerate(
            (
                (q_hbm, q_ref),
                (nk_hbm, nk_ref),
                (nv_hbm, nv_ref),
                (len_hbm, len_ref),
                (count_hbm, count_ref),
                (rank_hbm, rank_ref),
                (owner_hbm, owner_ref),
            )
        )
    ]
    pieces = [pl.ds(i * (cache // cuts), cache // cuts) for i in range(cuts)]
    keys, values = [
        [
            [
                pltpu.make_async_copy(src.at[r, at], dst.at[r, at], sems.at[r, j, i])
                for i, at in enumerate(pieces)
            ]
            for r in range(rows)
        ]
        for j, (src, dst) in enumerate(((k_hbm, k_ref), (v_hbm, v_ref)))
    ]
    deep = d_ref.shape[0] // store_sems.shape[1]
    store = [
        pltpu.make_async_copy(
            src.at[0, pl.ds(i * deep, deep)], dst.at[pl.ds(i * deep, deep)], store_sems.at[j, i]
        )
        for j, (src, dst) in enumerate(((d_hbm, d_ref), (u_hbm, u_ref)))
        for i in range(store_sems.shape[1])
    ]
    queue = [keys[0], values[0], keys[1]]
    for r in range(rows):
        queue += [values[r + 1]] if r + 1 < rows else [store]
        queue += [keys[r + 2]] if r + 2 < rows else []
    for copy in small + queue[0] + queue[1] + queue[2]:
        copy.start()
    for copy in small:
        copy.wait()
    for copy in queue[3] + queue[4]:
        copy.start()
    queue = queue[5:]

    flat = jnp.concatenate([q_ref[t].astype(F32) for t in range(steps)], axis=0)
    heads = []
    for k in range(KVH):
        group = jnp.stack(
            [flat[:, (k * GROUP + g) * HD : (k * GROUP + g + 1) * HD] for g in range(GROUP)]
        )
        heads.append(jnp.swapaxes(group, 0, 1))
    column = iota((HD, KVH * pack), 1)
    for r in range(rows):
        mine = jnp.concatenate(
            [heads[k][t * rows + r] for k in range(KVH) for t in range(steps)], axis=0
        )
        mine = jnp.transpose(mine)
        for k in range(KVH):
            turned_q[r, k * HD : (k + 1) * HD, :] = jnp.where(
                column // pack == k, mine, 0.0
            ).astype(BF16)
    for src, dst in ((nk_ref, nks), (nv_ref, nvs)):
        fresh = [src[t].astype(F32) for t in range(steps)]
        fresh.append(jnp.zeros((16 - both, src.shape[2]), F32))
        dst[...] = jnp.concatenate(fresh, axis=0).astype(BF16)

    write_plan(rows, count_ref, rank_ref, owner_ref, pick_ref, place_ref, order_ref)

    rate = HD ** (-0.5) * math.log2(math.e)
    pairs = [
        (slice(k * pack, (k + 2) * pack), slice(k * HD, (k + 2) * HD)) for k in range(0, KVH, 2)
    ]
    for turn in range(rows + 1):
        if turn < rows:
            for copy in keys[turn]:
                copy.wait()
        if turn > 0:
            for copy in values[turn - 1]:
                copy.wait()
        for copies in queue[2 * turn : 2 * turn + 2]:
            for copy in copies:
                copy.start()
        if turn < rows:
            raw[turn % 2] = dot(k_ref[turn], turned_q[turn])
        if turn == 0:
            continue
        r = turn - 1
        fresh = dot(nks[...], turned_q[r])
        slot = iota(fresh.shape, 0)
        step = (iota(fresh.shape, 1) // GROUP) % steps
        seen = (slot < both) & (slot % rows == r) & (slot // rows <= step)
        fresh = jnp.where(seen, fresh, -jnp.inf)
        older = raw[r % 2]
        older = jnp.where(iota(older.shape, 0) < len_ref[r], older, -jnp.inf)
        top = jnp.maximum(
            jnp.max(older, axis=0, keepdims=True), jnp.max(fresh, axis=0, keepdims=True)
        )
        e_older = jnp.exp2((older - top) * rate)
        e_fresh = jnp.exp2((fresh - top) * rate)
        total = jnp.sum(e_older, axis=0, keepdims=True) + jnp.sum(e_fresh, axis=0, keepdims=True)
        inverse = 1.0 / total
        p_older = jnp.transpose((e_older * inverse).astype(BF16))
        p_fresh = jnp.transpose((e_fresh * inverse).astype(BF16))
        for k, (own, cols_k) in zip(range(0, KVH, 2), pairs):
            pair = dot(p_older[own], v_ref[r, :, cols_k]) + dot(p_fresh[own], nvs[:, cols_k])
            mixed[r, k] = pair[:pack, :HD]
            mixed[r, k + 1] = pair[pack:, HD:]

    for k in range(KVH):
        turned = jnp.stack(
            [
                mixed[r, k, t * GROUP : (t + 1) * GROUP, :]
                for t in range(steps)
                for r in range(rows)
            ]
        )
        heads = jnp.swapaxes(turned, 0, 1)
        for g in range(GROUP):
            at = (k * GROUP + g) * HD
            out_ref[:, at : at + HD] = heads[g].astype(BF16)
    for copy in store:
        copy.wait()


def attend(
    queries,
    new_keys,
    new_values,
    cache_keys,
    cache_values,
    kv_len,
    store_down,
    store_up,
    tables,
    parts,
):
    steps, rows, width = queries.shape
    cache, kv_width = cache_keys.shape[1:]
    pack = steps * GROUP
    rank_w = store_down.shape[2]
    total = parts * steps * rows
    slots = steps * MOST
    shapes = [(steps * rows, width), (width, rank_w), (width, rank_w)]
    shapes += [(slots, total), (total, parts * slots), (total, total)]
    return pl.pallas_call(
        attend_kernel,
        out_shape=[jax.ShapeDtypeStruct(shape, BF16) for shape in shapes],
        in_specs=[pl.BlockSpec(memory_space=pl.ANY)] * 11,
        out_specs=[pl.BlockSpec(memory_space=pltpu.VMEM)] * len(shapes),
        scratch_shapes=[
            pltpu.SMEM(kv_len.shape, jnp.int32),
            *[pltpu.SMEM(table.shape, jnp.int32) for table in tables],
            pltpu.VMEM(queries.shape, BF16),
            pltpu.VMEM(new_keys.shape, BF16),
            pltpu.VMEM(new_values.shape, BF16),
            pltpu.VMEM(cache_keys.shape, BF16),
            pltpu.VMEM(cache_values.shape, BF16),
            pltpu.VMEM((rows, kv_width, KVH * pack), BF16),
            pltpu.VMEM((16, kv_width), BF16),
            pltpu.VMEM((16, kv_width), BF16),
            pltpu.VMEM((2, cache, KVH * pack), F32),
            pltpu.VMEM((rows, KVH, pack, HD), F32),
            pltpu.SemaphoreType.DMA((7,)),
            pltpu.SemaphoreType.DMA((rows, 2, 2)),
            pltpu.SemaphoreType.DMA((2, 4)),
        ],
        compiler_params=pltpu.CompilerParams(vmem_limit_bytes=32 * 2**20),
        cost_estimate=pl.CostEstimate(
            flops=4 * rows * steps * HQ * cache * HD,
            bytes_accessed=4 * rows * cache * kv_width,
            transcendentals=rows * steps * HQ * cache,
        ),
        name="attend",
    )(
        *in_hbm(
            kv_len,
            queries,
            new_keys,
            new_values,
            cache_keys,
            cache_values,
            store_down,
            store_up,
            *tables,
        )
    )


def swap(x, bits, parts):
    return lax.ppermute(x, "tensor", [(i, i ^ bits) for i in range(parts)])


def gather(block, parts):
    if parts != RING:
        whole = lax.all_gather(block, "tensor")
        return [whole[i] for i in range(parts)]
    core, y, near, far = 1, 2, 4, 8
    held = {0: block}
    held[far] = swap(block, far, parts)
    held[near] = swap(block, near, parts)
    held[y] = swap(block, y, parts)
    held[near | y] = swap(block, near | y, parts)
    held[far | y] = swap(held[far], y, parts)
    held[far | near | y] = swap(held[far], near | y, parts)
    held[far | near] = swap(held[far], near, parts)
    for slot in list(held):
        held[slot | core] = swap(held[slot], core, parts)
    return [held[slot] for slot in range(parts)]


def delta_kernel(at_slot, *refs):
    (*blocks, pick_ref, d_ref, u_ref, out_ref, rows_ref) = refs
    blocks = [blocks[at_slot.index(i)] for i in range(len(blocks))]
    parts, slots, cols = out_ref.shape
    each, width = blocks[0].shape
    cuts = 8
    deep = width // cuts
    low = jnp.zeros((parts * each, d_ref.shape[1]), F32)
    for i in range(cuts):
        at = slice(i * deep, (i + 1) * deep)
        piece = jnp.concatenate([b[:, at] for b in blocks], axis=0)
        rows_ref[:, at] = piece
        low = low + dot(piece, d_ref[at, :])
    chosen = dot(pick_ref[...], low.astype(BF16)).astype(BF16)
    for p in range(parts):
        at = (parts - 1 - p) * cols
        out_ref[p] = dot_nt(chosen, u_ref[at : at + cols, :]).astype(BF16)


def deltas(blocks, pick, down, up):
    parts = len(blocks)
    each, width = blocks[0].shape
    slots = pick.shape[0]
    rank_w = down.shape[1]
    vmem = pl.BlockSpec(memory_space=pltpu.VMEM)
    at_slot = ORDER if parts == RING else [*range(parts)]
    return pl.pallas_call(
        functools.partial(delta_kernel, at_slot),
        out_shape=(
            jax.ShapeDtypeStruct((parts, slots, width // parts), BF16),
            jax.ShapeDtypeStruct((parts * each, width), BF16),
        ),
        in_specs=[vmem] * (3 + parts),
        out_specs=(vmem, vmem),
        compiler_params=pltpu.CompilerParams(vmem_limit_bytes=24 * 2**20),
        cost_estimate=pl.CostEstimate(
            flops=2 * (parts * each + slots) * width * rank_w,
            bytes_accessed=2 * width * (2 * parts * each + 2 * rank_w + slots),
            transcendentals=0,
        ),
        name="delta",
    )(*[blocks[i] for i in at_slot], pick, down, up)


def base_kernel(a_ref, w_ref, order_ref, out_ref):
    width = a_ref.shape[1]
    cuts = 8
    deep = width // cuts
    for i in range(cuts):
        at = slice(i * deep, (i + 1) * deep)
        part = dot(dot(order_ref[...], a_ref[:, at]).astype(BF16), w_ref[at, :])
        out_ref[...] = part if i == 0 else out_ref[...] + part


def base_part(gathered, out_weight, order):
    total, width = gathered.shape
    cols = out_weight.shape[1]
    vmem = pl.BlockSpec(memory_space=pltpu.VMEM)
    return pl.pallas_call(
        base_kernel,
        out_shape=jax.ShapeDtypeStruct((total, cols), F32),
        in_specs=[vmem] * 3,
        out_specs=vmem,
        compiler_params=pltpu.CompilerParams(vmem_limit_bytes=24 * 2**20),
        cost_estimate=pl.CostEstimate(
            flops=2 * total * width * (cols + total),
            bytes_accessed=2 * width * (total + cols) + 4 * total * cols,
            transcendentals=0,
        ),
        name="base",
    )(gathered, out_weight, order)


def join_kernel(base_ref, place_ref, delta_ref, out_ref):
    steps, requests, cols = out_ref.shape
    parts, slots, _ = delta_ref.shape
    delta = dot(place_ref[...], delta_ref[...].reshape(parts * slots, cols))
    result = (base_ref[...] + delta).astype(BF16)
    for t in range(steps):
        out_ref[t] = result[t * requests : (t + 1) * requests]


def join(base, place, delta, steps):
    total, cols = base.shape
    vmem = pl.BlockSpec(memory_space=pltpu.VMEM)
    return pl.pallas_call(
        join_kernel,
        out_shape=jax.ShapeDtypeStruct((steps, total // steps, cols), BF16),
        in_specs=[vmem] * 3,
        out_specs=vmem,
        compiler_params=pltpu.CompilerParams(vmem_limit_bytes=24 * 2**20),
        name="join",
    )(base, place, delta)


def per_device(
    queries,
    new_keys,
    new_values,
    cache_keys,
    cache_values,
    kv_len,
    adapter_rows,
    adapter_rank,
    adapter_owner,
    out_weight,
    store_down,
    store_up,
):
    parts = lax.axis_size("tensor")
    steps, rows, width = queries.shape
    tables = (adapter_rows, adapter_rank, adapter_owner)
    attended, down, up, pick, place, order = attend(
        queries,
        new_keys,
        new_values,
        cache_keys,
        cache_values,
        kv_len,
        store_down,
        store_up,
        tables,
        parts,
    )
    blocks = gather(attended, parts)
    send, gathered = deltas(blocks, pick, down, up)
    turned = [list(range(parts))[::-1]]
    delta = lax.all_to_all(send, "tensor", 0, 0, axis_index_groups=turned, tiled=True)
    base = base_part(gathered, out_weight, order)
    return join(base, place, delta, steps)


def solution(mesh):
    in_specs = (
        P(None, ("groups", "tensor"), None),
        P(None, ("groups", "tensor"), None),
        P(None, ("groups", "tensor"), None),
        P(("groups", "tensor"), None, None),
        P(("groups", "tensor"), None, None),
        P(("groups", "tensor")),
        P("groups"),
        P(),
        P(),
        P(None, "tensor"),
        P("tensor", None, None),
        P("tensor", None, None),
    )
    out_specs = P(None, "groups", "tensor")
    return jax.shard_map(
        per_device, mesh=mesh, in_specs=in_specs, out_specs=out_specs, check_vma=False
    )
```

```python
import functools
import math

import jax
import jax.numpy as jnp
from jax import lax
from jax.experimental import pallas as pl
from jax.experimental.pallas import tpu as pltpu
from jax.sharding import PartitionSpec as P

HQ = 64
KVH = 8
HD = 128
GROUP = HQ // KVH
MOST = 8
RING = 16
ORDER = [0, 1, 2, 3, 4, 5, 6, 7, 8, 9, 10, 11, 12, 13, 14, 15]
EXCHANGE = [11, 10, 9, 8, 15, 14, 13, 12, 7, 6, 5, 4, 3, 2, 1, 0]
F32 = jnp.float32
BF16 = jnp.bfloat16
NT = (((1,), (1,)), ((), ()))


def in_hbm(*arrays):
    return [pltpu.with_memory_space_constraint(a, pltpu.HBM) for a in arrays]


def iota(shape, dim):
    return lax.broadcasted_iota(jnp.int32, shape, dim)


def one_hot(mask):
    return mask.astype(F32).astype(BF16)


def dot(a, b):
    return jnp.dot(a, b, preferred_element_type=F32)


def dot_nt(a, b):
    return lax.dot_general(a, b, NT, preferred_element_type=F32)


def sender(slot, me, parts):
    return me ^ slot if parts == RING else slot


def exchange_order(parts):
    return EXCHANGE if parts == RING else [*range(parts)]


def write_plan(rows, count_ref, rank_ref, owner_ref, pick_ref, place_ref, order_ref):
    me = lax.axis_index("tensor")
    slots, total = pick_ref.shape
    steps = slots // MOST
    each = steps * rows
    parts = total // each
    requests = parts * rows

    def adapter_of(block):
        first = jnp.zeros(block.shape, jnp.int32)
        amount = jnp.zeros(block.shape, jnp.int32)
        start = jnp.int32(0)
        for a in range(count_ref.shape[0]):
            owned = (owner_ref[a] <= block) & (block < owner_ref[a] + rank_ref[a])
            first = jnp.where(owned, start, first)
            amount = jnp.where(owned, count_ref[a], amount)
            start = start + count_ref[a]
        return first, amount

    def row_place(index):
        device = sender(index // each, me, parts)
        return device * rows + index % rows, (index % each) // rows

    row = iota((slots, 1), 0)
    nth = row % MOST
    first, amount = adapter_of(jnp.zeros_like(row) + me)
    request, step = row_place(iota((1, total), 1))
    pick = (request == first + nth) & (nth < amount) & (step == row // MOST)
    pick_ref[...] = one_hot(pick)

    request, step = row_place(iota((1, total), 1))
    order_ref[...] = one_hot(iota((total, total), 0) == step * requests + request)

    entry = iota((1, parts * slots), 1)
    nth = entry % MOST
    source = jnp.zeros_like(entry)
    for i, device in enumerate(exchange_order(parts)):
        source = jnp.where(entry // slots == i, device, source)
    first, amount = adapter_of(source)
    goal = jnp.where(nth < amount, (entry % slots) // MOST * requests + first + nth, -1)
    place_ref[...] = one_hot(iota((total, parts * slots), 0) == goal)


def attend_kernel(
    len_hbm, q_hbm, nk_hbm, nv_hbm, k_hbm, v_hbm, d_hbm, u_hbm, count_hbm, rank_hbm, owner_hbm,
    out_ref, d_ref, u_ref, pick_ref, place_ref, order_ref,
    len_ref, count_ref, rank_ref, owner_ref, q_ref, nk_ref, nv_ref, k_ref, v_ref, turned_q, nks, nvs, raw, mixed,
    small_sems, sems, store_sems,
):
    steps, rows, width = q_ref.shape
    cache = k_ref.shape[1]
    both = steps * rows
    pack = steps * GROUP
    cuts = sems.shape[2]

    small = [
        pltpu.make_async_copy(src, dst, small_sems.at[i])
        for i, (src, dst) in enumerate(
            (
                (q_hbm, q_ref),
                (nk_hbm, nk_ref),
                (nv_hbm, nv_ref),
                (len_hbm, len_ref),
                (count_hbm, count_ref),
                (rank_hbm, rank_ref),
                (owner_hbm, owner_ref),
            )
        )
    ]
    pieces = [pl.ds(i * (cache // cuts), cache // cuts) for i in range(cuts)]
    keys, values = [
        [
            [
                pltpu.make_async_copy(src.at[r, at], dst.at[r, at], sems.at[r, j, i])
                for i, at in enumerate(pieces)
            ]
            for r in range(rows)
        ]
        for j, (src, dst) in enumerate(((k_hbm, k_ref), (v_hbm, v_ref)))
    ]
    deep = d_ref.shape[0] // store_sems.shape[1]
    store = [
        pltpu.make_async_copy(
            src.at[0, pl.ds(i * deep, deep)], dst.at[pl.ds(i * deep, deep)], store_sems.at[j, i]
        )
        for j, (src, dst) in enumerate(((d_hbm, d_ref), (u_hbm, u_ref)))
        for i in range(store_sems.shape[1])
    ]
    queue = [keys[0], values[0], keys[1]]
    for r in range(rows):
        queue += [values[r + 1]] if r + 1 < rows else [store]
        queue += [keys[r + 2]] if r + 2 < rows else []
    for copy in small + queue[0] + queue[1] + queue[2]:
        copy.start()
    for copy in small:
        copy.wait()
    for copy in queue[3] + queue[4]:
        copy.start()
    queue = queue[5:]

    flat = jnp.concatenate([q_ref[t].astype(F32) for t in range(steps)], axis=0)
    heads = []
    for k in range(KVH):
        group = jnp.stack(
            [flat[:, (k * GROUP + g) * HD : (k * GROUP + g + 1) * HD] for g in range(GROUP)]
        )
        heads.append(jnp.swapaxes(group, 0, 1))
    column = iota((HD, KVH * pack), 1)
    for r in range(rows):
        mine = jnp.concatenate(
            [heads[k][t * rows + r] for k in range(KVH) for t in range(steps)], axis=0
        )
        mine = jnp.transpose(mine)
        for k in range(KVH):
            turned_q[r, k * HD : (k + 1) * HD, :] = jnp.where(
                column // pack == k, mine, 0.0
            ).astype(BF16)
    for src, dst in ((nk_ref, nks), (nv_ref, nvs)):
        fresh = [src[t].astype(F32) for t in range(steps)]
        fresh.append(jnp.zeros((16 - both, src.shape[2]), F32))
        dst[...] = jnp.concatenate(fresh, axis=0).astype(BF16)

    write_plan(rows, count_ref, rank_ref, owner_ref, pick_ref, place_ref, order_ref)

    rate = HD ** (-0.5) * math.log2(math.e)
    pairs = [
        (slice(k * pack, (k + 2) * pack), slice(k * HD, (k + 2) * HD)) for k in range(0, KVH, 2)
    ]
    for turn in range(rows + 1):
        if turn < rows:
            for copy in keys[turn]:
                copy.wait()
        if turn > 0:
            for copy in values[turn - 1]:
                copy.wait()
        for copies in queue[2 * turn : 2 * turn + 2]:
            for copy in copies:
                copy.start()
        if turn < rows:
            raw[turn % 2] = dot(k_ref[turn], turned_q[turn])
        if turn == 0:
            continue
        r = turn - 1
        fresh = dot(nks[...], turned_q[r])
        slot = iota(fresh.shape, 0)
        step = (iota(fresh.shape, 1) // GROUP) % steps
        seen = (slot < both) & (slot % rows == r) & (slot // rows <= step)
        fresh = jnp.where(seen, fresh, -jnp.inf)
        older = raw[r % 2]
        older = jnp.where(iota(older.shape, 0) < len_ref[r], older, -jnp.inf)
        top = jnp.maximum(
            jnp.max(older, axis=0, keepdims=True), jnp.max(fresh, axis=0, keepdims=True)
        )
        e_older = jnp.exp2((older - top) * rate)
        e_fresh = jnp.exp2((fresh - top) * rate)
        total = jnp.sum(e_older, axis=0, keepdims=True) + jnp.sum(e_fresh, axis=0, keepdims=True)
        inverse = 1.0 / total
        p_older = jnp.transpose((e_older * inverse).astype(BF16))
        p_fresh = jnp.transpose((e_fresh * inverse).astype(BF16))
        for k, (own, cols_k) in zip(range(0, KVH, 2), pairs):
            pair = dot(p_older[own], v_ref[r, :, cols_k]) + dot(p_fresh[own], nvs[:, cols_k])
            mixed[r, k] = pair[:pack, :HD]
            mixed[r, k + 1] = pair[pack:, HD:]

    for k in range(KVH):
        turned = jnp.stack(
            [
                mixed[r, k, t * GROUP : (t + 1) * GROUP, :]
                for t in range(steps)
                for r in range(rows)
            ]
        )
        heads = jnp.swapaxes(turned, 0, 1)
        for g in range(GROUP):
            at = (k * GROUP + g) * HD
            out_ref[:, at : at + HD] = heads[g].astype(BF16)
    for copy in store:
        copy.wait()


def attend(
    queries,
    new_keys,
    new_values,
    cache_keys,
    cache_values,
    kv_len,
    store_down,
    store_up,
    tables,
    parts,
):
    steps, rows, width = queries.shape
    cache, kv_width = cache_keys.shape[1:]
    pack = steps * GROUP
    rank_w = store_down.shape[2]
    total = parts * steps * rows
    slots = steps * MOST
    shapes = [(steps * rows, width), (width, rank_w), (width, rank_w)]
    shapes += [(slots, total), (total, parts * slots), (total, total)]
    return pl.pallas_call(
        attend_kernel,
        out_shape=[jax.ShapeDtypeStruct(shape, BF16) for shape in shapes],
        in_specs=[pl.BlockSpec(memory_space=pl.ANY)] * 11,
        out_specs=[pl.BlockSpec(memory_space=pltpu.VMEM)] * len(shapes),
        scratch_shapes=[
            pltpu.SMEM(kv_len.shape, jnp.int32),
            *[pltpu.SMEM(table.shape, jnp.int32) for table in tables],
            pltpu.VMEM(queries.shape, BF16),
            pltpu.VMEM(new_keys.shape, BF16),
            pltpu.VMEM(new_values.shape, BF16),
            pltpu.VMEM(cache_keys.shape, BF16),
            pltpu.VMEM(cache_values.shape, BF16),
            pltpu.VMEM((rows, kv_width, KVH * pack), BF16),
            pltpu.VMEM((16, kv_width), BF16),
            pltpu.VMEM((16, kv_width), BF16),
            pltpu.VMEM((2, cache, KVH * pack), F32),
            pltpu.VMEM((rows, KVH, pack, HD), F32),
            pltpu.SemaphoreType.DMA((7,)),
            pltpu.SemaphoreType.DMA((rows, 2, 2)),
            pltpu.SemaphoreType.DMA((2, 4)),
        ],
        compiler_params=pltpu.CompilerParams(vmem_limit_bytes=32 * 2**20),
        cost_estimate=pl.CostEstimate(
            flops=4 * rows * steps * HQ * cache * HD,
            bytes_accessed=4 * rows * cache * kv_width,
            transcendentals=rows * steps * HQ * cache,
        ),
        name="attend",
    )(
        *in_hbm(
            kv_len,
            queries,
            new_keys,
            new_values,
            cache_keys,
            cache_values,
            store_down,
            store_up,
            *tables,
        )
    )


def swap(x, bits, parts):
    return lax.ppermute(x, "tensor", [(i, i ^ bits) for i in range(parts)])


def gather(block, parts):
    if parts != RING:
        whole = lax.all_gather(block, "tensor")
        return [whole[i] for i in range(parts)]
    core, y, near, far = 1, 2, 4, 8
    held = {0: block}
    held[far] = swap(block, far, parts)
    held[near] = swap(block, near, parts)
    held[y] = swap(block, y, parts)
    held[near | y] = swap(block, near | y, parts)
    held[far | y] = swap(held[far], y, parts)
    held[far | near | y] = swap(held[far], near | y, parts)
    held[far | near] = swap(held[far], near, parts)
    for slot in list(held):
        held[slot | core] = swap(held[slot], core, parts)
    return [held[slot] for slot in range(parts)]


def delta_kernel(at_slot, *refs):
    (*blocks, pick_ref, d_ref, u_ref, out_ref, rows_ref) = refs
    blocks = [blocks[at_slot.index(i)] for i in range(len(blocks))]
    parts, slots, cols = out_ref.shape
    each, width = blocks[0].shape
    cuts = 8
    deep = width // cuts
    low = jnp.zeros((parts * each, d_ref.shape[1]), F32)
    for i in range(cuts):
        at = slice(i * deep, (i + 1) * deep)
        piece = jnp.concatenate([b[:, at] for b in blocks], axis=0)
        rows_ref[:, at] = piece
        low = low + dot(piece, d_ref[at, :])
    chosen = dot(pick_ref[...], low.astype(BF16)).astype(BF16)
    for p, device in enumerate(exchange_order(parts)):
        at = device * cols
        out_ref[p] = dot_nt(chosen, u_ref[at : at + cols, :]).astype(BF16)


def deltas(blocks, pick, down, up):
    parts = len(blocks)
    each, width = blocks[0].shape
    slots = pick.shape[0]
    rank_w = down.shape[1]
    vmem = pl.BlockSpec(memory_space=pltpu.VMEM)
    at_slot = ORDER if parts == RING else [*range(parts)]
    return pl.pallas_call(
        functools.partial(delta_kernel, at_slot),
        out_shape=(
            jax.ShapeDtypeStruct((parts, slots, width // parts), BF16),
            jax.ShapeDtypeStruct((parts * each, width), BF16),
        ),
        in_specs=[vmem] * (3 + parts),
        out_specs=(vmem, vmem),
        compiler_params=pltpu.CompilerParams(vmem_limit_bytes=24 * 2**20),
        cost_estimate=pl.CostEstimate(
            flops=2 * (parts * each + slots) * width * rank_w,
            bytes_accessed=2 * width * (2 * parts * each + 2 * rank_w + slots),
            transcendentals=0,
        ),
        name="delta",
    )(*[blocks[i] for i in at_slot], pick, down, up)


def base_kernel(a_ref, w_ref, order_ref, out_ref):
    width = a_ref.shape[1]
    cuts = 8
    deep = width // cuts
    for i in range(cuts):
        at = slice(i * deep, (i + 1) * deep)
        part = dot(dot(order_ref[...], a_ref[:, at]).astype(BF16), w_ref[at, :])
        out_ref[...] = part if i == 0 else out_ref[...] + part


def base_part(gathered, out_weight, order):
    total, width = gathered.shape
    cols = out_weight.shape[1]
    vmem = pl.BlockSpec(memory_space=pltpu.VMEM)
    return pl.pallas_call(
        base_kernel,
        out_shape=jax.ShapeDtypeStruct((total, cols), F32),
        in_specs=[vmem] * 3,
        out_specs=vmem,
        compiler_params=pltpu.CompilerParams(vmem_limit_bytes=24 * 2**20),
        cost_estimate=pl.CostEstimate(
            flops=2 * total * width * (cols + total),
            bytes_accessed=2 * width * (total + cols) + 4 * total * cols,
            transcendentals=0,
        ),
        name="base",
    )(gathered, out_weight, order)


def join_kernel(base_ref, place_ref, delta_ref, out_ref):
    steps, requests, cols = out_ref.shape
    parts, slots, _ = delta_ref.shape
    delta = dot(place_ref[...], delta_ref[...].reshape(parts * slots, cols))
    result = (base_ref[...] + delta).astype(BF16)
    for t in range(steps):
        out_ref[t] = result[t * requests : (t + 1) * requests]


def join(base, place, delta, steps):
    total, cols = base.shape
    vmem = pl.BlockSpec(memory_space=pltpu.VMEM)
    return pl.pallas_call(
        join_kernel,
        out_shape=jax.ShapeDtypeStruct((steps, total // steps, cols), BF16),
        in_specs=[vmem] * 3,
        out_specs=vmem,
        compiler_params=pltpu.CompilerParams(vmem_limit_bytes=24 * 2**20),
        name="join",
    )(base, place, delta)


def per_device(
    queries,
    new_keys,
    new_values,
    cache_keys,
    cache_values,
    kv_len,
    adapter_rows,
    adapter_rank,
    adapter_owner,
    out_weight,
    store_down,
    store_up,
):
    parts = lax.axis_size("tensor")
    steps, rows, width = queries.shape
    tables = (adapter_rows, adapter_rank, adapter_owner)
    attended, down, up, pick, place, order = attend(
        queries,
        new_keys,
        new_values,
        cache_keys,
        cache_values,
        kv_len,
        store_down,
        store_up,
        tables,
        parts,
    )
    blocks = gather(attended, parts)
    send, gathered = deltas(blocks, pick, down, up)
    groups = [exchange_order(parts)]
    delta = lax.all_to_all(send, "tensor", 0, 0, axis_index_groups=groups, tiled=True)
    base = base_part(gathered, out_weight, order)
    return join(base, place, delta, steps)


def solution(mesh):
    in_specs = (
        P(None, ("groups", "tensor"), None),
        P(None, ("groups", "tensor"), None),
        P(None, ("groups", "tensor"), None),
        P(("groups", "tensor"), None, None),
        P(("groups", "tensor"), None, None),
        P(("groups", "tensor")),
        P("groups"),
        P(),
        P(),
        P(None, "tensor"),
        P("tensor", None, None),
        P("tensor", None, None),
    )
    out_specs = P(None, "groups", "tensor")
    return jax.shard_map(
        per_device, mesh=mesh, in_specs=in_specs, out_specs=out_specs, check_vma=False
    )
```

```python
import functools
import math

import jax
import jax.numpy as jnp
from jax import lax
from jax.experimental import pallas as pl
from jax.experimental.pallas import tpu as pltpu
from jax.sharding import PartitionSpec as P

HQ = 64
KVH = 8
HD = 128
GROUP = HQ // KVH
MOST = 8
RING = 16
ORDER = [0, 1, 2, 3, 4, 5, 6, 7, 8, 9, 10, 11, 12, 13, 14, 15]
EXCHANGE = [8, 9, 10, 11, 12, 13, 14, 15, 4, 5, 6, 7, 0, 1, 2, 3]
F32 = jnp.float32
BF16 = jnp.bfloat16
NT = (((1,), (1,)), ((), ()))


def in_hbm(*arrays):
    return [pltpu.with_memory_space_constraint(a, pltpu.HBM) for a in arrays]


def iota(shape, dim):
    return lax.broadcasted_iota(jnp.int32, shape, dim)


def one_hot(mask):
    return mask.astype(F32).astype(BF16)


def dot(a, b):
    return jnp.dot(a, b, preferred_element_type=F32)


def dot_nt(a, b):
    return lax.dot_general(a, b, NT, preferred_element_type=F32)


def sender(slot, me, parts):
    return me ^ slot if parts == RING else slot


def exchange_order(parts):
    return EXCHANGE if parts == RING else [*range(parts)]


def write_plan(rows, count_ref, rank_ref, owner_ref, pick_ref, place_ref, order_ref):
    me = lax.axis_index("tensor")
    slots, total = pick_ref.shape
    steps = slots // MOST
    each = steps * rows
    parts = total // each
    requests = parts * rows

    def adapter_of(block):
        first = jnp.zeros(block.shape, jnp.int32)
        amount = jnp.zeros(block.shape, jnp.int32)
        start = jnp.int32(0)
        for a in range(count_ref.shape[0]):
            owned = (owner_ref[a] <= block) & (block < owner_ref[a] + rank_ref[a])
            first = jnp.where(owned, start, first)
            amount = jnp.where(owned, count_ref[a], amount)
            start = start + count_ref[a]
        return first, amount

    def row_place(index):
        device = sender(index // each, me, parts)
        return device * rows + index % rows, (index % each) // rows

    row = iota((slots, 1), 0)
    nth = row % MOST
    first, amount = adapter_of(jnp.zeros_like(row) + me)
    request, step = row_place(iota((1, total), 1))
    pick = (request == first + nth) & (nth < amount) & (step == row // MOST)
    pick_ref[...] = one_hot(pick)

    request, step = row_place(iota((1, total), 1))
    order_ref[...] = one_hot(iota((total, total), 0) == step * requests + request)

    entry = iota((1, parts * slots), 1)
    nth = entry % MOST
    source = jnp.zeros_like(entry)
    for i, device in enumerate(exchange_order(parts)):
        source = jnp.where(entry // slots == i, device, source)
    first, amount = adapter_of(source)
    goal = jnp.where(nth < amount, (entry % slots) // MOST * requests + first + nth, -1)
    place_ref[...] = one_hot(iota((total, parts * slots), 0) == goal)


def attend_kernel(
    len_hbm, q_hbm, nk_hbm, nv_hbm, k_hbm, v_hbm, d_hbm, u_hbm, count_hbm, rank_hbm, owner_hbm,
    out_ref, d_ref, u_ref, pick_ref, place_ref, order_ref,
    len_ref, count_ref, rank_ref, owner_ref, q_ref, nk_ref, nv_ref, k_ref, v_ref, turned_q, nks, nvs, raw, mixed,
    small_sems, sems, store_sems,
):
    steps, rows, width = q_ref.shape
    cache = k_ref.shape[1]
    both = steps * rows
    pack = steps * GROUP
    cuts = sems.shape[2]

    small = [
        pltpu.make_async_copy(src, dst, small_sems.at[i])
        for i, (src, dst) in enumerate(
            (
                (q_hbm, q_ref),
                (nk_hbm, nk_ref),
                (nv_hbm, nv_ref),
                (len_hbm, len_ref),
                (count_hbm, count_ref),
                (rank_hbm, rank_ref),
                (owner_hbm, owner_ref),
            )
        )
    ]
    pieces = [pl.ds(i * (cache // cuts), cache // cuts) for i in range(cuts)]
    keys, values = [
        [
            [
                pltpu.make_async_copy(src.at[r, at], dst.at[r, at], sems.at[r, j, i])
                for i, at in enumerate(pieces)
            ]
            for r in range(rows)
        ]
        for j, (src, dst) in enumerate(((k_hbm, k_ref), (v_hbm, v_ref)))
    ]
    deep = d_ref.shape[0] // store_sems.shape[1]
    store = [
        pltpu.make_async_copy(
            src.at[0, pl.ds(i * deep, deep)], dst.at[pl.ds(i * deep, deep)], store_sems.at[j, i]
        )
        for j, (src, dst) in enumerate(((d_hbm, d_ref), (u_hbm, u_ref)))
        for i in range(store_sems.shape[1])
    ]
    queue = [keys[0], values[0], keys[1]]
    for r in range(rows):
        queue += [values[r + 1]] if r + 1 < rows else [store]
        queue += [keys[r + 2]] if r + 2 < rows else []
    for copy in small + queue[0] + queue[1] + queue[2]:
        copy.start()
    for copy in small:
        copy.wait()
    for copy in queue[3] + queue[4]:
        copy.start()
    queue = queue[5:]

    flat = jnp.concatenate([q_ref[t].astype(F32) for t in range(steps)], axis=0)
    heads = []
    for k in range(KVH):
        group = jnp.stack(
            [flat[:, (k * GROUP + g) * HD : (k * GROUP + g + 1) * HD] for g in range(GROUP)]
        )
        heads.append(jnp.swapaxes(group, 0, 1))
    column = iota((HD, KVH * pack), 1)
    for r in range(rows):
        mine = jnp.concatenate(
            [heads[k][t * rows + r] for k in range(KVH) for t in range(steps)], axis=0
        )
        mine = jnp.transpose(mine)
        for k in range(KVH):
            turned_q[r, k * HD : (k + 1) * HD, :] = jnp.where(
                column // pack == k, mine, 0.0
            ).astype(BF16)
    for src, dst in ((nk_ref, nks), (nv_ref, nvs)):
        fresh = [src[t].astype(F32) for t in range(steps)]
        fresh.append(jnp.zeros((16 - both, src.shape[2]), F32))
        dst[...] = jnp.concatenate(fresh, axis=0).astype(BF16)

    write_plan(rows, count_ref, rank_ref, owner_ref, pick_ref, place_ref, order_ref)

    rate = HD ** (-0.5) * math.log2(math.e)
    pairs = [
        (slice(k * pack, (k + 2) * pack), slice(k * HD, (k + 2) * HD)) for k in range(0, KVH, 2)
    ]
    for turn in range(rows + 1):
        if turn < rows:
            for copy in keys[turn]:
                copy.wait()
        if turn > 0:
            for copy in values[turn - 1]:
                copy.wait()
        for copies in queue[2 * turn : 2 * turn + 2]:
            for copy in copies:
                copy.start()
        if turn < rows:
            raw[turn % 2] = dot(k_ref[turn], turned_q[turn])
        if turn == 0:
            continue
        r = turn - 1
        fresh = dot(nks[...], turned_q[r])
        slot = iota(fresh.shape, 0)
        step = (iota(fresh.shape, 1) // GROUP) % steps
        seen = (slot < both) & (slot % rows == r) & (slot // rows <= step)
        fresh = jnp.where(seen, fresh, -jnp.inf)
        older = raw[r % 2]
        older = jnp.where(iota(older.shape, 0) < len_ref[r], older, -jnp.inf)
        top = jnp.maximum(
            jnp.max(older, axis=0, keepdims=True), jnp.max(fresh, axis=0, keepdims=True)
        )
        e_older = jnp.exp2((older - top) * rate)
        e_fresh = jnp.exp2((fresh - top) * rate)
        total = jnp.sum(e_older, axis=0, keepdims=True) + jnp.sum(e_fresh, axis=0, keepdims=True)
        inverse = 1.0 / total
        p_older = jnp.transpose((e_older * inverse).astype(BF16))
        p_fresh = jnp.transpose((e_fresh * inverse).astype(BF16))
        for k, (own, cols_k) in zip(range(0, KVH, 2), pairs):
            pair = dot(p_older[own], v_ref[r, :, cols_k]) + dot(p_fresh[own], nvs[:, cols_k])
            mixed[r, k] = pair[:pack, :HD]
            mixed[r, k + 1] = pair[pack:, HD:]

    for k in range(KVH):
        turned = jnp.stack(
            [
                mixed[r, k, t * GROUP : (t + 1) * GROUP, :]
                for t in range(steps)
                for r in range(rows)
            ]
        )
        heads = jnp.swapaxes(turned, 0, 1)
        for g in range(GROUP):
            at = (k * GROUP + g) * HD
            out_ref[:, at : at + HD] = heads[g].astype(BF16)
    for copy in store:
        copy.wait()


def attend(
    queries,
    new_keys,
    new_values,
    cache_keys,
    cache_values,
    kv_len,
    store_down,
    store_up,
    tables,
    parts,
):
    steps, rows, width = queries.shape
    cache, kv_width = cache_keys.shape[1:]
    pack = steps * GROUP
    rank_w = store_down.shape[2]
    total = parts * steps * rows
    slots = steps * MOST
    shapes = [(steps * rows, width), (width, rank_w), (width, rank_w)]
    shapes += [(slots, total), (total, parts * slots), (total, total)]
    return pl.pallas_call(
        attend_kernel,
        out_shape=[jax.ShapeDtypeStruct(shape, BF16) for shape in shapes],
        in_specs=[pl.BlockSpec(memory_space=pl.ANY)] * 11,
        out_specs=[pl.BlockSpec(memory_space=pltpu.VMEM)] * len(shapes),
        scratch_shapes=[
            pltpu.SMEM(kv_len.shape, jnp.int32),
            *[pltpu.SMEM(table.shape, jnp.int32) for table in tables],
            pltpu.VMEM(queries.shape, BF16),
            pltpu.VMEM(new_keys.shape, BF16),
            pltpu.VMEM(new_values.shape, BF16),
            pltpu.VMEM(cache_keys.shape, BF16),
            pltpu.VMEM(cache_values.shape, BF16),
            pltpu.VMEM((rows, kv_width, KVH * pack), BF16),
            pltpu.VMEM((16, kv_width), BF16),
            pltpu.VMEM((16, kv_width), BF16),
            pltpu.VMEM((2, cache, KVH * pack), F32),
            pltpu.VMEM((rows, KVH, pack, HD), F32),
            pltpu.SemaphoreType.DMA((7,)),
            pltpu.SemaphoreType.DMA((rows, 2, 2)),
            pltpu.SemaphoreType.DMA((2, 4)),
        ],
        compiler_params=pltpu.CompilerParams(vmem_limit_bytes=32 * 2**20),
        cost_estimate=pl.CostEstimate(
            flops=4 * rows * steps * HQ * cache * HD,
            bytes_accessed=4 * rows * cache * kv_width,
            transcendentals=rows * steps * HQ * cache,
        ),
        name="attend",
    )(
        *in_hbm(
            kv_len,
            queries,
            new_keys,
            new_values,
            cache_keys,
            cache_values,
            store_down,
            store_up,
            *tables,
        )
    )


def swap(x, bits, parts):
    return lax.ppermute(x, "tensor", [(i, i ^ bits) for i in range(parts)])


def gather(block, parts):
    if parts != RING:
        whole = lax.all_gather(block, "tensor")
        return [whole[i] for i in range(parts)]
    core, y, near, far = 1, 2, 4, 8
    held = {0: block}
    held[far] = swap(block, far, parts)
    held[near] = swap(block, near, parts)
    held[y] = swap(block, y, parts)
    held[near | y] = swap(block, near | y, parts)
    held[far | y] = swap(held[far], y, parts)
    held[far | near | y] = swap(held[far], near | y, parts)
    held[far | near] = swap(held[far], near, parts)
    for slot in list(held):
        held[slot | core] = swap(held[slot], core, parts)
    return [held[slot] for slot in range(parts)]


def delta_kernel(at_slot, *refs):
    (*blocks, pick_ref, d_ref, u_ref, out_ref, rows_ref) = refs
    blocks = [blocks[at_slot.index(i)] for i in range(len(blocks))]
    parts, slots, cols = out_ref.shape
    each, width = blocks[0].shape
    cuts = 8
    deep = width // cuts
    low = jnp.zeros((parts * each, d_ref.shape[1]), F32)
    for i in range(cuts):
        at = slice(i * deep, (i + 1) * deep)
        piece = jnp.concatenate([b[:, at] for b in blocks], axis=0)
        rows_ref[:, at] = piece
        low = low + dot(piece, d_ref[at, :])
    chosen = dot(pick_ref[...], low.astype(BF16)).astype(BF16)
    for p, device in enumerate(exchange_order(parts)):
        at = device * cols
        out_ref[p] = dot_nt(chosen, u_ref[at : at + cols, :]).astype(BF16)


def deltas(blocks, pick, down, up):
    parts = len(blocks)
    each, width = blocks[0].shape
    slots = pick.shape[0]
    rank_w = down.shape[1]
    vmem = pl.BlockSpec(memory_space=pltpu.VMEM)
    at_slot = ORDER if parts == RING else [*range(parts)]
    return pl.pallas_call(
        functools.partial(delta_kernel, at_slot),
        out_shape=(
            jax.ShapeDtypeStruct((parts, slots, width // parts), BF16),
            jax.ShapeDtypeStruct((parts * each, width), BF16),
        ),
        in_specs=[vmem] * (3 + parts),
        out_specs=(vmem, vmem),
        compiler_params=pltpu.CompilerParams(vmem_limit_bytes=24 * 2**20),
        cost_estimate=pl.CostEstimate(
            flops=2 * (parts * each + slots) * width * rank_w,
            bytes_accessed=2 * width * (2 * parts * each + 2 * rank_w + slots),
            transcendentals=0,
        ),
        name="delta",
    )(*[blocks[i] for i in at_slot], pick, down, up)


def base_kernel(a_ref, order_ref, w_hbm, out_ref, w_ref, sems):
    width = a_ref.shape[1]
    cuts = sems.shape[0]
    deep = width // cuts
    copies = []
    for i in range(cuts):
        at = pl.ds(i * deep, deep)
        copies.append(pltpu.make_async_copy(w_hbm.at[at], w_ref.at[at], sems.at[i]))
        copies[-1].start()
    for i in range(cuts):
        at = slice(i * deep, (i + 1) * deep)
        rows = dot(order_ref[...], a_ref[:, at]).astype(BF16)
        copies[i].wait()
        part = dot(rows, w_ref[at, :])
        out_ref[...] = part if i == 0 else out_ref[...] + part


def base_part(gathered, out_weight, order):
    total, width = gathered.shape
    cols = out_weight.shape[1]
    vmem = pl.BlockSpec(memory_space=pltpu.VMEM)
    return pl.pallas_call(
        base_kernel,
        out_shape=jax.ShapeDtypeStruct((total, cols), F32),
        in_specs=[vmem] * 2 + [pl.BlockSpec(memory_space=pl.ANY)],
        out_specs=vmem,
        scratch_shapes=[pltpu.VMEM(out_weight.shape, BF16), pltpu.SemaphoreType.DMA((8,))],
        compiler_params=pltpu.CompilerParams(vmem_limit_bytes=24 * 2**20),
        cost_estimate=pl.CostEstimate(
            flops=2 * total * width * (cols + total),
            bytes_accessed=2 * width * (total + cols) + 4 * total * cols,
            transcendentals=0,
        ),
        name="base",
    )(gathered, order, *in_hbm(out_weight))


def join_kernel(base_ref, place_ref, delta_ref, out_ref):
    steps, requests, cols = out_ref.shape
    parts, slots, _ = delta_ref.shape
    delta = dot(place_ref[...], delta_ref[...].reshape(parts * slots, cols))
    result = (base_ref[...] + delta).astype(BF16)
    for t in range(steps):
        out_ref[t] = result[t * requests : (t + 1) * requests]


def join(base, place, delta, steps):
    total, cols = base.shape
    vmem = pl.BlockSpec(memory_space=pltpu.VMEM)
    return pl.pallas_call(
        join_kernel,
        out_shape=jax.ShapeDtypeStruct((steps, total // steps, cols), BF16),
        in_specs=[vmem] * 3,
        out_specs=vmem,
        compiler_params=pltpu.CompilerParams(vmem_limit_bytes=24 * 2**20),
        name="join",
    )(base, place, delta)


def per_device(
    queries,
    new_keys,
    new_values,
    cache_keys,
    cache_values,
    kv_len,
    adapter_rows,
    adapter_rank,
    adapter_owner,
    out_weight,
    store_down,
    store_up,
):
    parts = lax.axis_size("tensor")
    steps, rows, width = queries.shape
    tables = (adapter_rows, adapter_rank, adapter_owner)
    attended, down, up, pick, place, order = attend(
        queries,
        new_keys,
        new_values,
        cache_keys,
        cache_values,
        kv_len,
        store_down,
        store_up,
        tables,
        parts,
    )
    blocks = gather(attended, parts)
    send, gathered = deltas(blocks, pick, down, up)
    groups = [exchange_order(parts)]
    delta = lax.all_to_all(send, "tensor", 0, 0, axis_index_groups=groups, tiled=True)
    base = base_part(gathered, out_weight, order)
    return join(base, place, delta, steps)


def solution(mesh):
    in_specs = (
        P(None, ("groups", "tensor"), None),
        P(None, ("groups", "tensor"), None),
        P(None, ("groups", "tensor"), None),
        P(("groups", "tensor"), None, None),
        P(("groups", "tensor"), None, None),
        P(("groups", "tensor")),
        P("groups"),
        P(),
        P(),
        P(None, "tensor"),
        P("tensor", None, None),
        P("tensor", None, None),
    )
    out_specs = P(None, "groups", "tensor")
    return jax.shard_map(
        per_device, mesh=mesh, in_specs=in_specs, out_specs=out_specs, check_vma=False
    )
```

```python
import functools
import math

import jax
import jax.numpy as jnp
from jax import lax
from jax.experimental import pallas as pl
from jax.experimental.pallas import tpu as pltpu
from jax.sharding import PartitionSpec as P

HQ = 64
KVH = 8
HD = 128
GROUP = HQ // KVH
MOST = 8
RING = 16
ORDER = [0, 1, 2, 3, 4, 5, 6, 7, 8, 9, 10, 11, 12, 13, 14, 15]
EXCHANGE = [11, 10, 9, 8, 15, 14, 13, 12, 7, 6, 5, 4, 3, 2, 1, 0]
F32 = jnp.float32
BF16 = jnp.bfloat16
NT = (((1,), (1,)), ((), ()))


def in_hbm(*arrays):
    return [pltpu.with_memory_space_constraint(a, pltpu.HBM) for a in arrays]


def iota(shape, dim):
    return lax.broadcasted_iota(jnp.int32, shape, dim)


def one_hot(mask):
    return mask.astype(F32).astype(BF16)


def dot(a, b):
    return jnp.dot(a, b, preferred_element_type=F32)


def dot_nt(a, b):
    return lax.dot_general(a, b, NT, preferred_element_type=F32)


def sender(slot, me, parts):
    return me ^ slot if parts == RING else slot


def exchange_order(parts):
    return EXCHANGE if parts == RING else [*range(parts)]


def write_plan(rows, count_ref, rank_ref, owner_ref, pick_ref, place_ref, order_ref):
    me = lax.axis_index("tensor")
    slots, total = pick_ref.shape
    steps = slots // MOST
    each = steps * rows
    parts = total // each
    requests = parts * rows

    def adapter_of(block):
        first = jnp.zeros(block.shape, jnp.int32)
        amount = jnp.zeros(block.shape, jnp.int32)
        start = jnp.int32(0)
        for a in range(count_ref.shape[0]):
            owned = (owner_ref[a] <= block) & (block < owner_ref[a] + rank_ref[a])
            first = jnp.where(owned, start, first)
            amount = jnp.where(owned, count_ref[a], amount)
            start = start + count_ref[a]
        return first, amount

    def row_place(index):
        device = sender(index // each, me, parts)
        return device * rows + index % rows, (index % each) // rows

    row = iota((slots, 1), 0)
    nth = row % MOST
    first, amount = adapter_of(jnp.zeros_like(row) + me)
    request, step = row_place(iota((1, total), 1))
    pick = (request == first + nth) & (nth < amount) & (step == row // MOST)
    pick_ref[...] = one_hot(pick)

    request, step = row_place(iota((1, total), 1))
    order_ref[...] = one_hot(iota((total, total), 0) == step * requests + request)

    entry = iota((1, parts * slots), 1)
    nth = entry % MOST
    source = jnp.zeros_like(entry)
    for i, device in enumerate(exchange_order(parts)):
        source = jnp.where(entry // slots == i, device, source)
    first, amount = adapter_of(source)
    goal = jnp.where(nth < amount, (entry % slots) // MOST * requests + first + nth, -1)
    place_ref[...] = one_hot(iota((total, parts * slots), 0) == goal)


def attend_kernel(
    len_hbm, q_hbm, nk_hbm, nv_hbm, k_hbm, v_hbm, d_hbm, u_hbm, count_hbm, rank_hbm, owner_hbm,
    out_ref, d_ref, u_ref, pick_ref, place_ref, order_ref,
    len_ref, count_ref, rank_ref, owner_ref, q_ref, nk_ref, nv_ref, k_ref, v_ref, turned_q, nks, nvs, raw, mixed,
    small_sems, sems, store_sems,
):
    steps, rows, width = q_ref.shape
    cache = k_ref.shape[1]
    both = steps * rows
    pack = steps * GROUP
    cuts = sems.shape[2]

    small = [
        pltpu.make_async_copy(src, dst, small_sems.at[i])
        for i, (src, dst) in enumerate(
            (
                (q_hbm, q_ref),
                (nk_hbm, nk_ref),
                (nv_hbm, nv_ref),
                (len_hbm, len_ref),
                (count_hbm, count_ref),
                (rank_hbm, rank_ref),
                (owner_hbm, owner_ref),
            )
        )
    ]
    pieces = [pl.ds(i * (cache // cuts), cache // cuts) for i in range(cuts)]
    keys, values = [
        [
            [
                pltpu.make_async_copy(src.at[r, at], dst.at[r, at], sems.at[r, j, i])
                for i, at in enumerate(pieces)
            ]
            for r in range(rows)
        ]
        for j, (src, dst) in enumerate(((k_hbm, k_ref), (v_hbm, v_ref)))
    ]
    deep = d_ref.shape[0] // store_sems.shape[1]
    store = [
        pltpu.make_async_copy(
            src.at[0, pl.ds(i * deep, deep)], dst.at[pl.ds(i * deep, deep)], store_sems.at[j, i]
        )
        for j, (src, dst) in enumerate(((d_hbm, d_ref), (u_hbm, u_ref)))
        for i in range(store_sems.shape[1])
    ]
    queue = [keys[0], values[0], keys[1]]
    for r in range(rows):
        queue += [values[r + 1]] if r + 1 < rows else [store]
        queue += [keys[r + 2]] if r + 2 < rows else []
    for copy in small + queue[0] + queue[1] + queue[2]:
        copy.start()
    for copy in small:
        copy.wait()
    for copy in queue[3] + queue[4]:
        copy.start()
    queue = queue[5:]

    flat = jnp.concatenate([q_ref[t].astype(F32) for t in range(steps)], axis=0)
    heads = []
    for k in range(KVH):
        group = jnp.stack(
            [flat[:, (k * GROUP + g) * HD : (k * GROUP + g + 1) * HD] for g in range(GROUP)]
        )
        heads.append(jnp.swapaxes(group, 0, 1))
    column = iota((HD, KVH * pack), 1)
    for r in range(rows):
        mine = jnp.concatenate(
            [heads[k][t * rows + r] for k in range(KVH) for t in range(steps)], axis=0
        )
        mine = jnp.transpose(mine)
        for k in range(KVH):
            turned_q[r, k * HD : (k + 1) * HD, :] = jnp.where(
                column // pack == k, mine, 0.0
            ).astype(BF16)
    for src, dst in ((nk_ref, nks), (nv_ref, nvs)):
        fresh = [src[t].astype(F32) for t in range(steps)]
        fresh.append(jnp.zeros((16 - both, src.shape[2]), F32))
        dst[...] = jnp.concatenate(fresh, axis=0).astype(BF16)

    write_plan(rows, count_ref, rank_ref, owner_ref, pick_ref, place_ref, order_ref)

    rate = HD ** (-0.5) * math.log2(math.e)
    pairs = [
        (slice(k * pack, (k + 2) * pack), slice(k * HD, (k + 2) * HD)) for k in range(0, KVH, 2)
    ]
    for turn in range(rows + 1):
        if turn < rows:
            for copy in keys[turn]:
                copy.wait()
        if turn > 0:
            for copy in values[turn - 1]:
                copy.wait()
        for copies in queue[2 * turn : 2 * turn + 2]:
            for copy in copies:
                copy.start()
        if turn < rows:
            raw[turn % 2] = dot(k_ref[turn], turned_q[turn])
        if turn == 0:
            continue
        r = turn - 1
        fresh = dot(nks[...], turned_q[r])
        slot = iota(fresh.shape, 0)
        step = (iota(fresh.shape, 1) // GROUP) % steps
        seen = (slot < both) & (slot % rows == r) & (slot // rows <= step)
        fresh = jnp.where(seen, fresh, -jnp.inf)
        older = raw[r % 2]
        older = jnp.where(iota(older.shape, 0) < len_ref[r], older, -jnp.inf)
        top = jnp.maximum(
            jnp.max(older, axis=0, keepdims=True), jnp.max(fresh, axis=0, keepdims=True)
        )
        e_older = jnp.exp2((older - top) * rate)
        e_fresh = jnp.exp2((fresh - top) * rate)
        total = jnp.sum(e_older, axis=0, keepdims=True) + jnp.sum(e_fresh, axis=0, keepdims=True)
        inverse = 1.0 / total
        p_older = jnp.transpose((e_older * inverse).astype(BF16))
        p_fresh = jnp.transpose((e_fresh * inverse).astype(BF16))
        for k, (own, cols_k) in zip(range(0, KVH, 2), pairs):
            pair = dot(p_older[own], v_ref[r, :, cols_k]) + dot(p_fresh[own], nvs[:, cols_k])
            mixed[r, k] = pair[:pack, :HD]
            mixed[r, k + 1] = pair[pack:, HD:]

    for k in range(KVH):
        turned = jnp.stack(
            [
                mixed[r, k, t * GROUP : (t + 1) * GROUP, :]
                for t in range(steps)
                for r in range(rows)
            ]
        )
        heads = jnp.swapaxes(turned, 0, 1)
        for g in range(GROUP):
            at = (k * GROUP + g) * HD
            out_ref[:, at : at + HD] = heads[g].astype(BF16)
    for copy in store:
        copy.wait()


def attend(
    queries,
    new_keys,
    new_values,
    cache_keys,
    cache_values,
    kv_len,
    store_down,
    store_up,
    tables,
    parts,
):
    steps, rows, width = queries.shape
    cache, kv_width = cache_keys.shape[1:]
    pack = steps * GROUP
    rank_w = store_down.shape[2]
    total = parts * steps * rows
    slots = steps * MOST
    shapes = [(steps * rows, width), (width, rank_w), (width, rank_w)]
    shapes += [(slots, total), (total, parts * slots), (total, total)]
    return pl.pallas_call(
        attend_kernel,
        out_shape=[jax.ShapeDtypeStruct(shape, BF16) for shape in shapes],
        in_specs=[pl.BlockSpec(memory_space=pl.ANY)] * 11,
        out_specs=[pl.BlockSpec(memory_space=pltpu.VMEM)] * len(shapes),
        scratch_shapes=[
            pltpu.SMEM(kv_len.shape, jnp.int32),
            *[pltpu.SMEM(table.shape, jnp.int32) for table in tables],
            pltpu.VMEM(queries.shape, BF16),
            pltpu.VMEM(new_keys.shape, BF16),
            pltpu.VMEM(new_values.shape, BF16),
            pltpu.VMEM(cache_keys.shape, BF16),
            pltpu.VMEM(cache_values.shape, BF16),
            pltpu.VMEM((rows, kv_width, KVH * pack), BF16),
            pltpu.VMEM((16, kv_width), BF16),
            pltpu.VMEM((16, kv_width), BF16),
            pltpu.VMEM((2, cache, KVH * pack), F32),
            pltpu.VMEM((rows, KVH, pack, HD), F32),
            pltpu.SemaphoreType.DMA((7,)),
            pltpu.SemaphoreType.DMA((rows, 2, 2)),
            pltpu.SemaphoreType.DMA((2, 4)),
        ],
        compiler_params=pltpu.CompilerParams(vmem_limit_bytes=32 * 2**20),
        cost_estimate=pl.CostEstimate(
            flops=4 * rows * steps * HQ * cache * HD,
            bytes_accessed=4 * rows * cache * kv_width,
            transcendentals=rows * steps * HQ * cache,
        ),
        name="attend",
    )(
        *in_hbm(
            kv_len,
            queries,
            new_keys,
            new_values,
            cache_keys,
            cache_values,
            store_down,
            store_up,
            *tables,
        )
    )


def swap(x, bits, parts):
    return lax.ppermute(x, "tensor", [(i, i ^ bits) for i in range(parts)])


def gather(block, parts):
    if parts != RING:
        whole = lax.all_gather(block, "tensor")
        return [whole[i] for i in range(parts)]
    core, y, near, far = 1, 2, 4, 8
    held = {0: block}
    held[far] = swap(block, far, parts)
    held[near] = swap(block, near, parts)
    held[y] = swap(block, y, parts)
    held[near | y] = swap(block, near | y, parts)
    held[far | y] = swap(held[far], y, parts)
    held[far | near | y] = swap(held[far], near | y, parts)
    held[far | near] = swap(held[far], near, parts)
    for slot in list(held):
        held[slot | core] = swap(held[slot], core, parts)
    return [held[slot] for slot in range(parts)]


def delta_kernel(at_slot, *refs):
    (*blocks, pick_ref, d_ref, u_ref, out_ref) = refs
    blocks = [blocks[at_slot.index(i)] for i in range(len(blocks))]
    parts, slots, cols = out_ref.shape
    each, width = blocks[0].shape
    cuts = 8
    deep = width // cuts
    low = jnp.zeros((parts * each, d_ref.shape[1]), F32)
    for i in range(cuts):
        at = slice(i * deep, (i + 1) * deep)
        piece = jnp.concatenate([b[:, at] for b in blocks], axis=0)
        low = low + dot(piece, d_ref[at, :])
    chosen = dot(pick_ref[...], low.astype(BF16)).astype(BF16)
    for p, device in enumerate(exchange_order(parts)):
        at = device * cols
        out_ref[p] = dot_nt(chosen, u_ref[at : at + cols, :]).astype(BF16)


def deltas(blocks, pick, down, up):
    parts = len(blocks)
    each, width = blocks[0].shape
    slots = pick.shape[0]
    rank_w = down.shape[1]
    vmem = pl.BlockSpec(memory_space=pltpu.VMEM)
    at_slot = ORDER if parts == RING else [*range(parts)]
    return pl.pallas_call(
        functools.partial(delta_kernel, at_slot),
        out_shape=jax.ShapeDtypeStruct((parts, slots, width // parts), BF16),
        in_specs=[vmem] * (3 + parts),
        out_specs=vmem,
        compiler_params=pltpu.CompilerParams(vmem_limit_bytes=24 * 2**20),
        cost_estimate=pl.CostEstimate(
            flops=2 * (parts * each + slots) * width * rank_w,
            bytes_accessed=2 * width * (parts * each + 2 * rank_w + slots),
            transcendentals=0,
        ),
        name="delta",
    )(*[blocks[i] for i in at_slot], pick, down, up)


def base_kernel(at_slot, *refs):
    (*blocks, order_ref, w_hbm, out_ref, w_ref, sems) = refs
    blocks = [blocks[at_slot.index(i)] for i in range(len(blocks))]
    width = w_ref.shape[0]
    cuts = sems.shape[0]
    deep = width // cuts
    copies = []
    for i in range(cuts):
        at = pl.ds(i * deep, deep)
        copies.append(pltpu.make_async_copy(w_hbm.at[at], w_ref.at[at], sems.at[i]))
        copies[-1].start()
    for i in range(cuts):
        at = slice(i * deep, (i + 1) * deep)
        rows = jnp.concatenate([b[:, at] for b in blocks], axis=0)
        rows = dot(order_ref[...], rows).astype(BF16)
        copies[i].wait()
        part = dot(rows, w_ref[at, :])
        out_ref[...] = part if i == 0 else out_ref[...] + part


def base_part(blocks, out_weight, order):
    parts = len(blocks)
    total = order.shape[0]
    width, cols = out_weight.shape
    vmem = pl.BlockSpec(memory_space=pltpu.VMEM)
    at_slot = ORDER if parts == RING else [*range(parts)]
    return pl.pallas_call(
        functools.partial(base_kernel, at_slot),
        out_shape=jax.ShapeDtypeStruct((total, cols), F32),
        in_specs=[vmem] * (1 + parts) + [pl.BlockSpec(memory_space=pl.ANY)],
        out_specs=vmem,
        scratch_shapes=[pltpu.VMEM(out_weight.shape, BF16), pltpu.SemaphoreType.DMA((8,))],
        compiler_params=pltpu.CompilerParams(vmem_limit_bytes=24 * 2**20),
        cost_estimate=pl.CostEstimate(
            flops=2 * total * width * (cols + total),
            bytes_accessed=2 * width * (total + cols) + 4 * total * cols,
            transcendentals=0,
        ),
        name="base",
    )(*[blocks[i] for i in at_slot], order, *in_hbm(out_weight))


def join_kernel(base_ref, place_ref, delta_ref, out_ref):
    steps, requests, cols = out_ref.shape
    parts, slots, _ = delta_ref.shape
    delta = dot(place_ref[...], delta_ref[...].reshape(parts * slots, cols))
    result = (base_ref[...] + delta).astype(BF16)
    for t in range(steps):
        out_ref[t] = result[t * requests : (t + 1) * requests]


def join(base, place, delta, steps):
    total, cols = base.shape
    vmem = pl.BlockSpec(memory_space=pltpu.VMEM)
    return pl.pallas_call(
        join_kernel,
        out_shape=jax.ShapeDtypeStruct((steps, total // steps, cols), BF16),
        in_specs=[vmem] * 3,
        out_specs=vmem,
        compiler_params=pltpu.CompilerParams(vmem_limit_bytes=24 * 2**20),
        name="join",
    )(base, place, delta)


def per_device(
    queries,
    new_keys,
    new_values,
    cache_keys,
    cache_values,
    kv_len,
    adapter_rows,
    adapter_rank,
    adapter_owner,
    out_weight,
    store_down,
    store_up,
):
    parts = lax.axis_size("tensor")
    steps, rows, width = queries.shape
    tables = (adapter_rows, adapter_rank, adapter_owner)
    attended, down, up, pick, place, order = attend(
        queries,
        new_keys,
        new_values,
        cache_keys,
        cache_values,
        kv_len,
        store_down,
        store_up,
        tables,
        parts,
    )
    blocks = gather(attended, parts)
    send = deltas(blocks, pick, down, up)
    groups = [exchange_order(parts)]
    delta = lax.all_to_all(send, "tensor", 0, 0, axis_index_groups=groups, tiled=True)
    base = base_part(blocks, out_weight, order)
    return join(base, place, delta, steps)


def solution(mesh):
    in_specs = (
        P(None, ("groups", "tensor"), None),
        P(None, ("groups", "tensor"), None),
        P(None, ("groups", "tensor"), None),
        P(("groups", "tensor"), None, None),
        P(("groups", "tensor"), None, None),
        P(("groups", "tensor")),
        P("groups"),
        P(),
        P(),
        P(None, "tensor"),
        P("tensor", None, None),
        P("tensor", None, None),
    )
    out_specs = P(None, "groups", "tensor")
    return jax.shard_map(
        per_device, mesh=mesh, in_specs=in_specs, out_specs=out_specs, check_vma=False
    )
```

```python
import functools
import math

import jax
import jax.numpy as jnp
from jax import lax
from jax.experimental import pallas as pl
from jax.experimental.pallas import tpu as pltpu
from jax.sharding import PartitionSpec as P

HQ = 64
KVH = 8
HD = 128
GROUP = HQ // KVH
MOST = 8
RING = 16
ORDER = [0, 1, 2, 3, 4, 5, 6, 7, 8, 9, 14, 15, 12, 13, 10, 11]
EXCHANGE = [11, 10, 9, 8, 7, 6, 5, 4, 15, 14, 13, 12, 3, 2, 1, 0]
F32 = jnp.float32
BF16 = jnp.bfloat16
NT = (((1,), (1,)), ((), ()))


def in_hbm(*arrays):
    return [pltpu.with_memory_space_constraint(a, pltpu.HBM) for a in arrays]


def iota(shape, dim):
    return lax.broadcasted_iota(jnp.int32, shape, dim)


def one_hot(mask):
    return mask.astype(F32).astype(BF16)


def dot(a, b):
    return jnp.dot(a, b, preferred_element_type=F32)


def dot_nt(a, b):
    return lax.dot_general(a, b, NT, preferred_element_type=F32)


def sender(slot, me, parts):
    return me ^ slot if parts == RING else slot


def exchange_order(parts):
    return EXCHANGE if parts == RING else [*range(parts)]


def write_plan(rows, count_ref, rank_ref, owner_ref, pick_ref, place_ref, order_ref):
    me = lax.axis_index("tensor")
    slots, total = pick_ref.shape
    steps = slots // MOST
    each = steps * rows
    parts = total // each
    requests = parts * rows

    def adapter_of(block):
        first = jnp.zeros(block.shape, jnp.int32)
        amount = jnp.zeros(block.shape, jnp.int32)
        start = jnp.int32(0)
        for a in range(count_ref.shape[0]):
            owned = (owner_ref[a] <= block) & (block < owner_ref[a] + rank_ref[a])
            first = jnp.where(owned, start, first)
            amount = jnp.where(owned, count_ref[a], amount)
            start = start + count_ref[a]
        return first, amount

    def row_place(index):
        device = sender(index // each, me, parts)
        return device * rows + index % rows, (index % each) // rows

    row = iota((slots, 1), 0)
    nth = row % MOST
    first, amount = adapter_of(jnp.zeros_like(row) + me)
    request, step = row_place(iota((1, total), 1))
    pick = (request == first + nth) & (nth < amount) & (step == row // MOST)
    pick_ref[...] = one_hot(pick)

    request, step = row_place(iota((1, total), 1))
    order_ref[...] = one_hot(iota((total, total), 0) == step * requests + request)

    entry = iota((1, parts * slots), 1)
    nth = entry % MOST
    source = jnp.zeros_like(entry)
    for i, device in enumerate(exchange_order(parts)):
        source = jnp.where(entry // slots == i, device, source)
    first, amount = adapter_of(source)
    goal = jnp.where(nth < amount, (entry % slots) // MOST * requests + first + nth, -1)
    place_ref[...] = one_hot(iota((total, parts * slots), 0) == goal)


def attend_kernel(
    len_hbm, q_hbm, nk_hbm, nv_hbm, k_hbm, v_hbm, d_hbm, u_hbm, count_hbm, rank_hbm, owner_hbm,
    out_ref, d_ref, u_ref, pick_ref, place_ref, order_ref,
    len_ref, count_ref, rank_ref, owner_ref, q_ref, nk_ref, nv_ref, k_ref, v_ref, turned_q, nks, nvs, raw, mixed,
    small_sems, sems, store_sems,
):
    steps, rows, width = q_ref.shape
    cache = k_ref.shape[1]
    both = steps * rows
    pack = steps * GROUP
    cuts = sems.shape[2]

    small = [
        pltpu.make_async_copy(src, dst, small_sems.at[i])
        for i, (src, dst) in enumerate(
            (
                (q_hbm, q_ref),
                (nk_hbm, nk_ref),
                (nv_hbm, nv_ref),
                (len_hbm, len_ref),
                (count_hbm, count_ref),
                (rank_hbm, rank_ref),
                (owner_hbm, owner_ref),
            )
        )
    ]
    pieces = [pl.ds(i * (cache // cuts), cache // cuts) for i in range(cuts)]
    keys, values = [
        [
            [
                pltpu.make_async_copy(src.at[r, at], dst.at[r, at], sems.at[r, j, i])
                for i, at in enumerate(pieces)
            ]
            for r in range(rows)
        ]
        for j, (src, dst) in enumerate(((k_hbm, k_ref), (v_hbm, v_ref)))
    ]
    deep = d_ref.shape[0] // store_sems.shape[1]
    store = [
        pltpu.make_async_copy(
            src.at[0, pl.ds(i * deep, deep)], dst.at[pl.ds(i * deep, deep)], store_sems.at[j, i]
        )
        for j, (src, dst) in enumerate(((d_hbm, d_ref), (u_hbm, u_ref)))
        for i in range(store_sems.shape[1])
    ]
    queue = [keys[0], values[0], keys[1]]
    for r in range(rows):
        queue += [values[r + 1]] if r + 1 < rows else [store]
        queue += [keys[r + 2]] if r + 2 < rows else []
    for copy in small + queue[0] + queue[1] + queue[2]:
        copy.start()
    for copy in small:
        copy.wait()
    for copy in queue[3] + queue[4]:
        copy.start()
    queue = queue[5:]

    flat = jnp.concatenate([q_ref[t].astype(F32) for t in range(steps)], axis=0)
    heads = []
    for k in range(KVH):
        group = jnp.stack(
            [flat[:, (k * GROUP + g) * HD : (k * GROUP + g + 1) * HD] for g in range(GROUP)]
        )
        heads.append(jnp.swapaxes(group, 0, 1))
    column = iota((HD, KVH * pack), 1)
    for r in range(rows):
        mine = jnp.concatenate(
            [heads[k][t * rows + r] for k in range(KVH) for t in range(steps)], axis=0
        )
        mine = jnp.transpose(mine)
        for k in range(KVH):
            turned_q[r, k * HD : (k + 1) * HD, :] = jnp.where(
                column // pack == k, mine, 0.0
            ).astype(BF16)
    for src, dst in ((nk_ref, nks), (nv_ref, nvs)):
        fresh = [src[t].astype(F32) for t in range(steps)]
        fresh.append(jnp.zeros((16 - both, src.shape[2]), F32))
        dst[...] = jnp.concatenate(fresh, axis=0).astype(BF16)

    write_plan(rows, count_ref, rank_ref, owner_ref, pick_ref, place_ref, order_ref)

    rate = HD ** (-0.5) * math.log2(math.e)
    pairs = [
        (slice(k * pack, (k + 2) * pack), slice(k * HD, (k + 2) * HD)) for k in range(0, KVH, 2)
    ]
    for turn in range(rows + 1):
        if turn < rows:
            for copy in keys[turn]:
                copy.wait()
        if turn > 0:
            for copy in values[turn - 1]:
                copy.wait()
        for copies in queue[2 * turn : 2 * turn + 2]:
            for copy in copies:
                copy.start()
        if turn < rows:
            raw[turn % 2] = dot(k_ref[turn], turned_q[turn])
        if turn == 0:
            continue
        r = turn - 1
        fresh = dot(nks[...], turned_q[r])
        slot = iota(fresh.shape, 0)
        step = (iota(fresh.shape, 1) // GROUP) % steps
        seen = (slot < both) & (slot % rows == r) & (slot // rows <= step)
        fresh = jnp.where(seen, fresh, -jnp.inf)
        older = raw[r % 2]
        older = jnp.where(iota(older.shape, 0) < len_ref[r], older, -jnp.inf)
        top = jnp.maximum(
            jnp.max(older, axis=0, keepdims=True), jnp.max(fresh, axis=0, keepdims=True)
        )
        e_older = jnp.exp2((older - top) * rate)
        e_fresh = jnp.exp2((fresh - top) * rate)
        total = jnp.sum(e_older, axis=0, keepdims=True) + jnp.sum(e_fresh, axis=0, keepdims=True)
        inverse = 1.0 / total
        p_older = jnp.transpose((e_older * inverse).astype(BF16))
        p_fresh = jnp.transpose((e_fresh * inverse).astype(BF16))
        for k, (own, cols_k) in zip(range(0, KVH, 2), pairs):
            pair = dot(p_older[own], v_ref[r, :, cols_k]) + dot(p_fresh[own], nvs[:, cols_k])
            mixed[r, k] = pair[:pack, :HD]
            mixed[r, k + 1] = pair[pack:, HD:]

    for k in range(KVH):
        turned = jnp.stack(
            [
                mixed[r, k, t * GROUP : (t + 1) * GROUP, :]
                for t in range(steps)
                for r in range(rows)
            ]
        )
        heads = jnp.swapaxes(turned, 0, 1)
        for g in range(GROUP):
            at = (k * GROUP + g) * HD
            out_ref[:, at : at + HD] = heads[g].astype(BF16)
    for copy in store:
        copy.wait()


def attend(
    queries,
    new_keys,
    new_values,
    cache_keys,
    cache_values,
    kv_len,
    store_down,
    store_up,
    tables,
    parts,
):
    steps, rows, width = queries.shape
    cache, kv_width = cache_keys.shape[1:]
    pack = steps * GROUP
    rank_w = store_down.shape[2]
    total = parts * steps * rows
    slots = steps * MOST
    shapes = [(steps * rows, width), (width, rank_w), (width, rank_w)]
    shapes += [(slots, total), (total, parts * slots), (total, total)]
    return pl.pallas_call(
        attend_kernel,
        out_shape=[jax.ShapeDtypeStruct(shape, BF16) for shape in shapes],
        in_specs=[pl.BlockSpec(memory_space=pl.ANY)] * 11,
        out_specs=[pl.BlockSpec(memory_space=pltpu.VMEM)] * len(shapes),
        scratch_shapes=[
            pltpu.SMEM(kv_len.shape, jnp.int32),
            *[pltpu.SMEM(table.shape, jnp.int32) for table in tables],
            pltpu.VMEM(queries.shape, BF16),
            pltpu.VMEM(new_keys.shape, BF16),
            pltpu.VMEM(new_values.shape, BF16),
            pltpu.VMEM(cache_keys.shape, BF16),
            pltpu.VMEM(cache_values.shape, BF16),
            pltpu.VMEM((rows, kv_width, KVH * pack), BF16),
            pltpu.VMEM((16, kv_width), BF16),
            pltpu.VMEM((16, kv_width), BF16),
            pltpu.VMEM((2, cache, KVH * pack), F32),
            pltpu.VMEM((rows, KVH, pack, HD), F32),
            pltpu.SemaphoreType.DMA((7,)),
            pltpu.SemaphoreType.DMA((rows, 2, 2)),
            pltpu.SemaphoreType.DMA((2, 4)),
        ],
        compiler_params=pltpu.CompilerParams(vmem_limit_bytes=32 * 2**20),
        cost_estimate=pl.CostEstimate(
            flops=4 * rows * steps * HQ * cache * HD,
            bytes_accessed=4 * rows * cache * kv_width,
            transcendentals=rows * steps * HQ * cache,
        ),
        name="attend",
    )(
        *in_hbm(
            kv_len,
            queries,
            new_keys,
            new_values,
            cache_keys,
            cache_values,
            store_down,
            store_up,
            *tables,
        )
    )


def swap(x, bits, parts):
    return lax.ppermute(x, "tensor", [(i, i ^ bits) for i in range(parts)])


def gather(block, parts):
    if parts != RING:
        whole = lax.all_gather(block, "tensor")
        return [whole[i] for i in range(parts)]
    core, y, near, far = 1, 2, 4, 8
    held = {0: block}
    held[far] = swap(block, far, parts)
    held[near] = swap(block, near, parts)
    held[y] = swap(block, y, parts)
    held[near | y] = swap(block, near | y, parts)
    held[far | y] = swap(held[far], y, parts)
    held[far | near | y] = swap(held[far], near | y, parts)
    held[far | near] = swap(held[far], near, parts)
    for slot in list(held):
        held[slot | core] = swap(held[slot], core, parts)
    return [held[slot] for slot in range(parts)]


def delta_kernel(at_slot, *refs):
    (*blocks, pick_ref, d_ref, u_ref, out_ref) = refs
    blocks = [blocks[at_slot.index(i)] for i in range(len(blocks))]
    parts, slots, cols = out_ref.shape
    each, width = blocks[0].shape
    cuts = 8
    deep = width // cuts
    low = jnp.zeros((parts * each, d_ref.shape[1]), F32)
    for i in range(cuts):
        at = slice(i * deep, (i + 1) * deep)
        piece = jnp.concatenate([b[:, at] for b in blocks], axis=0)
        low = low + dot(piece, d_ref[at, :])
    chosen = dot(pick_ref[...], low.astype(BF16)).astype(BF16)
    for p, device in enumerate(exchange_order(parts)):
        at = device * cols
        out_ref[p] = dot_nt(chosen, u_ref[at : at + cols, :]).astype(BF16)


def deltas(blocks, pick, down, up):
    parts = len(blocks)
    each, width = blocks[0].shape
    slots = pick.shape[0]
    rank_w = down.shape[1]
    vmem = pl.BlockSpec(memory_space=pltpu.VMEM)
    at_slot = ORDER if parts == RING else [*range(parts)]
    return pl.pallas_call(
        functools.partial(delta_kernel, at_slot),
        out_shape=jax.ShapeDtypeStruct((parts, slots, width // parts), BF16),
        in_specs=[vmem] * (3 + parts),
        out_specs=vmem,
        compiler_params=pltpu.CompilerParams(vmem_limit_bytes=24 * 2**20),
        cost_estimate=pl.CostEstimate(
            flops=2 * (parts * each + slots) * width * rank_w,
            bytes_accessed=2 * width * (parts * each + 2 * rank_w + slots),
            transcendentals=0,
        ),
        name="delta",
    )(*[blocks[i] for i in at_slot], pick, down, up)


def base_kernel(at_slot, *refs):
    (*blocks, order_ref, w_hbm, out_ref, w_ref, sems) = refs
    blocks = [blocks[at_slot.index(i)] for i in range(len(blocks))]
    width = w_ref.shape[0]
    cuts = sems.shape[0]
    deep = width // cuts
    copies = []
    for i in range(cuts):
        at = pl.ds(i * deep, deep)
        copies.append(pltpu.make_async_copy(w_hbm.at[at], w_ref.at[at], sems.at[i]))
        copies[-1].start()
    for i in range(cuts):
        at = slice(i * deep, (i + 1) * deep)
        rows = jnp.concatenate([b[:, at] for b in blocks], axis=0)
        rows = dot(order_ref[...], rows).astype(BF16)
        copies[i].wait()
        part = dot(rows, w_ref[at, :])
        out_ref[...] = part if i == 0 else out_ref[...] + part


def base_part(blocks, out_weight, order):
    parts = len(blocks)
    total = order.shape[0]
    width, cols = out_weight.shape
    vmem = pl.BlockSpec(memory_space=pltpu.VMEM)
    at_slot = ORDER if parts == RING else [*range(parts)]
    return pl.pallas_call(
        functools.partial(base_kernel, at_slot),
        out_shape=jax.ShapeDtypeStruct((total, cols), F32),
        in_specs=[vmem] * (1 + parts) + [pl.BlockSpec(memory_space=pl.ANY)],
        out_specs=vmem,
        scratch_shapes=[pltpu.VMEM(out_weight.shape, BF16), pltpu.SemaphoreType.DMA((8,))],
        compiler_params=pltpu.CompilerParams(vmem_limit_bytes=24 * 2**20),
        cost_estimate=pl.CostEstimate(
            flops=2 * total * width * (cols + total),
            bytes_accessed=2 * width * (total + cols) + 4 * total * cols,
            transcendentals=0,
        ),
        name="base",
    )(*[blocks[i] for i in at_slot], order, *in_hbm(out_weight))


def join_kernel(base_ref, place_ref, delta_ref, out_ref):
    steps, requests, cols = out_ref.shape
    parts, slots, _ = delta_ref.shape
    delta = dot(place_ref[...], delta_ref[...].reshape(parts * slots, cols))
    result = (base_ref[...] + delta).astype(BF16)
    for t in range(steps):
        out_ref[t] = result[t * requests : (t + 1) * requests]


def join(base, place, delta, steps):
    total, cols = base.shape
    vmem = pl.BlockSpec(memory_space=pltpu.VMEM)
    return pl.pallas_call(
        join_kernel,
        out_shape=jax.ShapeDtypeStruct((steps, total // steps, cols), BF16),
        in_specs=[vmem] * 3,
        out_specs=vmem,
        compiler_params=pltpu.CompilerParams(vmem_limit_bytes=24 * 2**20),
        name="join",
    )(base, place, delta)


def per_device(
    queries,
    new_keys,
    new_values,
    cache_keys,
    cache_values,
    kv_len,
    adapter_rows,
    adapter_rank,
    adapter_owner,
    out_weight,
    store_down,
    store_up,
):
    parts = lax.axis_size("tensor")
    steps, rows, width = queries.shape
    tables = (adapter_rows, adapter_rank, adapter_owner)
    attended, down, up, pick, place, order = attend(
        queries,
        new_keys,
        new_values,
        cache_keys,
        cache_values,
        kv_len,
        store_down,
        store_up,
        tables,
        parts,
    )
    blocks = gather(attended, parts)
    send = deltas(blocks, pick, down, up)
    groups = [exchange_order(parts)]
    delta = lax.all_to_all(send, "tensor", 0, 0, axis_index_groups=groups, tiled=True)
    base = base_part(blocks, out_weight, order)
    return join(base, place, delta, steps)


def solution(mesh):
    in_specs = (
        P(None, ("groups", "tensor"), None),
        P(None, ("groups", "tensor"), None),
        P(None, ("groups", "tensor"), None),
        P(("groups", "tensor"), None, None),
        P(("groups", "tensor"), None, None),
        P(("groups", "tensor")),
        P("groups"),
        P(),
        P(),
        P(None, "tensor"),
        P("tensor", None, None),
        P("tensor", None, None),
    )
    out_specs = P(None, "groups", "tensor")
    return jax.shard_map(
        per_device, mesh=mesh, in_specs=in_specs, out_specs=out_specs, check_vma=False
    )
```

```python
import functools
import math

import jax
import jax.numpy as jnp
from jax import lax
from jax.experimental import pallas as pl
from jax.experimental.pallas import tpu as pltpu
from jax.sharding import PartitionSpec as P

HQ = 64
KVH = 8
HD = 128
GROUP = HQ // KVH
MOST = 8
RING = 16
ORDER = [0, 1, 2, 3, 4, 5, 6, 7, 8, 9, 10, 11, 12, 13, 14, 15]
EXCHANGE = [11, 10, 9, 8, 15, 14, 13, 12, 7, 6, 5, 4, 3, 2, 1, 0]
F32 = jnp.float32
BF16 = jnp.bfloat16
NT = (((1,), (1,)), ((), ()))


def in_hbm(*arrays):
    return [pltpu.with_memory_space_constraint(a, pltpu.HBM) for a in arrays]


def iota(shape, dim):
    return lax.broadcasted_iota(jnp.int32, shape, dim)


def one_hot(mask):
    return mask.astype(F32).astype(BF16)


def dot(a, b):
    return jnp.dot(a, b, preferred_element_type=F32)


def dot_nt(a, b):
    return lax.dot_general(a, b, NT, preferred_element_type=F32)


def sender(slot, me, parts):
    return me ^ slot if parts == RING else slot


def exchange_order(parts):
    return EXCHANGE if parts == RING else [*range(parts)]


def write_plan(rows, count_ref, rank_ref, owner_ref, pick_ref, place_ref, order_ref):
    me = lax.axis_index("tensor")
    slots, total = pick_ref.shape
    steps = slots // MOST
    each = steps * rows
    parts = total // each
    requests = parts * rows

    def adapter_of(block):
        first = jnp.zeros(block.shape, jnp.int32)
        amount = jnp.zeros(block.shape, jnp.int32)
        start = jnp.int32(0)
        for a in range(count_ref.shape[0]):
            owned = (owner_ref[a] <= block) & (block < owner_ref[a] + rank_ref[a])
            first = jnp.where(owned, start, first)
            amount = jnp.where(owned, count_ref[a], amount)
            start = start + count_ref[a]
        return first, amount

    def row_place(index):
        device = sender(index // each, me, parts)
        return device * rows + index % rows, (index % each) // rows

    row = iota((slots, 1), 0)
    nth = row % MOST
    first, amount = adapter_of(jnp.zeros_like(row) + me)
    request, step = row_place(iota((1, total), 1))
    pick = (request == first + nth) & (nth < amount) & (step == row // MOST)
    pick_ref[...] = one_hot(pick)

    request, step = row_place(iota((1, total), 1))
    order_ref[...] = one_hot(iota((total, total), 0) == step * requests + request)

    entry = iota((1, parts * slots), 1)
    nth = entry % MOST
    source = jnp.zeros_like(entry)
    for i, device in enumerate(exchange_order(parts)):
        source = jnp.where(entry // slots == i, device, source)
    first, amount = adapter_of(source)
    goal = jnp.where(nth < amount, (entry % slots) // MOST * requests + first + nth, -1)
    place_ref[...] = one_hot(iota((total, parts * slots), 0) == goal)


def attend_kernel(
    len_hbm, q_hbm, nk_hbm, nv_hbm, k_hbm, v_hbm, d_hbm, u_hbm, count_hbm, rank_hbm, owner_hbm,
    out_ref, d_ref, u_ref, pick_ref, place_ref, order_ref,
    len_ref, count_ref, rank_ref, owner_ref, q_ref, nk_ref, nv_ref, k_ref, v_ref, turned_q, nks, nvs, raw, mixed,
    small_sems, sems, store_sems,
):
    steps, rows, width = q_ref.shape
    cache = k_ref.shape[1]
    both = steps * rows
    pack = steps * GROUP
    cuts = sems.shape[2]

    small = [
        pltpu.make_async_copy(src, dst, small_sems.at[i])
        for i, (src, dst) in enumerate(
            (
                (q_hbm, q_ref),
                (nk_hbm, nk_ref),
                (nv_hbm, nv_ref),
                (len_hbm, len_ref),
                (count_hbm, count_ref),
                (rank_hbm, rank_ref),
                (owner_hbm, owner_ref),
            )
        )
    ]
    pieces = [pl.ds(i * (cache // cuts), cache // cuts) for i in range(cuts)]
    keys, values = [
        [
            [
                pltpu.make_async_copy(src.at[r, at], dst.at[r, at], sems.at[r, j, i])
                for i, at in enumerate(pieces)
            ]
            for r in range(rows)
        ]
        for j, (src, dst) in enumerate(((k_hbm, k_ref), (v_hbm, v_ref)))
    ]
    deep = d_ref.shape[0] // store_sems.shape[1]
    store = [
        pltpu.make_async_copy(
            src.at[0, pl.ds(i * deep, deep)], dst.at[pl.ds(i * deep, deep)], store_sems.at[j, i]
        )
        for j, (src, dst) in enumerate(((d_hbm, d_ref), (u_hbm, u_ref)))
        for i in range(store_sems.shape[1])
    ]
    queue = [keys[0], values[0], keys[1]]
    for r in range(rows):
        queue += [values[r + 1]] if r + 1 < rows else [store]
        queue += [keys[r + 2]] if r + 2 < rows else []
    for copy in small + queue[0] + queue[1] + queue[2] + queue[3] + queue[4]:
        copy.start()
    for copy in small:
        copy.wait()
    for copy in queue[5] + queue[6]:
        copy.start()
    queue = queue[7:]

    flat = jnp.concatenate([q_ref[t].astype(F32) for t in range(steps)], axis=0)
    heads = []
    for k in range(KVH):
        group = jnp.stack(
            [flat[:, (k * GROUP + g) * HD : (k * GROUP + g + 1) * HD] for g in range(GROUP)]
        )
        heads.append(jnp.swapaxes(group, 0, 1))
    column = iota((HD, KVH * pack), 1)
    for r in range(rows):
        mine = jnp.concatenate(
            [heads[k][t * rows + r] for k in range(KVH) for t in range(steps)], axis=0
        )
        mine = jnp.transpose(mine)
        for k in range(KVH):
            turned_q[r, k * HD : (k + 1) * HD, :] = jnp.where(
                column // pack == k, mine, 0.0
            ).astype(BF16)
    for src, dst in ((nk_ref, nks), (nv_ref, nvs)):
        fresh = [src[t].astype(F32) for t in range(steps)]
        fresh.append(jnp.zeros((16 - both, src.shape[2]), F32))
        dst[...] = jnp.concatenate(fresh, axis=0).astype(BF16)

    write_plan(rows, count_ref, rank_ref, owner_ref, pick_ref, place_ref, order_ref)

    rate = HD ** (-0.5) * math.log2(math.e)
    pairs = [
        (slice(k * pack, (k + 2) * pack), slice(k * HD, (k + 2) * HD)) for k in range(0, KVH, 2)
    ]
    for turn in range(rows + 1):
        if turn < rows:
            for copy in keys[turn]:
                copy.wait()
        if turn > 0:
            for copy in values[turn - 1]:
                copy.wait()
        for copies in queue[2 * turn : 2 * turn + 2]:
            for copy in copies:
                copy.start()
        if turn < rows:
            raw[turn % 2] = dot(k_ref[turn], turned_q[turn])
        if turn == 0:
            continue
        r = turn - 1
        fresh = dot(nks[...], turned_q[r])
        slot = iota(fresh.shape, 0)
        step = (iota(fresh.shape, 1) // GROUP) % steps
        seen = (slot < both) & (slot % rows == r) & (slot // rows <= step)
        fresh = jnp.where(seen, fresh, -jnp.inf)
        older = raw[r % 2]
        older = jnp.where(iota(older.shape, 0) < len_ref[r], older, -jnp.inf)
        top = jnp.maximum(
            jnp.max(older, axis=0, keepdims=True), jnp.max(fresh, axis=0, keepdims=True)
        )
        e_older = jnp.exp2((older - top) * rate)
        e_fresh = jnp.exp2((fresh - top) * rate)
        total = jnp.sum(e_older, axis=0, keepdims=True) + jnp.sum(e_fresh, axis=0, keepdims=True)
        inverse = 1.0 / total
        p_older = jnp.transpose((e_older * inverse).astype(BF16))
        p_fresh = jnp.transpose((e_fresh * inverse).astype(BF16))
        for k, (own, cols_k) in zip(range(0, KVH, 2), pairs):
            pair = dot(p_older[own], v_ref[r, :, cols_k]) + dot(p_fresh[own], nvs[:, cols_k])
            mixed[r, k] = pair[:pack, :HD]
            mixed[r, k + 1] = pair[pack:, HD:]

    for k in range(KVH):
        turned = jnp.stack(
            [
                mixed[r, k, t * GROUP : (t + 1) * GROUP, :]
                for t in range(steps)
                for r in range(rows)
            ]
        )
        heads = jnp.swapaxes(turned, 0, 1)
        for g in range(GROUP):
            at = (k * GROUP + g) * HD
            out_ref[:, at : at + HD] = heads[g].astype(BF16)
    for copy in store:
        copy.wait()


def attend(
    queries,
    new_keys,
    new_values,
    cache_keys,
    cache_values,
    kv_len,
    store_down,
    store_up,
    tables,
    parts,
):
    steps, rows, width = queries.shape
    cache, kv_width = cache_keys.shape[1:]
    pack = steps * GROUP
    rank_w = store_down.shape[2]
    total = parts * steps * rows
    slots = steps * MOST
    shapes = [(steps * rows, width), (width, rank_w), (width, rank_w)]
    shapes += [(slots, total), (total, parts * slots), (total, total)]
    return pl.pallas_call(
        attend_kernel,
        out_shape=[jax.ShapeDtypeStruct(shape, BF16) for shape in shapes],
        in_specs=[pl.BlockSpec(memory_space=pl.ANY)] * 11,
        out_specs=[pl.BlockSpec(memory_space=pltpu.VMEM)] * len(shapes),
        scratch_shapes=[
            pltpu.SMEM(kv_len.shape, jnp.int32),
            *[pltpu.SMEM(table.shape, jnp.int32) for table in tables],
            pltpu.VMEM(queries.shape, BF16),
            pltpu.VMEM(new_keys.shape, BF16),
            pltpu.VMEM(new_values.shape, BF16),
            pltpu.VMEM(cache_keys.shape, BF16),
            pltpu.VMEM(cache_values.shape, BF16),
            pltpu.VMEM((rows, kv_width, KVH * pack), BF16),
            pltpu.VMEM((16, kv_width), BF16),
            pltpu.VMEM((16, kv_width), BF16),
            pltpu.VMEM((2, cache, KVH * pack), F32),
            pltpu.VMEM((rows, KVH, pack, HD), F32),
            pltpu.SemaphoreType.DMA((7,)),
            pltpu.SemaphoreType.DMA((rows, 2, 2)),
            pltpu.SemaphoreType.DMA((2, 4)),
        ],
        compiler_params=pltpu.CompilerParams(vmem_limit_bytes=32 * 2**20),
        cost_estimate=pl.CostEstimate(
            flops=4 * rows * steps * HQ * cache * HD,
            bytes_accessed=4 * rows * cache * kv_width,
            transcendentals=rows * steps * HQ * cache,
        ),
        name="attend",
    )(
        *in_hbm(
            kv_len,
            queries,
            new_keys,
            new_values,
            cache_keys,
            cache_values,
            store_down,
            store_up,
            *tables,
        )
    )


def swap(x, bits, parts):
    return lax.ppermute(x, "tensor", [(i, i ^ bits) for i in range(parts)])


def gather(block, parts):
    if parts != RING:
        whole = lax.all_gather(block, "tensor")
        return [whole[i] for i in range(parts)]
    core, y, near, far = 1, 2, 4, 8
    held = {0: block}
    held[far] = swap(block, far, parts)
    held[near] = swap(block, near, parts)
    held[y] = swap(block, y, parts)
    held[near | y] = swap(block, near | y, parts)
    held[far | y] = swap(held[far], y, parts)
    held[far | near | y] = swap(held[far], near | y, parts)
    held[far | near] = swap(held[far], near, parts)
    for slot in list(held):
        held[slot | core] = swap(held[slot], core, parts)
    return [held[slot] for slot in range(parts)]


def delta_kernel(at_slot, *refs):
    (*blocks, pick_ref, d_ref, u_ref, out_ref) = refs
    blocks = [blocks[at_slot.index(i)] for i in range(len(blocks))]
    parts, slots, cols = out_ref.shape
    each, width = blocks[0].shape
    cuts = 8
    deep = width // cuts
    low = jnp.zeros((parts * each, d_ref.shape[1]), F32)
    for i in range(cuts):
        at = slice(i * deep, (i + 1) * deep)
        piece = jnp.concatenate([b[:, at] for b in blocks], axis=0)
        low = low + dot(piece, d_ref[at, :])
    chosen = dot(pick_ref[...], low.astype(BF16)).astype(BF16)
    for p, device in enumerate(exchange_order(parts)):
        at = device * cols
        out_ref[p] = dot_nt(chosen, u_ref[at : at + cols, :]).astype(BF16)


def deltas(blocks, pick, down, up):
    parts = len(blocks)
    each, width = blocks[0].shape
    slots = pick.shape[0]
    rank_w = down.shape[1]
    vmem = pl.BlockSpec(memory_space=pltpu.VMEM)
    at_slot = ORDER if parts == RING else [*range(parts)]
    return pl.pallas_call(
        functools.partial(delta_kernel, at_slot),
        out_shape=jax.ShapeDtypeStruct((parts, slots, width // parts), BF16),
        in_specs=[vmem] * (3 + parts),
        out_specs=vmem,
        compiler_params=pltpu.CompilerParams(vmem_limit_bytes=24 * 2**20),
        cost_estimate=pl.CostEstimate(
            flops=2 * (parts * each + slots) * width * rank_w,
            bytes_accessed=2 * width * (parts * each + 2 * rank_w + slots),
            transcendentals=0,
        ),
        name="delta",
    )(*[blocks[i] for i in at_slot], pick, down, up)


def base_kernel(at_slot, *refs):
    (*blocks, order_ref, w_hbm, out_ref, w_ref, sems) = refs
    blocks = [blocks[at_slot.index(i)] for i in range(len(blocks))]
    width = w_ref.shape[0]
    cuts = sems.shape[0]
    deep = width // cuts
    copies = []
    for i in range(cuts):
        at = pl.ds(i * deep, deep)
        copies.append(pltpu.make_async_copy(w_hbm.at[at], w_ref.at[at], sems.at[i]))
        copies[-1].start()
    for i in range(cuts):
        at = slice(i * deep, (i + 1) * deep)
        rows = jnp.concatenate([b[:, at] for b in blocks], axis=0)
        rows = dot(order_ref[...], rows).astype(BF16)
        copies[i].wait()
        part = dot(rows, w_ref[at, :])
        out_ref[...] = part if i == 0 else out_ref[...] + part


def base_part(blocks, out_weight, order):
    parts = len(blocks)
    total = order.shape[0]
    width, cols = out_weight.shape
    vmem = pl.BlockSpec(memory_space=pltpu.VMEM)
    at_slot = ORDER if parts == RING else [*range(parts)]
    return pl.pallas_call(
        functools.partial(base_kernel, at_slot),
        out_shape=jax.ShapeDtypeStruct((total, cols), F32),
        in_specs=[vmem] * (1 + parts) + [pl.BlockSpec(memory_space=pl.ANY)],
        out_specs=vmem,
        scratch_shapes=[pltpu.VMEM(out_weight.shape, BF16), pltpu.SemaphoreType.DMA((8,))],
        compiler_params=pltpu.CompilerParams(vmem_limit_bytes=24 * 2**20),
        cost_estimate=pl.CostEstimate(
            flops=2 * total * width * (cols + total),
            bytes_accessed=2 * width * (total + cols) + 4 * total * cols,
            transcendentals=0,
        ),
        name="base",
    )(*[blocks[i] for i in at_slot], order, *in_hbm(out_weight))


def join_kernel(base_ref, place_ref, delta_ref, out_ref):
    steps, requests, cols = out_ref.shape
    parts, slots, _ = delta_ref.shape
    delta = dot(place_ref[...], delta_ref[...].reshape(parts * slots, cols))
    result = (base_ref[...] + delta).astype(BF16)
    for t in range(steps):
        out_ref[t] = result[t * requests : (t + 1) * requests]


def join(base, place, delta, steps):
    total, cols = base.shape
    vmem = pl.BlockSpec(memory_space=pltpu.VMEM)
    return pl.pallas_call(
        join_kernel,
        out_shape=jax.ShapeDtypeStruct((steps, total // steps, cols), BF16),
        in_specs=[vmem] * 3,
        out_specs=vmem,
        compiler_params=pltpu.CompilerParams(vmem_limit_bytes=24 * 2**20),
        name="join",
    )(base, place, delta)


def per_device(
    queries,
    new_keys,
    new_values,
    cache_keys,
    cache_values,
    kv_len,
    adapter_rows,
    adapter_rank,
    adapter_owner,
    out_weight,
    store_down,
    store_up,
):
    parts = lax.axis_size("tensor")
    steps, rows, width = queries.shape
    tables = (adapter_rows, adapter_rank, adapter_owner)
    attended, down, up, pick, place, order = attend(
        queries,
        new_keys,
        new_values,
        cache_keys,
        cache_values,
        kv_len,
        store_down,
        store_up,
        tables,
        parts,
    )
    blocks = gather(attended, parts)
    send = deltas(blocks, pick, down, up)
    groups = [exchange_order(parts)]
    delta = lax.all_to_all(send, "tensor", 0, 0, axis_index_groups=groups, tiled=True)
    base = base_part(blocks, out_weight, order)
    return join(base, place, delta, steps)


def solution(mesh):
    in_specs = (
        P(None, ("groups", "tensor"), None),
        P(None, ("groups", "tensor"), None),
        P(None, ("groups", "tensor"), None),
        P(("groups", "tensor"), None, None),
        P(("groups", "tensor"), None, None),
        P(("groups", "tensor")),
        P("groups"),
        P(),
        P(),
        P(None, "tensor"),
        P("tensor", None, None),
        P("tensor", None, None),
    )
    out_specs = P(None, "groups", "tensor")
    return jax.shard_map(
        per_device, mesh=mesh, in_specs=in_specs, out_specs=out_specs, check_vma=False
    )
```

```python
import functools
import math

import jax
import jax.numpy as jnp
from jax import lax
from jax.experimental import pallas as pl
from jax.experimental.pallas import tpu as pltpu
from jax.sharding import PartitionSpec as P

HQ = 64
KVH = 8
HD = 128
GROUP = HQ // KVH
MOST = 8
RING = 16
ORDER = [0, 1, 2, 3, 4, 5, 6, 7, 8, 9, 10, 11, 12, 13, 14, 15]
EXCHANGE = [11, 10, 9, 8, 15, 14, 13, 12, 7, 6, 5, 4, 3, 2, 1, 0]
F32 = jnp.float32
BF16 = jnp.bfloat16
NT = (((1,), (1,)), ((), ()))


def in_hbm(*arrays):
    return [pltpu.with_memory_space_constraint(a, pltpu.HBM) for a in arrays]


def iota(shape, dim):
    return lax.broadcasted_iota(jnp.int32, shape, dim)


def one_hot(mask):
    return mask.astype(F32).astype(BF16)


def dot(a, b):
    return jnp.dot(a, b, preferred_element_type=F32)


def dot_nt(a, b):
    return lax.dot_general(a, b, NT, preferred_element_type=F32)


def sender(slot, me, parts):
    return me ^ slot if parts == RING else slot


def exchange_order(parts):
    return EXCHANGE if parts == RING else [*range(parts)]


def write_plan(rows, count_ref, rank_ref, owner_ref, pick_ref, place_ref, order_ref):
    me = lax.axis_index("tensor")
    slots, total = pick_ref.shape
    steps = slots // MOST
    each = steps * rows
    parts = total // each
    requests = parts * rows

    def adapter_of(block):
        first = jnp.zeros(block.shape, jnp.int32)
        amount = jnp.zeros(block.shape, jnp.int32)
        start = jnp.int32(0)
        for a in range(count_ref.shape[0]):
            owned = (owner_ref[a] <= block) & (block < owner_ref[a] + rank_ref[a])
            first = jnp.where(owned, start, first)
            amount = jnp.where(owned, count_ref[a], amount)
            start = start + count_ref[a]
        return first, amount

    def row_place(index):
        device = sender(index // each, me, parts)
        return device * rows + index % rows, (index % each) // rows

    row = iota((slots, 1), 0)
    nth = row % MOST
    first, amount = adapter_of(jnp.zeros_like(row) + me)
    request, step = row_place(iota((1, total), 1))
    pick = (request == first + nth) & (nth < amount) & (step == row // MOST)
    pick_ref[...] = one_hot(pick)

    request, step = row_place(iota((1, total), 1))
    order_ref[...] = one_hot(iota((total, total), 0) == step * requests + request)

    entry = iota((1, parts * slots), 1)
    nth = entry % MOST
    source = jnp.zeros_like(entry)
    for i, device in enumerate(exchange_order(parts)):
        source = jnp.where(entry // slots == i, device, source)
    first, amount = adapter_of(source)
    goal = jnp.where(nth < amount, (entry % slots) // MOST * requests + first + nth, -1)
    place_ref[...] = one_hot(iota((total, parts * slots), 0) == goal)


def attend_kernel(
    len_hbm, q_hbm, nk_hbm, nv_hbm, k_hbm, v_hbm, d_hbm, u_hbm, count_hbm, rank_hbm, owner_hbm,
    out_ref, d_ref, u_ref, pick_ref, place_ref, order_ref,
    len_ref, count_ref, rank_ref, owner_ref, q_ref, nk_ref, nv_ref, k_ref, v_ref, turned_q, nks, nvs, raw, mixed,
    small_sems, sems, store_sems,
):
    steps, rows, width = q_ref.shape
    cache = k_ref.shape[1]
    both = steps * rows
    pack = steps * GROUP
    cuts = sems.shape[2]

    small = [
        pltpu.make_async_copy(src, dst, small_sems.at[i])
        for i, (src, dst) in enumerate(
            (
                (q_hbm, q_ref),
                (nk_hbm, nk_ref),
                (nv_hbm, nv_ref),
                (len_hbm, len_ref),
                (count_hbm, count_ref),
                (rank_hbm, rank_ref),
                (owner_hbm, owner_ref),
            )
        )
    ]
    pieces = [pl.ds(i * (cache // cuts), cache // cuts) for i in range(cuts)]
    keys, values = [
        [
            [
                pltpu.make_async_copy(src.at[r, at], dst.at[r, at], sems.at[r, j, i])
                for i, at in enumerate(pieces)
            ]
            for r in range(rows)
        ]
        for j, (src, dst) in enumerate(((k_hbm, k_ref), (v_hbm, v_ref)))
    ]
    deep = d_ref.shape[0] // store_sems.shape[1]
    store = [
        pltpu.make_async_copy(
            src.at[0, pl.ds(i * deep, deep)], dst.at[pl.ds(i * deep, deep)], store_sems.at[j, i]
        )
        for j, (src, dst) in enumerate(((d_hbm, d_ref), (u_hbm, u_ref)))
        for i in range(store_sems.shape[1])
    ]
    queue = [keys[0], values[0], keys[1]]
    for r in range(rows):
        queue += [values[r + 1]] if r + 1 < rows else [store]
        queue += [keys[r + 2]] if r + 2 < rows else []
    for copy in small + queue[0] + queue[1]:
        copy.start()
    for copy in small:
        copy.wait()
    for copy in queue[2] + queue[3] + queue[4]:
        copy.start()
    queue = queue[5:]

    flat = jnp.concatenate([q_ref[t].astype(F32) for t in range(steps)], axis=0)
    heads = []
    for k in range(KVH):
        group = jnp.stack(
            [flat[:, (k * GROUP + g) * HD : (k * GROUP + g + 1) * HD] for g in range(GROUP)]
        )
        heads.append(jnp.swapaxes(group, 0, 1))
    column = iota((HD, KVH * pack), 1)
    for r in range(rows):
        mine = jnp.concatenate(
            [heads[k][t * rows + r] for k in range(KVH) for t in range(steps)], axis=0
        )
        mine = jnp.transpose(mine)
        for k in range(KVH):
            turned_q[r, k * HD : (k + 1) * HD, :] = jnp.where(
                column // pack == k, mine, 0.0
            ).astype(BF16)
    for src, dst in ((nk_ref, nks), (nv_ref, nvs)):
        fresh = [src[t].astype(F32) for t in range(steps)]
        fresh.append(jnp.zeros((16 - both, src.shape[2]), F32))
        dst[...] = jnp.concatenate(fresh, axis=0).astype(BF16)

    write_plan(rows, count_ref, rank_ref, owner_ref, pick_ref, place_ref, order_ref)

    rate = HD ** (-0.5) * math.log2(math.e)
    pairs = [
        (slice(k * pack, (k + 2) * pack), slice(k * HD, (k + 2) * HD)) for k in range(0, KVH, 2)
    ]
    for turn in range(rows + 1):
        if turn < rows:
            for copy in keys[turn]:
                copy.wait()
        if turn > 0:
            for copy in values[turn - 1]:
                copy.wait()
        for copies in queue[2 * turn : 2 * turn + 2]:
            for copy in copies:
                copy.start()
        if turn < rows:
            raw[turn % 2] = dot(k_ref[turn], turned_q[turn])
        if turn == 0:
            continue
        r = turn - 1
        fresh = dot(nks[...], turned_q[r])
        slot = iota(fresh.shape, 0)
        step = (iota(fresh.shape, 1) // GROUP) % steps
        seen = (slot < both) & (slot % rows == r) & (slot // rows <= step)
        fresh = jnp.where(seen, fresh, -jnp.inf)
        older = raw[r % 2]
        older = jnp.where(iota(older.shape, 0) < len_ref[r], older, -jnp.inf)
        top = jnp.maximum(
            jnp.max(older, axis=0, keepdims=True), jnp.max(fresh, axis=0, keepdims=True)
        )
        e_older = jnp.exp2((older - top) * rate)
        e_fresh = jnp.exp2((fresh - top) * rate)
        total = jnp.sum(e_older, axis=0, keepdims=True) + jnp.sum(e_fresh, axis=0, keepdims=True)
        inverse = 1.0 / total
        p_older = jnp.transpose((e_older * inverse).astype(BF16))
        p_fresh = jnp.transpose((e_fresh * inverse).astype(BF16))
        for k, (own, cols_k) in zip(range(0, KVH, 2), pairs):
            pair = dot(p_older[own], v_ref[r, :, cols_k]) + dot(p_fresh[own], nvs[:, cols_k])
            mixed[r, k] = pair[:pack, :HD]
            mixed[r, k + 1] = pair[pack:, HD:]

    for k in range(KVH):
        turned = jnp.stack(
            [
                mixed[r, k, t * GROUP : (t + 1) * GROUP, :]
                for t in range(steps)
                for r in range(rows)
            ]
        )
        heads = jnp.swapaxes(turned, 0, 1)
        for g in range(GROUP):
            at = (k * GROUP + g) * HD
            out_ref[:, at : at + HD] = heads[g].astype(BF16)
    for copy in store:
        copy.wait()


def attend(
    queries,
    new_keys,
    new_values,
    cache_keys,
    cache_values,
    kv_len,
    store_down,
    store_up,
    tables,
    parts,
):
    steps, rows, width = queries.shape
    cache, kv_width = cache_keys.shape[1:]
    pack = steps * GROUP
    rank_w = store_down.shape[2]
    total = parts * steps * rows
    slots = steps * MOST
    shapes = [(steps * rows, width), (width, rank_w), (width, rank_w)]
    shapes += [(slots, total), (total, parts * slots), (total, total)]
    return pl.pallas_call(
        attend_kernel,
        out_shape=[jax.ShapeDtypeStruct(shape, BF16) for shape in shapes],
        in_specs=[pl.BlockSpec(memory_space=pl.ANY)] * 11,
        out_specs=[pl.BlockSpec(memory_space=pltpu.VMEM)] * len(shapes),
        scratch_shapes=[
            pltpu.SMEM(kv_len.shape, jnp.int32),
            *[pltpu.SMEM(table.shape, jnp.int32) for table in tables],
            pltpu.VMEM(queries.shape, BF16),
            pltpu.VMEM(new_keys.shape, BF16),
            pltpu.VMEM(new_values.shape, BF16),
            pltpu.VMEM(cache_keys.shape, BF16),
            pltpu.VMEM(cache_values.shape, BF16),
            pltpu.VMEM((rows, kv_width, KVH * pack), BF16),
            pltpu.VMEM((16, kv_width), BF16),
            pltpu.VMEM((16, kv_width), BF16),
            pltpu.VMEM((2, cache, KVH * pack), F32),
            pltpu.VMEM((rows, KVH, pack, HD), F32),
            pltpu.SemaphoreType.DMA((7,)),
            pltpu.SemaphoreType.DMA((rows, 2, 2)),
            pltpu.SemaphoreType.DMA((2, 4)),
        ],
        compiler_params=pltpu.CompilerParams(vmem_limit_bytes=32 * 2**20),
        cost_estimate=pl.CostEstimate(
            flops=4 * rows * steps * HQ * cache * HD,
            bytes_accessed=4 * rows * cache * kv_width,
            transcendentals=rows * steps * HQ * cache,
        ),
        name="attend",
    )(
        *in_hbm(
            kv_len,
            queries,
            new_keys,
            new_values,
            cache_keys,
            cache_values,
            store_down,
            store_up,
            *tables,
        )
    )


def swap(x, bits, parts):
    return lax.ppermute(x, "tensor", [(i, i ^ bits) for i in range(parts)])


def gather(block, parts):
    if parts != RING:
        whole = lax.all_gather(block, "tensor")
        return [whole[i] for i in range(parts)]
    core, y, near, far = 1, 2, 4, 8
    held = {0: block}
    held[far] = swap(block, far, parts)
    held[near] = swap(block, near, parts)
    held[y] = swap(block, y, parts)
    held[near | y] = swap(block, near | y, parts)
    held[far | y] = swap(held[far], y, parts)
    held[far | near | y] = swap(held[far], near | y, parts)
    held[far | near] = swap(held[far], near, parts)
    for slot in list(held):
        held[slot | core] = swap(held[slot], core, parts)
    return [held[slot] for slot in range(parts)]


def delta_kernel(at_slot, *refs):
    (*blocks, pick_ref, d_ref, u_ref, out_ref) = refs
    blocks = [blocks[at_slot.index(i)] for i in range(len(blocks))]
    parts, slots, cols = out_ref.shape
    each, width = blocks[0].shape
    cuts = 8
    deep = width // cuts
    low = jnp.zeros((parts * each, d_ref.shape[1]), F32)
    for i in range(cuts):
        at = slice(i * deep, (i + 1) * deep)
        piece = jnp.concatenate([b[:, at] for b in blocks], axis=0)
        low = low + dot(piece, d_ref[at, :])
    chosen = dot(pick_ref[...], low.astype(BF16)).astype(BF16)
    for p, device in enumerate(exchange_order(parts)):
        at = device * cols
        out_ref[p] = dot_nt(chosen, u_ref[at : at + cols, :]).astype(BF16)


def deltas(blocks, pick, down, up):
    parts = len(blocks)
    each, width = blocks[0].shape
    slots = pick.shape[0]
    rank_w = down.shape[1]
    vmem = pl.BlockSpec(memory_space=pltpu.VMEM)
    at_slot = ORDER if parts == RING else [*range(parts)]
    return pl.pallas_call(
        functools.partial(delta_kernel, at_slot),
        out_shape=jax.ShapeDtypeStruct((parts, slots, width // parts), BF16),
        in_specs=[vmem] * (3 + parts),
        out_specs=vmem,
        compiler_params=pltpu.CompilerParams(vmem_limit_bytes=24 * 2**20),
        cost_estimate=pl.CostEstimate(
            flops=2 * (parts * each + slots) * width * rank_w,
            bytes_accessed=2 * width * (parts * each + 2 * rank_w + slots),
            transcendentals=0,
        ),
        name="delta",
    )(*[blocks[i] for i in at_slot], pick, down, up)


def base_kernel(at_slot, *refs):
    (*blocks, order_ref, w_hbm, out_ref, w_ref, sems) = refs
    blocks = [blocks[at_slot.index(i)] for i in range(len(blocks))]
    width = w_ref.shape[0]
    cuts = sems.shape[0]
    deep = width // cuts
    copies = []
    for i in range(cuts):
        at = pl.ds(i * deep, deep)
        copies.append(pltpu.make_async_copy(w_hbm.at[at], w_ref.at[at], sems.at[i]))
        copies[-1].start()
    for i in range(cuts):
        at = slice(i * deep, (i + 1) * deep)
        rows = jnp.concatenate([b[:, at] for b in blocks], axis=0)
        rows = dot(order_ref[...], rows).astype(BF16)
        copies[i].wait()
        part = dot(rows, w_ref[at, :])
        out_ref[...] = part if i == 0 else out_ref[...] + part


def base_part(blocks, out_weight, order):
    parts = len(blocks)
    total = order.shape[0]
    width, cols = out_weight.shape
    vmem = pl.BlockSpec(memory_space=pltpu.VMEM)
    at_slot = ORDER if parts == RING else [*range(parts)]
    return pl.pallas_call(
        functools.partial(base_kernel, at_slot),
        out_shape=jax.ShapeDtypeStruct((total, cols), F32),
        in_specs=[vmem] * (1 + parts) + [pl.BlockSpec(memory_space=pl.ANY)],
        out_specs=vmem,
        scratch_shapes=[pltpu.VMEM(out_weight.shape, BF16), pltpu.SemaphoreType.DMA((8,))],
        compiler_params=pltpu.CompilerParams(vmem_limit_bytes=24 * 2**20),
        cost_estimate=pl.CostEstimate(
            flops=2 * total * width * (cols + total),
            bytes_accessed=2 * width * (total + cols) + 4 * total * cols,
            transcendentals=0,
        ),
        name="base",
    )(*[blocks[i] for i in at_slot], order, *in_hbm(out_weight))


def join_kernel(base_ref, place_ref, delta_ref, out_ref):
    steps, requests, cols = out_ref.shape
    parts, slots, _ = delta_ref.shape
    delta = dot(place_ref[...], delta_ref[...].reshape(parts * slots, cols))
    result = (base_ref[...] + delta).astype(BF16)
    for t in range(steps):
        out_ref[t] = result[t * requests : (t + 1) * requests]


def join(base, place, delta, steps):
    total, cols = base.shape
    vmem = pl.BlockSpec(memory_space=pltpu.VMEM)
    return pl.pallas_call(
        join_kernel,
        out_shape=jax.ShapeDtypeStruct((steps, total // steps, cols), BF16),
        in_specs=[vmem] * 3,
        out_specs=vmem,
        compiler_params=pltpu.CompilerParams(vmem_limit_bytes=24 * 2**20),
        name="join",
    )(base, place, delta)


def per_device(
    queries,
    new_keys,
    new_values,
    cache_keys,
    cache_values,
    kv_len,
    adapter_rows,
    adapter_rank,
    adapter_owner,
    out_weight,
    store_down,
    store_up,
):
    parts = lax.axis_size("tensor")
    steps, rows, width = queries.shape
    tables = (adapter_rows, adapter_rank, adapter_owner)
    attended, down, up, pick, place, order = attend(
        queries,
        new_keys,
        new_values,
        cache_keys,
        cache_values,
        kv_len,
        store_down,
        store_up,
        tables,
        parts,
    )
    blocks = gather(attended, parts)
    send = deltas(blocks, pick, down, up)
    groups = [exchange_order(parts)]
    delta = lax.all_to_all(send, "tensor", 0, 0, axis_index_groups=groups, tiled=True)
    base = base_part(blocks, out_weight, order)
    return join(base, place, delta, steps)


def solution(mesh):
    in_specs = (
        P(None, ("groups", "tensor"), None),
        P(None, ("groups", "tensor"), None),
        P(None, ("groups", "tensor"), None),
        P(("groups", "tensor"), None, None),
        P(("groups", "tensor"), None, None),
        P(("groups", "tensor")),
        P("groups"),
        P(),
        P(),
        P(None, "tensor"),
        P("tensor", None, None),
        P("tensor", None, None),
    )
    out_specs = P(None, "groups", "tensor")
    return jax.shard_map(
        per_device, mesh=mesh, in_specs=in_specs, out_specs=out_specs, check_vma=False
    )
```

```python
import functools
import math

import jax
import jax.numpy as jnp
from jax import lax
from jax.experimental import pallas as pl
from jax.experimental.pallas import tpu as pltpu
from jax.sharding import PartitionSpec as P

HQ = 64
KVH = 8
HD = 128
GROUP = HQ // KVH
MOST = 8
RING = 16
ORDER = [0, 1, 2, 3, 4, 5, 6, 7, 8, 9, 10, 11, 12, 13, 14, 15]
EXCHANGE = [7, 6, 5, 4, 11, 10, 9, 8, 15, 14, 13, 12, 3, 2, 1, 0]
F32 = jnp.float32
BF16 = jnp.bfloat16
NT = (((1,), (1,)), ((), ()))


def in_hbm(*arrays):
    return [pltpu.with_memory_space_constraint(a, pltpu.HBM) for a in arrays]


def iota(shape, dim):
    return lax.broadcasted_iota(jnp.int32, shape, dim)


def one_hot(mask):
    return mask.astype(F32).astype(BF16)


def dot(a, b):
    return jnp.dot(a, b, preferred_element_type=F32)


def dot_nt(a, b):
    return lax.dot_general(a, b, NT, preferred_element_type=F32)


def sender(slot, me, parts):
    return me ^ slot if parts == RING else slot


def exchange_order(parts):
    return EXCHANGE if parts == RING else [*range(parts)]


def write_plan(rows, count_ref, rank_ref, owner_ref, pick_ref, place_ref, order_ref):
    me = lax.axis_index("tensor")
    slots, total = pick_ref.shape
    steps = slots // MOST
    each = steps * rows
    parts = total // each
    requests = parts * rows

    def adapter_of(block):
        first = jnp.zeros(block.shape, jnp.int32)
        amount = jnp.zeros(block.shape, jnp.int32)
        start = jnp.int32(0)
        for a in range(count_ref.shape[0]):
            owned = (owner_ref[a] <= block) & (block < owner_ref[a] + rank_ref[a])
            first = jnp.where(owned, start, first)
            amount = jnp.where(owned, count_ref[a], amount)
            start = start + count_ref[a]
        return first, amount

    def row_place(index):
        device = sender(index // each, me, parts)
        return device * rows + index % rows, (index % each) // rows

    row = iota((slots, 1), 0)
    nth = row % MOST
    first, amount = adapter_of(jnp.zeros_like(row) + me)
    request, step = row_place(iota((1, total), 1))
    pick = (request == first + nth) & (nth < amount) & (step == row // MOST)
    pick_ref[...] = one_hot(pick)

    request, step = row_place(iota((1, total), 1))
    order_ref[...] = one_hot(iota((total, total), 0) == step * requests + request)

    entry = iota((1, parts * slots), 1)
    nth = entry % MOST
    source = jnp.zeros_like(entry)
    for i, device in enumerate(exchange_order(parts)):
        source = jnp.where(entry // slots == i, device, source)
    first, amount = adapter_of(source)
    goal = jnp.where(nth < amount, (entry % slots) // MOST * requests + first + nth, -1)
    place_ref[...] = one_hot(iota((total, parts * slots), 0) == goal)


def attend_kernel(
    len_hbm, q_hbm, nk_hbm, nv_hbm, k_hbm, v_hbm, d_hbm, u_hbm, count_hbm, rank_hbm, owner_hbm,
    out_ref, d_ref, u_ref, pick_ref, place_ref, order_ref,
    len_ref, count_ref, rank_ref, owner_ref, q_ref, nk_ref, nv_ref, k_ref, v_ref, turned_q, nks, nvs, raw, mixed,
    small_sems, sems, store_sems,
):
    steps, rows, width = q_ref.shape
    cache = k_ref.shape[1]
    both = steps * rows
    pack = steps * GROUP
    cuts = sems.shape[2]

    small = [
        pltpu.make_async_copy(src, dst, small_sems.at[i])
        for i, (src, dst) in enumerate(
            (
                (q_hbm, q_ref),
                (nk_hbm, nk_ref),
                (nv_hbm, nv_ref),
                (len_hbm, len_ref),
                (count_hbm, count_ref),
                (rank_hbm, rank_ref),
                (owner_hbm, owner_ref),
            )
        )
    ]
    pieces = [pl.ds(i * (cache // cuts), cache // cuts) for i in range(cuts)]
    keys, values = [
        [
            [
                pltpu.make_async_copy(src.at[r, at], dst.at[r, at], sems.at[r, j, i])
                for i, at in enumerate(pieces)
            ]
            for r in range(rows)
        ]
        for j, (src, dst) in enumerate(((k_hbm, k_ref), (v_hbm, v_ref)))
    ]
    deep = d_ref.shape[0] // store_sems.shape[1]
    store = [
        pltpu.make_async_copy(
            src.at[0, pl.ds(i * deep, deep)], dst.at[pl.ds(i * deep, deep)], store_sems.at[j, i]
        )
        for j, (src, dst) in enumerate(((d_hbm, d_ref), (u_hbm, u_ref)))
        for i in range(store_sems.shape[1])
    ]
    queue = [keys[0], values[0], keys[1]]
    for r in range(rows):
        queue += [values[r + 1]] if r + 1 < rows else [store]
        queue += [keys[r + 2]] if r + 2 < rows else []
    for copy in small + queue[0] + queue[1] + queue[2]:
        copy.start()
    for copy in small:
        copy.wait()
    for copy in queue[3] + queue[4]:
        copy.start()
    queue = queue[5:]

    flat = jnp.concatenate([q_ref[t].astype(F32) for t in range(steps)], axis=0)
    heads = []
    for k in range(KVH):
        group = jnp.stack(
            [flat[:, (k * GROUP + g) * HD : (k * GROUP + g + 1) * HD] for g in range(GROUP)]
        )
        heads.append(jnp.swapaxes(group, 0, 1))
    column = iota((HD, KVH * pack), 1)
    for r in range(rows):
        mine = jnp.concatenate(
            [heads[k][t * rows + r] for k in range(KVH) for t in range(steps)], axis=0
        )
        mine = jnp.transpose(mine)
        for k in range(KVH):
            turned_q[r, k * HD : (k + 1) * HD, :] = jnp.where(
                column // pack == k, mine, 0.0
            ).astype(BF16)
    for src, dst in ((nk_ref, nks), (nv_ref, nvs)):
        fresh = [src[t].astype(F32) for t in range(steps)]
        fresh.append(jnp.zeros((16 - both, src.shape[2]), F32))
        dst[...] = jnp.concatenate(fresh, axis=0).astype(BF16)

    write_plan(rows, count_ref, rank_ref, owner_ref, pick_ref, place_ref, order_ref)

    rate = HD ** (-0.5) * math.log2(math.e)
    pairs = [
        (slice(k * pack, (k + 2) * pack), slice(k * HD, (k + 2) * HD)) for k in range(0, KVH, 2)
    ]
    for turn in range(rows + 1):
        if turn < rows:
            for copy in keys[turn]:
                copy.wait()
        if turn > 0:
            for copy in values[turn - 1]:
                copy.wait()
        for copies in queue[2 * turn : 2 * turn + 2]:
            for copy in copies:
                copy.start()
        if turn < rows:
            raw[turn % 2] = dot(k_ref[turn], turned_q[turn])
        if turn == 0:
            continue
        r = turn - 1
        fresh = dot(nks[...], turned_q[r])
        slot = iota(fresh.shape, 0)
        step = (iota(fresh.shape, 1) // GROUP) % steps
        seen = (slot < both) & (slot % rows == r) & (slot // rows <= step)
        fresh = jnp.where(seen, fresh, -jnp.inf)
        older = raw[r % 2]
        older = jnp.where(iota(older.shape, 0) < len_ref[r], older, -jnp.inf)
        top = jnp.maximum(
            jnp.max(older, axis=0, keepdims=True), jnp.max(fresh, axis=0, keepdims=True)
        )
        e_older = jnp.exp2((older - top) * rate)
        e_fresh = jnp.exp2((fresh - top) * rate)
        total = jnp.sum(e_older, axis=0, keepdims=True) + jnp.sum(e_fresh, axis=0, keepdims=True)
        inverse = 1.0 / total
        p_older = jnp.transpose((e_older * inverse).astype(BF16))
        p_fresh = jnp.transpose((e_fresh * inverse).astype(BF16))
        for k, (own, cols_k) in zip(range(0, KVH, 2), pairs):
            pair = dot(p_older[own], v_ref[r, :, cols_k]) + dot(p_fresh[own], nvs[:, cols_k])
            mixed[r, k] = pair[:pack, :HD]
            mixed[r, k + 1] = pair[pack:, HD:]

    for k in range(KVH):
        turned = jnp.stack(
            [
                mixed[r, k, t * GROUP : (t + 1) * GROUP, :]
                for t in range(steps)
                for r in range(rows)
            ]
        )
        heads = jnp.swapaxes(turned, 0, 1)
        for g in range(GROUP):
            at = (k * GROUP + g) * HD
            out_ref[:, at : at + HD] = heads[g].astype(BF16)
    for copy in store:
        copy.wait()


def attend(
    queries,
    new_keys,
    new_values,
    cache_keys,
    cache_values,
    kv_len,
    store_down,
    store_up,
    tables,
    parts,
):
    steps, rows, width = queries.shape
    cache, kv_width = cache_keys.shape[1:]
    pack = steps * GROUP
    rank_w = store_down.shape[2]
    total = parts * steps * rows
    slots = steps * MOST
    shapes = [(steps * rows, width), (width, rank_w), (width, rank_w)]
    shapes += [(slots, total), (total, parts * slots), (total, total)]
    return pl.pallas_call(
        attend_kernel,
        out_shape=[jax.ShapeDtypeStruct(shape, BF16) for shape in shapes],
        in_specs=[pl.BlockSpec(memory_space=pl.ANY)] * 11,
        out_specs=[pl.BlockSpec(memory_space=pltpu.VMEM)] * len(shapes),
        scratch_shapes=[
            pltpu.SMEM(kv_len.shape, jnp.int32),
            *[pltpu.SMEM(table.shape, jnp.int32) for table in tables],
            pltpu.VMEM(queries.shape, BF16),
            pltpu.VMEM(new_keys.shape, BF16),
            pltpu.VMEM(new_values.shape, BF16),
            pltpu.VMEM(cache_keys.shape, BF16),
            pltpu.VMEM(cache_values.shape, BF16),
            pltpu.VMEM((rows, kv_width, KVH * pack), BF16),
            pltpu.VMEM((16, kv_width), BF16),
            pltpu.VMEM((16, kv_width), BF16),
            pltpu.VMEM((2, cache, KVH * pack), F32),
            pltpu.VMEM((rows, KVH, pack, HD), F32),
            pltpu.SemaphoreType.DMA((7,)),
            pltpu.SemaphoreType.DMA((rows, 2, 2)),
            pltpu.SemaphoreType.DMA((2, 4)),
        ],
        compiler_params=pltpu.CompilerParams(vmem_limit_bytes=32 * 2**20),
        cost_estimate=pl.CostEstimate(
            flops=4 * rows * steps * HQ * cache * HD,
            bytes_accessed=4 * rows * cache * kv_width,
            transcendentals=rows * steps * HQ * cache,
        ),
        name="attend",
    )(
        *in_hbm(
            kv_len,
            queries,
            new_keys,
            new_values,
            cache_keys,
            cache_values,
            store_down,
            store_up,
            *tables,
        )
    )


def swap(x, bits, parts):
    return lax.ppermute(x, "tensor", [(i, i ^ bits) for i in range(parts)])


def gather(block, parts):
    if parts != RING:
        whole = lax.all_gather(block, "tensor")
        return [whole[i] for i in range(parts)]
    core, y, near, far = 1, 2, 4, 8
    held = {0: block}
    held[far] = swap(block, far, parts)
    held[near] = swap(block, near, parts)
    held[y] = swap(block, y, parts)
    held[near | y] = swap(block, near | y, parts)
    held[far | y] = swap(held[far], y, parts)
    held[far | near | y] = swap(held[far], near | y, parts)
    held[far | near] = swap(held[far], near, parts)
    for slot in list(held):
        held[slot | core] = swap(held[slot], core, parts)
    return [held[slot] for slot in range(parts)]


def delta_kernel(at_slot, *refs):
    (*blocks, pick_ref, d_ref, u_ref, out_ref) = refs
    blocks = [blocks[at_slot.index(i)] for i in range(len(blocks))]
    parts, slots, cols = out_ref.shape
    each, width = blocks[0].shape
    cuts = 8
    deep = width // cuts
    low = jnp.zeros((parts * each, d_ref.shape[1]), F32)
    for i in range(cuts):
        at = slice(i * deep, (i + 1) * deep)
        piece = jnp.concatenate([b[:, at] for b in blocks], axis=0)
        low = low + dot(piece, d_ref[at, :])
    chosen = dot(pick_ref[...], low.astype(BF16)).astype(BF16)
    for p, device in enumerate(exchange_order(parts)):
        at = device * cols
        out_ref[p] = dot_nt(chosen, u_ref[at : at + cols, :]).astype(BF16)


def deltas(blocks, pick, down, up):
    parts = len(blocks)
    each, width = blocks[0].shape
    slots = pick.shape[0]
    rank_w = down.shape[1]
    vmem = pl.BlockSpec(memory_space=pltpu.VMEM)
    at_slot = ORDER if parts == RING else [*range(parts)]
    return pl.pallas_call(
        functools.partial(delta_kernel, at_slot),
        out_shape=jax.ShapeDtypeStruct((parts, slots, width // parts), BF16),
        in_specs=[vmem] * (3 + parts),
        out_specs=vmem,
        compiler_params=pltpu.CompilerParams(vmem_limit_bytes=24 * 2**20),
        cost_estimate=pl.CostEstimate(
            flops=2 * (parts * each + slots) * width * rank_w,
            bytes_accessed=2 * width * (parts * each + 2 * rank_w + slots),
            transcendentals=0,
        ),
        name="delta",
    )(*[blocks[i] for i in at_slot], pick, down, up)


def base_kernel(at_slot, *refs):
    (*blocks, order_ref, w_hbm, out_ref, w_ref, sems) = refs
    blocks = [blocks[at_slot.index(i)] for i in range(len(blocks))]
    width = w_ref.shape[0]
    cuts = sems.shape[0]
    deep = width // cuts
    copies = []
    for i in range(cuts):
        at = pl.ds(i * deep, deep)
        copies.append(pltpu.make_async_copy(w_hbm.at[at], w_ref.at[at], sems.at[i]))
        copies[-1].start()
    for i in range(cuts):
        at = slice(i * deep, (i + 1) * deep)
        rows = jnp.concatenate([b[:, at] for b in blocks], axis=0)
        rows = dot(order_ref[...], rows).astype(BF16)
        copies[i].wait()
        part = dot(rows, w_ref[at, :])
        out_ref[...] = part if i == 0 else out_ref[...] + part


def base_part(blocks, out_weight, order):
    parts = len(blocks)
    total = order.shape[0]
    width, cols = out_weight.shape
    vmem = pl.BlockSpec(memory_space=pltpu.VMEM)
    at_slot = ORDER if parts == RING else [*range(parts)]
    return pl.pallas_call(
        functools.partial(base_kernel, at_slot),
        out_shape=jax.ShapeDtypeStruct((total, cols), F32),
        in_specs=[vmem] * (1 + parts) + [pl.BlockSpec(memory_space=pl.ANY)],
        out_specs=vmem,
        scratch_shapes=[pltpu.VMEM(out_weight.shape, BF16), pltpu.SemaphoreType.DMA((8,))],
        compiler_params=pltpu.CompilerParams(vmem_limit_bytes=24 * 2**20),
        cost_estimate=pl.CostEstimate(
            flops=2 * total * width * (cols + total),
            bytes_accessed=2 * width * (total + cols) + 4 * total * cols,
            transcendentals=0,
        ),
        name="base",
    )(*[blocks[i] for i in at_slot], order, *in_hbm(out_weight))


def join_kernel(base_ref, place_ref, delta_ref, out_ref):
    steps, requests, cols = out_ref.shape
    parts, slots, _ = delta_ref.shape
    delta = dot(place_ref[...], delta_ref[...].reshape(parts * slots, cols))
    result = (base_ref[...] + delta).astype(BF16)
    for t in range(steps):
        out_ref[t] = result[t * requests : (t + 1) * requests]


def join(base, place, delta, steps):
    total, cols = base.shape
    vmem = pl.BlockSpec(memory_space=pltpu.VMEM)
    return pl.pallas_call(
        join_kernel,
        out_shape=jax.ShapeDtypeStruct((steps, total // steps, cols), BF16),
        in_specs=[vmem] * 3,
        out_specs=vmem,
        compiler_params=pltpu.CompilerParams(vmem_limit_bytes=24 * 2**20),
        name="join",
    )(base, place, delta)


def per_device(
    queries,
    new_keys,
    new_values,
    cache_keys,
    cache_values,
    kv_len,
    adapter_rows,
    adapter_rank,
    adapter_owner,
    out_weight,
    store_down,
    store_up,
):
    parts = lax.axis_size("tensor")
    steps, rows, width = queries.shape
    tables = (adapter_rows, adapter_rank, adapter_owner)
    attended, down, up, pick, place, order = attend(
        queries,
        new_keys,
        new_values,
        cache_keys,
        cache_values,
        kv_len,
        store_down,
        store_up,
        tables,
        parts,
    )
    blocks = gather(attended, parts)
    send = deltas(blocks, pick, down, up)
    groups = [exchange_order(parts)]
    delta = lax.all_to_all(send, "tensor", 0, 0, axis_index_groups=groups, tiled=True)
    base = base_part(blocks, out_weight, order)
    return join(base, place, delta, steps)


def solution(mesh):
    in_specs = (
        P(None, ("groups", "tensor"), None),
        P(None, ("groups", "tensor"), None),
        P(None, ("groups", "tensor"), None),
        P(("groups", "tensor"), None, None),
        P(("groups", "tensor"), None, None),
        P(("groups", "tensor")),
        P("groups"),
        P(),
        P(),
        P(None, "tensor"),
        P("tensor", None, None),
        P("tensor", None, None),
    )
    out_specs = P(None, "groups", "tensor")
    return jax.shard_map(
        per_device, mesh=mesh, in_specs=in_specs, out_specs=out_specs, check_vma=False
    )
```

```python
import functools
import math

import jax
import jax.numpy as jnp
from jax import lax
from jax.experimental import pallas as pl
from jax.experimental.pallas import tpu as pltpu
from jax.sharding import PartitionSpec as P

HQ = 64
KVH = 8
HD = 128
GROUP = HQ // KVH
MOST = 8
RING = 16
ORDER = [0, 1, 2, 3, 4, 5, 6, 7, 8, 9, 14, 15, 12, 13, 10, 11]
EXCHANGE = [11, 10, 9, 8, 15, 14, 13, 12, 7, 6, 5, 4, 3, 2, 1, 0]
F32 = jnp.float32
BF16 = jnp.bfloat16
NT = (((1,), (1,)), ((), ()))


def in_hbm(*arrays):
    return [pltpu.with_memory_space_constraint(a, pltpu.HBM) for a in arrays]


def iota(shape, dim):
    return lax.broadcasted_iota(jnp.int32, shape, dim)


def one_hot(mask):
    return mask.astype(F32).astype(BF16)


def dot(a, b):
    return jnp.dot(a, b, preferred_element_type=F32)


def dot_nt(a, b):
    return lax.dot_general(a, b, NT, preferred_element_type=F32)


def sender(slot, me, parts):
    return me ^ slot if parts == RING else slot


def exchange_order(parts):
    return EXCHANGE if parts == RING else [*range(parts)]


def write_plan(rows, count_ref, rank_ref, owner_ref, pick_ref, place_ref, order_ref):
    me = lax.axis_index("tensor")
    slots, total = pick_ref.shape
    steps = slots // MOST
    each = steps * rows
    parts = total // each
    requests = parts * rows

    def adapter_of(block):
        first = jnp.zeros(block.shape, jnp.int32)
        amount = jnp.zeros(block.shape, jnp.int32)
        start = jnp.int32(0)
        for a in range(count_ref.shape[0]):
            owned = (owner_ref[a] <= block) & (block < owner_ref[a] + rank_ref[a])
            first = jnp.where(owned, start, first)
            amount = jnp.where(owned, count_ref[a], amount)
            start = start + count_ref[a]
        return first, amount

    def row_place(index):
        device = sender(index // each, me, parts)
        return device * rows + index % rows, (index % each) // rows

    row = iota((slots, 1), 0)
    nth = row % MOST
    first, amount = adapter_of(jnp.zeros_like(row) + me)
    request, step = row_place(iota((1, total), 1))
    pick = (request == first + nth) & (nth < amount) & (step == row // MOST)
    pick_ref[...] = one_hot(pick)

    request, step = row_place(iota((1, total), 1))
    order_ref[...] = one_hot(iota((total, total), 0) == step * requests + request)

    entry = iota((1, parts * slots), 1)
    nth = entry % MOST
    source = jnp.zeros_like(entry)
    for i, device in enumerate(exchange_order(parts)):
        source = jnp.where(entry // slots == i, device, source)
    first, amount = adapter_of(source)
    goal = jnp.where(nth < amount, (entry % slots) // MOST * requests + first + nth, -1)
    place_ref[...] = one_hot(iota((total, parts * slots), 0) == goal)


def attend_kernel(
    len_hbm, q_hbm, nk_hbm, nv_hbm, k_hbm, v_hbm, d_hbm, u_hbm, count_hbm, rank_hbm, owner_hbm,
    out_ref, d_ref, u_ref, pick_ref, place_ref, order_ref,
    len_ref, count_ref, rank_ref, owner_ref, q_ref, nk_ref, nv_ref, k_ref, v_ref, turned_q, nks, nvs, raw, mixed,
    small_sems, sems, store_sems,
):
    steps, rows, width = q_ref.shape
    cache = k_ref.shape[1]
    both = steps * rows
    pack = steps * GROUP
    cuts = sems.shape[2]

    small = [
        pltpu.make_async_copy(src, dst, small_sems.at[i])
        for i, (src, dst) in enumerate(
            (
                (q_hbm, q_ref),
                (nk_hbm, nk_ref),
                (nv_hbm, nv_ref),
                (len_hbm, len_ref),
                (count_hbm, count_ref),
                (rank_hbm, rank_ref),
                (owner_hbm, owner_ref),
            )
        )
    ]
    pieces = [pl.ds(i * (cache // cuts), cache // cuts) for i in range(cuts)]
    keys, values = [
        [
            [
                pltpu.make_async_copy(src.at[r, at], dst.at[r, at], sems.at[r, j, i])
                for i, at in enumerate(pieces)
            ]
            for r in range(rows)
        ]
        for j, (src, dst) in enumerate(((k_hbm, k_ref), (v_hbm, v_ref)))
    ]
    deep = d_ref.shape[0] // store_sems.shape[1]
    store = [
        pltpu.make_async_copy(
            src.at[0, pl.ds(i * deep, deep)], dst.at[pl.ds(i * deep, deep)], store_sems.at[j, i]
        )
        for j, (src, dst) in enumerate(((d_hbm, d_ref), (u_hbm, u_ref)))
        for i in range(store_sems.shape[1])
    ]
    queue = [keys[0], values[0], keys[1]]
    for r in range(rows):
        queue += [values[r + 1]] if r + 1 < rows else [store]
        queue += [keys[r + 2]] if r + 2 < rows else []
    for copy in small + queue[0] + queue[1] + queue[2]:
        copy.start()
    for copy in small:
        copy.wait()
    for copy in queue[3] + queue[4]:
        copy.start()
    queue = queue[5:]

    flat = jnp.concatenate([q_ref[t].astype(F32) for t in range(steps)], axis=0)
    heads = []
    for k in range(KVH):
        group = jnp.stack(
            [flat[:, (k * GROUP + g) * HD : (k * GROUP + g + 1) * HD] for g in range(GROUP)]
        )
        heads.append(jnp.swapaxes(group, 0, 1))
    column = iota((HD, KVH * pack), 1)
    for r in range(rows):
        mine = jnp.concatenate(
            [heads[k][t * rows + r] for k in range(KVH) for t in range(steps)], axis=0
        )
        mine = jnp.transpose(mine)
        for k in range(KVH):
            turned_q[r, k * HD : (k + 1) * HD, :] = jnp.where(
                column // pack == k, mine, 0.0
            ).astype(BF16)
    for src, dst in ((nk_ref, nks), (nv_ref, nvs)):
        fresh = [src[t].astype(F32) for t in range(steps)]
        fresh.append(jnp.zeros((16 - both, src.shape[2]), F32))
        dst[...] = jnp.concatenate(fresh, axis=0).astype(BF16)

    write_plan(rows, count_ref, rank_ref, owner_ref, pick_ref, place_ref, order_ref)

    rate = HD ** (-0.5) * math.log2(math.e)
    pairs = [
        (slice(k * pack, (k + 2) * pack), slice(k * HD, (k + 2) * HD)) for k in range(0, KVH, 2)
    ]
    for turn in range(rows + 1):
        if turn < rows:
            for copy in keys[turn]:
                copy.wait()
        if turn > 0:
            for copy in values[turn - 1]:
                copy.wait()
        for copies in queue[2 * turn : 2 * turn + 2]:
            for copy in copies:
                copy.start()
        if turn < rows:
            raw[turn % 2] = dot(k_ref[turn], turned_q[turn])
        if turn == 0:
            continue
        r = turn - 1
        fresh = dot(nks[...], turned_q[r])
        slot = iota(fresh.shape, 0)
        step = (iota(fresh.shape, 1) // GROUP) % steps
        seen = (slot < both) & (slot % rows == r) & (slot // rows <= step)
        fresh = jnp.where(seen, fresh, -jnp.inf)
        older = raw[r % 2]
        older = jnp.where(iota(older.shape, 0) < len_ref[r], older, -jnp.inf)
        top = jnp.maximum(
            jnp.max(older, axis=0, keepdims=True), jnp.max(fresh, axis=0, keepdims=True)
        )
        e_older = jnp.exp2((older - top) * rate)
        e_fresh = jnp.exp2((fresh - top) * rate)
        total = jnp.sum(e_older, axis=0, keepdims=True) + jnp.sum(e_fresh, axis=0, keepdims=True)
        inverse = 1.0 / total
        p_older = jnp.transpose((e_older * inverse).astype(BF16))
        p_fresh = jnp.transpose((e_fresh * inverse).astype(BF16))
        for k, (own, cols_k) in zip(range(0, KVH, 2), pairs):
            pair = dot(p_older[own], v_ref[r, :, cols_k]) + dot(p_fresh[own], nvs[:, cols_k])
            mixed[r, k] = pair[:pack, :HD]
            mixed[r, k + 1] = pair[pack:, HD:]

    for k in range(KVH):
        turned = jnp.stack(
            [
                mixed[r, k, t * GROUP : (t + 1) * GROUP, :]
                for t in range(steps)
                for r in range(rows)
            ]
        )
        heads = jnp.swapaxes(turned, 0, 1)
        for g in range(GROUP):
            at = (k * GROUP + g) * HD
            out_ref[:, at : at + HD] = heads[g].astype(BF16)
    for copy in store:
        copy.wait()


def attend(
    queries,
    new_keys,
    new_values,
    cache_keys,
    cache_values,
    kv_len,
    store_down,
    store_up,
    tables,
    parts,
):
    steps, rows, width = queries.shape
    cache, kv_width = cache_keys.shape[1:]
    pack = steps * GROUP
    rank_w = store_down.shape[2]
    total = parts * steps * rows
    slots = steps * MOST
    shapes = [(steps * rows, width), (width, rank_w), (width, rank_w)]
    shapes += [(slots, total), (total, parts * slots), (total, total)]
    return pl.pallas_call(
        attend_kernel,
        out_shape=[jax.ShapeDtypeStruct(shape, BF16) for shape in shapes],
        in_specs=[pl.BlockSpec(memory_space=pl.ANY)] * 11,
        out_specs=[pl.BlockSpec(memory_space=pltpu.VMEM)] * len(shapes),
        scratch_shapes=[
            pltpu.SMEM(kv_len.shape, jnp.int32),
            *[pltpu.SMEM(table.shape, jnp.int32) for table in tables],
            pltpu.VMEM(queries.shape, BF16),
            pltpu.VMEM(new_keys.shape, BF16),
            pltpu.VMEM(new_values.shape, BF16),
            pltpu.VMEM(cache_keys.shape, BF16),
            pltpu.VMEM(cache_values.shape, BF16),
            pltpu.VMEM((rows, kv_width, KVH * pack), BF16),
            pltpu.VMEM((16, kv_width), BF16),
            pltpu.VMEM((16, kv_width), BF16),
            pltpu.VMEM((2, cache, KVH * pack), F32),
            pltpu.VMEM((rows, KVH, pack, HD), F32),
            pltpu.SemaphoreType.DMA((7,)),
            pltpu.SemaphoreType.DMA((rows, 2, 2)),
            pltpu.SemaphoreType.DMA((2, 4)),
        ],
        compiler_params=pltpu.CompilerParams(vmem_limit_bytes=32 * 2**20),
        cost_estimate=pl.CostEstimate(
            flops=4 * rows * steps * HQ * cache * HD,
            bytes_accessed=4 * rows * cache * kv_width,
            transcendentals=rows * steps * HQ * cache,
        ),
        name="attend",
    )(
        *in_hbm(
            kv_len,
            queries,
            new_keys,
            new_values,
            cache_keys,
            cache_values,
            store_down,
            store_up,
            *tables,
        )
    )


def swap(x, bits, parts):
    return lax.ppermute(x, "tensor", [(i, i ^ bits) for i in range(parts)])


def gather(block, parts):
    if parts != RING:
        whole = lax.all_gather(block, "tensor")
        return [whole[i] for i in range(parts)]
    core, y, near, far = 1, 2, 4, 8
    held = {0: block}
    held[far] = swap(block, far, parts)
    held[near] = swap(block, near, parts)
    held[y] = swap(block, y, parts)
    held[near | y] = swap(block, near | y, parts)
    held[far | y] = swap(held[far], y, parts)
    held[far | near | y] = swap(held[far], near | y, parts)
    held[far | near] = swap(held[far], near, parts)
    for slot in list(held):
        held[slot | core] = swap(held[slot], core, parts)
    return [held[slot] for slot in range(parts)]


def delta_kernel(at_slot, *refs):
    (*blocks, pick_ref, d_ref, u_ref, out_ref) = refs
    blocks = [blocks[at_slot.index(i)] for i in range(len(blocks))]
    parts, slots, cols = out_ref.shape
    each, width = blocks[0].shape
    cuts = 8
    deep = width // cuts
    low = jnp.zeros((parts * each, d_ref.shape[1]), F32)
    for i in range(cuts):
        at = slice(i * deep, (i + 1) * deep)
        piece = jnp.concatenate([b[:, at] for b in blocks], axis=0)
        low = low + dot(piece, d_ref[at, :])
    chosen = dot(pick_ref[...], low.astype(BF16)).astype(BF16)
    for p, device in enumerate(exchange_order(parts)):
        at = device * cols
        out_ref[p] = dot_nt(chosen, u_ref[at : at + cols, :]).astype(BF16)


def deltas(blocks, pick, down, up):
    parts = len(blocks)
    each, width = blocks[0].shape
    slots = pick.shape[0]
    rank_w = down.shape[1]
    vmem = pl.BlockSpec(memory_space=pltpu.VMEM)
    at_slot = ORDER if parts == RING else [*range(parts)]
    return pl.pallas_call(
        functools.partial(delta_kernel, at_slot),
        out_shape=jax.ShapeDtypeStruct((parts, slots, width // parts), BF16),
        in_specs=[vmem] * (3 + parts),
        out_specs=vmem,
        compiler_params=pltpu.CompilerParams(vmem_limit_bytes=24 * 2**20),
        cost_estimate=pl.CostEstimate(
            flops=2 * (parts * each + slots) * width * rank_w,
            bytes_accessed=2 * width * (parts * each + 2 * rank_w + slots),
            transcendentals=0,
        ),
        name="delta",
    )(*[blocks[i] for i in at_slot], pick, down, up)


def base_kernel(at_slot, *refs):
    (*blocks, order_ref, w_hbm, out_ref, w_ref, sems) = refs
    blocks = [blocks[at_slot.index(i)] for i in range(len(blocks))]
    width = w_ref.shape[0]
    cuts = sems.shape[0]
    deep = width // cuts
    copies = []
    for i in range(cuts):
        at = pl.ds(i * deep, deep)
        copies.append(pltpu.make_async_copy(w_hbm.at[at], w_ref.at[at], sems.at[i]))
        copies[-1].start()
    for i in range(cuts):
        at = slice(i * deep, (i + 1) * deep)
        rows = jnp.concatenate([b[:, at] for b in blocks], axis=0)
        rows = dot(order_ref[...], rows).astype(BF16)
        copies[i].wait()
        part = dot(rows, w_ref[at, :])
        out_ref[...] = part if i == 0 else out_ref[...] + part


def base_part(blocks, out_weight, order):
    parts = len(blocks)
    total = order.shape[0]
    width, cols = out_weight.shape
    vmem = pl.BlockSpec(memory_space=pltpu.VMEM)
    at_slot = ORDER if parts == RING else [*range(parts)]
    return pl.pallas_call(
        functools.partial(base_kernel, at_slot),
        out_shape=jax.ShapeDtypeStruct((total, cols), F32),
        in_specs=[vmem] * (1 + parts) + [pl.BlockSpec(memory_space=pl.ANY)],
        out_specs=vmem,
        scratch_shapes=[pltpu.VMEM(out_weight.shape, BF16), pltpu.SemaphoreType.DMA((8,))],
        compiler_params=pltpu.CompilerParams(vmem_limit_bytes=24 * 2**20),
        cost_estimate=pl.CostEstimate(
            flops=2 * total * width * (cols + total),
            bytes_accessed=2 * width * (total + cols) + 4 * total * cols,
            transcendentals=0,
        ),
        name="base",
    )(*[blocks[i] for i in at_slot], order, *in_hbm(out_weight))


def join_kernel(base_ref, place_ref, delta_ref, out_ref):
    steps, requests, cols = out_ref.shape
    parts, slots, _ = delta_ref.shape
    delta = dot(place_ref[...], delta_ref[...].reshape(parts * slots, cols))
    result = (base_ref[...] + delta).astype(BF16)
    for t in range(steps):
        out_ref[t] = result[t * requests : (t + 1) * requests]


def join(base, place, delta, steps):
    total, cols = base.shape
    vmem = pl.BlockSpec(memory_space=pltpu.VMEM)
    return pl.pallas_call(
        join_kernel,
        out_shape=jax.ShapeDtypeStruct((steps, total // steps, cols), BF16),
        in_specs=[vmem] * 3,
        out_specs=vmem,
        compiler_params=pltpu.CompilerParams(vmem_limit_bytes=24 * 2**20),
        name="join",
    )(base, place, delta)


def per_device(
    queries,
    new_keys,
    new_values,
    cache_keys,
    cache_values,
    kv_len,
    adapter_rows,
    adapter_rank,
    adapter_owner,
    out_weight,
    store_down,
    store_up,
):
    parts = lax.axis_size("tensor")
    steps, rows, width = queries.shape
    tables = (adapter_rows, adapter_rank, adapter_owner)
    attended, down, up, pick, place, order = attend(
        queries,
        new_keys,
        new_values,
        cache_keys,
        cache_values,
        kv_len,
        store_down,
        store_up,
        tables,
        parts,
    )
    blocks = gather(attended, parts)
    send = deltas(blocks, pick, down, up)
    groups = [exchange_order(parts)]
    delta = lax.all_to_all(send, "tensor", 0, 0, axis_index_groups=groups, tiled=True)
    base = base_part(blocks, out_weight, order)
    return join(base, place, delta, steps)


def solution(mesh):
    in_specs = (
        P(None, ("groups", "tensor"), None),
        P(None, ("groups", "tensor"), None),
        P(None, ("groups", "tensor"), None),
        P(("groups", "tensor"), None, None),
        P(("groups", "tensor"), None, None),
        P(("groups", "tensor")),
        P("groups"),
        P(),
        P(),
        P(None, "tensor"),
        P("tensor", None, None),
        P("tensor", None, None),
    )
    out_specs = P(None, "groups", "tensor")
    return jax.shard_map(
        per_device, mesh=mesh, in_specs=in_specs, out_specs=out_specs, check_vma=False
    )
```

```python
import functools
import math

import jax
import jax.numpy as jnp
from jax import lax
from jax.experimental import pallas as pl
from jax.experimental.pallas import tpu as pltpu
from jax.sharding import PartitionSpec as P

HQ = 64
KVH = 8
HD = 128
GROUP = HQ // KVH
MOST = 8
RING = 16
ORDER = [0, 1, 2, 3, 4, 5, 6, 7, 8, 9, 10, 11, 12, 13, 14, 15]
EXCHANGE = [10, 11, 8, 9, 14, 15, 12, 13, 6, 7, 4, 5, 2, 3, 0, 1]
F32 = jnp.float32
BF16 = jnp.bfloat16
NT = (((1,), (1,)), ((), ()))


def in_hbm(*arrays):
    return [pltpu.with_memory_space_constraint(a, pltpu.HBM) for a in arrays]


def iota(shape, dim):
    return lax.broadcasted_iota(jnp.int32, shape, dim)


def one_hot(mask):
    return mask.astype(F32).astype(BF16)


def dot(a, b):
    return jnp.dot(a, b, preferred_element_type=F32)


def dot_nt(a, b):
    return lax.dot_general(a, b, NT, preferred_element_type=F32)


def sender(slot, me, parts):
    return me ^ slot if parts == RING else slot


def exchange_order(parts):
    return EXCHANGE if parts == RING else [*range(parts)]


def write_plan(rows, count_ref, rank_ref, owner_ref, pick_ref, place_ref, order_ref):
    me = lax.axis_index("tensor")
    slots, total = pick_ref.shape
    steps = slots // MOST
    each = steps * rows
    parts = total // each
    requests = parts * rows

    def adapter_of(block):
        first = jnp.zeros(block.shape, jnp.int32)
        amount = jnp.zeros(block.shape, jnp.int32)
        start = jnp.int32(0)
        for a in range(count_ref.shape[0]):
            owned = (owner_ref[a] <= block) & (block < owner_ref[a] + rank_ref[a])
            first = jnp.where(owned, start, first)
            amount = jnp.where(owned, count_ref[a], amount)
            start = start + count_ref[a]
        return first, amount

    def row_place(index):
        device = sender(index // each, me, parts)
        return device * rows + index % rows, (index % each) // rows

    row = iota((slots, 1), 0)
    nth = row % MOST
    first, amount = adapter_of(jnp.zeros_like(row) + me)
    request, step = row_place(iota((1, total), 1))
    pick = (request == first + nth) & (nth < amount) & (step == row // MOST)
    pick_ref[...] = one_hot(pick)

    request, step = row_place(iota((1, total), 1))
    order_ref[...] = one_hot(iota((total, total), 0) == step * requests + request)

    entry = iota((1, parts * slots), 1)
    nth = entry % MOST
    source = jnp.zeros_like(entry)
    for i, device in enumerate(exchange_order(parts)):
        source = jnp.where(entry // slots == i, device, source)
    first, amount = adapter_of(source)
    goal = jnp.where(nth < amount, (entry % slots) // MOST * requests + first + nth, -1)
    place_ref[...] = one_hot(iota((total, parts * slots), 0) == goal)


def attend_kernel(
    len_hbm, q_hbm, nk_hbm, nv_hbm, k_hbm, v_hbm, d_hbm, u_hbm, count_hbm, rank_hbm, owner_hbm,
    out_ref, d_ref, u_ref, pick_ref, place_ref, order_ref,
    len_ref, count_ref, rank_ref, owner_ref, q_ref, nk_ref, nv_ref, k_ref, v_ref, turned_q, nks, nvs, raw, mixed,
    small_sems, sems, store_sems,
):
    steps, rows, width = q_ref.shape
    cache = k_ref.shape[1]
    both = steps * rows
    pack = steps * GROUP
    cuts = sems.shape[2]

    small = [
        pltpu.make_async_copy(src, dst, small_sems.at[i])
        for i, (src, dst) in enumerate(
            (
                (q_hbm, q_ref),
                (nk_hbm, nk_ref),
                (nv_hbm, nv_ref),
                (len_hbm, len_ref),
                (count_hbm, count_ref),
                (rank_hbm, rank_ref),
                (owner_hbm, owner_ref),
            )
        )
    ]
    pieces = [pl.ds(i * (cache // cuts), cache // cuts) for i in range(cuts)]
    keys, values = [
        [
            [
                pltpu.make_async_copy(src.at[r, at], dst.at[r, at], sems.at[r, j, i])
                for i, at in enumerate(pieces)
            ]
            for r in range(rows)
        ]
        for j, (src, dst) in enumerate(((k_hbm, k_ref), (v_hbm, v_ref)))
    ]
    deep = d_ref.shape[0] // store_sems.shape[1]
    store = [
        pltpu.make_async_copy(
            src.at[0, pl.ds(i * deep, deep)], dst.at[pl.ds(i * deep, deep)], store_sems.at[j, i]
        )
        for j, (src, dst) in enumerate(((d_hbm, d_ref), (u_hbm, u_ref)))
        for i in range(store_sems.shape[1])
    ]
    queue = [keys[0], values[0], keys[1]]
    for r in range(rows):
        queue += [values[r + 1]] if r + 1 < rows else [store]
        queue += [keys[r + 2]] if r + 2 < rows else []
    for copy in small + queue[0] + queue[1] + queue[2]:
        copy.start()
    for copy in small:
        copy.wait()
    for copy in queue[3] + queue[4]:
        copy.start()
    queue = queue[5:]

    flat = jnp.concatenate([q_ref[t].astype(F32) for t in range(steps)], axis=0)
    heads = []
    for k in range(KVH):
        group = jnp.stack(
            [flat[:, (k * GROUP + g) * HD : (k * GROUP + g + 1) * HD] for g in range(GROUP)]
        )
        heads.append(jnp.swapaxes(group, 0, 1))
    column = iota((HD, KVH * pack), 1)
    for r in range(rows):
        mine = jnp.concatenate(
            [heads[k][t * rows + r] for k in range(KVH) for t in range(steps)], axis=0
        )
        mine = jnp.transpose(mine)
        for k in range(KVH):
            turned_q[r, k * HD : (k + 1) * HD, :] = jnp.where(
                column // pack == k, mine, 0.0
            ).astype(BF16)
    for src, dst in ((nk_ref, nks), (nv_ref, nvs)):
        fresh = [src[t].astype(F32) for t in range(steps)]
        fresh.append(jnp.zeros((16 - both, src.shape[2]), F32))
        dst[...] = jnp.concatenate(fresh, axis=0).astype(BF16)

    write_plan(rows, count_ref, rank_ref, owner_ref, pick_ref, place_ref, order_ref)

    rate = HD ** (-0.5) * math.log2(math.e)
    pairs = [
        (slice(k * pack, (k + 2) * pack), slice(k * HD, (k + 2) * HD)) for k in range(0, KVH, 2)
    ]
    for turn in range(rows + 1):
        if turn < rows:
            for copy in keys[turn]:
                copy.wait()
        if turn > 0:
            for copy in values[turn - 1]:
                copy.wait()
        for copies in queue[2 * turn : 2 * turn + 2]:
            for copy in copies:
                copy.start()
        if turn < rows:
            raw[turn % 2] = dot(k_ref[turn], turned_q[turn])
        if turn == 0:
            continue
        r = turn - 1
        fresh = dot(nks[...], turned_q[r])
        slot = iota(fresh.shape, 0)
        step = (iota(fresh.shape, 1) // GROUP) % steps
        seen = (slot < both) & (slot % rows == r) & (slot // rows <= step)
        fresh = jnp.where(seen, fresh, -jnp.inf)
        older = raw[r % 2]
        older = jnp.where(iota(older.shape, 0) < len_ref[r], older, -jnp.inf)
        top = jnp.maximum(
            jnp.max(older, axis=0, keepdims=True), jnp.max(fresh, axis=0, keepdims=True)
        )
        e_older = jnp.exp2((older - top) * rate)
        e_fresh = jnp.exp2((fresh - top) * rate)
        total = jnp.sum(e_older, axis=0, keepdims=True) + jnp.sum(e_fresh, axis=0, keepdims=True)
        inverse = 1.0 / total
        p_older = jnp.transpose((e_older * inverse).astype(BF16))
        p_fresh = jnp.transpose((e_fresh * inverse).astype(BF16))
        for k, (own, cols_k) in zip(range(0, KVH, 2), pairs):
            pair = dot(p_older[own], v_ref[r, :, cols_k]) + dot(p_fresh[own], nvs[:, cols_k])
            mixed[r, k] = pair[:pack, :HD]
            mixed[r, k + 1] = pair[pack:, HD:]

    for k in range(KVH):
        turned = jnp.stack(
            [
                mixed[r, k, t * GROUP : (t + 1) * GROUP, :]
                for t in range(steps)
                for r in range(rows)
            ]
        )
        heads = jnp.swapaxes(turned, 0, 1)
        for g in range(GROUP):
            at = (k * GROUP + g) * HD
            out_ref[:, at : at + HD] = heads[g].astype(BF16)
    for copy in store:
        copy.wait()


def attend(
    queries,
    new_keys,
    new_values,
    cache_keys,
    cache_values,
    kv_len,
    store_down,
    store_up,
    tables,
    parts,
):
    steps, rows, width = queries.shape
    cache, kv_width = cache_keys.shape[1:]
    pack = steps * GROUP
    rank_w = store_down.shape[2]
    total = parts * steps * rows
    slots = steps * MOST
    shapes = [(steps * rows, width), (width, rank_w), (width, rank_w)]
    shapes += [(slots, total), (total, parts * slots), (total, total)]
    return pl.pallas_call(
        attend_kernel,
        out_shape=[jax.ShapeDtypeStruct(shape, BF16) for shape in shapes],
        in_specs=[pl.BlockSpec(memory_space=pl.ANY)] * 11,
        out_specs=[pl.BlockSpec(memory_space=pltpu.VMEM)] * len(shapes),
        scratch_shapes=[
            pltpu.SMEM(kv_len.shape, jnp.int32),
            *[pltpu.SMEM(table.shape, jnp.int32) for table in tables],
            pltpu.VMEM(queries.shape, BF16),
            pltpu.VMEM(new_keys.shape, BF16),
            pltpu.VMEM(new_values.shape, BF16),
            pltpu.VMEM(cache_keys.shape, BF16),
            pltpu.VMEM(cache_values.shape, BF16),
            pltpu.VMEM((rows, kv_width, KVH * pack), BF16),
            pltpu.VMEM((16, kv_width), BF16),
            pltpu.VMEM((16, kv_width), BF16),
            pltpu.VMEM((2, cache, KVH * pack), F32),
            pltpu.VMEM((rows, KVH, pack, HD), F32),
            pltpu.SemaphoreType.DMA((7,)),
            pltpu.SemaphoreType.DMA((rows, 2, 2)),
            pltpu.SemaphoreType.DMA((2, 4)),
        ],
        compiler_params=pltpu.CompilerParams(vmem_limit_bytes=32 * 2**20),
        cost_estimate=pl.CostEstimate(
            flops=4 * rows * steps * HQ * cache * HD,
            bytes_accessed=4 * rows * cache * kv_width,
            transcendentals=rows * steps * HQ * cache,
        ),
        name="attend",
    )(
        *in_hbm(
            kv_len,
            queries,
            new_keys,
            new_values,
            cache_keys,
            cache_values,
            store_down,
            store_up,
            *tables,
        )
    )


def swap(x, bits, parts):
    return lax.ppermute(x, "tensor", [(i, i ^ bits) for i in range(parts)])


def gather(block, parts):
    if parts != RING:
        whole = lax.all_gather(block, "tensor")
        return [whole[i] for i in range(parts)]
    core, y, near, far = 1, 2, 4, 8
    held = {0: block}
    held[far] = swap(block, far, parts)
    held[near] = swap(block, near, parts)
    held[y] = swap(block, y, parts)
    held[near | y] = swap(block, near | y, parts)
    held[far | y] = swap(held[far], y, parts)
    held[far | near | y] = swap(held[far], near | y, parts)
    held[far | near] = swap(held[far], near, parts)
    for slot in list(held):
        held[slot | core] = swap(held[slot], core, parts)
    return [held[slot] for slot in range(parts)]


def delta_kernel(at_slot, *refs):
    (*blocks, pick_ref, d_ref, u_ref, out_ref) = refs
    blocks = [blocks[at_slot.index(i)] for i in range(len(blocks))]
    parts, slots, cols = out_ref.shape
    each, width = blocks[0].shape
    cuts = 8
    deep = width // cuts
    low = jnp.zeros((parts * each, d_ref.shape[1]), F32)
    for i in range(cuts):
        at = slice(i * deep, (i + 1) * deep)
        piece = jnp.concatenate([b[:, at] for b in blocks], axis=0)
        low = low + dot(piece, d_ref[at, :])
    chosen = dot(pick_ref[...], low.astype(BF16)).astype(BF16)
    for p, device in enumerate(exchange_order(parts)):
        at = device * cols
        out_ref[p] = dot_nt(chosen, u_ref[at : at + cols, :]).astype(BF16)


def deltas(blocks, pick, down, up):
    parts = len(blocks)
    each, width = blocks[0].shape
    slots = pick.shape[0]
    rank_w = down.shape[1]
    vmem = pl.BlockSpec(memory_space=pltpu.VMEM)
    at_slot = ORDER if parts == RING else [*range(parts)]
    return pl.pallas_call(
        functools.partial(delta_kernel, at_slot),
        out_shape=jax.ShapeDtypeStruct((parts, slots, width // parts), BF16),
        in_specs=[vmem] * (3 + parts),
        out_specs=vmem,
        compiler_params=pltpu.CompilerParams(vmem_limit_bytes=24 * 2**20),
        cost_estimate=pl.CostEstimate(
            flops=2 * (parts * each + slots) * width * rank_w,
            bytes_accessed=2 * width * (parts * each + 2 * rank_w + slots),
            transcendentals=0,
        ),
        name="delta",
    )(*[blocks[i] for i in at_slot], pick, down, up)


def base_kernel(at_slot, *refs):
    (*blocks, order_ref, w_hbm, out_ref, w_ref, sems) = refs
    blocks = [blocks[at_slot.index(i)] for i in range(len(blocks))]
    width = w_ref.shape[0]
    cuts = sems.shape[0]
    deep = width // cuts
    copies = []
    for i in range(cuts):
        at = pl.ds(i * deep, deep)
        copies.append(pltpu.make_async_copy(w_hbm.at[at], w_ref.at[at], sems.at[i]))
        copies[-1].start()
    for i in range(cuts):
        at = slice(i * deep, (i + 1) * deep)
        rows = jnp.concatenate([b[:, at] for b in blocks], axis=0)
        rows = dot(order_ref[...], rows).astype(BF16)
        copies[i].wait()
        part = dot(rows, w_ref[at, :])
        out_ref[...] = part if i == 0 else out_ref[...] + part


def base_part(blocks, out_weight, order):
    parts = len(blocks)
    total = order.shape[0]
    width, cols = out_weight.shape
    vmem = pl.BlockSpec(memory_space=pltpu.VMEM)
    at_slot = ORDER if parts == RING else [*range(parts)]
    return pl.pallas_call(
        functools.partial(base_kernel, at_slot),
        out_shape=jax.ShapeDtypeStruct((total, cols), F32),
        in_specs=[vmem] * (1 + parts) + [pl.BlockSpec(memory_space=pl.ANY)],
        out_specs=vmem,
        scratch_shapes=[pltpu.VMEM(out_weight.shape, BF16), pltpu.SemaphoreType.DMA((8,))],
        compiler_params=pltpu.CompilerParams(vmem_limit_bytes=24 * 2**20),
        cost_estimate=pl.CostEstimate(
            flops=2 * total * width * (cols + total),
            bytes_accessed=2 * width * (total + cols) + 4 * total * cols,
            transcendentals=0,
        ),
        name="base",
    )(*[blocks[i] for i in at_slot], order, *in_hbm(out_weight))


def join_kernel(base_ref, place_ref, delta_ref, out_ref):
    steps, requests, cols = out_ref.shape
    parts, slots, _ = delta_ref.shape
    delta = dot(place_ref[...], delta_ref[...].reshape(parts * slots, cols))
    result = (base_ref[...] + delta).astype(BF16)
    for t in range(steps):
        out_ref[t] = result[t * requests : (t + 1) * requests]


def join(base, place, delta, steps):
    total, cols = base.shape
    vmem = pl.BlockSpec(memory_space=pltpu.VMEM)
    return pl.pallas_call(
        join_kernel,
        out_shape=jax.ShapeDtypeStruct((steps, total // steps, cols), BF16),
        in_specs=[vmem] * 3,
        out_specs=vmem,
        compiler_params=pltpu.CompilerParams(vmem_limit_bytes=24 * 2**20),
        name="join",
    )(base, place, delta)


def per_device(
    queries,
    new_keys,
    new_values,
    cache_keys,
    cache_values,
    kv_len,
    adapter_rows,
    adapter_rank,
    adapter_owner,
    out_weight,
    store_down,
    store_up,
):
    parts = lax.axis_size("tensor")
    steps, rows, width = queries.shape
    tables = (adapter_rows, adapter_rank, adapter_owner)
    attended, down, up, pick, place, order = attend(
        queries,
        new_keys,
        new_values,
        cache_keys,
        cache_values,
        kv_len,
        store_down,
        store_up,
        tables,
        parts,
    )
    blocks = gather(attended, parts)
    send = deltas(blocks, pick, down, up)
    groups = [exchange_order(parts)]
    delta = lax.all_to_all(send, "tensor", 0, 0, axis_index_groups=groups, tiled=True)
    base = base_part(blocks, out_weight, order)
    return join(base, place, delta, steps)


def solution(mesh):
    in_specs = (
        P(None, ("groups", "tensor"), None),
        P(None, ("groups", "tensor"), None),
        P(None, ("groups", "tensor"), None),
        P(("groups", "tensor"), None, None),
        P(("groups", "tensor"), None, None),
        P(("groups", "tensor")),
        P("groups"),
        P(),
        P(),
        P(None, "tensor"),
        P("tensor", None, None),
        P("tensor", None, None),
    )
    out_specs = P(None, "groups", "tensor")
    return jax.shard_map(
        per_device, mesh=mesh, in_specs=in_specs, out_specs=out_specs, check_vma=False
    )
```
